32 devices in a mesh: dp: 8 (over z, y), tp: 4 (over x, core).
Axes of the slice: x: 2, y: 2, z: 4, core: 2. Of those that a mesh axis runs over, the one named last changes fastest.
Arguments:
- x_in: bfloat16 [1024, 8, 768], P('tp', 'dp'), may hold values from -6 to 6
- segments: int32 [1024, 8], P(None, 'dp'), may hold values from 0 to 4, as said below
- w_qkv: bfloat16 [2, 768, 2304], replicated, may hold values from -0.21875 to 0.21875
- w_out: bfloat16 [2, 768, 768], replicated, may hold values from -0.875 to 0.875
- mix_pre: float32 [2, 12, 12], replicated, may hold values from -1.75 to 1.75
- mix_post: float32 [2, 12, 12], replicated, may hold values from -1.75 to 1.75
- gain_attn: float32 [2, 768], replicated, may hold values from 0.5 to 1.5
- gain_ffn: float32 [2, 768], replicated, may hold values from 0.5 to 1.5
- w_in: bfloat16 [2, 768, 3072], P(None, None, 'tp'), may hold values from -0.21875 to 0.21875
- w_down: bfloat16 [2, 3072, 768], P(None, 'tp'), may hold values from -0.109375 to 0.109375
- cotangent: bfloat16 [1024, 8, 768], P('tp', 'dp'), may hold values from -6 to 6
Outputs:
- y_out: bfloat16 [1024, 8, 768], P('tp', 'dp')
- grad_x: float32 [1024, 8, 768], P('tp', 'dp')
- grad_qkv: float32 [2, 768, 2304], replicated
- grad_out: float32 [2, 768, 768], replicated
- grad_mix_pre: float32 [2, 12, 12], replicated
- grad_mix_post: float32 [2, 12, 12], replicated
- grad_gain_attn: float32 [2, 768], replicated
- grad_gain_ffn: float32 [2, 768], replicated
- grad_in: float32 [2, 768, 3072], P(None, 'dp', 'tp')
- grad_down: float32 [2, 3072, 768], P(None, 'tp', 'dp')
The draws below stay inside these ranges and needn't reach their ends.
Inputs may be any that keep to these rules, and one draw needn't show every extreme that they name: `segments`: along each sequence the ids start at 0 and rise by one at the first position of each document; every sequence holds five documents.
All inputs are finite; a program needn't handle non-finite values.
Results may differ from the reference program's by a relative error of at most 0.035.
Values may be sent and summed in bfloat16 or wider, within the bound.
No kernel may reach another device: no remote copies, remote signals or barrier semaphores. Data moves between devices by JAX's collectives and lax.ppermute only.
A program may use at most 256 MiB of HBM per device.

```python
import jax
import jax.numpy as jnp
from jax import lax

D = 768
H = 12
DH = 64
FF = 3072
LAYERS = 2
L = 1024
SEQ_DEV = 1
SEQS = 8


def draw_segments(key, part):
    key = jax.random.fold_in(key, 11)
    first_key, second_key, third_key = jax.random.split(key, 3)
    quarter = L // 4
    eighth = L // 8
    sixteenth = L // 16
    offsets = jax.random.randint(first_key, (SEQS, 4), 0, quarter - 1)
    normal_cuts = jnp.arange(4, dtype=jnp.int32)[None, :] * quarter + 1 + offsets
    long_offsets = jax.random.randint(third_key, (SEQS, 4), 0, sixteenth)
    long_base = jnp.array([1, sixteenth + 1, L - eighth, L - sixteenth], dtype=jnp.int32)
    long_cuts = long_base[None, :] + long_offsets
    chosen_slot = jax.random.randint(second_key, (SEQS // SEQ_DEV,), 0, SEQ_DEV)
    local_slot = jnp.arange(SEQS, dtype=jnp.int32) % SEQ_DEV
    chosen = local_slot == jnp.repeat(chosen_slot, SEQ_DEV)
    cut_points = jnp.where(chosen[:, None], long_cuts, normal_cuts)
    positions = jnp.arange(L, dtype=jnp.int32)
    seg_ids = jnp.sum((positions[:, None, None] >= cut_points[None, :, :]).astype(jnp.int32), -1)
    return seg_ids.astype(jnp.int32)


def steps_of(rng, dims, shards, smallest, largest):
    factor_of = 1.0
    for dim, blocks in shards:
        steps = jax.random.uniform(jax.random.fold_in(jax.random.fold_in(rng, 6), dim), (blocks,), jnp.float32, smallest / len(shards), largest / len(shards))
        factor_of = factor_of * jnp.repeat(jnp.exp(steps), dims[dim] // blocks).reshape((-1,) + (1,) * (len(dims) - 1 - dim))
    return factor_of


def centred(key, extent, scale, bound, pieces=(), held_as=jnp.bfloat16):
    result = scale * jax.random.normal(key, extent, jnp.float32)
    if pieces:
        result = result * steps_of(key, extent, pieces, -0.22, 0.18)
    return jnp.clip(result, -bound, bound).astype(held_as)


def setup_inputs(seed: int = 0) -> dict:
    key_list = jax.random.split(jax.random.key(seed), 12)
    x_in = centred(key_list[0], (L, SEQS, D), 1.0, 6.0, ((0, 4), (1, 8)))
    segments = draw_segments(jax.random.fold_in(key_list[11], 71), 0)
    w_qkv = centred(key_list[2], (LAYERS, D, 3 * D), D ** -0.5, 0.21875)
    w_out = centred(key_list[3], (LAYERS, D, D), (D // 16) ** -0.5, 0.875)
    mix_pre = centred(key_list[4], (LAYERS, H, H), H ** -0.5, 1.75, (), jnp.float32)
    mix_post = centred(key_list[5], (LAYERS, H, H), H ** -0.5, 1.75, (), jnp.float32)
    gain_attn = jnp.clip(1.0 + 0.1 * jax.random.normal(key_list[6], (LAYERS, D), jnp.float32), 0.5, 1.5)
    gain_ffn = jnp.clip(1.0 + 0.1 * jax.random.normal(key_list[7], (LAYERS, D), jnp.float32), 0.5, 1.5)
    w_in = centred(key_list[8], (LAYERS, D, FF), D ** -0.5, 0.21875, ((2, 4),))
    w_down = centred(key_list[9], (LAYERS, FF, D), FF ** -0.5, 0.109375, ((1, 4),))
    cotangent = centred(key_list[10], (L, SEQS, D), 1.0, 6.0, ((0, 4), (1, 8)))
    return dict(x_in=x_in, segments=segments, w_qkv=w_qkv, w_out=w_out, mix_pre=mix_pre, mix_post=mix_post, gain_attn=gain_attn, gain_ffn=gain_ffn, w_in=w_in, w_down=w_down, cotangent=cotangent)


EPSILON = 1e-06
HIGHEST = lax.Precision.HIGHEST
NEGATIVE = -1e+30

@jax.custom_vjp
def low(v):
    return lax.optimization_barrier(v.astype(jnp.bfloat16)).astype(jnp.float32)

@jax.custom_vjp
def low_back(v):
    return v

def low_keep(v):
    return (low(v), None)

def low_pass(kept, grad):
    return (grad,)

def back_keep(v):
    return (v, None)

def back_low(kept, grad):
    return (low(grad),)
low.defvjp(low_keep, low_pass)
low_back.defvjp(back_keep, back_low)

def rms_scale(values, gain_vec):
    return values * lax.rsqrt(lax.optimization_barrier(jnp.mean(values * values, -1, keepdims=True)) + EPSILON) * gain_vec

def gelu_exact(values):
    return jax.nn.gelu(values, approximate=False)

def one_layer(stream, allowed, w_qkv, w_out, mix_pre, mix_post, gain_attn, gain_ffn, w_in, w_down):
    length = stream.shape[0]
    group_size = stream.shape[1]
    normed = low_back(low(rms_scale(stream, gain_attn)))
    packed = jnp.einsum('isd,de->ise', normed, w_qkv, precision=HIGHEST)
    queries = low_back(low(packed[..., :D])).reshape(length, group_size, H, DH)
    keys = low_back(low(packed[..., D:2 * D])).reshape(length, group_size, H, DH)
    values = low_back(low(packed[..., 2 * D:])).reshape(length, group_size, H, DH)
    scores = low_back(jnp.einsum('ishd,jshd->shij', queries, keys, precision=HIGHEST) * DH ** (-0.5))
    mixed = jnp.einsum('hg,shij->sgij', mix_pre, scores, precision=HIGHEST)
    attend = jax.nn.softmax(jnp.where(allowed[:, None], mixed, NEGATIVE), axis=-1)
    post_mix = low(jnp.einsum('gk,sgij->skij', mix_post, attend, precision=HIGHEST))
    context = jnp.einsum('shij,jshd->ishd', post_mix, values, precision=HIGHEST)
    context = low_back(low(context.reshape(length, group_size, D)))
    middle = stream + low_back(jnp.einsum('isd,de->ise', context, w_out, precision=HIGHEST))
    normed_ffn = low_back(low(rms_scale(middle, gain_ffn)))
    preact = low_back(jnp.einsum('isd,df->isf', normed_ffn, w_in, precision=HIGHEST))
    hidden = low(gelu_exact(preact))
    return middle + low_back(jnp.einsum('isf,fd->isd', hidden, w_down, precision=HIGHEST))

def reference(x_in, segments, w_qkv, w_out, mix_pre, mix_post, gain_attn, gain_ffn, w_in, w_down, cotangent):
    params = (w_qkv.astype(jnp.float32), w_out.astype(jnp.float32), mix_pre.astype(jnp.float32), mix_post.astype(jnp.float32), gain_attn.astype(jnp.float32), gain_ffn.astype(jnp.float32), w_in.astype(jnp.float32), w_down.astype(jnp.float32))
    groups = SEQS // 2

    def regroup(values):
        return jnp.moveaxis(values.reshape((L, groups, 2) + values.shape[2:]), 1, 0)

    def ungroup(values):
        return jnp.moveaxis(values, 0, 1).reshape((L, SEQS) + values.shape[3:])
    streams = regroup(x_in.astype(jnp.float32))
    seg_groups = regroup(segments)
    cot_groups = regroup(cotangent.astype(jnp.float32))
    positions = jnp.arange(L, dtype=jnp.int32)
    causal = positions[None, :] <= positions[:, None]

    def group_step(totals, group_item):
        stream, seg_ids, cot_group = group_item
        allowed = (seg_ids.T[:, :, None] == seg_ids.T[:, None, :]) & causal[None]

        def network(start_stream, weights):
            for layer_idx in range(LAYERS):
                start_stream = one_layer(start_stream, allowed, weights[0][layer_idx], weights[1][layer_idx], weights[2][layer_idx], weights[3][layer_idx], weights[4][layer_idx], weights[5][layer_idx], weights[6][layer_idx], weights[7][layer_idx])
            return start_stream
        outputs, pullback = jax.vjp(network, stream, params)
        grad_stream, grad_params = pullback(cot_group)
        totals = jax.tree.map(jnp.add, totals, grad_params)
        return (totals, (outputs, grad_stream))
    totals, (outputs, grads) = lax.scan(group_step, jax.tree.map(jnp.zeros_like, params), (streams, seg_groups, cot_groups))
    return (ungroup(outputs).astype(jnp.bfloat16), ungroup(grads), totals[0], totals[1], totals[2], totals[3], totals[4], totals[5], totals[6], totals[7])
```

```python
import functools

import jax
import jax.numpy as jnp
from jax import lax
from jax.experimental import pallas as pl
from jax.experimental.pallas import tpu as pltpu
from jax.sharding import PartitionSpec as P

LAYERS = 2
EPSILON = 1e-06
NEGATIVE = -1e30
LOG2E = 1.4426950408889634
GP = 2
VMEM = 60 * 1024 * 1024
F32 = jnp.float32
BF16 = jnp.bfloat16


def dot_nn(a, b):
    return lax.dot_general(a, b, (((1,), (0,)), ((), ())), preferred_element_type=F32)


def dot_nt(a, b):
    return lax.dot_general(a, b, (((1,), (1,)), ((), ())), preferred_element_type=F32)


def dot_tn(a, b):
    return lax.dot_general(a, b, (((0,), (0,)), ((), ())), preferred_element_type=F32)


def rms(values, gain):
    return values * lax.rsqrt(jnp.mean(values * values, -1, keepdims=True) + EPSILON) * gain


def rms_back(grad, values, gain):
    inv = lax.rsqrt(jnp.mean(values * values, -1, keepdims=True) + EPSILON)
    unit = values * inv
    scaled = grad * gain
    grad_values = (scaled - unit * jnp.mean(scaled * unit, -1, keepdims=True)) * inv
    return grad_values, jnp.sum(grad * unit, axis=0)


def whole(shape):
    return pl.BlockSpec(shape, lambda *_: (0,) * len(shape))


def layer_of(array, layer):
    shape = array.shape[1:]
    return pl.BlockSpec((1,) + shape, lambda *_: (layer,) + (0,) * len(shape))


def attn_fwd_body(blocks, heads, *refs):
    n_refs = refs[:blocks]
    (x_ref, wqkv_ref, wout_ref, apre_ref, apost_ref, gain_ref, qpos_ref, qseg_ref, kpos_ref, kseg_ref) = refs[
        blocks : blocks + 10
    ]
    p_ref, u_ref, q_ref, k_ref, v_ref, o_ref, xm_ref, n2_ref, bias_ref, acc_ref = refs[blocks + 10 :]
    step = pl.program_id(0)
    rows, width = x_ref.shape

    @pl.when(step == 0)
    def _():
        q_ref[...] = dot_nn(n_refs[0][...], wqkv_ref[0, :, :width]).astype(BF16)
        for r in range(blocks):
            here = pl.ds(r * rows, rows)
            k_ref[here, :] = dot_nn(n_refs[r][...], wqkv_ref[0, :, width : 2 * width]).astype(BF16)
            v_ref[here, :] = dot_nn(n_refs[r][...], wqkv_ref[0, :, 2 * width :]).astype(BF16)
        ok = (qseg_ref[...] == kseg_ref[...]) & (kpos_ref[...] <= qpos_ref[...])
        bias_ref[...] = jnp.where(ok, 0.0, NEGATIVE)
        acc_ref[...] = jnp.zeros_like(acc_ref)

    q = q_ref[...].astype(F32)
    for u in range(GP):
        g = step * GP + u
        qm = (q * apre_ref[pl.ds(g, 1), :]).astype(BF16)
        m = dot_nt(qm, k_ref[...]) + bias_ref[...]
        e = jnp.exp2(m - jnp.max(m, -1, keepdims=True))
        p = (e * (1.0 / jnp.sum(e, -1, keepdims=True))).astype(BF16)
        p_ref[u] = p
        ctx = dot_nn(p, v_ref[...])
        u_ref[u] = ctx.astype(BF16)
        acc_ref[...] += ctx * apost_ref[pl.ds(g, 1), :]

    @pl.when(step == pl.num_programs(0) - 1)
    def _():
        o = acc_ref[...].astype(BF16)
        o_ref[...] = o
        xm = x_ref[...] + dot_nn(o, wout_ref[0])
        xm_ref[...] = xm
        n2_ref[...] = rms(xm, gain_ref[...]).astype(BF16)


def attn_fwd(layer, n_blocks, x, w_qkv, w_out, apre, apost, gain, where):
    rows, width = x.shape
    blocks = len(n_blocks)
    heads = apre.shape[0]
    keys = rows * blocks
    args = (*n_blocks, x, w_qkv, w_out, apre, apost, gain, *where)
    in_specs = [whole(a.shape) for a in args]
    in_specs[blocks + 1] = layer_of(w_qkv, layer)
    in_specs[blocks + 2] = layer_of(w_out, layer)
    out = [
        ((heads, rows, keys), BF16),
        ((heads, rows, width), BF16),
        ((rows, width), BF16),
        ((keys, width), BF16),
        ((keys, width), BF16),
        ((rows, width), BF16),
        ((rows, width), F32),
        ((rows, width), BF16),
    ]
    out_specs = [whole(s) for s, _ in out]
    out_specs[0] = pl.BlockSpec((GP, rows, keys), lambda i: (i, 0, 0))
    out_specs[1] = pl.BlockSpec((GP, rows, width), lambda i: (i, 0, 0))
    return pl.pallas_call(
        functools.partial(attn_fwd_body, blocks, heads),
        grid=(heads // GP,),
        in_specs=in_specs,
        out_specs=out_specs,
        out_shape=[jax.ShapeDtypeStruct(s, d) for s, d in out],
        scratch_shapes=[pltpu.VMEM((rows, keys), F32), pltpu.VMEM((rows, width), F32)],
        compiler_params=pltpu.CompilerParams(vmem_limit_bytes=VMEM),
        cost_estimate=pl.CostEstimate(
            flops=2 * rows * keys * width * heads * 2, bytes_accessed=20_000_000, transcendentals=rows * keys * heads
        ),
        name="attn_fwd",
    )(*args)


def attn_bwd_body(heads, *refs):
    (ga_ref, wout_ref, q_ref, k_ref, v_ref, p_ref, u_ref, apre_ref, apost_ref, apret_ref, apostt_ref) = refs[:11]
    gq_ref, gkt_ref, gvt_ref, zpre_ref, zpost_ref = refs[11:16]
    go_ref, got_ref, qt_ref, gq_acc, gk_acc, gv_acc = refs[16:]
    step = pl.program_id(0)

    @pl.when(step == 0)
    def _():
        go = dot_nt(ga_ref[...], wout_ref[0]).astype(BF16).astype(F32)
        go_ref[...] = go
        got_ref[...] = go.T
        qt_ref[...] = q_ref[...].astype(F32).T
        gq_acc[...] = jnp.zeros_like(gq_acc)
        gk_acc[...] = jnp.zeros_like(gk_acc)
        gv_acc[...] = jnp.zeros_like(gv_acc)

    go = go_ref[...]
    q = q_ref[...].astype(F32)
    lane = lax.broadcasted_iota(jnp.int32, apret_ref.shape, 1)
    gms, ps, qms, gos = [], [], [], []
    for u in range(GP):
        g = step * GP + u
        g_mix = go * apost_ref[pl.ds(g, 1), :]
        gp = dot_nt(g_mix.astype(BF16), v_ref[...])
        ctx = u_ref[u].astype(F32)
        zpost_ref[pl.ds(g, 1), :] = jnp.sum(ctx * go, axis=0, keepdims=True)
        delta = jnp.sum(ctx * g_mix, axis=1, keepdims=True)
        p = p_ref[u]
        gm = (p.astype(F32) * (gp - delta)).astype(BF16)
        t = dot_nn(gm, k_ref[...])
        zpre_ref[pl.ds(g, 1), :] = jnp.sum(t * q, axis=0, keepdims=True)
        gq_acc[...] += t * apre_ref[pl.ds(g, 1), :]
        qms.append((qt_ref[...] * jnp.sum(jnp.where(lane == g, apret_ref[...], 0.0), 1, keepdims=True)).astype(BF16))
        gos.append((got_ref[...] * jnp.sum(jnp.where(lane == g, apostt_ref[...], 0.0), 1, keepdims=True)).astype(BF16))
        gms.append(gm)
        ps.append(p)
    gk_acc[...] += dot_nn(jnp.concatenate(qms, 1), jnp.concatenate(gms, 0))
    gv_acc[...] += dot_nn(jnp.concatenate(gos, 1), jnp.concatenate(ps, 0))

    @pl.when(step == pl.num_programs(0) - 1)
    def _():
        gq_ref[...] = gq_acc[...].astype(BF16)
        gkt_ref[...] = gk_acc[...].astype(BF16)
        gvt_ref[...] = gv_acc[...].astype(BF16)


def attn_bwd(layer, ga, w_out, q, k, v, p, u, apre, apost, apret, apostt):
    rows, width = q.shape
    keys = k.shape[0]
    heads = p.shape[0]
    args = (ga, w_out, q, k, v, p, u, apre, apost, apret, apostt)
    in_specs = [whole(a.shape) for a in args]
    in_specs[1] = layer_of(w_out, layer)
    in_specs[5] = pl.BlockSpec((GP, rows, keys), lambda i: (i, 0, 0))
    in_specs[6] = pl.BlockSpec((GP, rows, width), lambda i: (i, 0, 0))
    out = [
        ((rows, width), BF16),
        ((width, keys), BF16),
        ((width, keys), BF16),
        ((heads, width), F32),
        ((heads, width), F32),
    ]
    return pl.pallas_call(
        functools.partial(attn_bwd_body, heads),
        grid=(heads // GP,),
        in_specs=in_specs,
        out_specs=[whole(s) for s, _ in out],
        out_shape=[jax.ShapeDtypeStruct(s, d) for s, d in out],
        scratch_shapes=[
            pltpu.VMEM((rows, width), F32),
            pltpu.VMEM((width, rows), F32),
            pltpu.VMEM((width, rows), F32),
            pltpu.VMEM((rows, width), F32),
            pltpu.VMEM((width, keys), F32),
            pltpu.VMEM((width, keys), F32),
        ],
        compiler_params=pltpu.CompilerParams(vmem_limit_bytes=VMEM),
        cost_estimate=pl.CostEstimate(
            flops=2 * rows * keys * width * heads * 4, bytes_accessed=20_000_000, transcendentals=0
        ),
        name="attn_bwd",
    )(*args)


def ffn_fwd_body(blocks, *refs):
    n_refs = refs[:blocks]
    win_ref, wdown_ref = refs[blocks : blocks + 2]
    out_refs = refs[blocks + 2 : 2 * blocks + 2]
    hid_ref, dgelu_ref = refs[2 * blocks + 2 :]
    rows = n_refs[0].shape[0]
    for r in range(blocks):
        here = pl.ds(r * rows, rows)
        pre = dot_nn(n_refs[r][...], win_ref[0])
        cdf = 0.5 + 0.5 * lax.erf(pre * (0.5**0.5))
        hid = (pre * cdf).astype(BF16)
        hid_ref[here, :] = hid
        density = jnp.exp2(pre * pre * (-0.5 * LOG2E)) * 0.3989422804014327
        dgelu_ref[here, :] = (cdf + pre * density).astype(BF16)
        out_refs[r][...] = dot_nn(hid, wdown_ref[0]).astype(BF16)


def ffn_fwd(layer, n_blocks, w_in, w_down):
    blocks = len(n_blocks)
    rows, width = n_blocks[0].shape
    hidden = w_in.shape[2]
    args = (*n_blocks, w_in, w_down)
    in_specs = [whole(a.shape) for a in args]
    in_specs[blocks] = layer_of(w_in, layer)
    in_specs[blocks + 1] = layer_of(w_down, layer)
    out = [((rows, width), BF16)] * blocks + [((rows * blocks, hidden), BF16)] * 2
    res = pl.pallas_call(
        functools.partial(ffn_fwd_body, blocks),
        grid=(1,),
        in_specs=in_specs,
        out_specs=[whole(s) for s, _ in out],
        out_shape=[jax.ShapeDtypeStruct(s, d) for s, d in out],
        compiler_params=pltpu.CompilerParams(vmem_limit_bytes=VMEM),
        cost_estimate=pl.CostEstimate(
            flops=4 * rows * blocks * width * hidden, bytes_accessed=6_000_000, transcendentals=rows * blocks * hidden
        ),
        name="ffn_fwd",
    )(*args)
    return res[:blocks], res[blocks], res[blocks + 1]


def ffn_bwd_body(blocks, *refs):
    g_refs = refs[:blocks]
    dgelu_ref, win_ref, wdown_ref = refs[blocks : blocks + 3]
    out_refs = refs[blocks + 3 : 2 * blocks + 3]
    gpre_ref = refs[2 * blocks + 3]
    rows = g_refs[0].shape[0]
    for r in range(blocks):
        here = pl.ds(r * rows, rows)
        gh = dot_nt(g_refs[r][...], wdown_ref[0])
        gpre = (gh * dgelu_ref[here, :].astype(F32)).astype(BF16)
        gpre_ref[here, :] = gpre
        out_refs[r][...] = dot_nt(gpre, win_ref[0]).astype(BF16)


def ffn_bwd(layer, g_blocks, dgelu, w_in, w_down):
    blocks = len(g_blocks)
    rows, width = g_blocks[0].shape
    hidden = w_in.shape[2]
    args = (*g_blocks, dgelu, w_in, w_down)
    in_specs = [whole(a.shape) for a in args]
    in_specs[blocks + 1] = layer_of(w_in, layer)
    in_specs[blocks + 2] = layer_of(w_down, layer)
    out = [((rows, width), BF16)] * blocks + [((rows * blocks, hidden), BF16)]
    res = pl.pallas_call(
        functools.partial(ffn_bwd_body, blocks),
        grid=(1,),
        in_specs=in_specs,
        out_specs=[whole(s) for s, _ in out],
        out_shape=[jax.ShapeDtypeStruct(s, d) for s, d in out],
        compiler_params=pltpu.CompilerParams(vmem_limit_bytes=VMEM),
        cost_estimate=pl.CostEstimate(
            flops=4 * rows * blocks * width * hidden, bytes_accessed=6_000_000, transcendentals=0
        ),
        name="ffn_bwd",
    )(*args)
    return res[:blocks], res[blocks]


def swap(value, axis, bit):
    size = lax.axis_size(axis)
    return lax.ppermute(value, axis, [(i, i ^ bit) for i in range(size)])


def gather_blocks(value):
    blocks = [value]
    bit = 1
    while bit < lax.axis_size("tp"):
        blocks += [swap(b, "tp", bit) for b in blocks]
        bit *= 2
    return blocks


def scatter_sum(blocks):
    blocks = list(blocks)
    bit = 1
    while bit < lax.axis_size("tp"):
        size = len(blocks)
        keep = [blocks[r] for r in range(size) if not r & 1]
        sent = [swap(blocks[r], "tp", bit) for r in range(size) if r & 1]
        blocks = [a.astype(F32) + b.astype(F32) for a, b in zip(keep, sent)]
        bit *= 2
        if bit < lax.axis_size("tp"):
            blocks = [blocks[0]] + [b.astype(BF16) for b in blocks[1:]]
    return blocks[0]


def butterfly(value):
    for axis in ("tp", "dp"):
        bit = 1
        while bit < lax.axis_size(axis):
            value = value + swap(value, axis, bit)
            bit *= 2
    return value


def on_device(
    x_in, segments, w_qkv, w_out, mix_pre, mix_post, gain_attn, gain_ffn, w_in, w_down, cotangent
):
    rows, _, width = x_in.shape
    heads = mix_pre.shape[1]
    head_size = width // heads
    tp_size = lax.axis_size("tp")
    dp_size = lax.axis_size("dp")
    tp_index = lax.axis_index("tp")
    seg = segments[:, 0]
    span = jnp.arange(rows, dtype=jnp.int32)
    kpos = jnp.concatenate([(tp_index ^ r) * rows + span for r in range(tp_size)])
    kseg = jnp.concatenate([lax.dynamic_slice_in_dim(seg, (tp_index ^ r) * rows, rows, 0) for r in range(tp_size)])
    where = (kpos[:rows, None], kseg[:rows, None], kpos[None, :], kseg[None, :])

    pre_rows = jnp.repeat(jnp.swapaxes(mix_pre, 1, 2), head_size, axis=2) * (head_size**-0.5)
    post_rows = jnp.repeat(mix_post, head_size, axis=2)

    def columns(table):
        return jnp.pad(table.T, ((0, 0), (0, 128 - heads)))

    grad_last = gather_blocks(cotangent[:, 0])
    stream = x_in[:, 0].astype(F32)
    kept = []
    for layer in range(LAYERS):
        n1_blocks = gather_blocks(rms(stream, gain_attn[layer]).astype(BF16))
        p, u, q, k, v, o, middle, n2 = attn_fwd(
            layer,
            n1_blocks,
            stream,
            w_qkv,
            w_out,
            pre_rows[layer] * LOG2E,
            post_rows[layer],
            gain_ffn[layer][None],
            where,
        )
        n2_blocks = gather_blocks(n2)
        half = tp_size // 2
        out_a, hid_a, dgelu_a = ffn_fwd(layer, n2_blocks[:half], w_in, w_down)
        out_b, hid_b, dgelu_b = ffn_fwd(layer, n2_blocks[half:], w_in, w_down)
        kept.append((stream, n1_blocks, p, u, q, k, v, o, middle, n2_blocks, hid_a, hid_b, dgelu_a, dgelu_b))
        stream = middle + scatter_sum([*out_a, *out_b])
    y_out = stream.astype(BF16)

    grad_flow = cotangent[:, 0].astype(F32)
    small = [None] * LAYERS
    big = [None] * LAYERS
    sharded = [None] * LAYERS
    for layer in range(LAYERS - 1, -1, -1):
        stream, n1_blocks, p, u, q, k, v, o, middle, n2_blocks, hid_a, hid_b, dgelu_a, dgelu_b = kept[layer]
        gf_blocks = grad_last if layer == LAYERS - 1 else gather_blocks(grad_flow.astype(BF16))
        gn2_a, gpre_a = ffn_bwd(layer, gf_blocks[:half], dgelu_a, w_in, w_down)
        gn2_b, gpre_b = ffn_bwd(layer, gf_blocks[half:], dgelu_b, w_in, w_down)
        gf_all = jnp.concatenate(gf_blocks, 0)
        n2_all = jnp.concatenate(n2_blocks, 0)
        gpre = jnp.concatenate([gpre_a, gpre_b], 0)
        hid = jnp.concatenate([hid_a, hid_b], 0)
        grad_win = dot_tn(n2_all, gpre).astype(BF16)
        grad_wdown_t = dot_tn(gf_all, hid).astype(BF16)
        per = width // dp_size
        packed = jnp.concatenate(
            [grad_win.reshape(dp_size, per, -1), grad_wdown_t.reshape(dp_size, per, -1)], 1
        ).reshape(2 * width, -1)
        summed = lax.psum_scatter(packed, "dp", scatter_dimension=0, tiled=True).astype(F32)
        sharded[layer] = (summed[:per], summed[per:].T)

        gn2 = scatter_sum([*gn2_a, *gn2_b]).astype(BF16).astype(F32)
        grad_norm, grad_gffn = rms_back(gn2, middle, gain_ffn[layer])
        grad_middle = grad_flow + grad_norm
        ga = grad_middle.astype(BF16)
        grad_wout = dot_tn(o, ga).astype(BF16)
        gq, gkt, gvt, zpre, zpost = attn_bwd(
            layer,
            ga,
            w_out,
            q,
            k,
            v,
            p,
            u,
            pre_rows[layer],
            post_rows[layer],
            columns(pre_rows[layer]),
            columns(post_rows[layer]),
        )
        n1_all = jnp.concatenate(n1_blocks, 0)
        gn1_all = lax.dot_general(
            gkt, w_qkv[layer, :, width : 2 * width], (((0,), (1,)), ((), ())), preferred_element_type=F32
        ) + lax.dot_general(gvt, w_qkv[layer, :, 2 * width :], (((0,), (1,)), ((), ())), preferred_element_type=F32)
        gn1_own = dot_nt(gq, w_qkv[layer, :, :width])
        parts = [gn1_all[r * rows : (r + 1) * rows] for r in range(tp_size)]
        parts = [(parts[0] + gn1_own).astype(BF16)] + [b.astype(BF16) for b in parts[1:]]
        grad_wq = dot_tn(n1_blocks[0], gq)
        grad_wk = lax.dot_general(n1_all, gkt, (((0,), (1,)), ((), ())), preferred_element_type=F32)
        grad_wv = lax.dot_general(n1_all, gvt, (((0,), (1,)), ((), ())), preferred_element_type=F32)
        big[layer] = lax.psum(
            jnp.concatenate([grad_wq.astype(BF16), grad_wk.astype(BF16), grad_wv.astype(BF16), grad_wout], 1),
            ("dp", "tp"),
        ).astype(F32)
        gn1 = scatter_sum(parts).astype(BF16).astype(F32)
        grad_norm, grad_gattn = rms_back(gn1, stream, gain_attn[layer])
        grad_flow = grad_middle + grad_norm
        grad_mpre = jnp.sum(zpre.reshape(heads, heads, head_size), -1).T * (head_size**-0.5)
        grad_mpost = jnp.sum(zpost.reshape(heads, heads, head_size), -1)
        small[layer] = (grad_mpre, grad_mpost, grad_gattn, grad_gffn)

    mixes = jnp.concatenate([a.reshape(-1) for s in small for a in s[:2]])
    count = mixes.shape[0]
    mix_rows = -(-count // width)
    flat = jnp.concatenate(
        [jnp.pad(mixes, (0, mix_rows * width - count)).reshape(mix_rows, width)]
        + [g[None] for s in small for g in s[2:]]
    )
    flat = jnp.pad(flat, ((0, -flat.shape[0] % 8), (0, 0)))
    flat = butterfly(flat)
    mixes = flat[:mix_rows].reshape(-1)[:count].reshape(LAYERS, 2, heads, heads)
    gains = flat[mix_rows : mix_rows + 2 * LAYERS].reshape(LAYERS, 2, width)
    return (
        y_out[:, None],
        grad_flow[:, None],
        jnp.stack([b[:, : 3 * width] for b in big]),
        jnp.stack([b[:, 3 * width :] for b in big]),
        mixes[:, 0],
        mixes[:, 1],
        gains[:, 0],
        gains[:, 1],
        jnp.stack([s[0] for s in sharded]),
        jnp.stack([s[1] for s in sharded]),
    )


def solution(mesh):
    in_specs = (
        P("tp", "dp", None),
        P(None, "dp"),
        P(),
        P(),
        P(),
        P(),
        P(),
        P(),
        P(None, None, "tp"),
        P(None, "tp", None),
        P("tp", "dp", None),
    )
    out_specs = (
        P("tp", "dp", None),
        P("tp", "dp", None),
        P(),
        P(),
        P(),
        P(),
        P(),
        P(),
        P(None, "dp", "tp"),
        P(None, "tp", "dp"),
    )
    return jax.shard_map(
        on_device, mesh=mesh, in_specs=in_specs, out_specs=out_specs, check_vma=False
    )
```

```python
import functools

import jax
import jax.numpy as jnp
from jax import lax
from jax.experimental import pallas as pl
from jax.experimental.pallas import tpu as pltpu
from jax.sharding import PartitionSpec as P

LAYERS = 2
EPSILON = 1e-06
NEGATIVE = -1e30
LOG2E = 1.4426950408889634
GP = 2
VMEM = 60 * 1024 * 1024
F32 = jnp.float32
BF16 = jnp.bfloat16


def dot_nn(a, b):
    return lax.dot_general(a, b, (((1,), (0,)), ((), ())), preferred_element_type=F32)


def dot_nt(a, b):
    return lax.dot_general(a, b, (((1,), (1,)), ((), ())), preferred_element_type=F32)


def dot_tn(a, b):
    return lax.dot_general(a, b, (((0,), (0,)), ((), ())), preferred_element_type=F32)


def rms(values, gain):
    return values * lax.rsqrt(jnp.mean(values * values, -1, keepdims=True) + EPSILON) * gain


def rms_back(grad, values, gain):
    inv = lax.rsqrt(jnp.mean(values * values, -1, keepdims=True) + EPSILON)
    unit = values * inv
    scaled = grad * gain
    grad_values = (scaled - unit * jnp.mean(scaled * unit, -1, keepdims=True)) * inv
    return grad_values, jnp.sum(grad * unit, axis=0)


def whole(shape):
    return pl.BlockSpec(shape, lambda *_: (0,) * len(shape))


def layer_of(array, layer):
    shape = array.shape[1:]
    return pl.BlockSpec((1,) + shape, lambda *_: (layer,) + (0,) * len(shape))


def attn_fwd_body(blocks, heads, layer, *refs):
    n_refs = refs[:blocks]
    x_ref, wqkv_ref, wout_ref, tab_ref, gain_ref, qinfo_ref, kinfo_ref = refs[blocks : blocks + 7]
    p_ref, u_ref, q_ref, k_ref, v_ref, o_ref, xm_ref, n2_ref, bias_ref, acc_ref = refs[blocks + 7 :]
    step = pl.program_id(0)
    rows, width = x_ref.shape

    @pl.when(step == 0)
    def _():
        q_ref[...] = dot_nn(n_refs[0][...], wqkv_ref[0, :, :width]).astype(BF16)
        for r in range(blocks):
            here = pl.ds(r * rows, rows)
            k_ref[here, :] = dot_nn(n_refs[r][...], wqkv_ref[0, :, width : 2 * width]).astype(BF16)
            v_ref[here, :] = dot_nn(n_refs[r][...], wqkv_ref[0, :, 2 * width :]).astype(BF16)
        ok = (qinfo_ref[:, 1:2] == kinfo_ref[1:2, :]) & (kinfo_ref[0:1, :] <= qinfo_ref[:, 0:1])
        bias_ref[...] = jnp.where(ok, 0.0, NEGATIVE)
        acc_ref[...] = jnp.zeros_like(acc_ref)

    q = q_ref[...].astype(F32)
    for u in range(GP):
        g = step * GP + u
        qm = (q * (tab_ref[0, pl.ds(g, 1), :] * LOG2E)).astype(BF16)
        m = dot_nt(qm, k_ref[...]) + bias_ref[...]
        e = jnp.exp2(m - jnp.max(m, -1, keepdims=True))
        p = (e * (1.0 / jnp.sum(e, -1, keepdims=True))).astype(BF16)
        p_ref[u] = p
        ctx = dot_nn(p, v_ref[...])
        u_ref[u] = ctx.astype(BF16)
        acc_ref[...] += ctx * tab_ref[0, pl.ds(heads + g, 1), :]

    @pl.when(step == pl.num_programs(0) - 1)
    def _():
        o = acc_ref[...].astype(BF16)
        o_ref[...] = o
        xm = x_ref[...] + dot_nn(o, wout_ref[0])
        xm_ref[...] = xm
        n2_ref[...] = rms(xm, gain_ref[pl.ds(layer, 1), :]).astype(BF16)


def attn_fwd(layer, n_blocks, x, w_qkv, w_out, tab, gain, where):
    rows, width = x.shape
    blocks = len(n_blocks)
    heads = tab.shape[1] // 2
    keys = rows * blocks
    args = (*n_blocks, x, w_qkv, w_out, tab, gain, *where)
    in_specs = [whole(a.shape) for a in args]
    in_specs[blocks + 1] = layer_of(w_qkv, layer)
    in_specs[blocks + 2] = layer_of(w_out, layer)
    in_specs[blocks + 3] = layer_of(tab, layer)
    out = [
        ((heads, rows, keys), BF16),
        ((heads, rows, width), BF16),
        ((rows, width), BF16),
        ((keys, width), BF16),
        ((keys, width), BF16),
        ((rows, width), BF16),
        ((rows, width), F32),
        ((rows, width), BF16),
    ]
    out_specs = [whole(s) for s, _ in out]
    out_specs[0] = pl.BlockSpec((GP, rows, keys), lambda i: (i, 0, 0))
    out_specs[1] = pl.BlockSpec((GP, rows, width), lambda i: (i, 0, 0))
    return pl.pallas_call(
        functools.partial(attn_fwd_body, blocks, heads, layer),
        grid=(heads // GP,),
        in_specs=in_specs,
        out_specs=out_specs,
        out_shape=[jax.ShapeDtypeStruct(s, d) for s, d in out],
        scratch_shapes=[pltpu.VMEM((rows, keys), F32), pltpu.VMEM((rows, width), F32)],
        compiler_params=pltpu.CompilerParams(vmem_limit_bytes=VMEM),
        cost_estimate=pl.CostEstimate(
            flops=2 * rows * keys * width * heads * 2, bytes_accessed=20_000_000, transcendentals=rows * keys * heads
        ),
        name="attn_fwd",
    )(*args)


def attn_bwd_body(heads, blocks, layer, *refs):
    (ga_ref, wout_ref, q_ref, k_ref, v_ref, p_ref, u_ref, tab_ref, tabt_ref, half_ref) = refs[:10]
    wqkv_hbm, n1t_hbm, ot_hbm = refs[10:13]
    gn1_refs = refs[13 : 13 + blocks]
    (ak_ref, as_ref, bk_ref, bs_ref, zpre_ref, zpost_ref) = refs[13 + blocks : 19 + blocks]
    go_ref, got_ref, qt_ref, gq_acc, gk_acc, gv_acc, wqkv_ref, n1t_ref, ot_ref, sems = refs[19 + blocks :]
    step = pl.program_id(0)
    rows, width = q_ref.shape
    half = width // 2

    late = [
        pltpu.make_async_copy(wqkv_hbm.at[layer], wqkv_ref, sems.at[0]),
        pltpu.make_async_copy(n1t_hbm, n1t_ref, sems.at[1]),
        pltpu.make_async_copy(ot_hbm, ot_ref, sems.at[2]),
    ]

    @pl.when(step == 0)
    def _():
        for copy in late:
            copy.start()
        go = dot_nt(ga_ref[...], wout_ref[0]).astype(BF16).astype(F32)
        go_ref[...] = go
        got_ref[...] = go.T
        qt_ref[...] = q_ref[...].astype(F32).T
        gq_acc[...] = jnp.zeros_like(gq_acc)
        gk_acc[...] = jnp.zeros_like(gk_acc)
        gv_acc[...] = jnp.zeros_like(gv_acc)

    go = go_ref[...]
    q = q_ref[...].astype(F32)
    lane = lax.broadcasted_iota(jnp.int32, tabt_ref.shape[1:], 1)
    gms, ps, qms, gos = [], [], [], []
    for u in range(GP):
        g = step * GP + u
        g_mix = go * tab_ref[0, pl.ds(heads + g, 1), :]
        gp = dot_nt(g_mix.astype(BF16), v_ref[...])
        ctx = u_ref[u].astype(F32)
        zpost_ref[pl.ds(g, 1), :] = jnp.sum(ctx * go, axis=0, keepdims=True)
        delta = jnp.sum(ctx * g_mix, axis=1, keepdims=True)
        p = p_ref[u]
        gm = (p.astype(F32) * (gp - delta)).astype(BF16)
        t = dot_nn(gm, k_ref[...])
        zpre_ref[pl.ds(g, 1), :] = jnp.sum(t * q, axis=0, keepdims=True)
        gq_acc[...] += t * tab_ref[0, pl.ds(g, 1), :]
        pre_col = jnp.sum(jnp.where(lane == g, tabt_ref[0], 0.0), 1, keepdims=True)
        post_col = jnp.sum(jnp.where(lane == heads + g, tabt_ref[0], 0.0), 1, keepdims=True)
        qms.append((qt_ref[...] * pre_col).astype(BF16))
        gos.append((got_ref[...] * post_col).astype(BF16))
        gms.append(gm)
        ps.append(p)
    gk_acc[...] += dot_nn(jnp.concatenate(qms, 1), jnp.concatenate(gms, 0))
    gv_acc[...] += dot_nn(jnp.concatenate(gos, 1), jnp.concatenate(ps, 0))

    @pl.when(step == pl.num_programs(0) - 1)
    def _():
        for copy in late:
            copy.wait()
        gq = gq_acc[...].astype(BF16)
        gkt = gk_acc[...].astype(BF16)
        gvt = gv_acc[...].astype(BF16)
        ga = ga_ref[...]
        for r in range(blocks):
            here = slice(r * rows, (r + 1) * rows)
            gk = gk_acc[:, here].T.astype(BF16)
            gv = gv_acc[:, here].T.astype(BF16)
            gn1 = dot_nt(gk, wqkv_ref[:, width : 2 * width]) + dot_nt(gv, wqkv_ref[:, 2 * width :])
            if r == 0:
                gn1 = gn1 + dot_nt(gq, wqkv_ref[:, :width])
            gn1_refs[r][...] = gn1.astype(BF16)
        which = half_ref[0]
        for part, a_ref, b_ref in ((which, ak_ref, bk_ref), (1 - which, as_ref, bs_ref)):
            mine = pl.ds(pl.multiple_of(part * half, half), half)
            a_ref[:, :width] = dot_nt(n1t_ref[mine, :], gvt).astype(BF16)
            a_ref[:, width:] = dot_nn(ot_ref[mine, :], ga).astype(BF16)
            b_ref[:, :width] = dot_nn(n1t_ref[mine, :rows], gq).astype(BF16)
            b_ref[:, width:] = dot_nt(n1t_ref[mine, :], gkt).astype(BF16)


def attn_bwd(layer, blocks, ga, w_out, q, k, v, p, u, tab, tabt, half, w_qkv, n1t, ot):
    rows, width = q.shape
    keys = k.shape[0]
    heads = p.shape[0]
    args = (ga, w_out, q, k, v, p, u, tab, tabt, half, w_qkv, n1t, ot)
    in_specs = [whole(a.shape) for a in args]
    in_specs[1] = layer_of(w_out, layer)
    in_specs[5] = pl.BlockSpec((GP, rows, keys), lambda i: (i, 0, 0))
    in_specs[6] = pl.BlockSpec((GP, rows, width), lambda i: (i, 0, 0))
    in_specs[7] = layer_of(tab, layer)
    in_specs[8] = layer_of(tabt, layer)
    in_specs[9] = pl.BlockSpec(memory_space=pltpu.SMEM)
    in_specs[10:13] = [pl.BlockSpec(memory_space=pl.ANY)] * 3
    out = (
        [((rows, width), BF16)] * blocks
        + [((width // 2, 2 * width), BF16)] * 4
        + [((heads, width), F32)] * 2
    )
    res = pl.pallas_call(
        functools.partial(attn_bwd_body, heads, blocks, layer),
        grid=(heads // GP,),
        in_specs=in_specs,
        out_specs=[whole(s) for s, _ in out],
        out_shape=[jax.ShapeDtypeStruct(s, d) for s, d in out],
        scratch_shapes=[
            pltpu.VMEM((rows, width), F32),
            pltpu.VMEM((width, rows), F32),
            pltpu.VMEM((width, rows), F32),
            pltpu.VMEM((rows, width), F32),
            pltpu.VMEM((width, keys), F32),
            pltpu.VMEM((width, keys), F32),
            pltpu.VMEM(w_qkv.shape[1:], BF16),
            pltpu.VMEM(n1t.shape, BF16),
            pltpu.VMEM(ot.shape, BF16),
            pltpu.SemaphoreType.DMA((3,)),
        ],
        compiler_params=pltpu.CompilerParams(vmem_limit_bytes=VMEM),
        cost_estimate=pl.CostEstimate(
            flops=2 * rows * keys * width * heads * 4 * 2, bytes_accessed=20_000_000, transcendentals=0
        ),
        name="attn_bwd",
    )(*args)
    return res[:blocks], res[blocks : blocks + 4], res[blocks + 4], res[blocks + 5]


def expand_body(*refs):
    which_ref, am_ref, ao_ref, bm_ref, bo_ref = refs[:5]
    qkv_ref, out_ref = refs[-2:]
    step = pl.program_id(0)
    width = out_ref.shape[2]
    other = (step // (pl.num_programs(0) // 2)) != which_ref[0]

    def write(a_ref, b_ref):
        qkv_ref[0, :, : 2 * width] = b_ref[...].astype(F32)
        qkv_ref[0, :, 2 * width :] = a_ref[:, :width].astype(F32)
        out_ref[0] = a_ref[:, width:].astype(F32)

    @pl.when(other)
    def _():
        write(ao_ref, bo_ref)

    @pl.when(jnp.logical_not(other))
    def _():
        write(am_ref, bm_ref)


def expand(layer, a_mine, a_other, b_mine, b_other, which, before=None):
    half, width2 = a_mine.shape
    width = width2 // 2
    steps = 8
    per = 2 * half // steps
    block = pl.BlockSpec((per, width2), lambda i: (i % (steps // 2), 0))
    in_specs = [pl.BlockSpec(memory_space=pltpu.SMEM)] + [block] * 4
    args = [which, a_mine, a_other, b_mine, b_other]
    aliases = {}
    if before is not None:
        in_specs += [pl.BlockSpec(memory_space=pl.ANY)] * 2
        args += before
        aliases = {5: 0, 6: 1}
    return pl.pallas_call(
        expand_body,
        grid=(steps,),
        in_specs=in_specs,
        out_specs=[
            pl.BlockSpec((1, per, 3 * width), lambda i: (layer, i, 0)),
            pl.BlockSpec((1, per, width), lambda i: (layer, i, 0)),
        ],
        out_shape=[
            jax.ShapeDtypeStruct((LAYERS, 2 * half, 3 * width), F32),
            jax.ShapeDtypeStruct((LAYERS, 2 * half, width), F32),
        ],
        input_output_aliases=aliases,
        cost_estimate=pl.CostEstimate(flops=0, bytes_accessed=20_000_000, transcendentals=0),
        name="expand",
    )(*args)


def ffn_fwd_body(blocks, *refs):
    n_refs = refs[:blocks]
    win_ref, wdown_ref = refs[blocks : blocks + 2]
    out_refs = refs[blocks + 2 : 2 * blocks + 2]
    hid_ref, dgelu_ref = refs[2 * blocks + 2 :]
    rows = n_refs[0].shape[0]
    for r in range(blocks):
        here = pl.ds(r * rows, rows)
        pre = dot_nn(n_refs[r][...], win_ref[0])
        cdf = 0.5 + 0.5 * lax.erf(pre * (0.5**0.5))
        hid = (pre * cdf).astype(BF16)
        hid_ref[here, :] = hid
        density = jnp.exp2(pre * pre * (-0.5 * LOG2E)) * 0.3989422804014327
        dgelu_ref[here, :] = (cdf + pre * density).astype(BF16)
        out_refs[r][...] = dot_nn(hid, wdown_ref[0]).astype(BF16)


def ffn_fwd(layer, n_blocks, w_in, w_down):
    blocks = len(n_blocks)
    rows, width = n_blocks[0].shape
    hidden = w_in.shape[2]
    args = (*n_blocks, w_in, w_down)
    in_specs = [whole(a.shape) for a in args]
    in_specs[blocks] = layer_of(w_in, layer)
    in_specs[blocks + 1] = layer_of(w_down, layer)
    out = [((rows, width), BF16)] * blocks + [((rows * blocks, hidden), BF16)] * 2
    res = pl.pallas_call(
        functools.partial(ffn_fwd_body, blocks),
        grid=(1,),
        in_specs=in_specs,
        out_specs=[whole(s) for s, _ in out],
        out_shape=[jax.ShapeDtypeStruct(s, d) for s, d in out],
        compiler_params=pltpu.CompilerParams(vmem_limit_bytes=VMEM),
        cost_estimate=pl.CostEstimate(
            flops=4 * rows * blocks * width * hidden, bytes_accessed=6_000_000, transcendentals=rows * blocks * hidden
        ),
        name="ffn_fwd",
    )(*args)
    return res[:blocks], res[blocks], res[blocks + 1]


def ffn_bwd_body(blocks, *refs):
    g_refs = refs[:blocks]
    dgelu_ref, win_ref, wdown_ref = refs[blocks : blocks + 3]
    out_refs = refs[blocks + 3 : 2 * blocks + 3]
    gpre_ref = refs[2 * blocks + 3]
    rows = g_refs[0].shape[0]
    for r in range(blocks):
        here = pl.ds(r * rows, rows)
        gh = dot_nt(g_refs[r][...], wdown_ref[0])
        gpre = (gh * dgelu_ref[here, :].astype(F32)).astype(BF16)
        gpre_ref[here, :] = gpre
        out_refs[r][...] = dot_nt(gpre, win_ref[0]).astype(BF16)


def ffn_bwd(layer, g_blocks, dgelu, w_in, w_down):
    blocks = len(g_blocks)
    rows, width = g_blocks[0].shape
    hidden = w_in.shape[2]
    args = (*g_blocks, dgelu, w_in, w_down)
    in_specs = [whole(a.shape) for a in args]
    in_specs[blocks + 1] = layer_of(w_in, layer)
    in_specs[blocks + 2] = layer_of(w_down, layer)
    out = [((rows, width), BF16)] * blocks + [((rows * blocks, hidden), BF16)]
    res = pl.pallas_call(
        functools.partial(ffn_bwd_body, blocks),
        grid=(1,),
        in_specs=in_specs,
        out_specs=[whole(s) for s, _ in out],
        out_shape=[jax.ShapeDtypeStruct(s, d) for s, d in out],
        compiler_params=pltpu.CompilerParams(vmem_limit_bytes=VMEM),
        cost_estimate=pl.CostEstimate(
            flops=4 * rows * blocks * width * hidden, bytes_accessed=6_000_000, transcendentals=0
        ),
        name="ffn_bwd",
    )(*args)
    return res[:blocks], res[blocks]


def swap(value, axis, bit):
    size = lax.axis_size(axis)
    return lax.ppermute(value, axis, [(i, i ^ bit) for i in range(size)])


def gather_blocks(value):
    blocks = {0: value}
    bit = lax.axis_size("tp") // 2
    while bit:
        for r in list(blocks):
            blocks[r | bit] = swap(blocks[r], "tp", bit)
        bit //= 2
    return [blocks[r] for r in range(len(blocks))]


def scatter_sum(blocks):
    blocks = list(blocks)
    bit = 1
    while bit < lax.axis_size("tp"):
        size = len(blocks)
        keep = [blocks[r] for r in range(size) if not r & 1]
        sent = [swap(blocks[r], "tp", bit) for r in range(size) if r & 1]
        blocks = [a.astype(F32) + b.astype(F32) for a, b in zip(keep, sent)]
        bit *= 2
        if bit < lax.axis_size("tp"):
            blocks = [blocks[0]] + [b.astype(BF16) for b in blocks[1:]]
    return blocks[0]


def halve(part, axis, bit):
    mine = (lax.axis_index(axis) // bit) & 1
    pair = part.reshape(2, part.shape[0] // 2, part.shape[1])
    sent = lax.dynamic_index_in_dim(pair, 1 - mine, 0, keepdims=False)
    kept = lax.dynamic_index_in_dim(pair, mine, 0, keepdims=False)
    return (kept.astype(F32) + swap(sent, axis, bit).astype(F32)).astype(BF16)


def double(part, axis, bit):
    first = ((lax.axis_index(axis) // bit) & 1) == 0
    got = swap(part, axis, bit)
    return jnp.concatenate([jnp.where(first, part, got), jnp.where(first, got, part)], 0)


def steps_of(axis):
    return [(axis, 1 << i) for i in range(lax.axis_size(axis).bit_length() - 1)]


def sum_halves(keep_a, send_a, keep_b, send_b):
    first, *tp_rest = steps_of("tp")
    dp_first, *dp_rest = steps_of("dp")
    orders = (tp_rest + [dp_first] + dp_rest, [dp_first] + tp_rest + dp_rest)
    parts = [
        (keep.astype(F32) + swap(send, *first).astype(F32)).astype(BF16)
        for keep, send in ((keep_a, send_a), (keep_b, send_b))
    ]
    for stage in range(len(orders[0])):
        parts = [halve(part, *order[stage]) for part, order in zip(parts, orders)]
    for stage in range(len(orders[0]) - 1, -1, -1):
        parts = [double(part, *order[stage]) for part, order in zip(parts, orders)]
    others = [swap(part, *first) for part in parts]
    return parts[0], others[0], parts[1], others[1]


def butterfly(value):
    for axis in ("tp", "dp"):
        bit = 1
        while bit < lax.axis_size(axis):
            value = value + swap(value, axis, bit)
            bit *= 2
    return value


def on_device(
    x_in, segments, w_qkv, w_out, mix_pre, mix_post, gain_attn, gain_ffn, w_in, w_down, cotangent
):
    rows, _, width = x_in.shape
    heads = mix_pre.shape[1]
    head_size = width // heads
    tp_size = lax.axis_size("tp")
    dp_size = lax.axis_size("dp")
    tp_index = lax.axis_index("tp")
    seg = segments[:, 0]
    span = jnp.arange(rows, dtype=jnp.int32)
    kpos = jnp.concatenate([(tp_index ^ r) * rows + span for r in range(tp_size)])
    kseg = jnp.concatenate([lax.dynamic_slice_in_dim(seg, (tp_index ^ r) * rows, rows, 0) for r in range(tp_size)])
    kinfo = jnp.pad(jnp.stack([kpos, kseg]), ((0, 6), (0, 0)))
    where = (kinfo[:, :rows].T, kinfo)

    tab = jnp.concatenate([jnp.swapaxes(mix_pre, 1, 2) * (head_size**-0.5), mix_post], 1)
    tabt = jnp.pad(jnp.repeat(jnp.swapaxes(tab, 1, 2), head_size, axis=1), ((0, 0), (0, 0), (0, 128 - 2 * heads)))
    tab = jnp.repeat(tab, head_size, axis=2)

    grad_last = gather_blocks(cotangent[:, 0])
    stream = x_in[:, 0].astype(F32)
    kept = []
    for layer in range(LAYERS):
        n1_blocks = gather_blocks(rms(stream, gain_attn[layer]).astype(BF16))
        p, u, q, k, v, o, middle, n2 = attn_fwd(
            layer,
            n1_blocks,
            stream,
            w_qkv,
            w_out,
            tab,
            gain_ffn,
            where,
        )
        n2_blocks = gather_blocks(n2)
        half = tp_size // 2
        out_a, hid_a, dgelu_a = ffn_fwd(layer, n2_blocks[:half], w_in, w_down)
        out_b, hid_b, dgelu_b = ffn_fwd(layer, n2_blocks[half:], w_in, w_down)
        kept.append((stream, n1_blocks, p, u, q, k, v, o, middle, n2_blocks, hid_a, hid_b, dgelu_a, dgelu_b))
        stream = middle + scatter_sum([*out_a, *out_b])
    y_out = stream.astype(BF16)

    grad_flow = cotangent[:, 0].astype(F32)
    small = [None] * LAYERS
    replicated = None
    sharded = [None] * LAYERS
    for layer in range(LAYERS - 1, -1, -1):
        stream, n1_blocks, p, u, q, k, v, o, middle, n2_blocks, hid_a, hid_b, dgelu_a, dgelu_b = kept[layer]
        gf_blocks = grad_last if layer == LAYERS - 1 else gather_blocks(grad_flow.astype(BF16))
        gn2_a, gpre_a = ffn_bwd(layer, gf_blocks[:half], dgelu_a, w_in, w_down)
        gn2_b, gpre_b = ffn_bwd(layer, gf_blocks[half:], dgelu_b, w_in, w_down)
        gf_all = jnp.concatenate(gf_blocks, 0)
        n2_all = jnp.concatenate(n2_blocks, 0)
        gpre = jnp.concatenate([gpre_a, gpre_b], 0)
        hid = jnp.concatenate([hid_a, hid_b], 0)
        grad_win = dot_tn(n2_all, gpre).astype(BF16)
        grad_wdown_t = dot_tn(gf_all, hid).astype(BF16)
        per = width // dp_size
        packed = jnp.concatenate(
            [grad_win.reshape(dp_size, per, -1), grad_wdown_t.reshape(dp_size, per, -1)], 1
        ).reshape(2 * width, -1)
        summed = lax.psum_scatter(packed, "dp", scatter_dimension=0, tiled=True).astype(F32)
        sharded[layer] = (summed[:per], summed[per:].T)

        gn2 = scatter_sum([*gn2_a, *gn2_b]).astype(BF16).astype(F32)
        grad_norm, grad_gffn = rms_back(gn2, middle, gain_ffn[layer])
        grad_middle = grad_flow + grad_norm
        ga = grad_middle.astype(BF16)
        core = tp_index & 1 if layer == 0 else jnp.int32(0)
        parts, grads, zpre, zpost = attn_bwd(
            layer,
            tp_size,
            ga,
            w_out,
            q,
            k,
            v,
            p,
            u,
            tab,
            tabt,
            core[None],
            w_qkv,
            jnp.concatenate(n1_blocks, 0).T,
            o.T,
        )
        if layer == 0:
            keep_a, send_a, keep_b, send_b = grads
            replicated = expand(layer, *sum_halves(keep_a, send_a, keep_b, send_b), core[None], replicated)
        else:
            keep_a, send_a, keep_b, send_b = lax.psum(tuple(grads), ("dp", "tp"))
            replicated = expand(layer, keep_a, send_a, keep_b, send_b, core[None], replicated)
        gn1 = scatter_sum(parts).astype(BF16).astype(F32)
        grad_norm, grad_gattn = rms_back(gn1, stream, gain_attn[layer])
        grad_flow = grad_middle + grad_norm
        grad_mpre = jnp.sum(zpre.reshape(heads, heads, head_size), -1).T * (head_size**-0.5)
        grad_mpost = jnp.sum(zpost.reshape(heads, heads, head_size), -1)
        small[layer] = (grad_mpre, grad_mpost, grad_gattn, grad_gffn)

    mixes = jnp.concatenate([a.reshape(-1) for s in small for a in s[:2]])
    count = mixes.shape[0]
    mix_rows = -(-count // width)
    flat = jnp.concatenate(
        [jnp.pad(mixes, (0, mix_rows * width - count)).reshape(mix_rows, width)]
        + [g[None] for s in small for g in s[2:]]
    )
    flat = jnp.pad(flat, ((0, -flat.shape[0] % 8), (0, 0)))
    flat = butterfly(flat)
    mixes = flat[:mix_rows].reshape(-1)[:count].reshape(LAYERS, 2, heads, heads)
    gains = flat[mix_rows : mix_rows + 2 * LAYERS].reshape(LAYERS, 2, width)
    return (
        y_out[:, None],
        grad_flow[:, None],
        *replicated,
        mixes[:, 0],
        mixes[:, 1],
        gains[:, 0],
        gains[:, 1],
        jnp.stack([s[0] for s in sharded]),
        jnp.stack([s[1] for s in sharded]),
    )


def solution(mesh):
    in_specs = (
        P("tp", "dp", None),
        P(None, "dp"),
        P(),
        P(),
        P(),
        P(),
        P(),
        P(),
        P(None, None, "tp"),
        P(None, "tp", None),
        P("tp", "dp", None),
    )
    out_specs = (
        P("tp", "dp", None),
        P("tp", "dp", None),
        P(),
        P(),
        P(),
        P(),
        P(),
        P(),
        P(None, "dp", "tp"),
        P(None, "tp", "dp"),
    )
    return jax.shard_map(
        on_device, mesh=mesh, in_specs=in_specs, out_specs=out_specs, check_vma=False
    )
```

```python
import functools

import jax
import jax.numpy as jnp
from jax import lax
from jax.experimental import pallas as pl
from jax.experimental.pallas import tpu as pltpu
from jax.sharding import PartitionSpec as P

LAYERS = 2
EPSILON = 1e-06
NEGATIVE = -1e30
LOG2E = 1.4426950408889634
GP = 2
VMEM = 60 * 1024 * 1024
F32 = jnp.float32
BF16 = jnp.bfloat16


def dot_nn(a, b):
    return lax.dot_general(a, b, (((1,), (0,)), ((), ())), preferred_element_type=F32)


def dot_nt(a, b):
    return lax.dot_general(a, b, (((1,), (1,)), ((), ())), preferred_element_type=F32)


def dot_tn(a, b):
    return lax.dot_general(a, b, (((0,), (0,)), ((), ())), preferred_element_type=F32)


def rms(values, gain):
    return values * lax.rsqrt(jnp.mean(values * values, -1, keepdims=True) + EPSILON) * gain


def rms_back(grad, values, gain):
    inv = lax.rsqrt(jnp.mean(values * values, -1, keepdims=True) + EPSILON)
    unit = values * inv
    scaled = grad * gain
    grad_values = (scaled - unit * jnp.mean(scaled * unit, -1, keepdims=True)) * inv
    return grad_values, jnp.sum(grad * unit, axis=0)


def whole(shape):
    return pl.BlockSpec(shape, lambda *_: (0,) * len(shape))


def layer_of(array, layer):
    shape = array.shape[1:]
    return pl.BlockSpec((1,) + shape, lambda *_: (layer,) + (0,) * len(shape))


def attn_fwd_body(blocks, heads, layer, *refs):
    n_refs = refs[:blocks]
    x_ref, wqkv_ref, wout_ref, tab_ref, gain_ref, qinfo_ref, kinfo_ref = refs[blocks : blocks + 7]
    p_ref, u_ref, q_ref, k_ref, v_ref, ot_ref, n1t_ref, xm_ref, n2_ref, bias_ref, acc_ref = refs[blocks + 7 :]
    step = pl.program_id(0)
    rows, width = x_ref.shape

    @pl.when(step == 0)
    def _():
        q_ref[...] = dot_nn(n_refs[0][...], wqkv_ref[0, :, :width]).astype(BF16)
        for r in range(blocks):
            here = pl.ds(r * rows, rows)
            k_ref[here, :] = dot_nn(n_refs[r][...], wqkv_ref[0, :, width : 2 * width]).astype(BF16)
            v_ref[here, :] = dot_nn(n_refs[r][...], wqkv_ref[0, :, 2 * width :]).astype(BF16)
        ok = (qinfo_ref[:, 1:2] == kinfo_ref[1:2, :]) & (kinfo_ref[0:1, :] <= qinfo_ref[:, 0:1])
        bias_ref[...] = jnp.where(ok, 0.0, NEGATIVE)
        acc_ref[...] = jnp.zeros_like(acc_ref)

    q = q_ref[...].astype(F32)
    for u in range(GP):
        g = step * GP + u
        qm = (q * (tab_ref[0, pl.ds(g, 1), :] * LOG2E)).astype(BF16)
        m = dot_nt(qm, k_ref[...]) + bias_ref[...]
        e = jnp.exp2(m - jnp.max(m, -1, keepdims=True))
        p = (e * (1.0 / jnp.sum(e, -1, keepdims=True))).astype(BF16)
        p_ref[u] = p
        ctx = dot_nn(p, v_ref[...])
        u_ref[u] = ctx.astype(BF16)
        acc_ref[...] += ctx * tab_ref[0, pl.ds(heads + g, 1), :]

    @pl.when(step == pl.num_programs(0) - 1)
    def _():
        o = acc_ref[...].astype(BF16)
        ot_ref[...] = o.T
        for r in range(blocks):
            n1t_ref[:, r * rows : (r + 1) * rows] = n_refs[r][...].T
        xm = x_ref[...] + dot_nn(o, wout_ref[0])
        xm_ref[...] = xm
        n2_ref[...] = rms(xm, gain_ref[pl.ds(layer, 1), :]).astype(BF16)


def attn_fwd(layer, n_blocks, x, w_qkv, w_out, tab, gain, where):
    rows, width = x.shape
    blocks = len(n_blocks)
    heads = tab.shape[1] // 2
    keys = rows * blocks
    args = (*n_blocks, x, w_qkv, w_out, tab, gain, *where)
    in_specs = [whole(a.shape) for a in args]
    in_specs[blocks + 1] = layer_of(w_qkv, layer)
    in_specs[blocks + 2] = layer_of(w_out, layer)
    in_specs[blocks + 3] = layer_of(tab, layer)
    out = [
        ((heads, rows, keys), BF16),
        ((heads, rows, width), BF16),
        ((rows, width), BF16),
        ((keys, width), BF16),
        ((keys, width), BF16),
        ((width, rows), BF16),
        ((width, keys), BF16),
        ((rows, width), F32),
        ((rows, width), BF16),
    ]
    out_specs = [whole(s) for s, _ in out]
    out_specs[0] = pl.BlockSpec((GP, rows, keys), lambda i: (i, 0, 0))
    out_specs[1] = pl.BlockSpec((GP, rows, width), lambda i: (i, 0, 0))
    return pl.pallas_call(
        functools.partial(attn_fwd_body, blocks, heads, layer),
        grid=(heads // GP,),
        in_specs=in_specs,
        out_specs=out_specs,
        out_shape=[jax.ShapeDtypeStruct(s, d) for s, d in out],
        scratch_shapes=[pltpu.VMEM((rows, keys), F32), pltpu.VMEM((rows, width), F32)],
        compiler_params=pltpu.CompilerParams(vmem_limit_bytes=VMEM),
        cost_estimate=pl.CostEstimate(
            flops=2 * rows * keys * width * heads * 2, bytes_accessed=20_000_000, transcendentals=rows * keys * heads
        ),
        name="attn_fwd",
    )(*args)


def attn_bwd_body(heads, blocks, layer, *refs):
    (ga_ref, wout_ref, q_ref, k_ref, v_ref, p_ref, u_ref, tab_ref, tabt_ref, half_ref) = refs[:10]
    wqkv_hbm, n1t_hbm, ot_hbm = refs[10:13]
    gn1_refs = refs[13 : 13 + blocks]
    (ak_ref, as_ref, bk_ref, bs_ref, zpre_ref, zpost_ref) = refs[13 + blocks : 19 + blocks]
    go_ref, got_ref, qt_ref, gq_acc, gk_acc, gv_acc, wqkv_ref, n1t_ref, ot_ref, sems = refs[19 + blocks :]
    step = pl.program_id(0)
    rows, width = q_ref.shape
    half = width // 2

    late = [
        pltpu.make_async_copy(wqkv_hbm.at[layer], wqkv_ref, sems.at[0]),
        pltpu.make_async_copy(n1t_hbm, n1t_ref, sems.at[1]),
        pltpu.make_async_copy(ot_hbm, ot_ref, sems.at[2]),
    ]

    @pl.when(step == 0)
    def _():
        for copy in late:
            copy.start()
        go = dot_nt(ga_ref[...], wout_ref[0]).astype(BF16).astype(F32)
        go_ref[...] = go
        got_ref[...] = go.T
        qt_ref[...] = q_ref[...].astype(F32).T
        gq_acc[...] = jnp.zeros_like(gq_acc)
        gk_acc[...] = jnp.zeros_like(gk_acc)
        gv_acc[...] = jnp.zeros_like(gv_acc)

    go = go_ref[...]
    q = q_ref[...].astype(F32)
    lane = lax.broadcasted_iota(jnp.int32, tabt_ref.shape[1:], 1)
    gms, ps, qms, gos = [], [], [], []
    for u in range(GP):
        g = step * GP + u
        g_mix = go * tab_ref[0, pl.ds(heads + g, 1), :]
        gp = dot_nt(g_mix.astype(BF16), v_ref[...])
        ctx = u_ref[u].astype(F32)
        zpost_ref[pl.ds(g, 1), :] = jnp.sum(ctx * go, axis=0, keepdims=True)
        delta = jnp.sum(ctx * g_mix, axis=1, keepdims=True)
        p = p_ref[u]
        gm = (p.astype(F32) * (gp - delta)).astype(BF16)
        t = dot_nn(gm, k_ref[...])
        zpre_ref[pl.ds(g, 1), :] = jnp.sum(t * q, axis=0, keepdims=True)
        gq_acc[...] += t * tab_ref[0, pl.ds(g, 1), :]
        pre_col = jnp.sum(jnp.where(lane == g, tabt_ref[0], 0.0), 1, keepdims=True)
        post_col = jnp.sum(jnp.where(lane == heads + g, tabt_ref[0], 0.0), 1, keepdims=True)
        qms.append((qt_ref[...] * pre_col).astype(BF16))
        gos.append((got_ref[...] * post_col).astype(BF16))
        gms.append(gm)
        ps.append(p)
    gk_acc[...] += dot_nn(jnp.concatenate(qms, 1), jnp.concatenate(gms, 0))
    gv_acc[...] += dot_nn(jnp.concatenate(gos, 1), jnp.concatenate(ps, 0))

    @pl.when(step == pl.num_programs(0) - 1)
    def _():
        for copy in late:
            copy.wait()
        gq = gq_acc[...].astype(BF16)
        gkt = gk_acc[...].astype(BF16)
        gvt = gv_acc[...].astype(BF16)
        ga = ga_ref[...]
        for r in range(blocks):
            here = slice(r * rows, (r + 1) * rows)
            gk = gk_acc[:, here].T.astype(BF16)
            gv = gv_acc[:, here].T.astype(BF16)
            gn1 = dot_nt(gk, wqkv_ref[:, width : 2 * width]) + dot_nt(gv, wqkv_ref[:, 2 * width :])
            if r == 0:
                gn1 = gn1 + dot_nt(gq, wqkv_ref[:, :width])
            gn1_refs[r][...] = gn1.astype(BF16)
        which = half_ref[0]
        for part, a_ref, b_ref in ((which, ak_ref, bk_ref), (1 - which, as_ref, bs_ref)):
            mine = pl.ds(pl.multiple_of(part * half, half), half)
            a_ref[:, :width] = dot_nt(n1t_ref[mine, :], gvt).astype(BF16)
            a_ref[:, width:] = dot_nn(ot_ref[mine, :], ga).astype(BF16)
            b_ref[:, :width] = dot_nn(n1t_ref[mine, :rows], gq).astype(BF16)
            b_ref[:, width:] = dot_nt(n1t_ref[mine, :], gkt).astype(BF16)


def attn_bwd(layer, blocks, ga, w_out, q, k, v, p, u, tab, tabt, half, w_qkv, n1t, ot):
    rows, width = q.shape
    keys = k.shape[0]
    heads = p.shape[0]
    args = (ga, w_out, q, k, v, p, u, tab, tabt, half, w_qkv, n1t, ot)
    in_specs = [whole(a.shape) for a in args]
    in_specs[1] = layer_of(w_out, layer)
    in_specs[5] = pl.BlockSpec((GP, rows, keys), lambda i: (i, 0, 0))
    in_specs[6] = pl.BlockSpec((GP, rows, width), lambda i: (i, 0, 0))
    in_specs[7] = layer_of(tab, layer)
    in_specs[8] = layer_of(tabt, layer)
    in_specs[9] = pl.BlockSpec(memory_space=pltpu.SMEM)
    in_specs[10:13] = [pl.BlockSpec(memory_space=pl.ANY)] * 3
    out = (
        [((rows, width), BF16)] * blocks
        + [((width // 2, 2 * width), BF16)] * 4
        + [((heads, width), F32)] * 2
    )
    res = pl.pallas_call(
        functools.partial(attn_bwd_body, heads, blocks, layer),
        grid=(heads // GP,),
        in_specs=in_specs,
        out_specs=[whole(s) for s, _ in out],
        out_shape=[jax.ShapeDtypeStruct(s, d) for s, d in out],
        scratch_shapes=[
            pltpu.VMEM((rows, width), F32),
            pltpu.VMEM((width, rows), F32),
            pltpu.VMEM((width, rows), F32),
            pltpu.VMEM((rows, width), F32),
            pltpu.VMEM((width, keys), F32),
            pltpu.VMEM((width, keys), F32),
            pltpu.VMEM(w_qkv.shape[1:], BF16),
            pltpu.VMEM(n1t.shape, BF16),
            pltpu.VMEM(ot.shape, BF16),
            pltpu.SemaphoreType.DMA((3,)),
        ],
        compiler_params=pltpu.CompilerParams(vmem_limit_bytes=VMEM),
        cost_estimate=pl.CostEstimate(
            flops=2 * rows * keys * width * heads * 4 * 2, bytes_accessed=20_000_000, transcendentals=0
        ),
        name="attn_bwd",
    )(*args)
    return res[:blocks], res[blocks : blocks + 4], res[blocks + 4], res[blocks + 5]


def expand_body(*refs):
    which_ref, am_ref, ao_ref, bm_ref, bo_ref = refs[:5]
    qkv_ref, out_ref = refs[-2:]
    step = pl.program_id(0)
    width = out_ref.shape[2]
    other = (step // (pl.num_programs(0) // 2)) != which_ref[0]

    def write(a_ref, b_ref):
        qkv_ref[0, :, : 2 * width] = b_ref[...].astype(F32)
        qkv_ref[0, :, 2 * width :] = a_ref[:, :width].astype(F32)
        out_ref[0] = a_ref[:, width:].astype(F32)

    @pl.when(other)
    def _():
        write(ao_ref, bo_ref)

    @pl.when(jnp.logical_not(other))
    def _():
        write(am_ref, bm_ref)


def expand_first_body(both_ref, qkv_ref, out_ref):
    width = out_ref.shape[2]
    qkv_ref[0, :, : 2 * width] = both_ref[:, 2 * width :].astype(F32)
    qkv_ref[0, :, 2 * width :] = both_ref[:, :width].astype(F32)
    out_ref[0] = both_ref[:, width : 2 * width].astype(F32)


def expand_first(layer, both):
    rows, width4 = both.shape
    width = width4 // 4
    steps = 8
    per = rows // steps
    return pl.pallas_call(
        expand_first_body,
        grid=(steps,),
        in_specs=[pl.BlockSpec((per, width4), lambda i: (i, 0))],
        out_specs=[
            pl.BlockSpec((1, per, 3 * width), lambda i: (layer, i, 0)),
            pl.BlockSpec((1, per, width), lambda i: (layer, i, 0)),
        ],
        out_shape=[
            jax.ShapeDtypeStruct((LAYERS, rows, 3 * width), F32),
            jax.ShapeDtypeStruct((LAYERS, rows, width), F32),
        ],
        compiler_params=pltpu.CompilerParams(vmem_limit_bytes=VMEM),
        cost_estimate=pl.CostEstimate(flops=0, bytes_accessed=14_000_000, transcendentals=0),
        name="expand_first",
    )(both)


def expand(layer, a_mine, a_other, b_mine, b_other, which, before):
    half, width2 = a_mine.shape
    width = width2 // 2
    steps = 8
    each = steps // 2
    per = half // each
    mine = pl.BlockSpec((per, width2), lambda i, w: (jnp.clip(i - each * w[0], 0, each - 1), 0))
    other = pl.BlockSpec((per, width2), lambda i, w: (jnp.clip(i - each * (1 - w[0]), 0, each - 1), 0))
    in_specs = [mine, other, mine, other]
    args = [which, a_mine, a_other, b_mine, b_other, *before]
    in_specs += [pl.BlockSpec(memory_space=pl.ANY)] * 2
    return pl.pallas_call(
        expand_body,
        grid_spec=pltpu.PrefetchScalarGridSpec(
            num_scalar_prefetch=1,
            grid=(steps,),
            in_specs=in_specs,
            out_specs=[
                pl.BlockSpec((1, per, 3 * width), lambda i, w: (layer, i, 0)),
                pl.BlockSpec((1, per, width), lambda i, w: (layer, i, 0)),
            ],
        ),
        out_shape=[
            jax.ShapeDtypeStruct((LAYERS, 2 * half, 3 * width), F32),
            jax.ShapeDtypeStruct((LAYERS, 2 * half, width), F32),
        ],
        input_output_aliases={5: 0, 6: 1},
        compiler_params=pltpu.CompilerParams(vmem_limit_bytes=VMEM),
        cost_estimate=pl.CostEstimate(flops=0, bytes_accessed=14_000_000, transcendentals=0),
        name="expand",
    )(*args)


def ffn_fwd_body(blocks, *refs):
    n_refs = refs[:blocks]
    win_ref, wdown_ref = refs[blocks : blocks + 2]
    out_refs = refs[blocks + 2 : 2 * blocks + 2]
    hid_ref, dgelu_ref = refs[2 * blocks + 2 :]
    rows = n_refs[0].shape[0]
    for r in range(blocks):
        here = pl.ds(r * rows, rows)
        pre = dot_nn(n_refs[r][...], win_ref[0])
        cdf = 0.5 + 0.5 * lax.erf(pre * (0.5**0.5))
        hid = (pre * cdf).astype(BF16)
        hid_ref[here, :] = hid
        density = jnp.exp2(pre * pre * (-0.5 * LOG2E)) * 0.3989422804014327
        dgelu_ref[here, :] = (cdf + pre * density).astype(BF16)
        out_refs[r][...] = dot_nn(hid, wdown_ref[0]).astype(BF16)


def ffn_fwd(layer, n_blocks, w_in, w_down):
    blocks = len(n_blocks)
    rows, width = n_blocks[0].shape
    hidden = w_in.shape[2]
    args = (*n_blocks, w_in, w_down)
    in_specs = [whole(a.shape) for a in args]
    in_specs[blocks] = layer_of(w_in, layer)
    in_specs[blocks + 1] = layer_of(w_down, layer)
    out = [((rows, width), BF16)] * blocks + [((rows * blocks, hidden), BF16)] * 2
    res = pl.pallas_call(
        functools.partial(ffn_fwd_body, blocks),
        grid=(1,),
        in_specs=in_specs,
        out_specs=[whole(s) for s, _ in out],
        out_shape=[jax.ShapeDtypeStruct(s, d) for s, d in out],
        compiler_params=pltpu.CompilerParams(vmem_limit_bytes=VMEM),
        cost_estimate=pl.CostEstimate(
            flops=4 * rows * blocks * width * hidden, bytes_accessed=6_000_000, transcendentals=rows * blocks * hidden
        ),
        name="ffn_fwd",
    )(*args)
    return res[:blocks], res[blocks], res[blocks + 1]


def ffn_bwd_body(blocks, *refs):
    g_refs = refs[:blocks]
    dgelu_ref, win_ref, wdown_ref = refs[blocks : blocks + 3]
    out_refs = refs[blocks + 3 : 2 * blocks + 3]
    gpre_ref = refs[2 * blocks + 3]
    rows = g_refs[0].shape[0]
    for r in range(blocks):
        here = pl.ds(r * rows, rows)
        gh = dot_nt(g_refs[r][...], wdown_ref[0])
        gpre = (gh * dgelu_ref[here, :].astype(F32)).astype(BF16)
        gpre_ref[here, :] = gpre
        out_refs[r][...] = dot_nt(gpre, win_ref[0]).astype(BF16)


def ffn_bwd(layer, g_blocks, dgelu, w_in, w_down):
    blocks = len(g_blocks)
    rows, width = g_blocks[0].shape
    hidden = w_in.shape[2]
    args = (*g_blocks, dgelu, w_in, w_down)
    in_specs = [whole(a.shape) for a in args]
    in_specs[blocks + 1] = layer_of(w_in, layer)
    in_specs[blocks + 2] = layer_of(w_down, layer)
    out = [((rows, width), BF16)] * blocks + [((rows * blocks, hidden), BF16)]
    res = pl.pallas_call(
        functools.partial(ffn_bwd_body, blocks),
        grid=(1,),
        in_specs=in_specs,
        out_specs=[whole(s) for s, _ in out],
        out_shape=[jax.ShapeDtypeStruct(s, d) for s, d in out],
        compiler_params=pltpu.CompilerParams(vmem_limit_bytes=VMEM),
        cost_estimate=pl.CostEstimate(
            flops=4 * rows * blocks * width * hidden, bytes_accessed=6_000_000, transcendentals=0
        ),
        name="ffn_bwd",
    )(*args)
    return res[:blocks], res[blocks]


def ffn_grads_body(blocks, chunks, *refs):
    n_refs, g_refs = refs[:blocks], refs[blocks : 2 * blocks]
    hid_refs, gpre_refs = refs[2 * blocks : 2 * blocks + 2], refs[2 * blocks + 2 : 2 * blocks + 4]
    out_ref = refs[-1]
    rows, width = n_refs[0].shape
    per = width // chunks
    for part, (left_refs, right_refs) in enumerate(((n_refs, gpre_refs), (g_refs, hid_refs))):
        left = jnp.concatenate([ref[...].T for ref in left_refs], 1)
        right = jnp.concatenate([ref[...] for ref in right_refs], 0)
        grad = dot_nn(left, right).astype(BF16)
        for c in range(chunks):
            place = 2 * sum(((c >> i) & 1) * (chunks >> (i + 1)) for i in range(chunks.bit_length() - 1)) + part
            out_ref[place * per : (place + 1) * per, :] = grad[c * per : (c + 1) * per]


def ffn_grads(n_blocks, g_blocks, hids, gpres, chunks):
    blocks = len(n_blocks)
    rows, width = n_blocks[0].shape
    hidden = hids[0].shape[1]
    args = (*n_blocks, *g_blocks, *hids, *gpres)
    return pl.pallas_call(
        functools.partial(ffn_grads_body, blocks, chunks),
        grid=(1,),
        in_specs=[whole(a.shape) for a in args],
        out_specs=whole((2 * width, hidden)),
        out_shape=jax.ShapeDtypeStruct((2 * width, hidden), BF16),
        compiler_params=pltpu.CompilerParams(vmem_limit_bytes=VMEM),
        cost_estimate=pl.CostEstimate(
            flops=4 * rows * blocks * width * hidden, bytes_accessed=9_000_000, transcendentals=0
        ),
        name="ffn_grads",
    )(*args)


def swap(value, axis, bit):
    size = lax.axis_size(axis)
    return lax.ppermute(value, axis, [(i, i ^ bit) for i in range(size)])


def after(values, *done):
    return lax.optimization_barrier((values, done))[0]


def gather_near(value):
    half = lax.axis_size("tp") // 2
    far = swap(value, "tp", half)
    near = [value]
    bit = 1
    while bit < half:
        near += [swap(b, "tp", bit) for b in near]
        bit *= 2
    return near, far


def gather_far(far):
    half = lax.axis_size("tp") // 2
    blocks = [far]
    bit = 1
    while bit < half:
        blocks += [swap(b, "tp", bit) for b in blocks]
        bit *= 2
    return blocks


def gather_blocks(value):
    near, far = gather_near(value)
    return near + gather_far(far)


def scatter_begin(blocks):
    blocks = list(blocks)
    bit = 1
    while bit < lax.axis_size("tp") // 2:
        size = len(blocks)
        keep = [blocks[r] for r in range(size) if not r & 1]
        sent = [swap(blocks[r], "tp", bit) for r in range(size) if r & 1]
        blocks = [a.astype(F32) + b.astype(F32) for a, b in zip(keep, sent)]
        bit *= 2
        blocks = [blocks[0]] + [b.astype(BF16) for b in blocks[1:]]
    return blocks[0].astype(F32), swap(blocks[1], "tp", bit)


def halve_begin(part, axis, bit):
    mine = (lax.axis_index(axis) // bit) & 1
    pair = part.reshape(2, part.shape[0] // 2, part.shape[1])
    sent = lax.dynamic_index_in_dim(pair, 1 - mine, 0, keepdims=False)
    kept = lax.dynamic_index_in_dim(pair, mine, 0, keepdims=False)
    return kept, swap(sent, axis, bit)


def halve_end(kept, got):
    return (kept.astype(F32) + got.astype(F32)).astype(BF16)


class Scatter:
    def __init__(self, parts, steps):
        self.steps = list(steps)
        self.begin(parts)

    def begin(self, parts):
        step = self.steps.pop(0)
        self.kept, self.got = zip(*[halve_begin(part, *step) for part in parts])

    def advance(self, *done):
        if self.steps:
            got = after(self.got, *done)
            self.begin([halve_end(a, b) for a, b in zip(self.kept, got)])

    def finish(self, *done):
        while self.steps:
            self.advance(*done)
        return [a.astype(F32) + b.astype(F32) for a, b in zip(self.kept, after(self.got, *done))]


def halve(part, axis, bit):
    return halve_end(*halve_begin(part, axis, bit))


def double(part, axis, bit):
    first = ((lax.axis_index(axis) // bit) & 1) == 0
    got = swap(part, axis, bit)
    return jnp.concatenate([jnp.where(first, part, got), jnp.where(first, got, part)], 0)


def steps_of(axis):
    return [(axis, 1 << i) for i in range(lax.axis_size(axis).bit_length() - 1)]


def sum_orders():
    first, *tp_rest = steps_of("tp")
    dp_first, *dp_rest = steps_of("dp")
    return first, (tp_rest + [dp_first] + dp_rest, [dp_first] + tp_rest + dp_rest)


def sum_begin(keep_a, send_a, keep_b, send_b):
    first, _ = sum_orders()
    return [halve_end(keep, swap(send, *first)) for keep, send in ((keep_a, send_a), (keep_b, send_b))]


def sum_middle(parts, first_stage, last_stage=None):
    _, orders = sum_orders()
    for stage in range(len(orders[0]))[first_stage:last_stage]:
        parts = [halve(part, *order[stage]) for part, order in zip(parts, orders)]
    return parts


def sum_end(parts):
    first, orders = sum_orders()
    for stage in range(len(orders[0]) - 1, -1, -1):
        parts = [double(part, *order[stage]) for part, order in zip(parts, orders)]
    others = [swap(part, *first) for part in parts]
    return parts[0], others[0], parts[1], others[1]


def gather_all(pieces, order):
    both = lax.all_gather(jnp.concatenate(pieces, 1), ("dp", "tp"))
    bits = len(order)
    names = steps_of("dp")[::-1] + steps_of("tp")[::-1]
    both = both.reshape((2,) * bits + both.shape[1:])
    both = both.transpose([names.index(step) for step in order] + [bits, bits + 1])
    return both.reshape(-1, both.shape[-1])


def butterfly(value):
    for axis in ("tp", "dp"):
        bit = 1
        while bit < lax.axis_size(axis):
            value = value + swap(value, axis, bit)
            bit *= 2
    return value


def on_device(
    x_in, segments, w_qkv, w_out, mix_pre, mix_post, gain_attn, gain_ffn, w_in, w_down, cotangent
):
    rows, _, width = x_in.shape
    heads = mix_pre.shape[1]
    head_size = width // heads
    tp_size = lax.axis_size("tp")
    dp_size = lax.axis_size("dp")
    tp_index = lax.axis_index("tp")
    seg = segments[:, 0]
    span = jnp.arange(rows, dtype=jnp.int32)
    kpos = jnp.concatenate([(tp_index ^ r) * rows + span for r in range(tp_size)])
    kseg = jnp.concatenate([lax.dynamic_slice_in_dim(seg, (tp_index ^ r) * rows, rows, 0) for r in range(tp_size)])
    kinfo = jnp.pad(jnp.stack([kpos, kseg]), ((0, 6), (0, 0)))
    where = (kinfo[:, :rows].T, kinfo)

    tab = jnp.concatenate([jnp.swapaxes(mix_pre, 1, 2) * (head_size**-0.5), mix_post], 1)
    tabt = jnp.pad(jnp.repeat(jnp.swapaxes(tab, 1, 2), head_size, axis=1), ((0, 0), (0, 0), (0, 128 - 2 * heads)))
    tab = jnp.repeat(tab, head_size, axis=2)

    stream = x_in[:, 0].astype(F32)
    kept = []
    half = tp_size // 2
    for layer in range(LAYERS):
        last = layer == LAYERS - 1
        n1_blocks = gather_blocks(rms(stream, gain_attn[layer]).astype(BF16))
        if last:
            grad_near, grad_far = gather_near(after(cotangent[:, 0], n1_blocks[half]))
        p, u, q, k, v, ot, n1t, middle, n2 = attn_fwd(
            layer,
            n1_blocks,
            stream,
            w_qkv,
            w_out,
            tab,
            gain_ffn,
            where,
        )
        if last:
            n2, grad_near, grad_far = after((n2, grad_near, grad_far))
        near, far = gather_near(n2)
        out_a, hid_a, dgelu_a = ffn_fwd(layer, near, w_in, w_down)
        if last:
            gn2_a, gpre_a = ffn_bwd(layer, grad_near, dgelu_a, w_in, w_down)
            far = after(far, gpre_a)
            gf_blocks = grad_near + gather_far(grad_far)
        n2_blocks = near + gather_far(after(far, hid_a))
        out_b, hid_b, dgelu_b = ffn_fwd(layer, n2_blocks[half:], w_in, w_down)
        kept.append((stream, n1t, p, u, q, k, v, ot, middle, n2_blocks, hid_a, hid_b, dgelu_a, dgelu_b))
        if not last:
            own, far = scatter_begin([*out_a, *out_b])
            stream = middle + (own + far.astype(F32))

    grad_flow = cotangent[:, 0].astype(F32)
    per = width // dp_size
    small = [None] * LAYERS
    sharded = [None] * LAYERS
    for layer in range(LAYERS - 1, -1, -1):
        last = layer == LAYERS - 1
        stream, n1t, p, u, q, k, v, ot, middle, n2_blocks, hid_a, hid_b, dgelu_a, dgelu_b = kept[layer]
        if not last:
            near, far = gather_near(grad_flow.astype(BF16))
            gn2_a, gpre_a = ffn_bwd(layer, near, dgelu_a, w_in, w_down)
            gf_blocks = near + gather_far(after(far, gpre_a))
        gn2_b, gpre_b = ffn_bwd(layer, gf_blocks[half:], dgelu_b, w_in, w_down)
        if not last:
            moving.advance(gpre_b)
            summing.advance(gpre_b)
        own, far = scatter_begin([*gn2_a, *gn2_b])
        packed = ffn_grads(n2_blocks, gf_blocks, (hid_a, hid_b), (gpre_a, gpre_b), dp_size)
        far, packed = after((far, packed))
        if not last:
            (summed,) = moving.finish(packed)
            sharded[layer + 1] = (summed[:per], summed[per:].T)
            summing.advance(packed)
        moving = Scatter([packed], steps_of("dp"))
        if last:
            own_y, far_y = scatter_begin(after([*out_a, *out_b], packed))
        gn2 = (own + far.astype(F32)).astype(BF16).astype(F32)
        grad_norm, grad_gffn = rms_back(gn2, middle, gain_ffn[layer])
        grad_middle = grad_flow + grad_norm
        ga = grad_middle.astype(BF16)
        core = (tp_index & 1)[None]
        parts, grads, zpre, zpost = attn_bwd(
            layer, tp_size, ga, w_out, q, k, v, p, u, tab, tabt, core, w_qkv, n1t, ot
        )
        if last:
            parts, grads, moving.got, far_y = after((parts, grads, moving.got, far_y))
            y_out = (middle + (own_y + far_y.astype(F32))).astype(BF16)
        else:
            parts, grads, moving.got, summing.got = after((parts, grads, moving.got, summing.got))
        pieces = sum_begin(*grads)
        own, far = scatter_begin(parts)
        if last:
            moving.advance()
            far = after(far, *pieces)
            order = steps_of("dp") + steps_of("tp")[1:]
            summing = Scatter(pieces, order)
        else:
            reduced = summing.finish()
            pieces = sum_middle(pieces, 0, 1)
            far = after(far, *pieces)
            moving.advance(*pieces)
            reduced = after([r.astype(BF16) for r in reduced], *pieces)
            gathered = gather_all(reduced, steps_of("tp")[:1] + order)
            pieces = sum_middle(pieces, 1)
            late = pieces
            moving.advance(*pieces)
            pieces = sum_end(pieces)
            replicated = expand(0, *pieces, core, expand_first(1, gathered))
            (summed,) = moving.finish()
            sharded[layer] = (summed[:per], summed[per:].T)
        gn1 = (own + far.astype(F32)).astype(BF16).astype(F32)
        grad_norm, grad_gattn = rms_back(gn1, stream, gain_attn[layer])
        grad_flow = grad_middle + grad_norm
        grad_mpre = jnp.sum(zpre.reshape(heads, heads, head_size), -1).T * (head_size**-0.5)
        grad_mpost = jnp.sum(zpost.reshape(heads, heads, head_size), -1)
        small[layer] = (grad_mpre, grad_mpost, grad_gattn, grad_gffn)

    mixes = jnp.concatenate([a.reshape(-1) for s in small for a in s[:2]])
    count = mixes.shape[0]
    mix_rows = -(-count // width)
    flat = jnp.concatenate(
        [jnp.pad(mixes, (0, mix_rows * width - count)).reshape(mix_rows, width)]
        + [g[None] for s in small for g in s[2:]]
    )
    flat = jnp.pad(flat, ((0, -flat.shape[0] % 8), (0, 0)))
    flat = butterfly(after(flat, *late))
    mixes = flat[:mix_rows].reshape(-1)[:count].reshape(LAYERS, 2, heads, heads)
    gains = flat[mix_rows : mix_rows + 2 * LAYERS].reshape(LAYERS, 2, width)
    return (
        y_out[:, None],
        grad_flow[:, None],
        *replicated,
        mixes[:, 0],
        mixes[:, 1],
        gains[:, 0],
        gains[:, 1],
        jnp.stack([s[0] for s in sharded]),
        jnp.stack([s[1] for s in sharded]),
    )


def solution(mesh):
    in_specs = (
        P("tp", "dp", None),
        P(None, "dp"),
        P(),
        P(),
        P(),
        P(),
        P(),
        P(),
        P(None, None, "tp"),
        P(None, "tp", None),
        P("tp", "dp", None),
    )
    out_specs = (
        P("tp", "dp", None),
        P("tp", "dp", None),
        P(),
        P(),
        P(),
        P(),
        P(),
        P(),
        P(None, "dp", "tp"),
        P(None, "tp", "dp"),
    )
    return jax.shard_map(
        on_device, mesh=mesh, in_specs=in_specs, out_specs=out_specs, check_vma=False
    )
```

```python
import functools

import jax
import jax.numpy as jnp
from jax import lax
from jax.experimental import pallas as pl
from jax.experimental.pallas import tpu as pltpu
from jax.sharding import PartitionSpec as P

LAYERS = 2
EPSILON = 1e-06
NEGATIVE = -1e30
LOG2E = 1.4426950408889634
PIECES = 8
GP = 2
VMEM = 60 * 1024 * 1024
F32 = jnp.float32
BF16 = jnp.bfloat16


def dot_nn(a, b):
    return lax.dot_general(a, b, (((1,), (0,)), ((), ())), preferred_element_type=F32)


def dot_nt(a, b):
    return lax.dot_general(a, b, (((1,), (1,)), ((), ())), preferred_element_type=F32)


def dot_tn(a, b):
    return lax.dot_general(a, b, (((0,), (0,)), ((), ())), preferred_element_type=F32)


def rms(values, gain):
    return values * lax.rsqrt(jnp.mean(values * values, -1, keepdims=True) + EPSILON) * gain


def rms_back(grad, values, gain):
    inv = lax.rsqrt(jnp.mean(values * values, -1, keepdims=True) + EPSILON)
    unit = values * inv
    scaled = grad * gain
    grad_values = (scaled - unit * jnp.mean(scaled * unit, -1, keepdims=True)) * inv
    return grad_values, jnp.sum(grad * unit, axis=0)


def whole(shape):
    return pl.BlockSpec(shape, lambda *_: (0,) * len(shape))


def layer_of(array, layer):
    shape = array.shape[1:]
    return pl.BlockSpec((1,) + shape, lambda *_: (layer,) + (0,) * len(shape))


def attn_fwd_body(blocks, heads, layer, *refs):
    n_refs = refs[:blocks]
    x_ref, wqkv_ref, wout_ref, tab_ref, gain_ref, qinfo_ref, kinfo_ref = refs[blocks : blocks + 7]
    p_ref, u_ref, q_ref, k_ref, v_ref, ot_ref, n1t_ref, xm_ref, n2_ref, bias_ref, acc_ref = refs[blocks + 7 :]
    step = pl.program_id(0)
    rows, width = x_ref.shape

    @pl.when(step == 0)
    def _():
        q_ref[...] = dot_nn(n_refs[0][...], wqkv_ref[0, :, :width]).astype(BF16)
        for r in range(blocks):
            here = pl.ds(r * rows, rows)
            k_ref[here, :] = dot_nn(n_refs[r][...], wqkv_ref[0, :, width : 2 * width]).astype(BF16)
            v_ref[here, :] = dot_nn(n_refs[r][...], wqkv_ref[0, :, 2 * width :]).astype(BF16)
        ok = (qinfo_ref[:, 1:2] == kinfo_ref[1:2, :]) & (kinfo_ref[0:1, :] <= qinfo_ref[:, 0:1])
        bias_ref[...] = jnp.where(ok, 0.0, NEGATIVE)
        acc_ref[...] = jnp.zeros_like(acc_ref)

    q = q_ref[...].astype(F32)
    for u in range(GP):
        g = step * GP + u
        qm = (q * (tab_ref[0, pl.ds(g, 1), :] * LOG2E)).astype(BF16)
        m = dot_nt(qm, k_ref[...]) + bias_ref[...]
        e = jnp.exp2(m - jnp.max(m, -1, keepdims=True))
        p = (e * (1.0 / jnp.sum(e, -1, keepdims=True))).astype(BF16)
        p_ref[u] = p
        ctx = dot_nn(p, v_ref[...])
        u_ref[u] = ctx.astype(BF16)
        acc_ref[...] += ctx * tab_ref[0, pl.ds(heads + g, 1), :]

    @pl.when(step == pl.num_programs(0) - 1)
    def _():
        o = acc_ref[...].astype(BF16)
        ot_ref[...] = o.T
        for r in range(blocks):
            n1t_ref[:, r * rows : (r + 1) * rows] = n_refs[r][...].T
        xm = x_ref[...] + dot_nn(o, wout_ref[0])
        xm_ref[...] = xm
        n2_ref[...] = rms(xm, gain_ref[pl.ds(layer, 1), :]).astype(BF16)


def attn_fwd(layer, n_blocks, x, w_qkv, w_out, tab, gain, where):
    rows, width = x.shape
    blocks = len(n_blocks)
    heads = tab.shape[1] // 2
    keys = rows * blocks
    args = (*n_blocks, x, w_qkv, w_out, tab, gain, *where)
    in_specs = [whole(a.shape) for a in args]
    in_specs[blocks + 1] = layer_of(w_qkv, layer)
    in_specs[blocks + 2] = layer_of(w_out, layer)
    in_specs[blocks + 3] = layer_of(tab, layer)
    out = [
        ((heads, rows, keys), BF16),
        ((heads, rows, width), BF16),
        ((rows, width), BF16),
        ((keys, width), BF16),
        ((keys, width), BF16),
        ((width, rows), BF16),
        ((width, keys), BF16),
        ((rows, width), F32),
        ((rows, width), BF16),
    ]
    out_specs = [whole(s) for s, _ in out]
    out_specs[0] = pl.BlockSpec((GP, rows, keys), lambda i: (i, 0, 0))
    out_specs[1] = pl.BlockSpec((GP, rows, width), lambda i: (i, 0, 0))
    return pl.pallas_call(
        functools.partial(attn_fwd_body, blocks, heads, layer),
        grid=(heads // GP,),
        in_specs=in_specs,
        out_specs=out_specs,
        out_shape=[jax.ShapeDtypeStruct(s, d) for s, d in out],
        scratch_shapes=[pltpu.VMEM((rows, keys), F32), pltpu.VMEM((rows, width), F32)],
        compiler_params=pltpu.CompilerParams(vmem_limit_bytes=VMEM),
        cost_estimate=pl.CostEstimate(
            flops=2 * rows * keys * width * heads * 2, bytes_accessed=20_000_000, transcendentals=rows * keys * heads
        ),
        name="attn_fwd",
    )(*args)


def attn_bwd_body(heads, blocks, layer, parts, *refs):
    (ga_ref, wout_ref, q_ref, k_ref, v_ref, p_ref, u_ref, tab_ref, tabt_ref, place_ref) = refs[:10]
    wqkv_hbm, n1t_hbm, ot_hbm = refs[10:13]
    gn1_refs = refs[13 : 13 + blocks]
    grad_refs = refs[13 + blocks : 13 + blocks + 2 * parts]
    zpre_ref, zpost_ref = refs[13 + blocks + 2 * parts : 15 + blocks + 2 * parts]
    go_ref, got_ref, qt_ref, gq_acc, gk_acc, gv_acc, wqkv_ref, n1t_ref, ot_ref, sems = refs[15 + blocks + 2 * parts :]
    step = pl.program_id(0)
    rows, width = q_ref.shape
    half = width // 2

    late = [
        pltpu.make_async_copy(wqkv_hbm.at[layer], wqkv_ref, sems.at[0]),
        pltpu.make_async_copy(n1t_hbm, n1t_ref, sems.at[1]),
        pltpu.make_async_copy(ot_hbm, ot_ref, sems.at[2]),
    ]

    @pl.when(step == 0)
    def _():
        for copy in late:
            copy.start()
        go = dot_nt(ga_ref[...], wout_ref[0]).astype(BF16).astype(F32)
        go_ref[...] = go
        got_ref[...] = go.T
        qt_ref[...] = q_ref[...].astype(F32).T
        gq_acc[...] = jnp.zeros_like(gq_acc)
        gk_acc[...] = jnp.zeros_like(gk_acc)
        gv_acc[...] = jnp.zeros_like(gv_acc)

    go = go_ref[...]
    q = q_ref[...].astype(F32)
    lane = lax.broadcasted_iota(jnp.int32, tabt_ref.shape[1:], 1)
    gms, ps, qms, gos = [], [], [], []
    for u in range(GP):
        g = step * GP + u
        g_mix = go * tab_ref[0, pl.ds(heads + g, 1), :]
        gp = dot_nt(g_mix.astype(BF16), v_ref[...])
        ctx = u_ref[u].astype(F32)
        zpost_ref[pl.ds(g, 1), :] = jnp.sum(ctx * go, axis=0, keepdims=True)
        delta = jnp.sum(ctx * g_mix, axis=1, keepdims=True)
        p = p_ref[u]
        gm = (p.astype(F32) * (gp - delta)).astype(BF16)
        t = dot_nn(gm, k_ref[...])
        zpre_ref[pl.ds(g, 1), :] = jnp.sum(t * q, axis=0, keepdims=True)
        gq_acc[...] += t * tab_ref[0, pl.ds(g, 1), :]
        pre_col = jnp.sum(jnp.where(lane == g, tabt_ref[0], 0.0), 1, keepdims=True)
        post_col = jnp.sum(jnp.where(lane == heads + g, tabt_ref[0], 0.0), 1, keepdims=True)
        qms.append((qt_ref[...] * pre_col).astype(BF16))
        gos.append((got_ref[...] * post_col).astype(BF16))
        gms.append(gm)
        ps.append(p)
    gk_acc[...] += dot_nn(jnp.concatenate(qms, 1), jnp.concatenate(gms, 0))
    gv_acc[...] += dot_nn(jnp.concatenate(gos, 1), jnp.concatenate(ps, 0))

    @pl.when(step == pl.num_programs(0) - 1)
    def _():
        for copy in late:
            copy.wait()
        gq = gq_acc[...].astype(BF16)
        gkt = gk_acc[...].astype(BF16)
        gvt = gv_acc[...].astype(BF16)
        ga = ga_ref[...]
        for r in range(blocks):
            here = slice(r * rows, (r + 1) * rows)
            gk = gk_acc[:, here].T.astype(BF16)
            gv = gv_acc[:, here].T.astype(BF16)
            gn1 = dot_nt(gk, wqkv_ref[:, width : 2 * width]) + dot_nt(gv, wqkv_ref[:, 2 * width :])
            if r == 0:
                gn1 = gn1 + dot_nt(gq, wqkv_ref[:, :width])
            gn1_refs[r][...] = gn1.astype(BF16)
        per = half // PIECES
        for side in range(2):
            core = place_ref[0] if side == 0 else 1 - place_ref[0]
            mine = pl.ds(pl.multiple_of(core * half, half), half)
            n1t = n1t_ref[mine, :]
            grads = (
                lambda: dot_nn(n1t_ref[mine, :rows], gq),
                lambda: dot_nt(n1t, gkt),
                lambda: dot_nt(n1t, gvt),
                lambda: dot_nn(ot_ref[mine, :], ga),
            )
            for index, grad in enumerate(grads):
                part = index * parts // len(grads)
                column = (index - part * (len(grads) // parts)) * width
                value = grad().astype(BF16)
                for piece in range(PIECES):
                    there = pl.multiple_of((piece ^ place_ref[1 + part]) * per, per)
                    grad_refs[2 * part + side][pl.ds(there, per), column : column + width] = value[
                        piece * per : (piece + 1) * per
                    ]


def attn_bwd(layer, blocks, ga, w_out, q, k, v, p, u, tab, tabt, place, w_qkv, n1t, ot):
    rows, width = q.shape
    keys = k.shape[0]
    heads = p.shape[0]
    parts = place.shape[0] - 1
    args = (ga, w_out, q, k, v, p, u, tab, tabt, place, w_qkv, n1t, ot)
    in_specs = [whole(a.shape) for a in args]
    in_specs[1] = layer_of(w_out, layer)
    in_specs[5] = pl.BlockSpec((GP, rows, keys), lambda i: (i, 0, 0))
    in_specs[6] = pl.BlockSpec((GP, rows, width), lambda i: (i, 0, 0))
    in_specs[7] = layer_of(tab, layer)
    in_specs[8] = layer_of(tabt, layer)
    in_specs[9] = pl.BlockSpec(memory_space=pltpu.SMEM)
    in_specs[10:13] = [pl.BlockSpec(memory_space=pl.ANY)] * 3
    out = (
        [((rows, width), BF16)] * blocks
        + [((width // 2, 4 // parts * width), BF16)] * (2 * parts)
        + [((heads, width), F32)] * 2
    )
    res = pl.pallas_call(
        functools.partial(attn_bwd_body, heads, blocks, layer, parts),
        grid=(heads // GP,),
        in_specs=in_specs,
        out_specs=[whole(s) for s, _ in out],
        out_shape=[jax.ShapeDtypeStruct(s, d) for s, d in out],
        scratch_shapes=[
            pltpu.VMEM((rows, width), F32),
            pltpu.VMEM((width, rows), F32),
            pltpu.VMEM((width, rows), F32),
            pltpu.VMEM((rows, width), F32),
            pltpu.VMEM((width, keys), F32),
            pltpu.VMEM((width, keys), F32),
            pltpu.VMEM(w_qkv.shape[1:], BF16),
            pltpu.VMEM(n1t.shape, BF16),
            pltpu.VMEM(ot.shape, BF16),
            pltpu.SemaphoreType.DMA((3,)),
        ],
        compiler_params=pltpu.CompilerParams(vmem_limit_bytes=VMEM),
        cost_estimate=pl.CostEstimate(
            flops=2 * rows * keys * width * heads * 4 * 2, bytes_accessed=20_000_000, transcendentals=0
        ),
        name="attn_bwd",
    )(*args)
    return res[:blocks], res[blocks:-2], res[-2], res[-1]


def expand_body(parts, place_ref, *refs):
    mine_refs, other_refs = refs[: 2 * parts : 2], refs[1 : 2 * parts : 2]
    qkv_ref, out_ref = refs[-2:]
    other = pl.program_id(0) // PIECES != place_ref[0]
    width3 = qkv_ref.shape[2]

    def write(part_refs):
        column = 0
        for ref in part_refs:
            end = column + ref.shape[1]
            cut = min(end, width3)
            qkv_ref[0, :, column:cut] = ref[:, : cut - column].astype(F32)
            if end > width3:
                out_ref[0] = ref[:, cut - column :].astype(F32)
            column = end

    @pl.when(other)
    def _():
        write(other_refs)

    @pl.when(jnp.logical_not(other))
    def _():
        write(mine_refs)


def expand(layer, place, mines, others, before=()):
    half = mines[0].shape[0]
    width = sum(m.shape[1] for m in mines) // 4
    per = half // PIECES
    in_specs, args = [], []
    for part, pair in enumerate(zip(mines, others)):
        for side, array in enumerate(pair):

            def piece(i, place, part=part, side=side):
                here = place[0] ^ side
                wanted = jnp.where(i // PIECES == here, i % PIECES, (PIECES - 1) * (1 - here))
                return wanted ^ place[1 + part], 0

            in_specs.append(pl.BlockSpec((per, array.shape[1]), piece))
            args.append(array)
    first = 1 + len(args)
    in_specs += [pl.BlockSpec(memory_space=pl.ANY)] * len(before)
    return pl.pallas_call(
        functools.partial(expand_body, len(mines)),
        grid_spec=pltpu.PrefetchScalarGridSpec(
            num_scalar_prefetch=1,
            grid=(2 * PIECES,),
            in_specs=in_specs,
            out_specs=[
                pl.BlockSpec((1, per, 3 * width), lambda i, w: (layer, i, 0)),
                pl.BlockSpec((1, per, width), lambda i, w: (layer, i, 0)),
            ],
        ),
        out_shape=[
            jax.ShapeDtypeStruct((LAYERS, 2 * half, 3 * width), F32),
            jax.ShapeDtypeStruct((LAYERS, 2 * half, width), F32),
        ],
        input_output_aliases={first + i: i for i in range(len(before))},
        compiler_params=pltpu.CompilerParams(vmem_limit_bytes=VMEM),
        cost_estimate=pl.CostEstimate(flops=0, bytes_accessed=14_000_000, transcendentals=0),
        name="expand",
    )(place, *args, *before)


def ffn_fwd_body(blocks, *refs):
    n_refs = refs[:blocks]
    win_ref, wdown_ref = refs[blocks : blocks + 2]
    out_refs = refs[blocks + 2 : 2 * blocks + 2]
    hid_ref, dgelu_ref = refs[2 * blocks + 2 :]
    rows = n_refs[0].shape[0]
    for r in range(blocks):
        here = pl.ds(r * rows, rows)
        pre = dot_nn(n_refs[r][...], win_ref[0])
        cdf = 0.5 + 0.5 * lax.erf(pre * (0.5**0.5))
        hid = (pre * cdf).astype(BF16)
        hid_ref[here, :] = hid
        density = jnp.exp2(pre * pre * (-0.5 * LOG2E)) * 0.3989422804014327
        dgelu_ref[here, :] = (cdf + pre * density).astype(BF16)
        out_refs[r][...] = dot_nn(hid, wdown_ref[0]).astype(BF16)


def ffn_fwd(layer, n_blocks, w_in, w_down):
    blocks = len(n_blocks)
    rows, width = n_blocks[0].shape
    hidden = w_in.shape[2]
    args = (*n_blocks, w_in, w_down)
    in_specs = [whole(a.shape) for a in args]
    in_specs[blocks] = layer_of(w_in, layer)
    in_specs[blocks + 1] = layer_of(w_down, layer)
    out = [((rows, width), BF16)] * blocks + [((rows * blocks, hidden), BF16)] * 2
    res = pl.pallas_call(
        functools.partial(ffn_fwd_body, blocks),
        grid=(1,),
        in_specs=in_specs,
        out_specs=[whole(s) for s, _ in out],
        out_shape=[jax.ShapeDtypeStruct(s, d) for s, d in out],
        compiler_params=pltpu.CompilerParams(vmem_limit_bytes=VMEM),
        cost_estimate=pl.CostEstimate(
            flops=4 * rows * blocks * width * hidden, bytes_accessed=6_000_000, transcendentals=rows * blocks * hidden
        ),
        name="ffn_fwd",
    )(*args)
    return res[:blocks], res[blocks], res[blocks + 1]


def ffn_bwd_body(blocks, *refs):
    g_refs = refs[:blocks]
    dgelu_ref, win_ref, wdown_ref = refs[blocks : blocks + 3]
    out_refs = refs[blocks + 3 : 2 * blocks + 3]
    gpre_ref = refs[2 * blocks + 3]
    rows = g_refs[0].shape[0]
    for r in range(blocks):
        here = pl.ds(r * rows, rows)
        gh = dot_nt(g_refs[r][...], wdown_ref[0])
        gpre = (gh * dgelu_ref[here, :].astype(F32)).astype(BF16)
        gpre_ref[here, :] = gpre
        out_refs[r][...] = dot_nt(gpre, win_ref[0]).astype(BF16)


def ffn_bwd(layer, g_blocks, dgelu, w_in, w_down):
    blocks = len(g_blocks)
    rows, width = g_blocks[0].shape
    hidden = w_in.shape[2]
    args = (*g_blocks, dgelu, w_in, w_down)
    in_specs = [whole(a.shape) for a in args]
    in_specs[blocks + 1] = layer_of(w_in, layer)
    in_specs[blocks + 2] = layer_of(w_down, layer)
    out = [((rows, width), BF16)] * blocks + [((rows * blocks, hidden), BF16)]
    res = pl.pallas_call(
        functools.partial(ffn_bwd_body, blocks),
        grid=(1,),
        in_specs=in_specs,
        out_specs=[whole(s) for s, _ in out],
        out_shape=[jax.ShapeDtypeStruct(s, d) for s, d in out],
        compiler_params=pltpu.CompilerParams(vmem_limit_bytes=VMEM),
        cost_estimate=pl.CostEstimate(
            flops=4 * rows * blocks * width * hidden, bytes_accessed=6_000_000, transcendentals=0
        ),
        name="ffn_bwd",
    )(*args)
    return res[:blocks], res[blocks]


def ffn_grads_body(blocks, chunks, *refs):
    n_refs, g_refs = refs[:blocks], refs[blocks : 2 * blocks]
    hid_refs, gpre_refs = refs[2 * blocks : 2 * blocks + 2], refs[2 * blocks + 2 : 2 * blocks + 4]
    out_ref = refs[-1]
    rows, width = n_refs[0].shape
    per = width // chunks
    for part, (left_refs, right_refs) in enumerate(((n_refs, gpre_refs), (g_refs, hid_refs))):
        left = jnp.concatenate([ref[...].T for ref in left_refs], 1)
        right = jnp.concatenate([ref[...] for ref in right_refs], 0)
        grad = dot_nn(left, right).astype(BF16)
        for c in range(chunks):
            place = 2 * sum(((c >> i) & 1) * (chunks >> (i + 1)) for i in range(chunks.bit_length() - 1)) + part
            out_ref[place * per : (place + 1) * per, :] = grad[c * per : (c + 1) * per]


def ffn_grads(n_blocks, g_blocks, hids, gpres, chunks):
    blocks = len(n_blocks)
    rows, width = n_blocks[0].shape
    hidden = hids[0].shape[1]
    args = (*n_blocks, *g_blocks, *hids, *gpres)
    return pl.pallas_call(
        functools.partial(ffn_grads_body, blocks, chunks),
        grid=(1,),
        in_specs=[whole(a.shape) for a in args],
        out_specs=whole((2 * width, hidden)),
        out_shape=jax.ShapeDtypeStruct((2 * width, hidden), BF16),
        compiler_params=pltpu.CompilerParams(vmem_limit_bytes=VMEM),
        cost_estimate=pl.CostEstimate(
            flops=4 * rows * blocks * width * hidden, bytes_accessed=9_000_000, transcendentals=0
        ),
        name="ffn_grads",
    )(*args)


def swap(value, axis, bit):
    size = lax.axis_size(axis)
    return lax.ppermute(value, axis, [(i, i ^ bit) for i in range(size)])


def after(values, *done):
    return lax.optimization_barrier((values, done))[0]


def gather_near(value):
    half = lax.axis_size("tp") // 2
    far = swap(value, "tp", half)
    near = [value]
    bit = 1
    while bit < half:
        near += [swap(b, "tp", bit) for b in near]
        bit *= 2
    return near, far


def gather_far(far):
    half = lax.axis_size("tp") // 2
    blocks = [far]
    bit = 1
    while bit < half:
        blocks += [swap(b, "tp", bit) for b in blocks]
        bit *= 2
    return blocks


def gather_blocks(value):
    near, far = gather_near(value)
    return near + gather_far(far)


def scatter_begin(blocks):
    blocks = list(blocks)
    bit = 1
    while bit < lax.axis_size("tp") // 2:
        size = len(blocks)
        keep = [blocks[r] for r in range(size) if not r & 1]
        sent = [swap(blocks[r], "tp", bit) for r in range(size) if r & 1]
        blocks = [a.astype(F32) + b.astype(F32) for a, b in zip(keep, sent)]
        bit *= 2
        blocks = [blocks[0]] + [b.astype(BF16) for b in blocks[1:]]
    return blocks[0].astype(F32), swap(blocks[1], "tp", bit)


def halve_begin(part, axis, bit):
    mine = (lax.axis_index(axis) // bit) & 1
    pair = part.reshape(2, part.shape[0] // 2, part.shape[1])
    sent = lax.dynamic_index_in_dim(pair, 1 - mine, 0, keepdims=False)
    kept = lax.dynamic_index_in_dim(pair, mine, 0, keepdims=False)
    return kept, swap(sent, axis, bit)


def halve_end(kept, got):
    return (kept.astype(F32) + got.astype(F32)).astype(BF16)


class Scatter:
    def __init__(self, parts, steps):
        self.steps = list(steps)
        self.begin(parts)

    def begin(self, parts):
        step = self.steps.pop(0)
        self.kept, self.got = zip(*[halve_begin(part, *step) for part in parts])

    def advance(self, *done):
        if self.steps:
            got = after(self.got, *done)
            self.begin([halve_end(a, b) for a, b in zip(self.kept, got)])

    def finish(self, *done):
        while self.steps:
            self.advance(*done)
        return [a.astype(F32) + b.astype(F32) for a, b in zip(self.kept, after(self.got, *done))]


def steps_of(axis):
    return [(axis, 1 << i) for i in range(lax.axis_size(axis).bit_length() - 1)]


HALVINGS = PIECES.bit_length() - 1


def place_of(order):
    number = 0
    for axis, bit in order[:HALVINGS]:
        number = 2 * number + ((lax.axis_index(axis) // bit) & 1)
    return number


def sum_start(part, order, stage):
    if stage < HALVINGS:
        rows = part.shape[0] // 2
        return part[:rows], swap(part[rows:], *order[stage])
    return part, swap(part, *order[stage])


def spread(part, got):
    return jnp.concatenate([part, got], 0)


class Butterfly:
    def __init__(self, value):
        self.value = value
        self.steps = steps_of("tp") + steps_of("dp")
        self.got = None

    def start(self):
        if self.steps:
            self.got = swap(self.value, *self.steps.pop(0))
            return [self.got]
        return []

    def end(self, got):
        for g in got:
            self.value = self.value + g


def on_device(
    x_in, segments, w_qkv, w_out, mix_pre, mix_post, gain_attn, gain_ffn, w_in, w_down, cotangent
):
    rows, _, width = x_in.shape
    heads = mix_pre.shape[1]
    head_size = width // heads
    tp_size = lax.axis_size("tp")
    dp_size = lax.axis_size("dp")
    tp_index = lax.axis_index("tp")
    seg = segments[:, 0]
    span = jnp.arange(rows, dtype=jnp.int32)
    kpos = jnp.concatenate([(tp_index ^ r) * rows + span for r in range(tp_size)])
    kseg = jnp.concatenate([lax.dynamic_slice_in_dim(seg, (tp_index ^ r) * rows, rows, 0) for r in range(tp_size)])
    kinfo = jnp.pad(jnp.stack([kpos, kseg]), ((0, 6), (0, 0)))
    where = (kinfo[:, :rows].T, kinfo)

    tab = jnp.concatenate([jnp.swapaxes(mix_pre, 1, 2) * (head_size**-0.5), mix_post], 1)
    tabt = jnp.pad(jnp.repeat(jnp.swapaxes(tab, 1, 2), head_size, axis=1), ((0, 0), (0, 0), (0, 128 - 2 * heads)))
    tab = jnp.repeat(tab, head_size, axis=2)

    stream = x_in[:, 0].astype(F32)
    kept = []
    half = tp_size // 2
    for layer in range(LAYERS):
        last = layer == LAYERS - 1
        n1_blocks = gather_blocks(rms(stream, gain_attn[layer]).astype(BF16))
        if last:
            low, n1_blocks[half] = after((cotangent[:, 0], n1_blocks[half]))
            grad_near, grad_far = gather_near(low)
        p, u, q, k, v, ot, n1t, middle, n2 = attn_fwd(
            layer,
            n1_blocks,
            stream,
            w_qkv,
            w_out,
            tab,
            gain_ffn,
            where,
        )
        if last:
            n2, grad_near, grad_far = after((n2, grad_near, grad_far))
        near, far = gather_near(n2)
        out_a, hid_a, dgelu_a = ffn_fwd(layer, near, w_in, w_down)
        if last:
            gn2_a, gpre_a = ffn_bwd(layer, grad_near, dgelu_a, w_in, w_down)
            far, gpre_a = after((far, gpre_a))
            gf_blocks = grad_near + gather_far(grad_far)
        far, hid_a = after((far, hid_a))
        n2_blocks = near + gather_far(far)
        out_b, hid_b, dgelu_b = ffn_fwd(layer, n2_blocks[half:], w_in, w_down)
        kept.append((stream, n1t, p, u, q, k, v, ot, middle, n2_blocks, hid_a, hid_b, dgelu_a, dgelu_b))
        if not last:
            own, far = scatter_begin([*out_a, *out_b])
            stream = middle + (own + far.astype(F32))

    grad_flow = cotangent[:, 0].astype(F32)
    per = width // dp_size
    small = [None] * LAYERS
    sharded = [None] * LAYERS
    for layer in range(LAYERS - 1, -1, -1):
        last = layer == LAYERS - 1
        stream, n1t, p, u, q, k, v, ot, middle, n2_blocks, hid_a, hid_b, dgelu_a, dgelu_b = kept[layer]
        if not last:
            near, far = gather_near(grad_flow.astype(BF16))
            gn2_a, gpre_a = ffn_bwd(layer, near, dgelu_a, w_in, w_down)
            far, gpre_a, moving.got = after((far, gpre_a, moving.got))
            (summed,) = moving.finish()
            sharded[layer + 1] = (summed[:per], summed[per:].T)
            gf_blocks = near + gather_far(far)
        gn2_b, gpre_b = ffn_bwd(layer, gf_blocks[half:], dgelu_b, w_in, w_down)
        if not last:
            total_got, gpre_b = after((total_got, gpre_b))
            total = halve_end(total_kept, total_got)
            total_kept, total_got = sum_start(total, total_order, 1)
        own, far = scatter_begin([*gn2_a, *gn2_b])
        packed = ffn_grads(n2_blocks, gf_blocks, (hid_a, hid_b), (gpre_a, gpre_b), dp_size)
        far, packed = after((far, packed))
        if not last:
            total_got, packed = after((total_got, packed))
            total = halve_end(total_kept, total_got)
            total_kept, total_got = sum_start(total, total_order, 2)
        moving = Scatter([packed], steps_of("dp"))
        if last:
            own_y, far_y = scatter_begin(after([*out_a, *out_b], packed))
        gn2 = (own + far.astype(F32)).astype(BF16).astype(F32)
        grad_norm, grad_gffn = rms_back(gn2, middle, gain_ffn[layer])
        grad_middle = grad_flow + grad_norm
        ga = grad_middle.astype(BF16)
        if last:
            orders = [steps_of("dp") + steps_of("tp")[1:]]
        else:
            (y_step, *dp_rest), x_steps = steps_of("dp"), steps_of("tp")[1:]
            orders = [x_steps + [y_step] + dp_rest, [y_step] + x_steps + dp_rest]
        place = jnp.stack([tp_index & 1] + [place_of(order) for order in orders])
        parts, grads, zpre, zpost = attn_bwd(
            layer, tp_size, ga, w_out, q, k, v, p, u, tab, tabt, place, w_qkv, n1t, ot
        )
        core_step = steps_of("tp")[0]
        if last:
            parts, grads, moving.got, far_y, own_y = after((parts, grads, moving.got, far_y, own_y))
            y_out = (middle + (own_y + far_y.astype(F32))).astype(BF16)
            keep, send = grads
            total = halve_end(keep, swap(send, *core_step))
            own, far = scatter_begin(parts)
            moving.advance()
            far, moving.got = after((far, moving.got), total)
            moving.advance()
            (total_order,), total_place = orders, place
            total_kept, total_got = sum_start(total, total_order, 0)
        else:
            parts, grads, moving.got, total_got = after((parts, grads, moving.got, total_got))
        if not last:
            break
        gn1 = (own + far.astype(F32)).astype(BF16).astype(F32)
        grad_norm, grad_gattn = rms_back(gn1, stream, gain_attn[layer])
        grad_flow = grad_middle + grad_norm
        grad_mpre = jnp.sum(zpre.reshape(heads, heads, head_size), -1).T * (head_size**-0.5)
        grad_mpost = jnp.sum(zpost.reshape(heads, heads, head_size), -1)
        small[layer] = (grad_mpre, grad_mpost, grad_gattn, grad_gffn)

    total = halve_end(total_kept, total_got)
    got = [swap(send, *core_step) for send in grads[1::2]]
    for stage in range(HALVINGS, len(total_order)):
        total_got = swap(total, *total_order[stage])
        got, total_got = after((got, total_got))
        total = halve_end(total, total_got)
    pieces = [halve_end(keep, g) for keep, g in zip(grads[::2], got)]
    own, far = scatter_begin(parts)
    for stage in range(HALVINGS):
        kept, got = zip(*[sum_start(part, order, stage) for part, order in zip(pieces, orders)])
        total_got = swap(total, *total_order[HALVINGS - 1 - stage])
        if stage < HALVINGS - 1:
            got, total_got = after((got, total_got))
            total = spread(total, total_got)
        pieces = [halve_end(a, b) for a, b in zip(kept, after(got))]
        if stage == 0:
            far, pieces = after((far, pieces))
            gn1 = (own + far.astype(F32)).astype(BF16).astype(F32)
            grad_norm, grad_gattn = rms_back(gn1, stream, gain_attn[layer])
            grad_flow = grad_middle + grad_norm
            grad_mpre = jnp.sum(zpre.reshape(heads, heads, head_size), -1).T * (head_size**-0.5)
            grad_mpost = jnp.sum(zpost.reshape(heads, heads, head_size), -1)
            small[layer] = (grad_mpre, grad_mpost, grad_gattn, grad_gffn)
    mixes = jnp.concatenate([a.reshape(-1) for s in small for a in s[:2]])
    count = mixes.shape[0]
    mix_rows = -(-count // width)
    flat = jnp.concatenate(
        [jnp.pad(mixes, (0, mix_rows * width - count)).reshape(mix_rows, width)]
        + [g[None] for s in small for g in s[2:]]
    )
    flat = jnp.pad(flat, ((0, -flat.shape[0] % 8), (0, 0)))
    flat, pieces = after((flat, pieces))
    flat = Butterfly(flat)
    for stage in range(HALVINGS, len(orders[0])):
        got = [swap(part, *order[stage]) for part, order in zip(pieces, orders)]
        flat_got = flat.start()
        if stage == HALVINGS:
            got, flat_got, total_got = after((got, flat_got, total_got))
            total = spread(total, total_got)
        got, flat_got = after((got, flat_got))
        flat.end(flat_got)
        pieces = [halve_end(a, b) for a, b in zip(pieces, got)]
    total_other = swap(total, *core_step)
    moving.advance(*pieces)
    for stage in range(HALVINGS - 1, -1, -1):
        got = [swap(part, *order[stage]) for part, order in zip(pieces, orders)]
        flat_got = flat.start()
        if stage == HALVINGS - 1:
            got, flat_got, total_other = after((got, flat_got, total_other))
        if stage < HALVINGS - 1:
            got, moving.got = after((got, moving.got))
            moving.advance()
        if stage == 0:
            replicated = expand(1, total_place, [total], [total_other])
            got, flat_got, replicated = after((got, flat_got, replicated))
        got, flat_got = after((got, flat_got))
        flat.end(flat_got)
        pieces = [spread(a, b) for a, b in zip(pieces, got)]
    got = [swap(part, *core_step) for part in pieces]
    while flat.steps:
        flat.end(flat.start())
    flat = flat.value
    (summed,) = moving.finish()
    sharded[0] = (summed[:per], summed[per:].T)
    got, sharded = after((got, sharded))
    replicated = expand(0, place, pieces, got, replicated)
    mixes = flat[:mix_rows].reshape(-1)[:count].reshape(LAYERS, 2, heads, heads)
    gains = flat[mix_rows : mix_rows + 2 * LAYERS].reshape(LAYERS, 2, width)
    return (
        y_out[:, None],
        grad_flow[:, None],
        *replicated,
        mixes[:, 0],
        mixes[:, 1],
        gains[:, 0],
        gains[:, 1],
        jnp.stack([s[0] for s in sharded]),
        jnp.stack([s[1] for s in sharded]),
    )


def solution(mesh):
    in_specs = (
        P("tp", "dp", None),
        P(None, "dp"),
        P(),
        P(),
        P(),
        P(),
        P(),
        P(),
        P(None, None, "tp"),
        P(None, "tp", None),
        P("tp", "dp", None),
    )
    out_specs = (
        P("tp", "dp", None),
        P("tp", "dp", None),
        P(),
        P(),
        P(),
        P(),
        P(),
        P(),
        P(None, "dp", "tp"),
        P(None, "tp", "dp"),
    )
    return jax.shard_map(
        on_device, mesh=mesh, in_specs=in_specs, out_specs=out_specs, check_vma=False
    )
```

```python
import functools

import jax
import jax.numpy as jnp
from jax import lax
from jax.experimental import pallas as pl
from jax.experimental.pallas import tpu as pltpu
from jax.sharding import PartitionSpec as P

LAYERS = 2
EPSILON = 1e-06
NEGATIVE = -1e30
LOG2E = 1.4426950408889634
GROUPS = 2
PIECES = 8
GP = 4
GB = 4
VMEM = 60 * 1024 * 1024
F32 = jnp.float32
BF16 = jnp.bfloat16


def dot_nn(a, b):
    return lax.dot_general(a, b, (((1,), (0,)), ((), ())), preferred_element_type=F32)


def dot_nt(a, b):
    return lax.dot_general(a, b, (((1,), (1,)), ((), ())), preferred_element_type=F32)


def dot_tn(a, b):
    return lax.dot_general(a, b, (((0,), (0,)), ((), ())), preferred_element_type=F32)


def rms(values, gain):
    return values * lax.rsqrt(jnp.mean(values * values, -1, keepdims=True) + EPSILON) * gain


def rms_back(grad, values, gain):
    inv = lax.rsqrt(jnp.mean(values * values, -1, keepdims=True) + EPSILON)
    unit = values * inv
    scaled = grad * gain
    grad_values = (scaled - unit * jnp.mean(scaled * unit, -1, keepdims=True)) * inv
    return grad_values, jnp.sum(grad * unit, axis=0)


def whole(shape):
    return pl.BlockSpec(shape, lambda *_: (0,) * len(shape))


def layer_of(array, layer):
    shape = array.shape[1:]
    return pl.BlockSpec((1,) + shape, lambda *_: (layer,) + (0,) * len(shape))


def attn_fwd_body(blocks, heads, layer, plain, *refs):
    n_refs = refs[:blocks]
    x_ref, wqkv_ref, wout_ref, tab_ref, gain_ref, qinfo_ref, kinfo_ref, at_ref = refs[blocks : blocks + 8]
    p_ref, u_ref, q_ref, k_ref, v_ref, ot_ref, n1t_ref, xm_ref, n2_ref, bias_ref, acc_ref = refs[blocks + 8 :]
    step = pl.program_id(0)
    rows, width = x_ref.shape
    half = rows // 2
    at = at_ref[0]

    def place(r, second):
        block = chunk_of(at ^ r, second, blocks, plain)
        return pl.ds(pl.multiple_of(block * half, half), half)

    @pl.when(step == 0)
    def _():
        n_second = n_refs[blocks - 1 if plain else 0]
        q_ref[:half] = dot_nn(n_refs[0][:half], wqkv_ref[0, :, :width]).astype(BF16)
        q_ref[half:] = dot_nn(n_second[half:], wqkv_ref[0, :, :width]).astype(BF16)
        for r in range(blocks):
            k = dot_nn(n_refs[r][...], wqkv_ref[0, :, width : 2 * width]).astype(BF16)
            v = dot_nn(n_refs[r][...], wqkv_ref[0, :, 2 * width :]).astype(BF16)
            for second in range(2):
                here = slice(second * half, (second + 1) * half)
                k_ref[place(r, second), :] = k[here]
                v_ref[place(r, second), :] = v[here]
        ok = (qinfo_ref[:, 1:2] == kinfo_ref[1:2, :]) & (kinfo_ref[0:1, :] <= qinfo_ref[:, 0:1])
        bias_ref[...] = jnp.where(ok, 0.0, NEGATIVE)
        acc_ref[...] = jnp.zeros_like(acc_ref)

    def work(here, keys):
        q = q_ref[here, :].astype(F32)
        gs = [step * GP + u for u in range(GP)]
        qm = jnp.concatenate([(q * (tab_ref[0, pl.ds(g, 1), :] * LOG2E)).astype(BF16) for g in gs], 0)
        m = dot_nt(qm, k_ref[:keys, :])
        bias = bias_ref[here, :keys]
        ps = []
        for u in range(GP):
            mu = m[u * half : (u + 1) * half] + bias
            e = jnp.exp2(mu - jnp.max(mu, -1, keepdims=True))
            p = (e * (1.0 / jnp.sum(e, -1, keepdims=True))).astype(BF16)
            p_ref[u, here, :keys] = p
            ps.append(p)
        ctx = dot_nn(jnp.concatenate(ps, 0), v_ref[:keys, :])
        total = acc_ref[here, :]
        for u in range(GP):
            cu = ctx[u * half : (u + 1) * half]
            u_ref[u, here, :] = cu.astype(BF16)
            total = total + cu * tab_ref[0, pl.ds(heads + gs[u], 1), :]
        acc_ref[here, :] = total

    for device in range(blocks):

        @pl.when(at == device)
        def _(device=device):
            for second in range(2):
                keys = (chunk_of(device, second, blocks, False) + 1) * half
                work(slice(second * half, (second + 1) * half), keys)

    @pl.when(step == pl.num_programs(0) - 1)
    def _():
        o = acc_ref[...].astype(BF16)
        ot_ref[...] = o.T
        for r in range(blocks):
            for second in range(2):
                n1t_ref[:, place(r, second)] = n_refs[r][second * half : (second + 1) * half, :].T
        xm = x_ref[...] + dot_nn(o, wout_ref[0])
        xm_ref[...] = xm
        n2_ref[...] = rms(xm, gain_ref[pl.ds(layer, 1), :]).astype(BF16)


def chunk_of(device, second, devices, plain):
    if not second:
        return 2 * device
    return 2 * device + 1 if plain else 2 * (devices - 1 - device) + 1


def attn_fwd(layer, plain, n_blocks, x, w_qkv, w_out, tab, gain, where):
    rows, width = x.shape
    blocks = len(n_blocks)
    heads = tab.shape[1] // 2
    keys = rows * blocks
    args = (*n_blocks, x, w_qkv, w_out, tab, gain, *where)
    in_specs = [whole(a.shape) for a in args]
    in_specs[blocks + 1] = layer_of(w_qkv, layer)
    in_specs[blocks + 2] = layer_of(w_out, layer)
    in_specs[blocks + 3] = layer_of(tab, layer)
    in_specs[-1] = pl.BlockSpec(memory_space=pltpu.SMEM)
    out = [
        ((heads, rows, keys), BF16),
        ((heads, rows, width), BF16),
        ((rows, width), BF16),
        ((keys, width), BF16),
        ((keys, width), BF16),
        ((width, rows), BF16),
        ((width, keys), BF16),
        ((rows, width), F32),
        ((rows, width), BF16),
    ]
    out_specs = [whole(s) for s, _ in out]
    out_specs[0] = pl.BlockSpec((GP, rows, keys), lambda i: (i, 0, 0))
    out_specs[1] = pl.BlockSpec((GP, rows, width), lambda i: (i, 0, 0))
    return pl.pallas_call(
        functools.partial(attn_fwd_body, blocks, heads, layer, plain),
        grid=(heads // GP,),
        in_specs=in_specs,
        out_specs=out_specs,
        out_shape=[jax.ShapeDtypeStruct(s, d) for s, d in out],
        scratch_shapes=[pltpu.VMEM((rows, keys), F32), pltpu.VMEM((rows, width), F32)],
        compiler_params=pltpu.CompilerParams(vmem_limit_bytes=VMEM),
        cost_estimate=pl.CostEstimate(
            flops=2 * rows * keys * width * heads * 2, bytes_accessed=20_000_000, transcendentals=rows * keys * heads
        ),
        name="attn_fwd",
    )(*args)


def attn_bwd_body(heads, blocks, layer, parts, *refs):
    (ga_ref, wout_ref, q_ref, k_ref, v_ref, p_ref, u_ref, tab_ref, tabt_ref, place_ref) = refs[:10]
    wqkv_hbm, n1t_hbm, ot_hbm = refs[10:13]
    gn1_refs = refs[13 : 13 + blocks]
    grad_refs = refs[13 + blocks : 13 + blocks + 2 * parts]
    zpre_ref, zpost_ref = refs[13 + blocks + 2 * parts : 15 + blocks + 2 * parts]
    go_ref, got_ref, qt_ref, gq_acc, gk_acc, gv_acc, wqkv_ref, n1t_ref, ot_ref, sems = refs[15 + blocks + 2 * parts :]
    step = pl.program_id(0)
    rows, width = q_ref.shape

    late = [
        pltpu.make_async_copy(wqkv_hbm.at[layer], wqkv_ref, sems.at[0]),
        pltpu.make_async_copy(n1t_hbm, n1t_ref, sems.at[1]),
        pltpu.make_async_copy(ot_hbm, ot_ref, sems.at[2]),
    ]

    @pl.when(step == 0)
    def _():
        for copy in late:
            copy.start()
        go = dot_nt(ga_ref[...], wout_ref[0]).astype(BF16).astype(F32)
        go_ref[...] = go
        got_ref[...] = go.T
        qt_ref[...] = q_ref[...].astype(F32).T
        gq_acc[...] = jnp.zeros_like(gq_acc)
        gk_acc[...] = jnp.zeros_like(gk_acc)
        gv_acc[...] = jnp.zeros_like(gv_acc)

    half = rows // 2
    at = place_ref[1 + parts]
    lane = lax.broadcasted_iota(jnp.int32, tabt_ref.shape[1:], 1)
    gs = [step * GB + u for u in range(GB)]
    cols = []
    for g in gs:
        pre_col = jnp.sum(jnp.where(lane == g, tabt_ref[0], 0.0), 1, keepdims=True)
        post_col = jnp.sum(jnp.where(lane == heads + g, tabt_ref[0], 0.0), 1, keepdims=True)
        cols.append((pre_col, post_col))

    def work(second, keys):
        here = slice(second * half, (second + 1) * half)
        go = go_ref[here, :]
        q = q_ref[here, :].astype(F32)
        mixed = [go * tab_ref[0, pl.ds(heads + g, 1), :] for g in gs]
        gp = dot_nt(jnp.concatenate([x.astype(BF16) for x in mixed], 0), v_ref[:keys, :])
        gms, ps, zposts = [], [], []
        for u in range(GB):
            ctx = u_ref[u, here, :].astype(F32)
            zposts.append(jnp.sum(ctx * go, axis=0, keepdims=True))
            delta = jnp.sum(ctx * mixed[u], axis=1, keepdims=True)
            p = p_ref[u, here, :keys]
            gms.append((p.astype(F32) * (gp[u * half : (u + 1) * half] - delta)).astype(BF16))
            ps.append(p)
        gm = jnp.concatenate(gms, 0)
        t = dot_nn(gm, k_ref[:keys, :])
        total = gq_acc[here, :]
        zpres = []
        for u in range(GB):
            tu = t[u * half : (u + 1) * half]
            zpres.append(jnp.sum(tu * q, axis=0, keepdims=True))
            total = total + tu * tab_ref[0, pl.ds(gs[u], 1), :]
        gq_acc[here, :] = total
        qm = jnp.concatenate([(qt_ref[:, here] * pre).astype(BF16) for pre, _ in cols], 1)
        gk_acc[:, :keys] += dot_nn(qm, gm)
        gm2 = jnp.concatenate([(got_ref[:, here] * post).astype(BF16) for _, post in cols], 1)
        gv_acc[:, :keys] += dot_nn(gm2, jnp.concatenate(ps, 0))
        return zpres, zposts

    for device in range(blocks):

        @pl.when(at == device)
        def _(device=device):
            first, last = [work(s, (chunk_of(device, s, blocks, False) + 1) * half) for s in range(2)]
            for u, g in enumerate(gs):
                zpre_ref[pl.ds(g, 1), :] = first[0][u] + last[0][u]
                zpost_ref[pl.ds(g, 1), :] = first[1][u] + last[1][u]

    @pl.when(step == pl.num_programs(0) - 1)
    def _():
        for copy in late:
            copy.wait()
        gq = gq_acc[...].astype(BF16)
        gkt = gk_acc[...].astype(BF16)
        gvt = gv_acc[...].astype(BF16)
        ga = ga_ref[...]
        for r in range(blocks):
            there = [pl.ds(pl.multiple_of(chunk_of(at ^ r, x, blocks, False) * half, half), half) for x in range(2)]
            gk = jnp.concatenate([gk_acc[:, x].T.astype(BF16) for x in there], 0)
            gv = jnp.concatenate([gv_acc[:, x].T.astype(BF16) for x in there], 0)
            gn1 = dot_nt(gk, wqkv_ref[:, width : 2 * width]) + dot_nt(gv, wqkv_ref[:, 2 * width :])
            if r == 0:
                gn1 = gn1 + dot_nt(gq, wqkv_ref[:, :width])
            gn1_refs[r][...] = gn1.astype(BF16)
        hand = width // 2
        per = hand // PIECES
        own = [pl.ds(pl.multiple_of(chunk_of(at, x, blocks, False) * half, half), half) for x in range(2)]
        for side in range(2):
            core = place_ref[0] if side == 0 else 1 - place_ref[0]
            mine = pl.ds(pl.multiple_of(core * hand, hand), hand)
            n1t = n1t_ref[mine, :]
            n1t_own = jnp.concatenate([n1t_ref[mine, x] for x in own], 1)
            grads = (
                lambda: dot_nn(n1t_own, gq),
                lambda: dot_nt(n1t, gkt),
                lambda: dot_nt(n1t, gvt),
                lambda: dot_nn(ot_ref[mine, :], ga),
            )
            for index, grad in enumerate(grads):
                part = index * parts // len(grads)
                column = (index - part * (len(grads) // parts)) * width
                value = grad().astype(BF16)
                for piece in range(PIECES):
                    there = pl.multiple_of((piece ^ place_ref[1 + part]) * per, per)
                    grad_refs[2 * part + side][pl.ds(there, per), column : column + width] = value[
                        piece * per : (piece + 1) * per
                    ]


def attn_bwd(layer, blocks, ga, w_out, q, k, v, p, u, tab, tabt, place, w_qkv, n1t, ot):
    rows, width = q.shape
    keys = k.shape[0]
    heads = p.shape[0]
    parts = place.shape[0] - 2
    args = (ga, w_out, q, k, v, p, u, tab, tabt, place, w_qkv, n1t, ot)
    in_specs = [whole(a.shape) for a in args]
    in_specs[1] = layer_of(w_out, layer)
    in_specs[5] = pl.BlockSpec((GB, rows, keys), lambda i: (i, 0, 0))
    in_specs[6] = pl.BlockSpec((GB, rows, width), lambda i: (i, 0, 0))
    in_specs[7] = layer_of(tab, layer)
    in_specs[8] = layer_of(tabt, layer)
    in_specs[9] = pl.BlockSpec(memory_space=pltpu.SMEM)
    in_specs[10:13] = [pl.BlockSpec(memory_space=pl.ANY)] * 3
    out = (
        [((rows, width), BF16)] * blocks
        + [((width // 2, 4 // parts * width), BF16)] * (2 * parts)
        + [((heads, width), F32)] * 2
    )
    res = pl.pallas_call(
        functools.partial(attn_bwd_body, heads, blocks, layer, parts),
        grid=(heads // GB,),
        in_specs=in_specs,
        out_specs=[whole(s) for s, _ in out],
        out_shape=[jax.ShapeDtypeStruct(s, d) for s, d in out],
        scratch_shapes=[
            pltpu.VMEM((rows, width), F32),
            pltpu.VMEM((width, rows), F32),
            pltpu.VMEM((width, rows), F32),
            pltpu.VMEM((rows, width), F32),
            pltpu.VMEM((width, keys), F32),
            pltpu.VMEM((width, keys), F32),
            pltpu.VMEM(w_qkv.shape[1:], BF16),
            pltpu.VMEM(n1t.shape, BF16),
            pltpu.VMEM(ot.shape, BF16),
            pltpu.SemaphoreType.DMA((3,)),
        ],
        compiler_params=pltpu.CompilerParams(vmem_limit_bytes=VMEM),
        cost_estimate=pl.CostEstimate(
            flops=2 * rows * keys * width * heads * 4 * 2, bytes_accessed=20_000_000, transcendentals=0
        ),
        name="attn_bwd",
    )(*args)
    return res[:blocks], res[blocks:-2], res[-2], res[-1]


def expand_body(parts, place_ref, *refs):
    mine_refs, other_refs = refs[: 2 * parts : 2], refs[1 : 2 * parts : 2]
    qkv_ref, out_ref = refs[-2:]
    other = pl.program_id(0) // GROUPS != place_ref[0]
    width3 = qkv_ref.shape[2]
    inner = PIECES // GROUPS
    per = qkv_ref.shape[1] // inner

    def write(part_refs):
        column = 0
        for part, ref in enumerate(part_refs):
            end = column + ref.shape[1]
            cut = min(end, width3)
            for piece in range(inner):
                here = slice(piece * per, (piece + 1) * per)
                there = piece ^ lax.rem(place_ref[1 + part], inner)
                value = ref[pl.ds(pl.multiple_of(there * per, per), per), :].astype(F32)
                qkv_ref[0, here, column:cut] = value[:, : cut - column]
                if end > width3:
                    out_ref[0, here, :] = value[:, cut - column :]
            column = end

    @pl.when(other)
    def _():
        write(other_refs)

    @pl.when(jnp.logical_not(other))
    def _():
        write(mine_refs)


def expand(layer, place, mines, others, before=()):
    half = mines[0].shape[0]
    width = sum(m.shape[1] for m in mines) // 4
    per = half // GROUPS
    in_specs, args = [], []
    for part, pair in enumerate(zip(mines, others)):
        for side, array in enumerate(pair):

            def piece(i, place, part=part, side=side):
                here = place[0] ^ side
                wanted = jnp.where(i // GROUPS == here, i % GROUPS, (GROUPS - 1) * (1 - here))
                return wanted ^ (place[1 + part] // (PIECES // GROUPS)), 0

            in_specs.append(pl.BlockSpec((per, array.shape[1]), piece))
            args.append(array)
    first = 1 + len(args)
    in_specs += [pl.BlockSpec(memory_space=pl.ANY)] * len(before)
    return pl.pallas_call(
        functools.partial(expand_body, len(mines)),
        grid_spec=pltpu.PrefetchScalarGridSpec(
            num_scalar_prefetch=1,
            grid=(2 * GROUPS,),
            in_specs=in_specs,
            out_specs=[
                pl.BlockSpec((1, per, 3 * width), lambda i, w: (layer, i, 0)),
                pl.BlockSpec((1, per, width), lambda i, w: (layer, i, 0)),
            ],
        ),
        out_shape=[
            jax.ShapeDtypeStruct((LAYERS, 2 * half, 3 * width), F32),
            jax.ShapeDtypeStruct((LAYERS, 2 * half, width), F32),
        ],
        input_output_aliases={first + i: i for i in range(len(before))},
        compiler_params=pltpu.CompilerParams(vmem_limit_bytes=VMEM),
        cost_estimate=pl.CostEstimate(flops=0, bytes_accessed=14_000_000, transcendentals=0),
        name="expand",
    )(place, *args, *before)


def ffn_fwd_body(blocks, *refs):
    n_refs = refs[:blocks]
    win_ref, wdown_ref = refs[blocks : blocks + 2]
    out_refs = refs[blocks + 2 : 2 * blocks + 2]
    hid_ref, dgelu_ref = refs[2 * blocks + 2 :]
    rows = n_refs[0].shape[0]
    for r in range(blocks):
        here = pl.ds(r * rows, rows)
        pre = dot_nn(n_refs[r][...], win_ref[0])
        cdf = 0.5 + 0.5 * lax.erf(pre * (0.5**0.5))
        hid = (pre * cdf).astype(BF16)
        hid_ref[here, :] = hid
        density = jnp.exp2(pre * pre * (-0.5 * LOG2E)) * 0.3989422804014327
        dgelu_ref[here, :] = (cdf + pre * density).astype(BF16)
        out_refs[r][...] = dot_nn(hid, wdown_ref[0]).astype(BF16)


def ffn_fwd(layer, n_blocks, w_in, w_down):
    blocks = len(n_blocks)
    rows, width = n_blocks[0].shape
    hidden = w_in.shape[2]
    args = (*n_blocks, w_in, w_down)
    in_specs = [whole(a.shape) for a in args]
    in_specs[blocks] = layer_of(w_in, layer)
    in_specs[blocks + 1] = layer_of(w_down, layer)
    out = [((rows, width), BF16)] * blocks + [((rows * blocks, hidden), BF16)] * 2
    res = pl.pallas_call(
        functools.partial(ffn_fwd_body, blocks),
        grid=(1,),
        in_specs=in_specs,
        out_specs=[whole(s) for s, _ in out],
        out_shape=[jax.ShapeDtypeStruct(s, d) for s, d in out],
        compiler_params=pltpu.CompilerParams(vmem_limit_bytes=VMEM),
        cost_estimate=pl.CostEstimate(
            flops=4 * rows * blocks * width * hidden, bytes_accessed=6_000_000, transcendentals=rows * blocks * hidden
        ),
        name="ffn_fwd",
    )(*args)
    return res[:blocks], res[blocks], res[blocks + 1]


def ffn_bwd_body(blocks, *refs):
    g_refs = refs[:blocks]
    dgelu_ref, win_ref, wdown_ref = refs[blocks : blocks + 3]
    out_refs = refs[blocks + 3 : 2 * blocks + 3]
    gpre_ref = refs[2 * blocks + 3]
    rows = g_refs[0].shape[0]
    for r in range(blocks):
        here = pl.ds(r * rows, rows)
        gh = dot_nt(g_refs[r][...], wdown_ref[0])
        gpre = (gh * dgelu_ref[here, :].astype(F32)).astype(BF16)
        gpre_ref[here, :] = gpre
        out_refs[r][...] = dot_nt(gpre, win_ref[0]).astype(BF16)


def ffn_bwd(layer, g_blocks, dgelu, w_in, w_down):
    blocks = len(g_blocks)
    rows, width = g_blocks[0].shape
    hidden = w_in.shape[2]
    args = (*g_blocks, dgelu, w_in, w_down)
    in_specs = [whole(a.shape) for a in args]
    in_specs[blocks + 1] = layer_of(w_in, layer)
    in_specs[blocks + 2] = layer_of(w_down, layer)
    out = [((rows, width), BF16)] * blocks + [((rows * blocks, hidden), BF16)]
    res = pl.pallas_call(
        functools.partial(ffn_bwd_body, blocks),
        grid=(1,),
        in_specs=in_specs,
        out_specs=[whole(s) for s, _ in out],
        out_shape=[jax.ShapeDtypeStruct(s, d) for s, d in out],
        compiler_params=pltpu.CompilerParams(vmem_limit_bytes=VMEM),
        cost_estimate=pl.CostEstimate(
            flops=4 * rows * blocks * width * hidden, bytes_accessed=6_000_000, transcendentals=0
        ),
        name="ffn_bwd",
    )(*args)
    return res[:blocks], res[blocks]


def ffn_grads_body(blocks, chunks, *refs):
    n_refs, g_refs = refs[:blocks], refs[blocks : 2 * blocks]
    hid_refs, gpre_refs = refs[2 * blocks : 2 * blocks + 2], refs[2 * blocks + 2 : 2 * blocks + 4]
    out_ref = refs[-1]
    rows, width = n_refs[0].shape
    per = width // chunks
    for part, (left_refs, right_refs) in enumerate(((n_refs, gpre_refs), (g_refs, hid_refs))):
        left = jnp.concatenate([ref[...].T for ref in left_refs], 1)
        right = jnp.concatenate([ref[...] for ref in right_refs], 0)
        grad = dot_nn(left, right).astype(BF16)
        for c in range(chunks):
            place = 2 * sum(((c >> i) & 1) * (chunks >> (i + 1)) for i in range(chunks.bit_length() - 1)) + part
            out_ref[place * per : (place + 1) * per, :] = grad[c * per : (c + 1) * per]


def ffn_grads(n_blocks, g_blocks, hids, gpres, chunks):
    blocks = len(n_blocks)
    rows, width = n_blocks[0].shape
    hidden = hids[0].shape[1]
    args = (*n_blocks, *g_blocks, *hids, *gpres)
    return pl.pallas_call(
        functools.partial(ffn_grads_body, blocks, chunks),
        grid=(1,),
        in_specs=[whole(a.shape) for a in args],
        out_specs=whole((2 * width, hidden)),
        out_shape=jax.ShapeDtypeStruct((2 * width, hidden), BF16),
        compiler_params=pltpu.CompilerParams(vmem_limit_bytes=VMEM),
        cost_estimate=pl.CostEstimate(
            flops=4 * rows * blocks * width * hidden, bytes_accessed=9_000_000, transcendentals=0
        ),
        name="ffn_grads",
    )(*args)


def swap(value, axis, bit):
    size = lax.axis_size(axis)
    return lax.ppermute(value, axis, [(i, i ^ bit) for i in range(size)])


def after(values, *done):
    return lax.optimization_barrier((values, done))[0]


def gather_near(value):
    half = lax.axis_size("tp") // 2
    far = swap(value, "tp", half)
    near = [value]
    bit = 1
    while bit < half:
        near += [swap(b, "tp", bit) for b in near]
        bit *= 2
    return near, far


def gather_far(far):
    half = lax.axis_size("tp") // 2
    blocks = [far]
    bit = 1
    while bit < half:
        blocks += [swap(b, "tp", bit) for b in blocks]
        bit *= 2
    return blocks


def gather_blocks(value):
    near, far = gather_near(value)
    return near + gather_far(far)


def scatter_begin(blocks):
    blocks = list(blocks)
    bit = 1
    while bit < lax.axis_size("tp") // 2:
        size = len(blocks)
        keep = [blocks[r] for r in range(size) if not r & 1]
        sent = [swap(blocks[r], "tp", bit) for r in range(size) if r & 1]
        blocks = [a.astype(F32) + b.astype(F32) for a, b in zip(keep, sent)]
        bit *= 2
        blocks = [blocks[0]] + [b.astype(BF16) for b in blocks[1:]]
    return blocks[0].astype(F32), swap(blocks[1], "tp", bit)


def halve_begin(part, axis, bit):
    mine = (lax.axis_index(axis) // bit) & 1
    pair = part.reshape(2, part.shape[0] // 2, part.shape[1])
    sent = lax.dynamic_index_in_dim(pair, 1 - mine, 0, keepdims=False)
    kept = lax.dynamic_index_in_dim(pair, mine, 0, keepdims=False)
    return kept, swap(sent, axis, bit)


def halve_end(kept, got):
    return (kept.astype(F32) + got.astype(F32)).astype(BF16)


class Scatter:
    def __init__(self, parts, steps):
        self.steps = list(steps)
        self.begin(parts)

    def begin(self, parts):
        step = self.steps.pop(0)
        self.kept, self.got = zip(*[halve_begin(part, *step) for part in parts])

    def advance(self, *done):
        if self.steps:
            got = after(self.got, *done)
            self.begin([halve_end(a, b) for a, b in zip(self.kept, got)])

    def finish(self, *done):
        while self.steps:
            self.advance(*done)
        return [a.astype(F32) + b.astype(F32) for a, b in zip(self.kept, after(self.got, *done))]


def steps_of(axis):
    return [(axis, 1 << i) for i in range(lax.axis_size(axis).bit_length() - 1)]


HALVINGS = PIECES.bit_length() - 1


def place_of(order):
    number = 0
    for axis, bit in order[:HALVINGS]:
        number = 2 * number + ((lax.axis_index(axis) // bit) & 1)
    return number


def sum_start(part, order, stage):
    if stage < HALVINGS:
        rows = part.shape[0] // 2
        return part[:rows], swap(part[rows:], *order[stage])
    return part, swap(part, *order[stage])


def spread(part, got):
    return jnp.concatenate([part, got], 0)


class Butterfly:
    def __init__(self, value):
        self.value = value
        self.steps = steps_of("tp") + steps_of("dp")
        self.got = None

    def start(self):
        if self.steps:
            self.got = swap(self.value, *self.steps.pop(0))
            return [self.got]
        return []

    def end(self, got):
        for g in got:
            self.value = self.value + g


def on_device(
    x_in, segments, w_qkv, w_out, mix_pre, mix_post, gain_attn, gain_ffn, w_in, w_down, cotangent
):
    rows, _, width = x_in.shape
    heads = mix_pre.shape[1]
    head_size = width // heads
    tp_size = lax.axis_size("tp")
    dp_size = lax.axis_size("dp")
    tp_index = lax.axis_index("tp")
    seg = segments[:, 0]
    side = rows // 2
    span = jnp.arange(side, dtype=jnp.int32)
    starts = [chunk_of(tp_index, x, tp_size, False) * side for x in range(2)]
    qpos = jnp.concatenate([start + span for start in starts])
    qseg = jnp.concatenate([lax.dynamic_slice_in_dim(seg, start, side, 0) for start in starts])
    qinfo = jnp.stack([qpos, qseg] + [qpos] * 6, 1)
    kinfo = jnp.pad(jnp.stack([jnp.arange(seg.shape[0], dtype=jnp.int32), seg]), ((0, 6), (0, 0)))
    where = (qinfo, kinfo, tp_index[None])

    def mirror(value):
        moved = lax.ppermute(value[side:], "tp", [(i, tp_size - 1 - i) for i in range(tp_size)])
        return value[:side], moved

    tab = jnp.concatenate([jnp.swapaxes(mix_pre, 1, 2) * (head_size**-0.5), mix_post], 1)
    tabt = jnp.pad(jnp.repeat(jnp.swapaxes(tab, 1, 2), head_size, axis=1), ((0, 0), (0, 0), (0, 128 - 2 * heads)))
    tab = jnp.repeat(tab, head_size, axis=2)

    stream = x_in[:, 0].astype(F32)
    x_folded = jnp.concatenate(mirror(x_in[:, 0]), 0).astype(F32)
    kept = []
    half = tp_size // 2
    for layer in range(LAYERS):
        last = layer == LAYERS - 1
        n1_blocks = gather_blocks(rms(stream, gain_attn[layer]).astype(BF16))
        if last:
            low, n1_blocks[half] = after((cotangent[:, 0], n1_blocks[half]))
            grad_near, grad_far = gather_near(low)
        else:
            stream = x_folded
        p, u, q, k, v, ot, n1t, middle, n2 = attn_fwd(
            layer,
            layer == 0,
            n1_blocks,
            stream,
            w_qkv,
            w_out,
            tab,
            gain_ffn,
            where,
        )
        if last:
            n2, grad_near, grad_far = after((n2, grad_near, grad_far))
        near, far = gather_near(n2)
        out_a, hid_a, dgelu_a = ffn_fwd(layer, near, w_in, w_down)
        if last:
            given = grad_near + gather_far(grad_far)
            gf_blocks = [jnp.concatenate([given[r][:side], given[tp_size - 1 - r][side:]], 0) for r in range(tp_size)]
            gn2_a, gpre_a = ffn_bwd(layer, gf_blocks[:half], dgelu_a, w_in, w_down)
            far, gpre_a = after((far, gpre_a))
        far, hid_a = after((far, hid_a))
        n2_blocks = near + gather_far(far)
        out_b, hid_b, dgelu_b = ffn_fwd(layer, n2_blocks[half:], w_in, w_down)
        kept.append((stream, n1t, p, u, q, k, v, ot, middle, n2_blocks, hid_a, hid_b, dgelu_a, dgelu_b))
        if not last:
            own, far = scatter_begin([*out_a, *out_b])
            stream = middle + (own + far.astype(F32))

    grad_flow = gf_blocks[0].astype(F32)
    per = width // dp_size
    small = [None] * LAYERS
    sharded = [None] * LAYERS
    for layer in range(LAYERS - 1, -1, -1):
        last = layer == LAYERS - 1
        stream, n1t, p, u, q, k, v, ot, middle, n2_blocks, hid_a, hid_b, dgelu_a, dgelu_b = kept[layer]
        if not last:
            near, far = gather_near(grad_flow.astype(BF16))
            gn2_a, gpre_a = ffn_bwd(layer, near, dgelu_a, w_in, w_down)
            far, gpre_a, moving.got = after((far, gpre_a, moving.got))
            (summed,) = moving.finish()
            sharded[layer + 1] = (summed[:per], summed[per:].T)
            gf_blocks = near + gather_far(far)
        gn2_b, gpre_b = ffn_bwd(layer, gf_blocks[half:], dgelu_b, w_in, w_down)
        if not last:
            total_got, gpre_b = after((total_got, gpre_b))
            total = halve_end(total_kept, total_got)
            total_kept, total_got = sum_start(total, total_order, 1)
        own, far = scatter_begin([*gn2_a, *gn2_b])
        packed = ffn_grads(n2_blocks, gf_blocks, (hid_a, hid_b), (gpre_a, gpre_b), dp_size)
        far, packed = after((far, packed))
        if not last:
            total_got, packed = after((total_got, packed))
            total = halve_end(total_kept, total_got)
            total_kept, total_got = sum_start(total, total_order, 2)
        moving = Scatter([packed], steps_of("dp"))
        if last:
            own_y, far_y = scatter_begin(after([*out_a, *out_b], packed))
        gn2 = (own + far.astype(F32)).astype(BF16).astype(F32)
        grad_norm, grad_gffn = rms_back(gn2, middle, gain_ffn[layer])
        grad_middle = grad_flow + grad_norm
        ga = grad_middle.astype(BF16)
        if last:
            orders = [steps_of("dp") + steps_of("tp")[1:]]
        else:
            (y_step, *dp_rest), x_steps = steps_of("dp"), steps_of("tp")[1:]
            orders = [x_steps + [y_step] + dp_rest, [y_step] + x_steps + dp_rest]
        place = jnp.stack([tp_index & 1] + [place_of(order) for order in orders] + [tp_index])
        parts, grads, zpre, zpost = attn_bwd(
            layer, tp_size, ga, w_out, q, k, v, p, u, tab, tabt, place, w_qkv, n1t, ot
        )
        core_step = steps_of("tp")[0]
        if last:
            parts, grads, moving.got, far_y, own_y = after((parts, grads, moving.got, far_y, own_y))
            y_out = (middle + (own_y + far_y.astype(F32))).astype(BF16)
            y_out = jnp.concatenate(mirror(y_out), 0)
            keep, send = grads
            total = halve_end(keep, swap(send, *core_step))
            own, far = scatter_begin(parts)
            moving.advance()
            far, moving.got = after((far, moving.got), total)
            moving.advance()
            (total_order,), total_place = orders, place
            total_kept, total_got = sum_start(total, total_order, 0)
        else:
            parts, grads, moving.got, total_got = after((parts, grads, moving.got, total_got))
        if not last:
            break
        gn1 = (own + far.astype(F32)).astype(BF16).astype(F32)
        grad_norm, grad_gattn = rms_back(gn1, stream, gain_attn[layer])
        grad_flow = grad_middle + grad_norm
        grad_mpre = jnp.sum(zpre.reshape(heads, heads, head_size), -1).T * (head_size**-0.5)
        grad_mpost = jnp.sum(zpost.reshape(heads, heads, head_size), -1)
        small[layer] = (grad_mpre, grad_mpost, grad_gattn, grad_gffn)

    total = halve_end(total_kept, total_got)
    got = [swap(send, *core_step) for send in grads[1::2]]
    pieces = [halve_end(keep, g) for keep, g in zip(grads[::2], got)]
    for stage in range(HALVINGS, len(total_order)):
        total_got = swap(total, *total_order[stage])
        pieces, total_got = after((pieces, total_got))
        total = halve_end(total, total_got)
    own, far = scatter_begin(parts)
    for stage in range(HALVINGS):
        kept, got = zip(*[sum_start(part, order, stage) for part, order in zip(pieces, orders)])
        total_got = swap(total, *total_order[HALVINGS - 1 - stage])
        if stage < HALVINGS - 1:
            got, total_got = after((got, total_got))
            total = spread(total, total_got)
        pieces = [halve_end(a, b) for a, b in zip(kept, after(got))]
        if stage == 0:
            far, pieces = after((far, pieces))
            gn1 = (own + far.astype(F32)).astype(BF16).astype(F32)
            grad_norm, grad_gattn = rms_back(gn1, stream, gain_attn[layer])
            grad_flow = grad_middle + grad_norm
            grad_mpre = jnp.sum(zpre.reshape(heads, heads, head_size), -1).T * (head_size**-0.5)
            grad_mpost = jnp.sum(zpost.reshape(heads, heads, head_size), -1)
            small[layer] = (grad_mpre, grad_mpost, grad_gattn, grad_gffn)
    mixes = jnp.concatenate([a.reshape(-1) for s in small for a in s[:2]])
    count = mixes.shape[0]
    mix_rows = -(-count // width)
    flat = jnp.concatenate(
        [jnp.pad(mixes, (0, mix_rows * width - count)).reshape(mix_rows, width)]
        + [g[None] for s in small for g in s[2:]]
    )
    flat = jnp.pad(flat, ((0, -flat.shape[0] % 8), (0, 0)))
    flat, pieces = after((flat, pieces))
    flat = Butterfly(flat)
    for stage in range(HALVINGS, len(orders[0])):
        got = [swap(part, *order[stage]) for part, order in zip(pieces, orders)]
        if stage == HALVINGS:
            first_rows, second_rows = mirror(grad_flow)
            got, second_rows = after((got, second_rows))
            grad_x = jnp.concatenate([first_rows, second_rows], 0)
        flat_got = flat.start()
        if stage == HALVINGS:
            got, flat_got, total_got = after((got, flat_got, total_got))
            total = spread(total, total_got)
        got, flat_got = after((got, flat_got))
        flat.end(flat_got)
        pieces = [halve_end(a, b) for a, b in zip(pieces, got)]
    total_other = swap(total, *core_step)
    moving.advance(*pieces)
    for stage in range(HALVINGS - 1, -1, -1):
        got = [swap(part, *order[stage]) for part, order in zip(pieces, orders)]
        flat_got = flat.start()
        if stage == HALVINGS - 1:
            got, flat_got, total_other = after((got, flat_got, total_other))
        if stage < HALVINGS - 1:
            got, moving.got = after((got, moving.got))
            moving.advance()
        if stage == 0:
            replicated = expand(1, total_place, [total], [total_other])
            got, flat_got, replicated = after((got, flat_got, replicated))
        got, flat_got = after((got, flat_got))
        flat.end(flat_got)
        pieces = [spread(a, b) for a, b in zip(pieces, got)]
    got = [swap(part, *core_step) for part in pieces]
    while flat.steps:
        flat.end(flat.start())
    flat = flat.value
    (summed,) = moving.finish()
    sharded[0] = (summed[:per], summed[per:].T)
    got, sharded = after((got, sharded))
    replicated = expand(0, place, pieces, got, replicated)
    mixes = flat[:mix_rows].reshape(-1)[:count].reshape(LAYERS, 2, heads, heads)
    gains = flat[mix_rows : mix_rows + 2 * LAYERS].reshape(LAYERS, 2, width)
    return (
        y_out[:, None],
        grad_x[:, None],
        *replicated,
        mixes[:, 0],
        mixes[:, 1],
        gains[:, 0],
        gains[:, 1],
        jnp.stack([s[0] for s in sharded]),
        jnp.stack([s[1] for s in sharded]),
    )


def solution(mesh):
    in_specs = (
        P("tp", "dp", None),
        P(None, "dp"),
        P(),
        P(),
        P(),
        P(),
        P(),
        P(),
        P(None, None, "tp"),
        P(None, "tp", None),
        P("tp", "dp", None),
    )
    out_specs = (
        P("tp", "dp", None),
        P("tp", "dp", None),
        P(),
        P(),
        P(),
        P(),
        P(),
        P(),
        P(None, "dp", "tp"),
        P(None, "tp", "dp"),
    )
    return jax.shard_map(
        on_device, mesh=mesh, in_specs=in_specs, out_specs=out_specs, check_vma=False
    )
```

```python
import functools

import jax
import jax.numpy as jnp
from jax import lax
from jax.experimental import pallas as pl
from jax.experimental.pallas import tpu as pltpu
from jax.sharding import PartitionSpec as P

LAYERS = 2
EPSILON = 1e-06
NEGATIVE = -1e30
LOG2E = 1.4426950408889634
GROUPS = 4
PIECES = 8
GP = 4
GB = 4
VMEM = 60 * 1024 * 1024
F32 = jnp.float32
BF16 = jnp.bfloat16


def dot_nn(a, b):
    return lax.dot_general(a, b, (((1,), (0,)), ((), ())), preferred_element_type=F32)


def dot_nt(a, b):
    return lax.dot_general(a, b, (((1,), (1,)), ((), ())), preferred_element_type=F32)


def dot_tn(a, b):
    return lax.dot_general(a, b, (((0,), (0,)), ((), ())), preferred_element_type=F32)


def rms(values, gain):
    return values * lax.rsqrt(jnp.mean(values * values, -1, keepdims=True) + EPSILON) * gain


def rms_back(grad, values, gain):
    inv = lax.rsqrt(jnp.mean(values * values, -1, keepdims=True) + EPSILON)
    unit = values * inv
    scaled = grad * gain
    grad_values = (scaled - unit * jnp.mean(scaled * unit, -1, keepdims=True)) * inv
    return grad_values, jnp.sum(grad * unit, axis=0)


def whole(shape):
    return pl.BlockSpec(shape, lambda *_: (0,) * len(shape))


def layer_of(array, layer):
    shape = array.shape[1:]
    return pl.BlockSpec((1,) + shape, lambda *_: (layer,) + (0,) * len(shape))


def attn_fwd_body(blocks, heads, layer, plain, *refs):
    n_refs = refs[:blocks]
    x_hbm, wqkv_hbm, wout_hbm, tab_ref, gain_ref, qinfo_ref, kinfo_ref, at_ref = refs[blocks : blocks + 8]
    p_ref, u_ref, q_ref, k_hbm, v_hbm, ot_ref, n1t_hbm, xm_ref, n2_ref = refs[blocks + 8 : blocks + 17]
    bias_ref, acc_ref, k_ref, v_ref, n1t_ref, x_ref, wqkv_ref, wout_ref, sems = refs[blocks + 17 :]
    step = pl.program_id(0)
    rows, width = x_ref.shape
    q_cols, k_cols, v_cols = [slice(i * width, (i + 1) * width) for i in range(3)]
    weights = [
        pltpu.make_async_copy(wqkv_hbm.at[layer, :, cols], wqkv_ref.at[i], sems.at[i])
        for i, cols in enumerate((k_cols, v_cols, q_cols))
    ]
    late = [
        pltpu.make_async_copy(wout_hbm.at[layer], wout_ref, sems.at[3]),
        pltpu.make_async_copy(x_hbm, x_ref, sems.at[4]),
    ]
    early = [
        pltpu.make_async_copy(k_ref, k_hbm, sems.at[5]),
        pltpu.make_async_copy(v_ref, v_hbm, sems.at[6]),
    ]
    turned = pltpu.make_async_copy(n1t_ref, n1t_hbm, sems.at[7])
    half = rows // 2
    at = at_ref[0]

    def place(r, second):
        block = chunk_of(at ^ r, second, blocks, plain)
        return pl.ds(pl.multiple_of(block * half, half), half)

    @pl.when(step == 0)
    def _():
        for copy in weights + late:
            copy.start()
        for i, ref in enumerate((k_ref, v_ref)):
            weights[i].wait()
            for r in range(blocks):
                value = dot_nn(n_refs[r][...], wqkv_ref[i]).astype(BF16)
                ref[place(r, 0), :] = value[:half]
                ref[place(r, 1), :] = value[half:]
            early[i].start()
        weights[2].wait()
        n_second = n_refs[blocks - 1 if plain else 0]
        q_ref[:half] = dot_nn(n_refs[0][:half], wqkv_ref[2]).astype(BF16)
        q_ref[half:] = dot_nn(n_second[half:], wqkv_ref[2]).astype(BF16)
        ok = (qinfo_ref[:, 1:2] == kinfo_ref[1:2, :]) & (kinfo_ref[0:1, :] <= qinfo_ref[:, 0:1])
        bias_ref[...] = jnp.where(ok, 0.0, NEGATIVE)
        acc_ref[...] = jnp.zeros_like(acc_ref)

    def work(here, keys):
        q = q_ref[here, :].astype(F32)
        gs = [step * GP + u for u in range(GP)]
        qm = jnp.concatenate([(q * (tab_ref[0, pl.ds(g, 1), :] * LOG2E)).astype(BF16) for g in gs], 0)
        m = dot_nt(qm, k_ref[:keys, :])
        bias = bias_ref[here, :keys]
        ps = []
        for u in range(GP):
            mu = m[u * half : (u + 1) * half] + bias
            e = jnp.exp2(mu - jnp.max(mu, -1, keepdims=True))
            p = (e * (1.0 / jnp.sum(e, -1, keepdims=True))).astype(BF16)
            p_ref[u, here, :keys] = p
            ps.append(p)
        ctx = dot_nn(jnp.concatenate(ps, 0), v_ref[:keys, :])
        total = acc_ref[here, :]
        for u in range(GP):
            cu = ctx[u * half : (u + 1) * half]
            u_ref[u, here, :] = cu.astype(BF16)
            total = total + cu * tab_ref[0, pl.ds(heads + gs[u], 1), :]
        acc_ref[here, :] = total

    for device in range(blocks):

        @pl.when(at == device)
        def _(device=device):
            for second in range(2):
                keys = (chunk_of(device, second, blocks, False) + 1) * half
                work(slice(second * half, (second + 1) * half), keys)

    @pl.when(step == 0)
    def _():
        for r in range(blocks):
            for second in range(2):
                n1t_ref[:, place(r, second)] = n_refs[r][second * half : (second + 1) * half, :].T
        turned.start()

    @pl.when(step == pl.num_programs(0) - 1)
    def _():
        o = acc_ref[...].astype(BF16)
        ot_ref[...] = o.T
        for copy in late + early + [turned]:
            copy.wait()
        xm = x_ref[...] + dot_nn(o, wout_ref[...])
        xm_ref[...] = xm
        n2_ref[...] = rms(xm, gain_ref[pl.ds(layer, 1), :]).astype(BF16)


def chunk_of(device, second, devices, plain):
    if not second:
        return 2 * device
    return 2 * device + 1 if plain else 2 * (devices - 1 - device) + 1


def attn_fwd(layer, plain, n_blocks, x, w_qkv, w_out, tab, gain, where):
    rows, width = x.shape
    blocks = len(n_blocks)
    heads = tab.shape[1] // 2
    keys = rows * blocks
    args = (*n_blocks, x, w_qkv, w_out, tab, gain, *where)
    in_specs = [whole(a.shape) for a in args]
    in_specs[blocks : blocks + 3] = [pl.BlockSpec(memory_space=pl.ANY)] * 3
    in_specs[blocks + 3] = layer_of(tab, layer)
    in_specs[-1] = pl.BlockSpec(memory_space=pltpu.SMEM)
    out = [
        ((heads, rows, keys), BF16),
        ((heads, rows, width), BF16),
        ((rows, width), BF16),
        ((keys, width), BF16),
        ((keys, width), BF16),
        ((width, rows), BF16),
        ((width, keys), BF16),
        ((rows, width), F32),
        ((rows, width), BF16),
    ]
    out_specs = [whole(s) for s, _ in out]
    out_specs[0] = pl.BlockSpec((GP, rows, keys), lambda i: (i, 0, 0))
    out_specs[1] = pl.BlockSpec((GP, rows, width), lambda i: (i, 0, 0))
    for i in (3, 4, 6):
        out_specs[i] = pl.BlockSpec(memory_space=pl.ANY)
    return pl.pallas_call(
        functools.partial(attn_fwd_body, blocks, heads, layer, plain),
        grid=(heads // GP,),
        in_specs=in_specs,
        out_specs=out_specs,
        out_shape=[jax.ShapeDtypeStruct(s, d) for s, d in out],
        scratch_shapes=[
            pltpu.VMEM((rows, keys), F32),
            pltpu.VMEM((rows, width), F32),
            pltpu.VMEM((keys, width), BF16),
            pltpu.VMEM((keys, width), BF16),
            pltpu.VMEM((width, keys), BF16),
            pltpu.VMEM((rows, width), F32),
            pltpu.VMEM((3, width, width), BF16),
            pltpu.VMEM((width, width), BF16),
            pltpu.SemaphoreType.DMA((8,)),
        ],
        compiler_params=pltpu.CompilerParams(vmem_limit_bytes=VMEM),
        cost_estimate=pl.CostEstimate(
            flops=2 * rows * keys * width * heads * 2, bytes_accessed=20_000_000, transcendentals=rows * keys * heads
        ),
        name="attn_fwd",
    )(*args)


def attn_bwd_body(heads, blocks, layer, parts, *refs):
    (ga_ref, wout_ref, q_ref, k_ref, v_ref, p_ref, u_ref, tab_ref, tabt_ref, place_ref) = refs[:10]
    wqkv_hbm, n1t_hbm, ot_hbm = refs[10:13]
    gn1_refs = refs[13 : 13 + blocks]
    grad_refs = refs[13 + blocks : 13 + blocks + 2 * parts]
    zpre_ref, zpost_ref = refs[13 + blocks + 2 * parts : 15 + blocks + 2 * parts]
    go_ref, got_ref, qt_ref, gq_acc, gk_acc, gv_acc, wqkv_ref, n1t_ref, ot_ref, sems = refs[15 + blocks + 2 * parts :]
    step = pl.program_id(0)
    rows, width = q_ref.shape

    late = [
        pltpu.make_async_copy(wqkv_hbm.at[layer], wqkv_ref, sems.at[0]),
        pltpu.make_async_copy(n1t_hbm, n1t_ref, sems.at[1]),
        pltpu.make_async_copy(ot_hbm, ot_ref, sems.at[2]),
    ]

    @pl.when(step == 0)
    def _():
        for copy in late:
            copy.start()
        go = dot_nt(ga_ref[...], wout_ref[0]).astype(BF16).astype(F32)
        go_ref[...] = go
        got_ref[...] = go.T
        qt_ref[...] = q_ref[...].astype(F32).T
        gq_acc[...] = jnp.zeros_like(gq_acc)
        gk_acc[...] = jnp.zeros_like(gk_acc)
        gv_acc[...] = jnp.zeros_like(gv_acc)

    half = rows // 2
    at = place_ref[1 + parts]
    lane = lax.broadcasted_iota(jnp.int32, tabt_ref.shape[1:], 1)
    gs = [step * GB + u for u in range(GB)]
    cols = []
    for g in gs:
        pre_col = jnp.sum(jnp.where(lane == g, tabt_ref[0], 0.0), 1, keepdims=True)
        post_col = jnp.sum(jnp.where(lane == heads + g, tabt_ref[0], 0.0), 1, keepdims=True)
        cols.append((pre_col, post_col))

    def work(second, keys):
        here = slice(second * half, (second + 1) * half)
        go = go_ref[here, :]
        q = q_ref[here, :].astype(F32)
        mixed = [go * tab_ref[0, pl.ds(heads + g, 1), :] for g in gs]
        gp = dot_nt(jnp.concatenate([x.astype(BF16) for x in mixed], 0), v_ref[:keys, :])
        gms, ps, zposts = [], [], []
        for u in range(GB):
            ctx = u_ref[u, here, :].astype(F32)
            zposts.append(jnp.sum(ctx * go, axis=0, keepdims=True))
            delta = jnp.sum(ctx * mixed[u], axis=1, keepdims=True)
            p = p_ref[u, here, :keys]
            gms.append((p.astype(F32) * (gp[u * half : (u + 1) * half] - delta)).astype(BF16))
            ps.append(p)
        gm = jnp.concatenate(gms, 0)
        t = dot_nn(gm, k_ref[:keys, :])
        total = gq_acc[here, :]
        zpres = []
        for u in range(GB):
            tu = t[u * half : (u + 1) * half]
            zpres.append(jnp.sum(tu * q, axis=0, keepdims=True))
            total = total + tu * tab_ref[0, pl.ds(gs[u], 1), :]
        gq_acc[here, :] = total
        qm = jnp.concatenate([(qt_ref[:, here] * pre).astype(BF16) for pre, _ in cols], 1)
        gk_acc[:, :keys] += dot_nn(qm, gm)
        gm2 = jnp.concatenate([(got_ref[:, here] * post).astype(BF16) for _, post in cols], 1)
        gv_acc[:, :keys] += dot_nn(gm2, jnp.concatenate(ps, 0))
        return zpres, zposts

    for device in range(blocks):

        @pl.when(at == device)
        def _(device=device):
            first, last = [work(s, (chunk_of(device, s, blocks, False) + 1) * half) for s in range(2)]
            for u, g in enumerate(gs):
                zpre_ref[pl.ds(g, 1), :] = first[0][u] + last[0][u]
                zpost_ref[pl.ds(g, 1), :] = first[1][u] + last[1][u]

    @pl.when(step == pl.num_programs(0) - 1)
    def _():
        for copy in late:
            copy.wait()
        gq = gq_acc[...].astype(BF16)
        gkt = gk_acc[...].astype(BF16)
        gvt = gv_acc[...].astype(BF16)
        ga = ga_ref[...]
        for r in range(blocks):
            there = [pl.ds(pl.multiple_of(chunk_of(at ^ r, x, blocks, False) * half, half), half) for x in range(2)]
            gk = jnp.concatenate([gk_acc[:, x].T.astype(BF16) for x in there], 0)
            gv = jnp.concatenate([gv_acc[:, x].T.astype(BF16) for x in there], 0)
            gn1 = dot_nt(gk, wqkv_ref[:, width : 2 * width]) + dot_nt(gv, wqkv_ref[:, 2 * width :])
            if r == 0:
                gn1 = gn1 + dot_nt(gq, wqkv_ref[:, :width])
            gn1_refs[r][...] = gn1.astype(BF16)
        hand = width // 2
        per = hand // PIECES
        own = [pl.ds(pl.multiple_of(chunk_of(at, x, blocks, False) * half, half), half) for x in range(2)]
        for side in range(2):
            core = place_ref[0] if side == 0 else 1 - place_ref[0]
            mine = pl.ds(pl.multiple_of(core * hand, hand), hand)
            n1t = n1t_ref[mine, :]
            n1t_own = jnp.concatenate([n1t_ref[mine, x] for x in own], 1)
            grads = (
                lambda: dot_nn(n1t_own, gq),
                lambda: dot_nt(n1t, gkt),
                lambda: dot_nt(n1t, gvt),
                lambda: dot_nn(ot_ref[mine, :], ga),
            )
            for index, grad in enumerate(grads):
                part = index * parts // len(grads)
                column = (index - part * (len(grads) // parts)) * width
                value = grad().astype(BF16)
                for piece in range(PIECES):
                    there = pl.multiple_of((piece ^ place_ref[1 + part]) * per, per)
                    grad_refs[2 * part + side][pl.ds(there, per), column : column + width] = value[
                        piece * per : (piece + 1) * per
                    ]


def attn_bwd(layer, blocks, ga, w_out, q, k, v, p, u, tab, tabt, place, w_qkv, n1t, ot):
    rows, width = q.shape
    keys = k.shape[0]
    heads = p.shape[0]
    parts = place.shape[0] - 2
    args = (ga, w_out, q, k, v, p, u, tab, tabt, place, w_qkv, n1t, ot)
    in_specs = [whole(a.shape) for a in args]
    in_specs[1] = layer_of(w_out, layer)
    in_specs[5] = pl.BlockSpec((GB, rows, keys), lambda i: (i, 0, 0))
    in_specs[6] = pl.BlockSpec((GB, rows, width), lambda i: (i, 0, 0))
    in_specs[7] = layer_of(tab, layer)
    in_specs[8] = layer_of(tabt, layer)
    in_specs[9] = pl.BlockSpec(memory_space=pltpu.SMEM)
    in_specs[10:13] = [pl.BlockSpec(memory_space=pl.ANY)] * 3
    out = (
        [((rows, width), BF16)] * blocks
        + [((width // 2, 4 // parts * width), BF16)] * (2 * parts)
        + [((heads, width), F32)] * 2
    )
    res = pl.pallas_call(
        functools.partial(attn_bwd_body, heads, blocks, layer, parts),
        grid=(heads // GB,),
        in_specs=in_specs,
        out_specs=[whole(s) for s, _ in out],
        out_shape=[jax.ShapeDtypeStruct(s, d) for s, d in out],
        scratch_shapes=[
            pltpu.VMEM((rows, width), F32),
            pltpu.VMEM((width, rows), F32),
            pltpu.VMEM((width, rows), F32),
            pltpu.VMEM((rows, width), F32),
            pltpu.VMEM((width, keys), F32),
            pltpu.VMEM((width, keys), F32),
            pltpu.VMEM(w_qkv.shape[1:], BF16),
            pltpu.VMEM(n1t.shape, BF16),
            pltpu.VMEM(ot.shape, BF16),
            pltpu.SemaphoreType.DMA((3,)),
        ],
        compiler_params=pltpu.CompilerParams(vmem_limit_bytes=VMEM),
        cost_estimate=pl.CostEstimate(
            flops=2 * rows * keys * width * heads * 4 * 2, bytes_accessed=20_000_000, transcendentals=0
        ),
        name="attn_bwd",
    )(*args)
    return res[:blocks], res[blocks:-2], res[-2], res[-1]


def expand_body(parts, place_ref, *refs):
    qkv_ref, out_ref = refs[-2:]
    width3 = qkv_ref.shape[2]
    inner = PIECES // GROUPS
    per = qkv_ref.shape[1] // inner
    column = 0
    for part, ref in enumerate(refs[:parts]):
        end = column + ref.shape[1]
        cut = min(end, width3)
        for piece in range(inner):
            here = slice(piece * per, (piece + 1) * per)
            there = piece ^ lax.rem(place_ref[1 + part], inner)
            value = ref[pl.ds(pl.multiple_of(there * per, per), per), :].astype(F32)
            qkv_ref[0, here, column:cut] = value[:, : cut - column]
            if end > width3:
                out_ref[0, here, :] = value[:, cut - column :]
        column = end


def expand(layer, side, place, halves, before=()):
    half = halves[0].shape[0]
    width = sum(h.shape[1] for h in halves) // 4
    per = half // GROUPS
    in_specs = []
    for part, array in enumerate(halves):

        def piece(i, place, part=part):
            return i ^ (place[1 + part] // (PIECES // GROUPS)), 0

        in_specs.append(pl.BlockSpec((per, array.shape[1]), piece))
    first = 1 + len(halves)
    in_specs += [pl.BlockSpec(memory_space=pl.ANY)] * len(before)

    def there(i, place):
        return layer, (place[0] ^ side) * GROUPS + i, 0

    return pl.pallas_call(
        functools.partial(expand_body, len(halves)),
        grid_spec=pltpu.PrefetchScalarGridSpec(
            num_scalar_prefetch=1,
            grid=(GROUPS,),
            in_specs=in_specs,
            out_specs=[pl.BlockSpec((1, per, 3 * width), there), pl.BlockSpec((1, per, width), there)],
        ),
        out_shape=[
            jax.ShapeDtypeStruct((LAYERS, 2 * half, 3 * width), F32),
            jax.ShapeDtypeStruct((LAYERS, 2 * half, width), F32),
        ],
        input_output_aliases={first + i: i for i in range(len(before))},
        compiler_params=pltpu.CompilerParams(vmem_limit_bytes=VMEM),
        cost_estimate=pl.CostEstimate(flops=0, bytes_accessed=7_000_000, transcendentals=0),
        name="expand",
    )(place, *halves, *before)


def ffn_fwd_body(blocks, *refs):
    n_refs = refs[:blocks]
    win_ref, wdown_ref = refs[blocks : blocks + 2]
    out_refs = refs[blocks + 2 : 2 * blocks + 2]
    hid_ref, dgelu_ref = refs[2 * blocks + 2 :]
    rows = n_refs[0].shape[0]
    for r in range(blocks):
        here = pl.ds(r * rows, rows)
        pre = dot_nn(n_refs[r][...], win_ref[0])
        cdf = 0.5 + 0.5 * lax.erf(pre * (0.5**0.5))
        hid = (pre * cdf).astype(BF16)
        hid_ref[here, :] = hid
        density = jnp.exp2(pre * pre * (-0.5 * LOG2E)) * 0.3989422804014327
        dgelu_ref[here, :] = (cdf + pre * density).astype(BF16)
        out_refs[r][...] = dot_nn(hid, wdown_ref[0]).astype(BF16)


def ffn_fwd(layer, n_blocks, w_in, w_down):
    blocks = len(n_blocks)
    rows, width = n_blocks[0].shape
    hidden = w_in.shape[2]
    args = (*n_blocks, w_in, w_down)
    in_specs = [whole(a.shape) for a in args]
    in_specs[blocks] = layer_of(w_in, layer)
    in_specs[blocks + 1] = layer_of(w_down, layer)
    out = [((rows, width), BF16)] * blocks + [((rows * blocks, hidden), BF16)] * 2
    res = pl.pallas_call(
        functools.partial(ffn_fwd_body, blocks),
        grid=(1,),
        in_specs=in_specs,
        out_specs=[whole(s) for s, _ in out],
        out_shape=[jax.ShapeDtypeStruct(s, d) for s, d in out],
        compiler_params=pltpu.CompilerParams(vmem_limit_bytes=VMEM),
        cost_estimate=pl.CostEstimate(
            flops=4 * rows * blocks * width * hidden, bytes_accessed=6_000_000, transcendentals=rows * blocks * hidden
        ),
        name="ffn_fwd",
    )(*args)
    return res[:blocks], res[blocks], res[blocks + 1]


def ffn_bwd_body(blocks, *refs):
    g_refs = refs[:blocks]
    dgelu_ref, win_ref, wdown_ref = refs[blocks : blocks + 3]
    out_refs = refs[blocks + 3 : 2 * blocks + 3]
    gpre_ref = refs[2 * blocks + 3]
    rows = g_refs[0].shape[0]
    for r in range(blocks):
        here = pl.ds(r * rows, rows)
        gh = dot_nt(g_refs[r][...], wdown_ref[0])
        gpre = (gh * dgelu_ref[here, :].astype(F32)).astype(BF16)
        gpre_ref[here, :] = gpre
        out_refs[r][...] = dot_nt(gpre, win_ref[0]).astype(BF16)


def ffn_bwd(layer, g_blocks, dgelu, w_in, w_down):
    blocks = len(g_blocks)
    rows, width = g_blocks[0].shape
    hidden = w_in.shape[2]
    args = (*g_blocks, dgelu, w_in, w_down)
    in_specs = [whole(a.shape) for a in args]
    in_specs[blocks + 1] = layer_of(w_in, layer)
    in_specs[blocks + 2] = layer_of(w_down, layer)
    out = [((rows, width), BF16)] * blocks + [((rows * blocks, hidden), BF16)]
    res = pl.pallas_call(
        functools.partial(ffn_bwd_body, blocks),
        grid=(1,),
        in_specs=in_specs,
        out_specs=[whole(s) for s, _ in out],
        out_shape=[jax.ShapeDtypeStruct(s, d) for s, d in out],
        compiler_params=pltpu.CompilerParams(vmem_limit_bytes=VMEM),
        cost_estimate=pl.CostEstimate(
            flops=4 * rows * blocks * width * hidden, bytes_accessed=6_000_000, transcendentals=0
        ),
        name="ffn_bwd",
    )(*args)
    return res[:blocks], res[blocks]


def ffn_grads_body(blocks, chunks, *refs):
    n_refs, g_refs = refs[:blocks], refs[blocks : 2 * blocks]
    hid_refs, gpre_refs = refs[2 * blocks : 2 * blocks + 2], refs[2 * blocks + 2 : 2 * blocks + 4]
    out_ref = refs[-1]
    rows, width = n_refs[0].shape
    per = width // chunks
    for part, (left_refs, right_refs) in enumerate(((n_refs, gpre_refs), (g_refs, hid_refs))):
        left = jnp.concatenate([ref[...].T for ref in left_refs], 1)
        right = jnp.concatenate([ref[...] for ref in right_refs], 0)
        grad = dot_nn(left, right).astype(BF16)
        for c in range(chunks):
            place = 2 * sum(((c >> i) & 1) * (chunks >> (i + 1)) for i in range(chunks.bit_length() - 1)) + part
            out_ref[place * per : (place + 1) * per, :] = grad[c * per : (c + 1) * per]


def ffn_grads(n_blocks, g_blocks, hids, gpres, chunks):
    blocks = len(n_blocks)
    rows, width = n_blocks[0].shape
    hidden = hids[0].shape[1]
    args = (*n_blocks, *g_blocks, *hids, *gpres)
    return pl.pallas_call(
        functools.partial(ffn_grads_body, blocks, chunks),
        grid=(1,),
        in_specs=[whole(a.shape) for a in args],
        out_specs=whole((2 * width, hidden)),
        out_shape=jax.ShapeDtypeStruct((2 * width, hidden), BF16),
        compiler_params=pltpu.CompilerParams(vmem_limit_bytes=VMEM),
        cost_estimate=pl.CostEstimate(
            flops=4 * rows * blocks * width * hidden, bytes_accessed=9_000_000, transcendentals=0
        ),
        name="ffn_grads",
    )(*args)


def swap(value, axis, bit):
    size = lax.axis_size(axis)
    return lax.ppermute(value, axis, [(i, i ^ bit) for i in range(size)])


def after(values, *done):
    return lax.optimization_barrier((values, done))[0]


def gather_near(value):
    half = lax.axis_size("tp") // 2
    far = swap(value, "tp", half)
    near = [value]
    bit = 1
    while bit < half:
        near += [swap(b, "tp", bit) for b in near]
        bit *= 2
    return near, far


def gather_far(far):
    half = lax.axis_size("tp") // 2
    blocks = [far]
    bit = 1
    while bit < half:
        blocks += [swap(b, "tp", bit) for b in blocks]
        bit *= 2
    return blocks


def gather_blocks(value):
    near, far = gather_near(value)
    return near + gather_far(far)


def scatter_begin(blocks):
    blocks = list(blocks)
    bit = 1
    while bit < lax.axis_size("tp") // 2:
        size = len(blocks)
        keep = [blocks[r] for r in range(size) if not r & 1]
        sent = [swap(blocks[r], "tp", bit) for r in range(size) if r & 1]
        blocks = [a.astype(F32) + b.astype(F32) for a, b in zip(keep, sent)]
        bit *= 2
        blocks = [blocks[0]] + [b.astype(BF16) for b in blocks[1:]]
    return blocks[0].astype(F32), swap(blocks[1], "tp", bit)


def halve_begin(part, axis, bit):
    mine = (lax.axis_index(axis) // bit) & 1
    pair = part.reshape(2, part.shape[0] // 2, part.shape[1])
    sent = lax.dynamic_index_in_dim(pair, 1 - mine, 0, keepdims=False)
    kept = lax.dynamic_index_in_dim(pair, mine, 0, keepdims=False)
    return kept, swap(sent, axis, bit)


def halve_end(kept, got):
    return (kept.astype(F32) + got.astype(F32)).astype(BF16)


class Scatter:
    def __init__(self, parts, steps):
        self.steps = list(steps)
        self.begin(parts)

    def begin(self, parts):
        step = self.steps.pop(0)
        self.kept, self.got = zip(*[halve_begin(part, *step) for part in parts])

    def advance(self, *done):
        if self.steps:
            got = after(self.got, *done)
            self.begin([halve_end(a, b) for a, b in zip(self.kept, got)])

    def finish(self, *done):
        while self.steps:
            self.advance(*done)
        return [a.astype(F32) + b.astype(F32) for a, b in zip(self.kept, after(self.got, *done))]


def steps_of(axis):
    return [(axis, 1 << i) for i in range(lax.axis_size(axis).bit_length() - 1)]


HALVINGS = PIECES.bit_length() - 1


def place_of(order):
    number = 0
    for axis, bit in order[:HALVINGS]:
        number = 2 * number + ((lax.axis_index(axis) // bit) & 1)
    return number


def sum_start(part, order, stage):
    if stage < HALVINGS:
        rows = part.shape[0] // 2
        return part[:rows], swap(part[rows:], *order[stage])
    return part, swap(part, *order[stage])


def spread(part, got):
    return jnp.concatenate([part, got], 0)


class Butterfly:
    def __init__(self, value):
        self.value = value
        self.steps = steps_of("tp") + steps_of("dp")
        self.got = None

    def start(self):
        if self.steps:
            self.got = swap(self.value, *self.steps.pop(0))
            return [self.got]
        return []

    def end(self, got):
        for g in got:
            self.value = self.value + g


def on_device(
    x_in, segments, w_qkv, w_out, mix_pre, mix_post, gain_attn, gain_ffn, w_in, w_down, cotangent
):
    rows, _, width = x_in.shape
    heads = mix_pre.shape[1]
    head_size = width // heads
    tp_size = lax.axis_size("tp")
    dp_size = lax.axis_size("dp")
    tp_index = lax.axis_index("tp")
    seg = segments[:, 0]
    side = rows // 2
    span = jnp.arange(side, dtype=jnp.int32)
    starts = [chunk_of(tp_index, x, tp_size, False) * side for x in range(2)]
    qpos = jnp.concatenate([start + span for start in starts])
    qseg = jnp.concatenate([lax.dynamic_slice_in_dim(seg, start, side, 0) for start in starts])
    qinfo = jnp.stack([qpos, qseg] + [qpos] * 6, 1)
    kinfo = jnp.pad(jnp.stack([jnp.arange(seg.shape[0], dtype=jnp.int32), seg]), ((0, 6), (0, 0)))
    where = (qinfo, kinfo, tp_index[None])

    def mirror(value):
        moved = lax.ppermute(value[side:], "tp", [(i, tp_size - 1 - i) for i in range(tp_size)])
        return value[:side], moved

    tab = jnp.concatenate([jnp.swapaxes(mix_pre, 1, 2) * (head_size**-0.5), mix_post], 1)
    tabt = jnp.pad(jnp.repeat(jnp.swapaxes(tab, 1, 2), head_size, axis=1), ((0, 0), (0, 0), (0, 128 - 2 * heads)))
    tab = jnp.repeat(tab, head_size, axis=2)

    stream = x_in[:, 0].astype(F32)
    x_folded = jnp.concatenate(mirror(x_in[:, 0]), 0).astype(F32)
    kept = []
    half = tp_size // 2
    for layer in range(LAYERS):
        last = layer == LAYERS - 1
        n1_blocks = gather_blocks(rms(stream, gain_attn[layer]).astype(BF16))
        if last:
            low, n1_blocks[half] = after((cotangent[:, 0], n1_blocks[half]))
            grad_near, grad_far = gather_near(low)
        else:
            stream = x_folded
        p, u, q, k, v, ot, n1t, middle, n2 = attn_fwd(
            layer,
            layer == 0,
            n1_blocks,
            stream,
            w_qkv,
            w_out,
            tab,
            gain_ffn,
            where,
        )
        if last:
            n2, grad_near, grad_far = after((n2, grad_near, grad_far))
        near, far = gather_near(n2)
        out_a, hid_a, dgelu_a = ffn_fwd(layer, near, w_in, w_down)
        if last:
            given = grad_near + gather_far(grad_far)
            gf_blocks = [jnp.concatenate([given[r][:side], given[tp_size - 1 - r][side:]], 0) for r in range(tp_size)]
            gn2_a, gpre_a = ffn_bwd(layer, gf_blocks[:half], dgelu_a, w_in, w_down)
            far, gpre_a = after((far, gpre_a))
        far, hid_a = after((far, hid_a))
        n2_blocks = near + gather_far(far)
        out_b, hid_b, dgelu_b = ffn_fwd(layer, n2_blocks[half:], w_in, w_down)
        kept.append((stream, n1t, p, u, q, k, v, ot, middle, n2_blocks, hid_a, hid_b, dgelu_a, dgelu_b))
        if not last:
            own, far = scatter_begin([*out_a, *out_b])
            stream = middle + (own + far.astype(F32))

    grad_flow = gf_blocks[0].astype(F32)
    per = width // dp_size
    small = [None] * LAYERS
    sharded = [None] * LAYERS
    for layer in range(LAYERS - 1, -1, -1):
        last = layer == LAYERS - 1
        stream, n1t, p, u, q, k, v, ot, middle, n2_blocks, hid_a, hid_b, dgelu_a, dgelu_b = kept[layer]
        if not last:
            near, far = gather_near(grad_flow.astype(BF16))
            gn2_a, gpre_a = ffn_bwd(layer, near, dgelu_a, w_in, w_down)
            far, gpre_a = after((far, gpre_a))
            gf_blocks = near + gather_far(far)
        gn2_b, gpre_b = ffn_bwd(layer, gf_blocks[half:], dgelu_b, w_in, w_down)
        if not last:
            total_got, gpre_b = after((total_got, gpre_b))
            total = halve_end(total_kept, total_got)
            total_kept, total_got = sum_start(total, total_order, 1)
        own, far = scatter_begin([*gn2_a, *gn2_b])
        packed = ffn_grads(n2_blocks, gf_blocks, (hid_a, hid_b), (gpre_a, gpre_b), dp_size)
        far, packed = after((far, packed))
        if not last:
            total_got, packed = after((total_got, packed))
            total = halve_end(total_kept, total_got)
            total_kept, total_got = sum_start(total, total_order, 2)
        if not last:
            previous = moving
        moving = Scatter([packed], steps_of("dp"))
        if last:
            own_y, far_y = scatter_begin(after([*out_a, *out_b], packed))
        gn2 = (own + far.astype(F32)).astype(BF16).astype(F32)
        grad_norm, grad_gffn = rms_back(gn2, middle, gain_ffn[layer])
        grad_middle = grad_flow + grad_norm
        ga = grad_middle.astype(BF16)
        if last:
            orders = [steps_of("dp") + steps_of("tp")[1:]]
        else:
            (y_step, *dp_rest), x_steps = steps_of("dp"), steps_of("tp")[1:]
            orders = [x_steps + [y_step] + dp_rest, [y_step] + x_steps + dp_rest]
        place = jnp.stack([tp_index & 1] + [place_of(order) for order in orders] + [tp_index])
        parts, grads, zpre, zpost = attn_bwd(
            layer, tp_size, ga, w_out, q, k, v, p, u, tab, tabt, place, w_qkv, n1t, ot
        )
        core_step = steps_of("tp")[0]
        if last:
            parts, grads, moving.got, far_y, own_y = after((parts, grads, moving.got, far_y, own_y))
            y_out = (middle + (own_y + far_y.astype(F32))).astype(BF16)
            y_out = jnp.concatenate(mirror(y_out), 0)
            keep, send = grads
            total = halve_end(keep, swap(send, *core_step))
            own, far = scatter_begin(parts)
            moving.advance()
            far, moving.got = after((far, moving.got), total)
            moving.advance()
            (total_order,), total_place = orders, place
            total_kept, total_got = sum_start(total, total_order, 0)
        else:
            parts, grads, moving.got, total_got, previous.got = after(
                (parts, grads, moving.got, total_got, previous.got)
            )
            (summed,) = previous.finish()
            sharded[layer + 1] = (summed[:per], summed[per:].T)
        if not last:
            break
        gn1 = (own + far.astype(F32)).astype(BF16).astype(F32)
        grad_norm, grad_gattn = rms_back(gn1, stream, gain_attn[layer])
        grad_flow = grad_middle + grad_norm
        grad_mpre = jnp.sum(zpre.reshape(heads, heads, head_size), -1).T * (head_size**-0.5)
        grad_mpost = jnp.sum(zpost.reshape(heads, heads, head_size), -1)
        small[layer] = (grad_mpre, grad_mpost, grad_gattn, grad_gffn)

    total = halve_end(total_kept, total_got)
    got = [swap(send, *core_step) for send in grads[1::2]]
    pieces = [halve_end(keep, g) for keep, g in zip(grads[::2], got)]
    for stage in range(HALVINGS, len(total_order)):
        total_got = swap(total, *total_order[stage])
        pieces, total_got = after((pieces, total_got))
        total = halve_end(total, total_got)
    own, far = scatter_begin(parts)
    for stage in range(HALVINGS):
        kept, got = zip(*[sum_start(part, order, stage) for part, order in zip(pieces, orders)])
        total_got = swap(total, *total_order[HALVINGS - 1 - stage])
        if stage < HALVINGS - 1:
            got, total_got = after((got, total_got))
            total = spread(total, total_got)
        if stage == HALVINGS - 1:
            flat_got = flat.start()
            got, flat_got = after((got, flat_got))
            flat.end(flat_got)
        pieces = [halve_end(a, b) for a, b in zip(kept, after(got))]
        if stage == 0:
            far, pieces = after((far, pieces))
            gn1 = (own + far.astype(F32)).astype(BF16).astype(F32)
            grad_norm, grad_gattn = rms_back(gn1, stream, gain_attn[layer])
            grad_flow = grad_middle + grad_norm
            grad_mpre = jnp.sum(zpre.reshape(heads, heads, head_size), -1).T * (head_size**-0.5)
            grad_mpost = jnp.sum(zpost.reshape(heads, heads, head_size), -1)
            small[layer] = (grad_mpre, grad_mpost, grad_gattn, grad_gffn)
            mixes = jnp.concatenate([a.reshape(-1) for s in small for a in s[:2]])
            count = mixes.shape[0]
            mix_rows = -(-count // width)
            flat = jnp.concatenate(
                [jnp.pad(mixes, (0, mix_rows * width - count)).reshape(mix_rows, width)]
                + [g[None] for s in small for g in s[2:]]
            )
            flat = jnp.pad(flat, ((0, -flat.shape[0] % 8), (0, 0)))
            flat = Butterfly(flat)
        if stage == 1:
            moving.advance(*pieces)
    for stage in range(HALVINGS, len(orders[0])):
        got = [swap(part, *order[stage]) for part, order in zip(pieces, orders)]
        flat_got = flat.start()
        if stage == HALVINGS:
            first_rows, second_rows = mirror(grad_flow)
            got, second_rows, total_got, moving.got = after((got, second_rows, total_got, moving.got))
            grad_x = jnp.concatenate([first_rows, second_rows], 0)
            total = spread(total, total_got)
            moving.advance()
        got, flat_got = after((got, flat_got))
        flat.end(flat_got)
        pieces = [halve_end(a, b) for a, b in zip(pieces, got)]
    total_other = swap(total, *core_step)
    replicated = ()
    for stage in range(HALVINGS - 1, -1, -1):
        got = [swap(part, *order[stage]) for part, order in zip(pieces, orders)]
        flat_got = flat.start()
        if stage == HALVINGS - 1:
            got, total_other = after((got, total_other))
        elif stage == HALVINGS - 2:
            replicated = expand(1, 0, total_place, [total])
            got, replicated, moving.got = after((got, replicated, moving.got))
        elif stage == 0:
            replicated = expand(1, 1, total_place, [total_other], replicated)
            got, replicated = after((got, replicated))
        got, flat_got = after((got, flat_got))
        flat.end(flat_got)
        pieces = [spread(a, b) for a, b in zip(pieces, got)]
    got = [swap(part, *core_step) for part in pieces]
    while flat.steps:
        flat.end(flat.start())
    flat = flat.value
    (summed,) = moving.finish()
    sharded[0] = (summed[:per], summed[per:].T)
    replicated = expand(0, 0, place, pieces, replicated)
    got, replicated, sharded = after((got, replicated, sharded))
    replicated = expand(0, 1, place, got, replicated)
    mixes = flat[:mix_rows].reshape(-1)[:count].reshape(LAYERS, 2, heads, heads)
    gains = flat[mix_rows : mix_rows + 2 * LAYERS].reshape(LAYERS, 2, width)
    return (
        y_out[:, None],
        grad_x[:, None],
        *replicated,
        mixes[:, 0],
        mixes[:, 1],
        gains[:, 0],
        gains[:, 1],
        jnp.stack([s[0] for s in sharded]),
        jnp.stack([s[1] for s in sharded]),
    )


def solution(mesh):
    in_specs = (
        P("tp", "dp", None),
        P(None, "dp"),
        P(),
        P(),
        P(),
        P(),
        P(),
        P(),
        P(None, None, "tp"),
        P(None, "tp", None),
        P("tp", "dp", None),
    )
    out_specs = (
        P("tp", "dp", None),
        P("tp", "dp", None),
        P(),
        P(),
        P(),
        P(),
        P(),
        P(),
        P(None, "dp", "tp"),
        P(None, "tp", "dp"),
    )
    return jax.shard_map(
        on_device, mesh=mesh, in_specs=in_specs, out_specs=out_specs, check_vma=False
    )
```

```python
import functools

import jax
import jax.numpy as jnp
from jax import lax
from jax.experimental import pallas as pl
from jax.experimental.pallas import tpu as pltpu
from jax.sharding import PartitionSpec as P

LAYERS = 2
EPSILON = 1e-06
NEGATIVE = -1e30
LOG2E = 1.4426950408889634
GROUPS = 4
PIECES = 8
GP = 4
GB = 4
VMEM = 60 * 1024 * 1024
MIDDLE = 40 * 1024 * 1024
SMALL = 24 * 1024 * 1024
F32 = jnp.float32
BF16 = jnp.bfloat16


def dot_nn(a, b):
    return lax.dot_general(a, b, (((1,), (0,)), ((), ())), preferred_element_type=F32)


def dot_nt(a, b):
    return lax.dot_general(a, b, (((1,), (1,)), ((), ())), preferred_element_type=F32)


def dot_tn(a, b):
    return lax.dot_general(a, b, (((0,), (0,)), ((), ())), preferred_element_type=F32)


def rms(values, gain):
    return values * lax.rsqrt(jnp.mean(values * values, -1, keepdims=True) + EPSILON) * gain


def rms_back(grad, values, gain):
    inv = lax.rsqrt(jnp.mean(values * values, -1, keepdims=True) + EPSILON)
    unit = values * inv
    scaled = grad * gain
    grad_values = (scaled - unit * jnp.mean(scaled * unit, -1, keepdims=True)) * inv
    return grad_values, jnp.sum(grad * unit, axis=0)


def whole(shape):
    return pl.BlockSpec(shape, lambda *_: (0,) * len(shape))


def layer_of(array, layer):
    shape = array.shape[1:]
    return pl.BlockSpec((1,) + shape, lambda *_: (layer,) + (0,) * len(shape))


def attn_fwd_body(blocks, heads, layer, plain, *refs):
    n_refs = refs[:blocks]
    x_hbm, wqkv_hbm, wout_hbm, tab_ref, gain_ref, qinfo_ref, kinfo_ref, at_ref = refs[blocks : blocks + 8]
    p_ref, u_ref, q_ref, k_hbm, v_hbm, ot_ref, n1t_hbm, xm_ref, n2_ref = refs[blocks + 8 : blocks + 17]
    bias_ref, acc_ref, k_ref, v_ref, n1t_ref, x_ref, wqkv_ref, wout_ref, sems = refs[blocks + 17 :]
    step = pl.program_id(0)
    rows, width = x_ref.shape
    q_cols, k_cols, v_cols = [slice(i * width, (i + 1) * width) for i in range(3)]
    weights = [
        pltpu.make_async_copy(wqkv_hbm.at[layer, :, cols], wqkv_ref.at[i], sems.at[i])
        for i, cols in enumerate((k_cols, v_cols, q_cols))
    ]
    late = [
        pltpu.make_async_copy(wout_hbm.at[layer], wout_ref, sems.at[3]),
        pltpu.make_async_copy(x_hbm, x_ref, sems.at[4]),
    ]
    early = [
        pltpu.make_async_copy(k_ref, k_hbm, sems.at[5]),
        pltpu.make_async_copy(v_ref, v_hbm, sems.at[6]),
    ]
    turned = pltpu.make_async_copy(n1t_ref, n1t_hbm, sems.at[7])
    half = rows // 2
    at = at_ref[0]

    def place(r, second):
        block = chunk_of(at ^ r, second, blocks, plain)
        return pl.ds(pl.multiple_of(block * half, half), half)

    @pl.when(step == 0)
    def _():
        for copy in weights + late:
            copy.start()
        for i, ref in enumerate((k_ref, v_ref)):
            weights[i].wait()
            for r in range(blocks):
                value = dot_nn(n_refs[r][...], wqkv_ref[i]).astype(BF16)
                ref[place(r, 0), :] = value[:half]
                ref[place(r, 1), :] = value[half:]
            early[i].start()
        weights[2].wait()
        n_second = n_refs[blocks - 1 if plain else 0]
        q_ref[:half] = dot_nn(n_refs[0][:half], wqkv_ref[2]).astype(BF16)
        q_ref[half:] = dot_nn(n_second[half:], wqkv_ref[2]).astype(BF16)
        ok = (qinfo_ref[:, 1:2] == kinfo_ref[1:2, :]) & (kinfo_ref[0:1, :] <= qinfo_ref[:, 0:1])
        bias_ref[...] = jnp.where(ok, 0.0, NEGATIVE)
        acc_ref[...] = jnp.zeros_like(acc_ref)

    def work(here, keys):
        q = q_ref[here, :].astype(F32)
        gs = [step * GP + u for u in range(GP)]
        qm = jnp.concatenate([(q * (tab_ref[0, pl.ds(g, 1), :] * LOG2E)).astype(BF16) for g in gs], 0)
        m = dot_nt(qm, k_ref[:keys, :])
        bias = bias_ref[here, :keys]
        ps = []
        for u in range(GP):
            mu = m[u * half : (u + 1) * half] + bias
            e = jnp.exp2(mu - jnp.max(mu, -1, keepdims=True))
            p = (e * (1.0 / jnp.sum(e, -1, keepdims=True))).astype(BF16)
            p_ref[u, here, :keys] = p
            ps.append(p)
        ctx = dot_nn(jnp.concatenate(ps, 0), v_ref[:keys, :])
        total = acc_ref[here, :]
        for u in range(GP):
            cu = ctx[u * half : (u + 1) * half]
            u_ref[u, here, :] = cu.astype(BF16)
            total = total + cu * tab_ref[0, pl.ds(heads + gs[u], 1), :]
        acc_ref[here, :] = total

    for device in range(blocks):

        @pl.when(at == device)
        def _(device=device):
            for second in range(2):
                keys = (chunk_of(device, second, blocks, False) + 1) * half
                work(slice(second * half, (second + 1) * half), keys)

    @pl.when(step == 0)
    def _():
        for r in range(blocks):
            for second in range(2):
                n1t_ref[:, place(r, second)] = n_refs[r][second * half : (second + 1) * half, :].T
        turned.start()

    @pl.when(step == pl.num_programs(0) - 1)
    def _():
        o = acc_ref[...].astype(BF16)
        ot_ref[...] = o.T
        for copy in late + early + [turned]:
            copy.wait()
        xm = x_ref[...] + dot_nn(o, wout_ref[...])
        xm_ref[...] = xm
        n2_ref[...] = rms(xm, gain_ref[pl.ds(layer, 1), :]).astype(BF16)


def chunk_of(device, second, devices, plain):
    if not second:
        return 2 * device
    return 2 * device + 1 if plain else 2 * (devices - 1 - device) + 1


def attn_fwd(layer, plain, n_blocks, x, w_qkv, w_out, tab, gain, where):
    rows, width = x.shape
    blocks = len(n_blocks)
    heads = tab.shape[1] // 2
    keys = rows * blocks
    args = (*n_blocks, x, w_qkv, w_out, tab, gain, *where)
    in_specs = [whole(a.shape) for a in args]
    in_specs[blocks : blocks + 3] = [pl.BlockSpec(memory_space=pl.ANY)] * 3
    in_specs[blocks + 3] = layer_of(tab, layer)
    in_specs[-1] = pl.BlockSpec(memory_space=pltpu.SMEM)
    out = [
        ((heads, rows, keys), BF16),
        ((heads, rows, width), BF16),
        ((rows, width), BF16),
        ((keys, width), BF16),
        ((keys, width), BF16),
        ((width, rows), BF16),
        ((width, keys), BF16),
        ((rows, width), F32),
        ((rows, width), BF16),
    ]
    out_specs = [whole(s) for s, _ in out]
    out_specs[0] = pl.BlockSpec((GP, rows, keys), lambda i: (i, 0, 0))
    out_specs[1] = pl.BlockSpec((GP, rows, width), lambda i: (i, 0, 0))
    for i in (3, 4, 6):
        out_specs[i] = pl.BlockSpec(memory_space=pl.ANY)
    return pl.pallas_call(
        functools.partial(attn_fwd_body, blocks, heads, layer, plain),
        grid=(heads // GP,),
        in_specs=in_specs,
        out_specs=out_specs,
        out_shape=[jax.ShapeDtypeStruct(s, d) for s, d in out],
        scratch_shapes=[
            pltpu.VMEM((rows, keys), F32),
            pltpu.VMEM((rows, width), F32),
            pltpu.VMEM((keys, width), BF16),
            pltpu.VMEM((keys, width), BF16),
            pltpu.VMEM((width, keys), BF16),
            pltpu.VMEM((rows, width), F32),
            pltpu.VMEM((3, width, width), BF16),
            pltpu.VMEM((width, width), BF16),
            pltpu.SemaphoreType.DMA((8,)),
        ],
        compiler_params=pltpu.CompilerParams(vmem_limit_bytes=MIDDLE),
        cost_estimate=pl.CostEstimate(
            flops=2 * rows * keys * width * heads * 2, bytes_accessed=20_000_000, transcendentals=rows * keys * heads
        ),
        name="attn_fwd",
    )(*args)


def attn_bwd_body(heads, blocks, layer, parts, *refs):
    (ga_ref, wout_ref, q_ref, k_ref, v_ref, p_ref, u_ref, tab_ref, tabt_ref, place_ref) = refs[:10]
    wqkv_hbm, n1t_hbm, ot_hbm = refs[10:13]
    gn1_refs = refs[13 : 13 + blocks]
    grad_refs = refs[13 + blocks : 13 + blocks + 2 * parts]
    zpre_ref, zpost_ref = refs[13 + blocks + 2 * parts : 15 + blocks + 2 * parts]
    go_ref, got_ref, qt_ref, gq_acc, gk_acc, gv_acc, wqkv_ref, n1t_ref, ot_ref, sems = refs[15 + blocks + 2 * parts :]
    step = pl.program_id(0)
    rows, width = q_ref.shape

    late = [
        pltpu.make_async_copy(wqkv_hbm.at[layer], wqkv_ref, sems.at[0]),
        pltpu.make_async_copy(n1t_hbm, n1t_ref, sems.at[1]),
        pltpu.make_async_copy(ot_hbm, ot_ref, sems.at[2]),
    ]

    @pl.when(step == 0)
    def _():
        for copy in late:
            copy.start()
        go = dot_nt(ga_ref[...], wout_ref[0]).astype(BF16).astype(F32)
        go_ref[...] = go
        got_ref[...] = go.T
        qt_ref[...] = q_ref[...].astype(F32).T
        gq_acc[...] = jnp.zeros_like(gq_acc)
        gk_acc[...] = jnp.zeros_like(gk_acc)
        gv_acc[...] = jnp.zeros_like(gv_acc)

    half = rows // 2
    at = place_ref[1 + parts]
    lane = lax.broadcasted_iota(jnp.int32, tabt_ref.shape[1:], 1)
    gs = [step * GB + u for u in range(GB)]
    cols = []
    for g in gs:
        pre_col = jnp.sum(jnp.where(lane == g, tabt_ref[0], 0.0), 1, keepdims=True)
        post_col = jnp.sum(jnp.where(lane == heads + g, tabt_ref[0], 0.0), 1, keepdims=True)
        cols.append((pre_col, post_col))

    def work(second, keys):
        here = slice(second * half, (second + 1) * half)
        go = go_ref[here, :]
        q = q_ref[here, :].astype(F32)
        mixed = [go * tab_ref[0, pl.ds(heads + g, 1), :] for g in gs]
        gp = dot_nt(jnp.concatenate([x.astype(BF16) for x in mixed], 0), v_ref[:keys, :])
        gms, ps, zposts = [], [], []
        for u in range(GB):
            ctx = u_ref[u, here, :].astype(F32)
            zposts.append(jnp.sum(ctx * go, axis=0, keepdims=True))
            delta = jnp.sum(ctx * mixed[u], axis=1, keepdims=True)
            p = p_ref[u, here, :keys]
            gms.append((p.astype(F32) * (gp[u * half : (u + 1) * half] - delta)).astype(BF16))
            ps.append(p)
        gm = jnp.concatenate(gms, 0)
        t = dot_nn(gm, k_ref[:keys, :])
        total = gq_acc[here, :]
        zpres = []
        for u in range(GB):
            tu = t[u * half : (u + 1) * half]
            zpres.append(jnp.sum(tu * q, axis=0, keepdims=True))
            total = total + tu * tab_ref[0, pl.ds(gs[u], 1), :]
        gq_acc[here, :] = total
        qm = jnp.concatenate([(qt_ref[:, here] * pre).astype(BF16) for pre, _ in cols], 1)
        gk_acc[:, :keys] += dot_nn(qm, gm)
        gm2 = jnp.concatenate([(got_ref[:, here] * post).astype(BF16) for _, post in cols], 1)
        gv_acc[:, :keys] += dot_nn(gm2, jnp.concatenate(ps, 0))
        return zpres, zposts

    for device in range(blocks):

        @pl.when(at == device)
        def _(device=device):
            first, last = [work(s, (chunk_of(device, s, blocks, False) + 1) * half) for s in range(2)]
            for u, g in enumerate(gs):
                zpre_ref[pl.ds(g, 1), :] = first[0][u] + last[0][u]
                zpost_ref[pl.ds(g, 1), :] = first[1][u] + last[1][u]

    @pl.when(step == pl.num_programs(0) - 1)
    def _():
        for copy in late:
            copy.wait()
        gq = gq_acc[...].astype(BF16)
        gkt = gk_acc[...].astype(BF16)
        gvt = gv_acc[...].astype(BF16)
        ga = ga_ref[...]
        for r in range(blocks):
            there = [pl.ds(pl.multiple_of(chunk_of(at ^ r, x, blocks, False) * half, half), half) for x in range(2)]
            gk = jnp.concatenate([gk_acc[:, x].T.astype(BF16) for x in there], 0)
            gv = jnp.concatenate([gv_acc[:, x].T.astype(BF16) for x in there], 0)
            gn1 = dot_nt(gk, wqkv_ref[:, width : 2 * width]) + dot_nt(gv, wqkv_ref[:, 2 * width :])
            if r == 0:
                gn1 = gn1 + dot_nt(gq, wqkv_ref[:, :width])
            gn1_refs[r][...] = gn1.astype(BF16)
        hand = width // 2
        per = hand // PIECES
        own = [pl.ds(pl.multiple_of(chunk_of(at, x, blocks, False) * half, half), half) for x in range(2)]
        for side in range(2):
            core = place_ref[0] if side == 0 else 1 - place_ref[0]
            mine = pl.ds(pl.multiple_of(core * hand, hand), hand)
            n1t = n1t_ref[mine, :]
            n1t_own = jnp.concatenate([n1t_ref[mine, x] for x in own], 1)
            grads = (
                lambda: dot_nn(n1t_own, gq),
                lambda: dot_nt(n1t, gkt),
                lambda: dot_nt(n1t, gvt),
                lambda: dot_nn(ot_ref[mine, :], ga),
            )
            for index, grad in enumerate(grads):
                part = index * parts // len(grads)
                column = (index - part * (len(grads) // parts)) * width
                value = grad().astype(BF16)
                for piece in range(PIECES):
                    there = pl.multiple_of((piece ^ place_ref[1 + part]) * per, per)
                    grad_refs[2 * part + side][pl.ds(there, per), column : column + width] = value[
                        piece * per : (piece + 1) * per
                    ]


def attn_bwd(layer, blocks, ga, w_out, q, k, v, p, u, tab, tabt, place, w_qkv, n1t, ot):
    rows, width = q.shape
    keys = k.shape[0]
    heads = p.shape[0]
    parts = place.shape[0] - 2
    args = (ga, w_out, q, k, v, p, u, tab, tabt, place, w_qkv, n1t, ot)
    in_specs = [whole(a.shape) for a in args]
    in_specs[1] = layer_of(w_out, layer)
    in_specs[5] = pl.BlockSpec((GB, rows, keys), lambda i: (i, 0, 0))
    in_specs[6] = pl.BlockSpec((GB, rows, width), lambda i: (i, 0, 0))
    in_specs[7] = layer_of(tab, layer)
    in_specs[8] = layer_of(tabt, layer)
    in_specs[9] = pl.BlockSpec(memory_space=pltpu.SMEM)
    in_specs[10:13] = [pl.BlockSpec(memory_space=pl.ANY)] * 3
    out = (
        [((rows, width), BF16)] * blocks
        + [((width // 2, 4 // parts * width), BF16)] * (2 * parts)
        + [((heads, width), F32)] * 2
    )
    res = pl.pallas_call(
        functools.partial(attn_bwd_body, heads, blocks, layer, parts),
        grid=(heads // GB,),
        in_specs=in_specs,
        out_specs=[whole(s) for s, _ in out],
        out_shape=[jax.ShapeDtypeStruct(s, d) for s, d in out],
        scratch_shapes=[
            pltpu.VMEM((rows, width), F32),
            pltpu.VMEM((width, rows), F32),
            pltpu.VMEM((width, rows), F32),
            pltpu.VMEM((rows, width), F32),
            pltpu.VMEM((width, keys), F32),
            pltpu.VMEM((width, keys), F32),
            pltpu.VMEM(w_qkv.shape[1:], BF16),
            pltpu.VMEM(n1t.shape, BF16),
            pltpu.VMEM(ot.shape, BF16),
            pltpu.SemaphoreType.DMA((3,)),
        ],
        compiler_params=pltpu.CompilerParams(vmem_limit_bytes=VMEM),
        cost_estimate=pl.CostEstimate(
            flops=2 * rows * keys * width * heads * 4 * 2, bytes_accessed=20_000_000, transcendentals=0
        ),
        name="attn_bwd",
    )(*args)
    return res[:blocks], res[blocks:-2], res[-2], res[-1]


def expand_body(parts, place_ref, *refs):
    qkv_ref, out_ref = refs[-2:]
    width3 = qkv_ref.shape[2]
    inner = PIECES // GROUPS
    per = qkv_ref.shape[1] // inner
    column = 0
    for part, ref in enumerate(refs[:parts]):
        end = column + ref.shape[1]
        cut = min(end, width3)
        for piece in range(inner):
            here = slice(piece * per, (piece + 1) * per)
            there = piece ^ lax.rem(place_ref[1 + part], inner)
            value = ref[pl.ds(pl.multiple_of(there * per, per), per), :].astype(F32)
            qkv_ref[0, here, column:cut] = value[:, : cut - column]
            if end > width3:
                out_ref[0, here, :] = value[:, cut - column :]
        column = end


def expand(layer, side, place, halves, before=()):
    half = halves[0].shape[0]
    width = sum(h.shape[1] for h in halves) // 4
    per = half // GROUPS
    in_specs = []
    for part, array in enumerate(halves):

        def piece(i, place, part=part):
            return i ^ (place[1 + part] // (PIECES // GROUPS)), 0

        in_specs.append(pl.BlockSpec((per, array.shape[1]), piece))
    first = 1 + len(halves)
    in_specs += [pl.BlockSpec(memory_space=pl.ANY)] * len(before)

    def there(i, place):
        return layer, (place[0] ^ side) * GROUPS + i, 0

    return pl.pallas_call(
        functools.partial(expand_body, len(halves)),
        grid_spec=pltpu.PrefetchScalarGridSpec(
            num_scalar_prefetch=1,
            grid=(GROUPS,),
            in_specs=in_specs,
            out_specs=[pl.BlockSpec((1, per, 3 * width), there), pl.BlockSpec((1, per, width), there)],
        ),
        out_shape=[
            jax.ShapeDtypeStruct((LAYERS, 2 * half, 3 * width), F32),
            jax.ShapeDtypeStruct((LAYERS, 2 * half, width), F32),
        ],
        input_output_aliases={first + i: i for i in range(len(before))},
        compiler_params=pltpu.CompilerParams(vmem_limit_bytes=SMALL),
        cost_estimate=pl.CostEstimate(flops=0, bytes_accessed=7_000_000, transcendentals=0),
        name="expand",
    )(place, *halves, *before)


def ffn_fwd_body(blocks, *refs):
    n_refs = refs[:blocks]
    win_ref, wdown_ref = refs[blocks : blocks + 2]
    out_refs = refs[blocks + 2 : 2 * blocks + 2]
    hid_ref, dgelu_ref = refs[2 * blocks + 2 :]
    rows = n_refs[0].shape[0]
    for r in range(blocks):
        here = pl.ds(r * rows, rows)
        pre = dot_nn(n_refs[r][...], win_ref[0])
        cdf = 0.5 + 0.5 * lax.erf(pre * (0.5**0.5))
        hid = (pre * cdf).astype(BF16)
        hid_ref[here, :] = hid
        density = jnp.exp2(pre * pre * (-0.5 * LOG2E)) * 0.3989422804014327
        dgelu_ref[here, :] = (cdf + pre * density).astype(BF16)
        out_refs[r][...] = dot_nn(hid, wdown_ref[0]).astype(BF16)


def ffn_fwd(layer, n_blocks, w_in, w_down):
    blocks = len(n_blocks)
    rows, width = n_blocks[0].shape
    hidden = w_in.shape[2]
    args = (*n_blocks, w_in, w_down)
    in_specs = [whole(a.shape) for a in args]
    in_specs[blocks] = layer_of(w_in, layer)
    in_specs[blocks + 1] = layer_of(w_down, layer)
    out = [((rows, width), BF16)] * blocks + [((rows * blocks, hidden), BF16)] * 2
    res = pl.pallas_call(
        functools.partial(ffn_fwd_body, blocks),
        grid=(1,),
        in_specs=in_specs,
        out_specs=[whole(s) for s, _ in out],
        out_shape=[jax.ShapeDtypeStruct(s, d) for s, d in out],
        compiler_params=pltpu.CompilerParams(vmem_limit_bytes=SMALL),
        cost_estimate=pl.CostEstimate(
            flops=4 * rows * blocks * width * hidden, bytes_accessed=6_000_000, transcendentals=rows * blocks * hidden
        ),
        name="ffn_fwd",
    )(*args)
    return res[:blocks], res[blocks], res[blocks + 1]


def ffn_bwd_body(blocks, *refs):
    g_refs = refs[:blocks]
    dgelu_ref, win_ref, wdown_ref = refs[blocks : blocks + 3]
    out_refs = refs[blocks + 3 : 2 * blocks + 3]
    gpre_ref = refs[2 * blocks + 3]
    rows = g_refs[0].shape[0]
    for r in range(blocks):
        here = pl.ds(r * rows, rows)
        gh = dot_nt(g_refs[r][...], wdown_ref[0])
        gpre = (gh * dgelu_ref[here, :].astype(F32)).astype(BF16)
        gpre_ref[here, :] = gpre
        out_refs[r][...] = dot_nt(gpre, win_ref[0]).astype(BF16)


def ffn_bwd(layer, g_blocks, dgelu, w_in, w_down):
    blocks = len(g_blocks)
    rows, width = g_blocks[0].shape
    hidden = w_in.shape[2]
    args = (*g_blocks, dgelu, w_in, w_down)
    in_specs = [whole(a.shape) for a in args]
    in_specs[blocks + 1] = layer_of(w_in, layer)
    in_specs[blocks + 2] = layer_of(w_down, layer)
    out = [((rows, width), BF16)] * blocks + [((rows * blocks, hidden), BF16)]
    res = pl.pallas_call(
        functools.partial(ffn_bwd_body, blocks),
        grid=(1,),
        in_specs=in_specs,
        out_specs=[whole(s) for s, _ in out],
        out_shape=[jax.ShapeDtypeStruct(s, d) for s, d in out],
        compiler_params=pltpu.CompilerParams(vmem_limit_bytes=SMALL),
        cost_estimate=pl.CostEstimate(
            flops=4 * rows * blocks * width * hidden, bytes_accessed=6_000_000, transcendentals=0
        ),
        name="ffn_bwd",
    )(*args)
    return res[:blocks], res[blocks]


def ffn_grads_body(blocks, chunks, *refs):
    n_refs, g_refs = refs[:blocks], refs[blocks : 2 * blocks]
    hid_refs, gpre_refs = refs[2 * blocks : 2 * blocks + 2], refs[2 * blocks + 2 : 2 * blocks + 4]
    out_ref = refs[-1]
    rows, width = n_refs[0].shape
    per = width // chunks
    for part, (left_refs, right_refs) in enumerate(((n_refs, gpre_refs), (g_refs, hid_refs))):
        left = jnp.concatenate([ref[...].T for ref in left_refs], 1)
        right = jnp.concatenate([ref[...] for ref in right_refs], 0)
        grad = dot_nn(left, right).astype(BF16)
        for c in range(chunks):
            place = 2 * sum(((c >> i) & 1) * (chunks >> (i + 1)) for i in range(chunks.bit_length() - 1)) + part
            out_ref[place * per : (place + 1) * per, :] = grad[c * per : (c + 1) * per]


def ffn_grads(n_blocks, g_blocks, hids, gpres, chunks):
    blocks = len(n_blocks)
    rows, width = n_blocks[0].shape
    hidden = hids[0].shape[1]
    args = (*n_blocks, *g_blocks, *hids, *gpres)
    return pl.pallas_call(
        functools.partial(ffn_grads_body, blocks, chunks),
        grid=(1,),
        in_specs=[whole(a.shape) for a in args],
        out_specs=whole((2 * width, hidden)),
        out_shape=jax.ShapeDtypeStruct((2 * width, hidden), BF16),
        compiler_params=pltpu.CompilerParams(vmem_limit_bytes=SMALL),
        cost_estimate=pl.CostEstimate(
            flops=4 * rows * blocks * width * hidden, bytes_accessed=9_000_000, transcendentals=0
        ),
        name="ffn_grads",
    )(*args)


def swap(value, axis, bit):
    size = lax.axis_size(axis)
    return lax.ppermute(value, axis, [(i, i ^ bit) for i in range(size)])


def after(values, *done):
    return lax.optimization_barrier((values, done))[0]


def gather_near(value):
    half = lax.axis_size("tp") // 2
    far = swap(value, "tp", half)
    near = [value]
    bit = 1
    while bit < half:
        near += [swap(b, "tp", bit) for b in near]
        bit *= 2
    return near, far


def gather_far(far):
    half = lax.axis_size("tp") // 2
    blocks = [far]
    bit = 1
    while bit < half:
        blocks += [swap(b, "tp", bit) for b in blocks]
        bit *= 2
    return blocks


def gather_blocks(value):
    near, far = gather_near(value)
    return near + gather_far(far)


def scatter_begin(blocks):
    blocks = list(blocks)
    bit = 1
    while bit < lax.axis_size("tp") // 2:
        size = len(blocks)
        keep = [blocks[r] for r in range(size) if not r & 1]
        sent = [swap(blocks[r], "tp", bit) for r in range(size) if r & 1]
        blocks = [a.astype(F32) + b.astype(F32) for a, b in zip(keep, sent)]
        bit *= 2
        blocks = [blocks[0]] + [b.astype(BF16) for b in blocks[1:]]
    return blocks[0].astype(F32), swap(blocks[1], "tp", bit)


def halve_begin(part, axis, bit):
    mine = (lax.axis_index(axis) // bit) & 1
    pair = part.reshape(2, part.shape[0] // 2, part.shape[1])
    sent = lax.dynamic_index_in_dim(pair, 1 - mine, 0, keepdims=False)
    kept = lax.dynamic_index_in_dim(pair, mine, 0, keepdims=False)
    return kept, swap(sent, axis, bit)


def halve_end(kept, got):
    return (kept.astype(F32) + got.astype(F32)).astype(BF16)


class Scatter:
    def __init__(self, parts, steps):
        self.steps = list(steps)
        self.begin(parts)

    def begin(self, parts):
        step = self.steps.pop(0)
        self.kept, self.got = zip(*[halve_begin(part, *step) for part in parts])

    def advance(self, *done):
        if self.steps:
            got = after(self.got, *done)
            self.begin([halve_end(a, b) for a, b in zip(self.kept, got)])

    def finish(self, *done):
        while self.steps:
            self.advance(*done)
        return [a.astype(F32) + b.astype(F32) for a, b in zip(self.kept, after(self.got, *done))]


def steps_of(axis):
    return [(axis, 1 << i) for i in range(lax.axis_size(axis).bit_length() - 1)]


HALVINGS = PIECES.bit_length() - 1


def place_of(order):
    number = 0
    for axis, bit in order[:HALVINGS]:
        number = 2 * number + ((lax.axis_index(axis) // bit) & 1)
    return number


def sum_start(part, order, stage):
    if stage < HALVINGS:
        rows = part.shape[0] // 2
        return part[:rows], swap(part[rows:], *order[stage])
    return part, swap(part, *order[stage])


def spread(part, got):
    return jnp.concatenate([part, got], 0)


class Butterfly:
    def __init__(self, value):
        self.value = value
        self.steps = steps_of("tp") + steps_of("dp")
        self.got = None

    def start(self):
        if self.steps:
            self.got = swap(self.value, *self.steps.pop(0))
            return [self.got]
        return []

    def end(self, got):
        for g in got:
            self.value = self.value + g


def on_device(
    x_in, segments, w_qkv, w_out, mix_pre, mix_post, gain_attn, gain_ffn, w_in, w_down, cotangent
):
    rows, _, width = x_in.shape
    heads = mix_pre.shape[1]
    head_size = width // heads
    tp_size = lax.axis_size("tp")
    dp_size = lax.axis_size("dp")
    tp_index = lax.axis_index("tp")
    seg = segments[:, 0]
    side = rows // 2
    span = jnp.arange(side, dtype=jnp.int32)
    starts = [chunk_of(tp_index, x, tp_size, False) * side for x in range(2)]
    qpos = jnp.concatenate([start + span for start in starts])
    qseg = jnp.concatenate([lax.dynamic_slice_in_dim(seg, start, side, 0) for start in starts])
    qinfo = jnp.stack([qpos, qseg] + [qpos] * 6, 1)
    kinfo = jnp.pad(jnp.stack([jnp.arange(seg.shape[0], dtype=jnp.int32), seg]), ((0, 6), (0, 0)))
    where = (qinfo, kinfo, tp_index[None])

    def mirror(value):
        moved = lax.ppermute(value[side:], "tp", [(i, tp_size - 1 - i) for i in range(tp_size)])
        return value[:side], moved

    tab = jnp.concatenate([jnp.swapaxes(mix_pre, 1, 2) * (head_size**-0.5), mix_post], 1)
    tabt = jnp.pad(jnp.repeat(jnp.swapaxes(tab, 1, 2), head_size, axis=1), ((0, 0), (0, 0), (0, 128 - 2 * heads)))
    tab = jnp.repeat(tab, head_size, axis=2)

    stream = x_in[:, 0].astype(F32)
    x_folded = jnp.concatenate(mirror(x_in[:, 0]), 0).astype(F32)
    kept = []
    half = tp_size // 2
    for layer in range(LAYERS):
        last = layer == LAYERS - 1
        n1_blocks = gather_blocks(rms(stream, gain_attn[layer]).astype(BF16))
        if last:
            low, n1_blocks[half] = after((cotangent[:, 0], n1_blocks[half]))
            grad_near, grad_far = gather_near(low)
        else:
            stream = x_folded
        p, u, q, k, v, ot, n1t, middle, n2 = attn_fwd(
            layer,
            layer == 0,
            n1_blocks,
            stream,
            w_qkv,
            w_out,
            tab,
            gain_ffn,
            where,
        )
        if last:
            n2, grad_near, grad_far = after((n2, grad_near, grad_far))
        near, far = gather_near(n2)
        out_a, hid_a, dgelu_a = ffn_fwd(layer, near, w_in, w_down)
        if last:
            given = grad_near + gather_far(grad_far)
            gf_blocks = [jnp.concatenate([given[r][:side], given[tp_size - 1 - r][side:]], 0) for r in range(tp_size)]
            gn2_a, gpre_a = ffn_bwd(layer, gf_blocks[:half], dgelu_a, w_in, w_down)
            far, gpre_a = after((far, gpre_a))
        far, hid_a = after((far, hid_a))
        n2_blocks = near + gather_far(far)
        out_b, hid_b, dgelu_b = ffn_fwd(layer, n2_blocks[half:], w_in, w_down)
        kept.append((stream, n1t, p, u, q, k, v, ot, middle, n2_blocks, hid_a, hid_b, dgelu_a, dgelu_b))
        if not last:
            own, far = scatter_begin([*out_a, *out_b])
            stream = middle + (own + far.astype(F32))

    grad_flow = gf_blocks[0].astype(F32)
    per = width // dp_size
    small = [None] * LAYERS
    sharded = [None] * LAYERS
    for layer in range(LAYERS - 1, -1, -1):
        last = layer == LAYERS - 1
        stream, n1t, p, u, q, k, v, ot, middle, n2_blocks, hid_a, hid_b, dgelu_a, dgelu_b = kept[layer]
        if not last:
            near, far = gather_near(grad_flow.astype(BF16))
            gn2_a, gpre_a = ffn_bwd(layer, near, dgelu_a, w_in, w_down)
            far, gpre_a = after((far, gpre_a))
            gf_blocks = near + gather_far(far)
        gn2_b, gpre_b = ffn_bwd(layer, gf_blocks[half:], dgelu_b, w_in, w_down)
        if not last:
            total_got, gpre_b = after((total_got, gpre_b))
            total = halve_end(total_kept, total_got)
            total_kept, total_got = sum_start(total, total_order, 1)
        own, far = scatter_begin([*gn2_a, *gn2_b])
        packed = ffn_grads(n2_blocks, gf_blocks, (hid_a, hid_b), (gpre_a, gpre_b), dp_size)
        far, packed = after((far, packed))
        if not last:
            total_got, packed = after((total_got, packed))
            total = halve_end(total_kept, total_got)
            total_kept, total_got = sum_start(total, total_order, 2)
        if not last:
            previous = moving
        moving = Scatter([packed], steps_of("dp"))
        gn2 = (own + far.astype(F32)).astype(BF16).astype(F32)
        grad_norm, grad_gffn = rms_back(gn2, middle, gain_ffn[layer])
        grad_middle = grad_flow + grad_norm
        ga = grad_middle.astype(BF16)
        if last:
            orders = [steps_of("dp") + steps_of("tp")[1:]]
        else:
            (y_step, *dp_rest), x_steps = steps_of("dp"), steps_of("tp")[1:]
            orders = [x_steps + [y_step] + dp_rest, [y_step] + x_steps + dp_rest]
        place = jnp.stack([tp_index & 1] + [place_of(order) for order in orders] + [tp_index])
        parts, grads, zpre, zpost = attn_bwd(
            layer, tp_size, ga, w_out, q, k, v, p, u, tab, tabt, place, w_qkv, n1t, ot
        )
        core_step = steps_of("tp")[0]
        if last:
            parts, grads, moving.got = after((parts, grads, moving.got))
            y_middle = middle
            keep, send = grads
            total = halve_end(keep, swap(send, *core_step))
            own, far = scatter_begin(parts)
            moving.advance()
            far, moving.got = after((far, moving.got), total)
            moving.advance()
            (total_order,), total_place = orders, place
            total_kept, total_got = sum_start(total, total_order, 0)
        else:
            parts, grads, moving.got, total_got, previous.got = after(
                (parts, grads, moving.got, total_got, previous.got)
            )
            (summed,) = previous.finish()
            sharded[layer + 1] = (summed[:per], summed[per:].T)
        if not last:
            break
        gn1 = (own + far.astype(F32)).astype(BF16).astype(F32)
        grad_norm, grad_gattn = rms_back(gn1, stream, gain_attn[layer])
        grad_flow = grad_middle + grad_norm
        grad_mpre = jnp.sum(zpre.reshape(heads, heads, head_size), -1).T * (head_size**-0.5)
        grad_mpost = jnp.sum(zpost.reshape(heads, heads, head_size), -1)
        small[layer] = (grad_mpre, grad_mpost, grad_gattn, grad_gffn)

    total = halve_end(total_kept, total_got)
    got = [swap(send, *core_step) for send in grads[1::2]]
    pieces = [halve_end(keep, g) for keep, g in zip(grads[::2], got)]
    for stage in range(HALVINGS, len(total_order)):
        total_got = swap(total, *total_order[stage])
        pieces, total_got = after((pieces, total_got))
        total = halve_end(total, total_got)
    own, far = scatter_begin(parts)
    for stage in range(HALVINGS):
        kept, got = zip(*[sum_start(part, order, stage) for part, order in zip(pieces, orders)])
        total_got = swap(total, *total_order[HALVINGS - 1 - stage])
        if stage < HALVINGS - 1:
            got, total_got = after((got, total_got))
            total = spread(total, total_got)
        if stage == HALVINGS - 1:
            flat_got = flat.start()
            got, flat_got = after((got, flat_got))
            flat.end(flat_got)
        pieces = [halve_end(a, b) for a, b in zip(kept, after(got))]
        if stage == 0:
            far, pieces = after((far, pieces))
            gn1 = (own + far.astype(F32)).astype(BF16).astype(F32)
            grad_norm, grad_gattn = rms_back(gn1, stream, gain_attn[layer])
            grad_flow = grad_middle + grad_norm
            grad_mpre = jnp.sum(zpre.reshape(heads, heads, head_size), -1).T * (head_size**-0.5)
            grad_mpost = jnp.sum(zpost.reshape(heads, heads, head_size), -1)
            small[layer] = (grad_mpre, grad_mpost, grad_gattn, grad_gffn)
            mixes = jnp.concatenate([a.reshape(-1) for s in small for a in s[:2]])
            count = mixes.shape[0]
            mix_rows = -(-count // width)
            flat = jnp.concatenate(
                [jnp.pad(mixes, (0, mix_rows * width - count)).reshape(mix_rows, width)]
                + [g[None] for s in small for g in s[2:]]
            )
            flat = jnp.pad(flat, ((0, -flat.shape[0] % 8), (0, 0)))
            flat = Butterfly(flat)
        if stage == 1:
            moving.advance(*pieces)
            y_parts, pieces = after(([*out_a, *out_b], pieces))
            own_y, far_y = scatter_begin(y_parts)
    for stage in range(HALVINGS, len(orders[0])):
        got = [swap(part, *order[stage]) for part, order in zip(pieces, orders)]
        flat_got = flat.start()
        if stage == HALVINGS:
            first_rows, second_rows = mirror(grad_flow)
            got, second_rows, total_got, moving.got, far_y = after((got, second_rows, total_got, moving.got, far_y))
            y_out = (y_middle + (own_y + far_y.astype(F32))).astype(BF16)
            y_first, y_second = mirror(y_out)
            grad_x = jnp.concatenate([first_rows, second_rows], 0)
            total = spread(total, total_got)
            moving.advance()
        got, flat_got = after((got, flat_got))
        flat.end(flat_got)
        pieces = [halve_end(a, b) for a, b in zip(pieces, got)]
    total_other = swap(total, *core_step)
    replicated = ()
    for stage in range(HALVINGS - 1, -1, -1):
        got = [swap(part, *order[stage]) for part, order in zip(pieces, orders)]
        flat_got = flat.start()
        if stage == HALVINGS - 1:
            got, total_other = after((got, total_other))
        elif stage == HALVINGS - 2:
            replicated = expand(1, 0, total_place, [total])
            got, replicated, moving.got, y_second = after((got, replicated, moving.got, y_second))
            y_out = jnp.concatenate([y_first, y_second], 0)
        elif stage == 0:
            replicated = expand(1, 1, total_place, [total_other], replicated)
            got, replicated = after((got, replicated))
        got, flat_got = after((got, flat_got))
        flat.end(flat_got)
        pieces = [spread(a, b) for a, b in zip(pieces, got)]
    got = [swap(part, *core_step) for part in pieces]
    while flat.steps:
        flat.end(flat.start())
    flat = flat.value
    (summed,) = moving.finish()
    sharded[0] = (summed[:per], summed[per:].T)
    replicated = expand(0, 0, place, pieces, replicated)
    got, replicated, sharded = after((got, replicated, sharded))
    replicated = expand(0, 1, place, got, replicated)
    mixes = flat[:mix_rows].reshape(-1)[:count].reshape(LAYERS, 2, heads, heads)
    gains = flat[mix_rows : mix_rows + 2 * LAYERS].reshape(LAYERS, 2, width)
    return (
        y_out[:, None],
        grad_x[:, None],
        *replicated,
        mixes[:, 0],
        mixes[:, 1],
        gains[:, 0],
        gains[:, 1],
        jnp.stack([s[0] for s in sharded]),
        jnp.stack([s[1] for s in sharded]),
    )


def solution(mesh):
    in_specs = (
        P("tp", "dp", None),
        P(None, "dp"),
        P(),
        P(),
        P(),
        P(),
        P(),
        P(),
        P(None, None, "tp"),
        P(None, "tp", None),
        P("tp", "dp", None),
    )
    out_specs = (
        P("tp", "dp", None),
        P("tp", "dp", None),
        P(),
        P(),
        P(),
        P(),
        P(),
        P(),
        P(None, "dp", "tp"),
        P(None, "tp", "dp"),
    )
    return jax.shard_map(
        on_device, mesh=mesh, in_specs=in_specs, out_specs=out_specs, check_vma=False
    )
```

```python
import functools

import jax
import jax.numpy as jnp
from jax import lax
from jax.experimental import pallas as pl
from jax.experimental.pallas import tpu as pltpu
from jax.sharding import PartitionSpec as P

LAYERS = 2
EPSILON = 1e-06
NEGATIVE = -1e30
LOG2E = 1.4426950408889634
GROUPS = 4
PIECES = 8
GP = 4
GB = 4
VMEM = 60 * 1024 * 1024
MIDDLE = 40 * 1024 * 1024
SMALL = 18 * 1024 * 1024
F32 = jnp.float32
BF16 = jnp.bfloat16


def dot_nn(a, b):
    return lax.dot_general(a, b, (((1,), (0,)), ((), ())), preferred_element_type=F32)


def dot_nt(a, b):
    return lax.dot_general(a, b, (((1,), (1,)), ((), ())), preferred_element_type=F32)


def dot_tn(a, b):
    return lax.dot_general(a, b, (((0,), (0,)), ((), ())), preferred_element_type=F32)


def rms(values, gain):
    return values * lax.rsqrt(jnp.mean(values * values, -1, keepdims=True) + EPSILON) * gain


def rms_back(grad, values, gain):
    inv = lax.rsqrt(jnp.mean(values * values, -1, keepdims=True) + EPSILON)
    unit = values * inv
    scaled = grad * gain
    grad_values = (scaled - unit * jnp.mean(scaled * unit, -1, keepdims=True)) * inv
    return grad_values, jnp.sum(grad * unit, axis=0)


def whole(shape):
    return pl.BlockSpec(shape, lambda *_: (0,) * len(shape))


def layer_of(array, layer):
    shape = array.shape[1:]
    return pl.BlockSpec((1,) + shape, lambda *_: (layer,) + (0,) * len(shape))


def attn_fwd_body(blocks, heads, layer, plain, *refs):
    n_refs = refs[:blocks]
    x_hbm, wqkv_hbm, wout_hbm, tab_ref, gain_ref, qinfo_ref, kinfo_ref, at_ref = refs[blocks : blocks + 8]
    p_ref, u_ref, q_ref, k_hbm, v_hbm, ot_ref, n1t_hbm, xm_ref, n2_ref = refs[blocks + 8 : blocks + 17]
    bias_ref, acc_ref, k_ref, v_ref, n1t_ref, x_ref, wqkv_ref, wout_ref, sems = refs[blocks + 17 :]
    step = pl.program_id(0)
    rows, width = x_ref.shape
    q_cols, k_cols, v_cols = [slice(i * width, (i + 1) * width) for i in range(3)]
    weights = [
        pltpu.make_async_copy(wqkv_hbm.at[layer, :, cols], wqkv_ref.at[i], sems.at[i])
        for i, cols in enumerate((k_cols, v_cols, q_cols))
    ]
    last_used = [
        pltpu.make_async_copy(wout_hbm.at[layer], wout_ref, sems.at[3]),
        pltpu.make_async_copy(x_hbm, x_ref, sems.at[4]),
    ]
    early = [
        pltpu.make_async_copy(k_ref, k_hbm, sems.at[5]),
        pltpu.make_async_copy(v_ref, v_hbm, sems.at[6]),
    ]
    turned = pltpu.make_async_copy(n1t_ref, n1t_hbm, sems.at[7])
    half = rows // 2
    at = at_ref[0]

    def place(r, second):
        block = chunk_of(at ^ r, second, blocks, plain)
        return pl.ds(pl.multiple_of(block * half, half), half)

    @pl.when(step == 0)
    def _():
        for copy in weights + last_used:
            copy.start()
        for i, ref in enumerate((k_ref, v_ref)):
            weights[i].wait()
            for r in range(blocks):
                value = dot_nn(n_refs[r][...], wqkv_ref[i]).astype(BF16)
                ref[place(r, 0), :] = value[:half]
                ref[place(r, 1), :] = value[half:]
            early[i].start()
        weights[2].wait()
        n_second = n_refs[blocks - 1 if plain else 0]
        q_ref[:half] = dot_nn(n_refs[0][:half], wqkv_ref[2]).astype(BF16)
        q_ref[half:] = dot_nn(n_second[half:], wqkv_ref[2]).astype(BF16)
        ok = (qinfo_ref[:, 1:2] == kinfo_ref[1:2, :]) & (kinfo_ref[0:1, :] <= qinfo_ref[:, 0:1])
        bias_ref[...] = jnp.where(ok, 0.0, NEGATIVE)
        acc_ref[...] = jnp.zeros_like(acc_ref)

    def work(second, keys):
        here = pl.ds(pl.multiple_of(second * half, half), half)
        q = q_ref[here, :].astype(F32)
        gs = [step * GP + u for u in range(GP)]
        qm = jnp.concatenate([(q * (tab_ref[0, pl.ds(g, 1), :] * LOG2E)).astype(BF16) for g in gs], 0)
        m = dot_nt(qm, k_ref[:keys, :])
        bias = bias_ref[here, :keys]
        ps = []
        for u in range(GP):
            mu = m[u * half : (u + 1) * half] + bias
            e = jnp.exp2(mu - jnp.max(mu, -1, keepdims=True))
            p = (e * (1.0 / jnp.sum(e, -1, keepdims=True))).astype(BF16)
            p_ref[u, here, :keys] = p
            ps.append(p)
        ctx = dot_nn(jnp.concatenate(ps, 0), v_ref[:keys, :])
        total = acc_ref[here, :]
        for u in range(GP):
            cu = ctx[u * half : (u + 1) * half]
            u_ref[u, here, :] = cu.astype(BF16)
            total = total + cu * tab_ref[0, pl.ds(heads + gs[u], 1), :]
        acc_ref[here, :] = total

    for pairs in range(1, blocks + 1):
        late = at == blocks - pairs

        @pl.when(late | (at == pairs - 1))
        def _(pairs=pairs, late=late):
            work(late.astype(jnp.int32), 2 * pairs * half)

    @pl.when(step == 0)
    def _():
        for r in range(blocks):
            for second in range(2):
                n1t_ref[:, place(r, second)] = n_refs[r][second * half : (second + 1) * half, :].T
        turned.start()

    @pl.when(step == pl.num_programs(0) - 1)
    def _():
        o = acc_ref[...].astype(BF16)
        ot_ref[...] = o.T
        for copy in last_used + early + [turned]:
            copy.wait()
        xm = x_ref[...] + dot_nn(o, wout_ref[...])
        xm_ref[...] = xm
        n2_ref[...] = rms(xm, gain_ref[pl.ds(layer, 1), :]).astype(BF16)


def chunk_of(device, second, devices, plain):
    if not second:
        return 2 * device
    return 2 * device + 1 if plain else 2 * (devices - 1 - device) + 1


def attn_fwd(layer, plain, n_blocks, x, w_qkv, w_out, tab, gain, where):
    rows, width = x.shape
    blocks = len(n_blocks)
    heads = tab.shape[1] // 2
    keys = rows * blocks
    args = (*n_blocks, x, w_qkv, w_out, tab, gain, *where)
    in_specs = [whole(a.shape) for a in args]
    in_specs[blocks : blocks + 3] = [pl.BlockSpec(memory_space=pl.ANY)] * 3
    in_specs[blocks + 3] = layer_of(tab, layer)
    in_specs[-1] = pl.BlockSpec(memory_space=pltpu.SMEM)
    out = [
        ((heads, rows, keys), BF16),
        ((heads, rows, width), BF16),
        ((rows, width), BF16),
        ((keys, width), BF16),
        ((keys, width), BF16),
        ((width, rows), BF16),
        ((width, keys), BF16),
        ((rows, width), F32),
        ((rows, width), BF16),
    ]
    out_specs = [whole(s) for s, _ in out]
    out_specs[0] = pl.BlockSpec((GP, rows, keys), lambda i: (i, 0, 0))
    out_specs[1] = pl.BlockSpec((GP, rows, width), lambda i: (i, 0, 0))
    for i in (3, 4, 6):
        out_specs[i] = pl.BlockSpec(memory_space=pltpu.HBM)
    return pl.pallas_call(
        functools.partial(attn_fwd_body, blocks, heads, layer, plain),
        grid=(heads // GP,),
        in_specs=in_specs,
        out_specs=out_specs,
        out_shape=[jax.ShapeDtypeStruct(s, d) for s, d in out],
        scratch_shapes=[
            pltpu.VMEM((rows, keys), F32),
            pltpu.VMEM((rows, width), F32),
            pltpu.VMEM((keys, width), BF16),
            pltpu.VMEM((keys, width), BF16),
            pltpu.VMEM((width, keys), BF16),
            pltpu.VMEM((rows, width), F32),
            pltpu.VMEM((3, width, width), BF16),
            pltpu.VMEM((width, width), BF16),
            pltpu.SemaphoreType.DMA((8,)),
        ],
        compiler_params=pltpu.CompilerParams(vmem_limit_bytes=MIDDLE),
        cost_estimate=pl.CostEstimate(
            flops=2 * rows * keys * width * heads * 2, bytes_accessed=20_000_000, transcendentals=rows * keys * heads
        ),
        name="attn_fwd",
    )(*args)


def attn_bwd_body(heads, blocks, layer, parts, *refs):
    (ga_ref, wout_ref, q_ref, k_ref, v_ref, p_ref, u_ref, tab_ref, tabt_ref, place_ref) = refs[:10]
    wqkv_hbm, n1t_hbm, ot_hbm = refs[10:13]
    gn1_refs = refs[13 : 13 + blocks]
    grad_refs = refs[13 + blocks : 13 + blocks + 2 * parts]
    zpre_ref, zpost_ref = refs[13 + blocks + 2 * parts : 15 + blocks + 2 * parts]
    go_ref, got_ref, qt_ref, gq_acc, gk_acc, gv_acc, wqkv_ref, n1t_ref, ot_ref, sems = refs[15 + blocks + 2 * parts :]
    step = pl.program_id(0)
    rows, width = q_ref.shape

    late = [
        pltpu.make_async_copy(wqkv_hbm.at[layer], wqkv_ref, sems.at[0]),
        pltpu.make_async_copy(n1t_hbm, n1t_ref, sems.at[1]),
        pltpu.make_async_copy(ot_hbm, ot_ref, sems.at[2]),
    ]

    @pl.when(step == 0)
    def _():
        for copy in late:
            copy.start()
        go = dot_nt(ga_ref[...], wout_ref[0]).astype(BF16).astype(F32)
        go_ref[...] = go
        got_ref[...] = go.T
        qt_ref[...] = q_ref[...].astype(F32).T
        gq_acc[...] = jnp.zeros_like(gq_acc)
        gk_acc[...] = jnp.zeros_like(gk_acc)
        gv_acc[...] = jnp.zeros_like(gv_acc)
        zpre_ref[...] = jnp.zeros_like(zpre_ref)
        zpost_ref[...] = jnp.zeros_like(zpost_ref)

    half = rows // 2
    at = place_ref[1 + parts]
    lane = lax.broadcasted_iota(jnp.int32, tabt_ref.shape[1:], 1)
    gs = [step * GB + u for u in range(GB)]
    cols = []
    for g in gs:
        pre_col = jnp.sum(jnp.where(lane == g, tabt_ref[0], 0.0), 1, keepdims=True)
        post_col = jnp.sum(jnp.where(lane == heads + g, tabt_ref[0], 0.0), 1, keepdims=True)
        cols.append((pre_col, post_col))

    def work(second, keys):
        here = pl.ds(pl.multiple_of(second * half, half), half)
        go = go_ref[here, :]
        q = q_ref[here, :].astype(F32)
        mixed = [go * tab_ref[0, pl.ds(heads + g, 1), :] for g in gs]
        gp = dot_nt(jnp.concatenate([x.astype(BF16) for x in mixed], 0), v_ref[:keys, :])
        gms, ps, zposts = [], [], []
        for u in range(GB):
            ctx = u_ref[u, here, :].astype(F32)
            zposts.append(jnp.sum(ctx * go, axis=0, keepdims=True))
            delta = jnp.sum(ctx * mixed[u], axis=1, keepdims=True)
            p = p_ref[u, here, :keys]
            gms.append((p.astype(F32) * (gp[u * half : (u + 1) * half] - delta)).astype(BF16))
            ps.append(p)
        gm = jnp.concatenate(gms, 0)
        t = dot_nn(gm, k_ref[:keys, :])
        total = gq_acc[here, :]
        zpres = []
        for u in range(GB):
            tu = t[u * half : (u + 1) * half]
            zpres.append(jnp.sum(tu * q, axis=0, keepdims=True))
            total = total + tu * tab_ref[0, pl.ds(gs[u], 1), :]
        gq_acc[here, :] = total
        qm = jnp.concatenate([(qt_ref[:, here] * pre).astype(BF16) for pre, _ in cols], 1)
        gk_acc[:, :keys] += dot_nn(qm, gm)
        gm2 = jnp.concatenate([(got_ref[:, here] * post).astype(BF16) for _, post in cols], 1)
        gv_acc[:, :keys] += dot_nn(gm2, jnp.concatenate(ps, 0))
        return zpres, zposts

    for pairs in range(1, blocks + 1):
        is_late = at == blocks - pairs

        @pl.when(is_late | (at == pairs - 1))
        def _(pairs=pairs, is_late=is_late):
            zpres, zposts = work(is_late.astype(jnp.int32), 2 * pairs * half)
            for u, g in enumerate(gs):
                zpre_ref[pl.ds(g, 1), :] += zpres[u]
                zpost_ref[pl.ds(g, 1), :] += zposts[u]

    @pl.when(step == pl.num_programs(0) - 1)
    def _():
        for copy in late:
            copy.wait()
        gq = gq_acc[...].astype(BF16)
        gkt = gk_acc[...].astype(BF16)
        gvt = gv_acc[...].astype(BF16)
        ga = ga_ref[...]
        for r in range(blocks):
            there = [pl.ds(pl.multiple_of(chunk_of(at ^ r, x, blocks, False) * half, half), half) for x in range(2)]
            gk = jnp.concatenate([gk_acc[:, x].T.astype(BF16) for x in there], 0)
            gv = jnp.concatenate([gv_acc[:, x].T.astype(BF16) for x in there], 0)
            gn1 = dot_nt(gk, wqkv_ref[:, width : 2 * width]) + dot_nt(gv, wqkv_ref[:, 2 * width :])
            if r == 0:
                gn1 = gn1 + dot_nt(gq, wqkv_ref[:, :width])
            gn1_refs[r][...] = gn1.astype(BF16)
        hand = width // 2
        per = hand // PIECES
        own = [pl.ds(pl.multiple_of(chunk_of(at, x, blocks, False) * half, half), half) for x in range(2)]
        for side in range(2):
            core = place_ref[0] if side == 0 else 1 - place_ref[0]
            mine = pl.ds(pl.multiple_of(core * hand, hand), hand)
            n1t = n1t_ref[mine, :]
            n1t_own = jnp.concatenate([n1t_ref[mine, x] for x in own], 1)
            grads = (
                lambda: dot_nn(n1t_own, gq),
                lambda: dot_nt(n1t, gkt),
                lambda: dot_nt(n1t, gvt),
                lambda: dot_nn(ot_ref[mine, :], ga),
            )
            for index, grad in enumerate(grads):
                part = index * parts // len(grads)
                column = (index - part * (len(grads) // parts)) * width
                value = grad().astype(BF16)
                for piece in range(PIECES):
                    there = pl.multiple_of((piece ^ place_ref[1 + part]) * per, per)
                    grad_refs[2 * part + side][pl.ds(there, per), column : column + width] = value[
                        piece * per : (piece + 1) * per
                    ]


def attn_bwd(layer, blocks, ga, w_out, q, k, v, p, u, tab, tabt, place, w_qkv, n1t, ot):
    rows, width = q.shape
    keys = k.shape[0]
    heads = p.shape[0]
    parts = place.shape[0] - 2
    args = (ga, w_out, q, k, v, p, u, tab, tabt, place, w_qkv, n1t, ot)
    in_specs = [whole(a.shape) for a in args]
    in_specs[1] = layer_of(w_out, layer)
    in_specs[5] = pl.BlockSpec((GB, rows, keys), lambda i: (i, 0, 0))
    in_specs[6] = pl.BlockSpec((GB, rows, width), lambda i: (i, 0, 0))
    in_specs[7] = layer_of(tab, layer)
    in_specs[8] = layer_of(tabt, layer)
    in_specs[9] = pl.BlockSpec(memory_space=pltpu.SMEM)
    in_specs[10:13] = [pl.BlockSpec(memory_space=pl.ANY)] * 3
    out = (
        [((rows, width), BF16)] * blocks
        + [((width // 2, 4 // parts * width), BF16)] * (2 * parts)
        + [((heads, width), F32)] * 2
    )
    res = pl.pallas_call(
        functools.partial(attn_bwd_body, heads, blocks, layer, parts),
        grid=(heads // GB,),
        in_specs=in_specs,
        out_specs=[whole(s) for s, _ in out],
        out_shape=[jax.ShapeDtypeStruct(s, d) for s, d in out],
        scratch_shapes=[
            pltpu.VMEM((rows, width), F32),
            pltpu.VMEM((width, rows), F32),
            pltpu.VMEM((width, rows), F32),
            pltpu.VMEM((rows, width), F32),
            pltpu.VMEM((width, keys), F32),
            pltpu.VMEM((width, keys), F32),
            pltpu.VMEM(w_qkv.shape[1:], BF16),
            pltpu.VMEM(n1t.shape, BF16),
            pltpu.VMEM(ot.shape, BF16),
            pltpu.SemaphoreType.DMA((3,)),
        ],
        compiler_params=pltpu.CompilerParams(vmem_limit_bytes=VMEM),
        cost_estimate=pl.CostEstimate(
            flops=2 * rows * keys * width * heads * 4 * 2, bytes_accessed=20_000_000, transcendentals=0
        ),
        name="attn_bwd",
    )(*args)
    return res[:blocks], res[blocks:-2], res[-2], res[-1]


def expand_body(parts, place_ref, *refs):
    qkv_ref, out_ref = refs[-2:]
    width3 = qkv_ref.shape[2]
    inner = PIECES // GROUPS
    per = qkv_ref.shape[1] // inner
    column = 0
    for part, ref in enumerate(refs[:parts]):
        end = column + ref.shape[1]
        cut = min(end, width3)
        for piece in range(inner):
            here = slice(piece * per, (piece + 1) * per)
            there = piece ^ lax.rem(place_ref[1 + part], inner)
            value = ref[pl.ds(pl.multiple_of(there * per, per), per), :].astype(F32)
            qkv_ref[0, here, column:cut] = value[:, : cut - column]
            if end > width3:
                out_ref[0, here, :] = value[:, cut - column :]
        column = end


def expand(layer, side, place, halves, before=()):
    half = halves[0].shape[0]
    width = sum(h.shape[1] for h in halves) // 4
    per = half // GROUPS
    in_specs = []
    for part, array in enumerate(halves):

        def piece(i, place, part=part):
            return i ^ (place[1 + part] // (PIECES // GROUPS)), 0

        in_specs.append(pl.BlockSpec((per, array.shape[1]), piece))
    first = 1 + len(halves)
    in_specs += [pl.BlockSpec(memory_space=pl.ANY)] * len(before)

    def there(i, place):
        return layer, (place[0] ^ side) * GROUPS + i, 0

    return pl.pallas_call(
        functools.partial(expand_body, len(halves)),
        grid_spec=pltpu.PrefetchScalarGridSpec(
            num_scalar_prefetch=1,
            grid=(GROUPS,),
            in_specs=in_specs,
            out_specs=[pl.BlockSpec((1, per, 3 * width), there), pl.BlockSpec((1, per, width), there)],
        ),
        out_shape=[
            jax.ShapeDtypeStruct((LAYERS, 2 * half, 3 * width), F32),
            jax.ShapeDtypeStruct((LAYERS, 2 * half, width), F32),
        ],
        input_output_aliases={first + i: i for i in range(len(before))},
        compiler_params=pltpu.CompilerParams(vmem_limit_bytes=SMALL),
        cost_estimate=pl.CostEstimate(flops=0, bytes_accessed=7_000_000, transcendentals=0),
        name="expand",
    )(place, *halves, *before)


def ffn_fwd_body(blocks, *refs):
    n_refs = refs[:blocks]
    win_ref, wdown_ref = refs[blocks : blocks + 2]
    out_refs = refs[blocks + 2 : 2 * blocks + 2]
    hid_ref, dgelu_ref = refs[2 * blocks + 2 :]
    rows = n_refs[0].shape[0]
    for r in range(blocks):
        here = pl.ds(r * rows, rows)
        pre = dot_nn(n_refs[r][...], win_ref[0])
        cdf = 0.5 + 0.5 * lax.erf(pre * (0.5**0.5))
        hid = (pre * cdf).astype(BF16)
        hid_ref[here, :] = hid
        density = jnp.exp2(pre * pre * (-0.5 * LOG2E)) * 0.3989422804014327
        dgelu_ref[here, :] = (cdf + pre * density).astype(BF16)
        out_refs[r][...] = dot_nn(hid, wdown_ref[0]).astype(BF16)


def ffn_fwd(layer, n_blocks, w_in, w_down):
    blocks = len(n_blocks)
    rows, width = n_blocks[0].shape
    hidden = w_in.shape[2]
    args = (*n_blocks, w_in, w_down)
    in_specs = [whole(a.shape) for a in args]
    in_specs[blocks] = layer_of(w_in, layer)
    in_specs[blocks + 1] = layer_of(w_down, layer)
    out = [((rows, width), BF16)] * blocks + [((rows * blocks, hidden), BF16)] * 2
    res = pl.pallas_call(
        functools.partial(ffn_fwd_body, blocks),
        grid=(1,),
        in_specs=in_specs,
        out_specs=[whole(s) for s, _ in out],
        out_shape=[jax.ShapeDtypeStruct(s, d) for s, d in out],
        compiler_params=pltpu.CompilerParams(vmem_limit_bytes=SMALL),
        cost_estimate=pl.CostEstimate(
            flops=4 * rows * blocks * width * hidden, bytes_accessed=6_000_000, transcendentals=rows * blocks * hidden
        ),
        name="ffn_fwd",
    )(*args)
    return res[:blocks], res[blocks], res[blocks + 1]


def ffn_bwd_body(blocks, *refs):
    g_refs = refs[:blocks]
    dgelu_ref, win_ref, wdown_ref = refs[blocks : blocks + 3]
    out_refs = refs[blocks + 3 : 2 * blocks + 3]
    gpre_ref = refs[2 * blocks + 3]
    rows = g_refs[0].shape[0]
    for r in range(blocks):
        here = pl.ds(r * rows, rows)
        gh = dot_nt(g_refs[r][...], wdown_ref[0])
        gpre = (gh * dgelu_ref[here, :].astype(F32)).astype(BF16)
        gpre_ref[here, :] = gpre
        out_refs[r][...] = dot_nt(gpre, win_ref[0]).astype(BF16)


def ffn_bwd(layer, g_blocks, dgelu, w_in, w_down):
    blocks = len(g_blocks)
    rows, width = g_blocks[0].shape
    hidden = w_in.shape[2]
    args = (*g_blocks, dgelu, w_in, w_down)
    in_specs = [whole(a.shape) for a in args]
    in_specs[blocks + 1] = layer_of(w_in, layer)
    in_specs[blocks + 2] = layer_of(w_down, layer)
    out = [((rows, width), BF16)] * blocks + [((rows * blocks, hidden), BF16)]
    res = pl.pallas_call(
        functools.partial(ffn_bwd_body, blocks),
        grid=(1,),
        in_specs=in_specs,
        out_specs=[whole(s) for s, _ in out],
        out_shape=[jax.ShapeDtypeStruct(s, d) for s, d in out],
        compiler_params=pltpu.CompilerParams(vmem_limit_bytes=SMALL),
        cost_estimate=pl.CostEstimate(
            flops=4 * rows * blocks * width * hidden, bytes_accessed=6_000_000, transcendentals=0
        ),
        name="ffn_bwd",
    )(*args)
    return res[:blocks], res[blocks]


def ffn_grads_body(blocks, chunks, *refs):
    n_refs, g_refs = refs[:blocks], refs[blocks : 2 * blocks]
    hid_refs, gpre_refs = refs[2 * blocks : 2 * blocks + 2], refs[2 * blocks + 2 : 2 * blocks + 4]
    out_ref = refs[-1]
    rows, width = n_refs[0].shape
    per = width // chunks
    for part, (left_refs, right_refs) in enumerate(((n_refs, gpre_refs), (g_refs, hid_refs))):
        left = jnp.concatenate([ref[...].T for ref in left_refs], 1)
        right = jnp.concatenate([ref[...] for ref in right_refs], 0)
        grad = dot_nn(left, right).astype(BF16)
        for c in range(chunks):
            place = 2 * sum(((c >> i) & 1) * (chunks >> (i + 1)) for i in range(chunks.bit_length() - 1)) + part
            out_ref[place * per : (place + 1) * per, :] = grad[c * per : (c + 1) * per]


def ffn_grads(n_blocks, g_blocks, hids, gpres, chunks):
    blocks = len(n_blocks)
    rows, width = n_blocks[0].shape
    hidden = hids[0].shape[1]
    args = (*n_blocks, *g_blocks, *hids, *gpres)
    return pl.pallas_call(
        functools.partial(ffn_grads_body, blocks, chunks),
        grid=(1,),
        in_specs=[whole(a.shape) for a in args],
        out_specs=whole((2 * width, hidden)),
        out_shape=jax.ShapeDtypeStruct((2 * width, hidden), BF16),
        compiler_params=pltpu.CompilerParams(vmem_limit_bytes=VMEM),
        cost_estimate=pl.CostEstimate(
            flops=4 * rows * blocks * width * hidden, bytes_accessed=9_000_000, transcendentals=0
        ),
        name="ffn_grads",
    )(*args)


def swap(value, axis, bit):
    size = lax.axis_size(axis)
    return lax.ppermute(value, axis, [(i, i ^ bit) for i in range(size)])


def after(values, *done):
    return lax.optimization_barrier((values, done))[0]


def gather_near(value):
    half = lax.axis_size("tp") // 2
    far = swap(value, "tp", half)
    near = [value]
    bit = 1
    while bit < half:
        near += [swap(b, "tp", bit) for b in near]
        bit *= 2
    return near, far


def gather_far(far):
    half = lax.axis_size("tp") // 2
    blocks = [far]
    bit = 1
    while bit < half:
        blocks += [swap(b, "tp", bit) for b in blocks]
        bit *= 2
    return blocks


def gather_blocks(value):
    near, far = gather_near(value)
    return near + gather_far(far)


def scatter_begin(blocks):
    blocks = list(blocks)
    bit = 1
    while bit < lax.axis_size("tp") // 2:
        size = len(blocks)
        keep = [blocks[r] for r in range(size) if not r & 1]
        sent = [swap(blocks[r], "tp", bit) for r in range(size) if r & 1]
        blocks = [a.astype(F32) + b.astype(F32) for a, b in zip(keep, sent)]
        bit *= 2
        blocks = [blocks[0]] + [b.astype(BF16) for b in blocks[1:]]
    return blocks[0].astype(F32), swap(blocks[1], "tp", bit)


def halve_begin(part, axis, bit):
    mine = (lax.axis_index(axis) // bit) & 1
    pair = part.reshape(2, part.shape[0] // 2, part.shape[1])
    sent = lax.dynamic_index_in_dim(pair, 1 - mine, 0, keepdims=False)
    kept = lax.dynamic_index_in_dim(pair, mine, 0, keepdims=False)
    return kept, swap(sent, axis, bit)


def halve_end(kept, got):
    return (kept.astype(F32) + got.astype(F32)).astype(BF16)


class Scatter:
    def __init__(self, parts, steps):
        self.steps = list(steps)
        self.begin(parts)

    def begin(self, parts):
        step = self.steps.pop(0)
        self.kept, self.got = zip(*[halve_begin(part, *step) for part in parts])

    def advance(self, *done):
        if self.steps:
            got = after(self.got, *done)
            self.begin([halve_end(a, b) for a, b in zip(self.kept, got)])

    def finish(self, *done):
        while self.steps:
            self.advance(*done)
        return [a.astype(F32) + b.astype(F32) for a, b in zip(self.kept, after(self.got, *done))]


def steps_of(axis):
    return [(axis, 1 << i) for i in range(lax.axis_size(axis).bit_length() - 1)]


HALVINGS = PIECES.bit_length() - 1


def place_of(order):
    number = 0
    for axis, bit in order[:HALVINGS]:
        number = 2 * number + ((lax.axis_index(axis) // bit) & 1)
    return number


def sum_start(part, order, stage):
    if stage < HALVINGS:
        rows = part.shape[0] // 2
        return part[:rows], swap(part[rows:], *order[stage])
    return part, swap(part, *order[stage])


def spread(part, got):
    return jnp.concatenate([part, got], 0)


class Butterfly:
    def __init__(self, value):
        self.value = value
        self.steps = steps_of("tp") + steps_of("dp")
        self.got = None

    def start(self):
        if self.steps:
            self.got = swap(self.value, *self.steps.pop(0))
            return [self.got]
        return []

    def end(self, got):
        for g in got:
            self.value = self.value + g


def on_device(
    x_in, segments, w_qkv, w_out, mix_pre, mix_post, gain_attn, gain_ffn, w_in, w_down, cotangent
):
    rows, _, width = x_in.shape
    heads = mix_pre.shape[1]
    head_size = width // heads
    tp_size = lax.axis_size("tp")
    dp_size = lax.axis_size("dp")
    tp_index = lax.axis_index("tp")
    seg = segments[:, 0]
    side = rows // 2
    span = jnp.arange(side, dtype=jnp.int32)
    starts = [chunk_of(tp_index, x, tp_size, False) * side for x in range(2)]
    qpos = jnp.concatenate([start + span for start in starts])
    qseg = jnp.concatenate([lax.dynamic_slice_in_dim(seg, start, side, 0) for start in starts])
    qinfo = jnp.stack([qpos, qseg] + [qpos] * 6, 1)
    kinfo = jnp.pad(jnp.stack([jnp.arange(seg.shape[0], dtype=jnp.int32), seg]), ((0, 6), (0, 0)))
    where = (qinfo, kinfo, tp_index[None])

    def mirror(value):
        moved = lax.ppermute(value[side:], "tp", [(i, tp_size - 1 - i) for i in range(tp_size)])
        return value[:side], moved

    tab = jnp.concatenate([jnp.swapaxes(mix_pre, 1, 2) * (head_size**-0.5), mix_post], 1)
    tabt = jnp.pad(jnp.repeat(jnp.swapaxes(tab, 1, 2), head_size, axis=1), ((0, 0), (0, 0), (0, 128 - 2 * heads)))
    tab = jnp.repeat(tab, head_size, axis=2)

    stream = x_in[:, 0].astype(F32)
    x_folded = jnp.concatenate(mirror(x_in[:, 0]), 0).astype(F32)
    kept = []
    half = tp_size // 2
    for layer in range(LAYERS):
        last = layer == LAYERS - 1
        n1_blocks = gather_blocks(rms(stream, gain_attn[layer]).astype(BF16))
        if last:
            low, n1_blocks[half] = after((cotangent[:, 0], n1_blocks[half]))
            grad_near, grad_far = gather_near(low)
        else:
            stream = x_folded
        p, u, q, k, v, ot, n1t, middle, n2 = attn_fwd(
            layer,
            layer == 0,
            n1_blocks,
            stream,
            w_qkv,
            w_out,
            tab,
            gain_ffn,
            where,
        )
        if last:
            n2, grad_near, grad_far = after((n2, grad_near, grad_far))
        near, far = gather_near(n2)
        out_a, hid_a, dgelu_a = ffn_fwd(layer, near, w_in, w_down)
        if last:
            given = grad_near + gather_far(grad_far)
            gf_blocks = [jnp.concatenate([given[r][:side], given[tp_size - 1 - r][side:]], 0) for r in range(tp_size)]
            gn2_a, gpre_a = ffn_bwd(layer, gf_blocks[:half], dgelu_a, w_in, w_down)
            far, gpre_a = after((far, gpre_a))
        far, hid_a = after((far, hid_a))
        n2_blocks = near + gather_far(far)
        out_b, hid_b, dgelu_b = ffn_fwd(layer, n2_blocks[half:], w_in, w_down)
        kept.append((stream, n1t, p, u, q, k, v, ot, middle, n2_blocks, hid_a, hid_b, dgelu_a, dgelu_b))
        if not last:
            own, far = scatter_begin([*out_a, *out_b])
            stream = middle + (own + far.astype(F32))

    grad_flow = gf_blocks[0].astype(F32)
    per = width // dp_size
    small = [None] * LAYERS
    sharded = [None] * LAYERS
    for layer in range(LAYERS - 1, -1, -1):
        last = layer == LAYERS - 1
        stream, n1t, p, u, q, k, v, ot, middle, n2_blocks, hid_a, hid_b, dgelu_a, dgelu_b = kept[layer]
        if not last:
            near, far = gather_near(grad_flow.astype(BF16))
            gn2_a, gpre_a = ffn_bwd(layer, near, dgelu_a, w_in, w_down)
            far, gpre_a = after((far, gpre_a))
            gf_blocks = near + gather_far(far)
        gn2_b, gpre_b = ffn_bwd(layer, gf_blocks[half:], dgelu_b, w_in, w_down)
        if not last:
            total_got, gpre_b = after((total_got, gpre_b))
            total = halve_end(total_kept, total_got)
            total_kept, total_got = sum_start(total, total_order, 1)
        own, far = scatter_begin([*gn2_a, *gn2_b])
        packed = ffn_grads(n2_blocks, gf_blocks, (hid_a, hid_b), (gpre_a, gpre_b), dp_size)
        far, packed = after((far, packed))
        if not last:
            total_got, packed = after((total_got, packed))
            total = halve_end(total_kept, total_got)
            total_kept, total_got = sum_start(total, total_order, 2)
        if not last:
            previous = moving
        moving = Scatter([packed], steps_of("dp"))
        gn2 = (own + far.astype(F32)).astype(BF16).astype(F32)
        grad_norm, grad_gffn = rms_back(gn2, middle, gain_ffn[layer])
        grad_middle = grad_flow + grad_norm
        ga = grad_middle.astype(BF16)
        if last:
            orders = [steps_of("dp") + steps_of("tp")[1:]]
        else:
            (y_step, *dp_rest), x_steps = steps_of("dp"), steps_of("tp")[1:]
            orders = [x_steps + [y_step] + dp_rest, [y_step] + x_steps + dp_rest]
        place = jnp.stack([tp_index & 1] + [place_of(order) for order in orders] + [tp_index])
        parts, grads, zpre, zpost = attn_bwd(
            layer, tp_size, ga, w_out, q, k, v, p, u, tab, tabt, place, w_qkv, n1t, ot
        )
        core_step = steps_of("tp")[0]
        if last:
            parts, grads, moving.got = after((parts, grads, moving.got))
            y_middle = middle
            keep, send = grads
            total = halve_end(keep, swap(send, *core_step))
            own, far = scatter_begin(parts)
            moving.advance()
            far, moving.got = after((far, moving.got), total)
            moving.advance()
            (total_order,), total_place = orders, place
            total_kept, total_got = sum_start(total, total_order, 0)
        else:
            parts, grads, moving.got, total_got, previous.got = after(
                (parts, grads, moving.got, total_got, previous.got)
            )
            (summed,) = previous.finish()
            sharded[layer + 1] = (summed[:per], summed[per:].T)
        if not last:
            break
        gn1 = (own + far.astype(F32)).astype(BF16).astype(F32)
        grad_norm, grad_gattn = rms_back(gn1, stream, gain_attn[layer])
        grad_flow = grad_middle + grad_norm
        grad_mpre = jnp.sum(zpre.reshape(heads, heads, head_size), -1).T * (head_size**-0.5)
        grad_mpost = jnp.sum(zpost.reshape(heads, heads, head_size), -1)
        small[layer] = (grad_mpre, grad_mpost, grad_gattn, grad_gffn)

    total = halve_end(total_kept, total_got)
    got = [swap(send, *core_step) for send in grads[1::2]]
    pieces = [halve_end(keep, g) for keep, g in zip(grads[::2], got)]
    for stage in range(HALVINGS, len(total_order)):
        total_got = swap(total, *total_order[stage])
        pieces, total_got = after((pieces, total_got))
        total = halve_end(total, total_got)
    own, far = scatter_begin(parts)
    for stage in range(HALVINGS):
        kept, got = zip(*[sum_start(part, order, stage) for part, order in zip(pieces, orders)])
        total_got = swap(total, *total_order[HALVINGS - 1 - stage])
        if stage < HALVINGS - 1:
            got, total_got = after((got, total_got))
            total = spread(total, total_got)
        if stage == HALVINGS - 1:
            flat_got = flat.start()
            got, flat_got = after((got, flat_got))
            flat.end(flat_got)
        pieces = [halve_end(a, b) for a, b in zip(kept, after(got))]
        if stage == 0:
            far, pieces = after((far, pieces))
            gn1 = (own + far.astype(F32)).astype(BF16).astype(F32)
            grad_norm, grad_gattn = rms_back(gn1, stream, gain_attn[layer])
            grad_flow = grad_middle + grad_norm
            grad_mpre = jnp.sum(zpre.reshape(heads, heads, head_size), -1).T * (head_size**-0.5)
            grad_mpost = jnp.sum(zpost.reshape(heads, heads, head_size), -1)
            small[layer] = (grad_mpre, grad_mpost, grad_gattn, grad_gffn)
            mixes = jnp.concatenate([a.reshape(-1) for s in small for a in s[:2]])
            count = mixes.shape[0]
            mix_rows = -(-count // width)
            flat = jnp.concatenate(
                [jnp.pad(mixes, (0, mix_rows * width - count)).reshape(mix_rows, width)]
                + [g[None] for s in small for g in s[2:]]
            )
            flat = jnp.pad(flat, ((0, -flat.shape[0] % 8), (0, 0)))
            flat = Butterfly(flat)
        if stage == 1:
            moving.advance(*pieces)
            y_parts, pieces = after(([*out_a, *out_b], pieces))
            own_y, far_y = scatter_begin(y_parts)
    for stage in range(HALVINGS, len(orders[0])):
        got = [swap(part, *order[stage]) for part, order in zip(pieces, orders)]
        flat_got = flat.start()
        if stage == HALVINGS:
            first_rows, second_rows = mirror(grad_flow)
            got, second_rows, total_got, moving.got, far_y = after((got, second_rows, total_got, moving.got, far_y))
            y_out = (y_middle + (own_y + far_y.astype(F32))).astype(BF16)
            y_first, y_second = mirror(y_out)
            grad_x = jnp.concatenate([first_rows, second_rows], 0)
            total = spread(total, total_got)
            moving.advance()
        got, flat_got = after((got, flat_got))
        flat.end(flat_got)
        pieces = [halve_end(a, b) for a, b in zip(pieces, got)]
    total_other = swap(total, *core_step)
    replicated = ()
    for stage in range(HALVINGS - 1, -1, -1):
        got = [swap(part, *order[stage]) for part, order in zip(pieces, orders)]
        flat_got = flat.start()
        if stage == HALVINGS - 1:
            got, total_other = after((got, total_other))
        elif stage == HALVINGS - 2:
            replicated = expand(1, 0, total_place, [total])
            got, replicated, moving.got, y_second = after((got, replicated, moving.got, y_second))
            y_out = jnp.concatenate([y_first, y_second], 0)
        elif stage == 0:
            replicated = expand(1, 1, total_place, [total_other], replicated)
            got, replicated = after((got, replicated))
        got, flat_got = after((got, flat_got))
        flat.end(flat_got)
        pieces = [spread(a, b) for a, b in zip(pieces, got)]
    got = [swap(part, *core_step) for part in pieces]
    while flat.steps:
        flat.end(flat.start())
    flat = flat.value
    (summed,) = moving.finish()
    sharded[0] = (summed[:per], summed[per:].T)
    replicated = expand(0, 0, place, pieces, replicated)
    got, replicated, sharded = after((got, replicated, sharded))
    replicated = expand(0, 1, place, got, replicated)
    mixes = flat[:mix_rows].reshape(-1)[:count].reshape(LAYERS, 2, heads, heads)
    gains = flat[mix_rows : mix_rows + 2 * LAYERS].reshape(LAYERS, 2, width)
    return (
        y_out[:, None],
        grad_x[:, None],
        *replicated,
        mixes[:, 0],
        mixes[:, 1],
        gains[:, 0],
        gains[:, 1],
        jnp.stack([s[0] for s in sharded]),
        jnp.stack([s[1] for s in sharded]),
    )


def solution(mesh):
    in_specs = (
        P("tp", "dp", None),
        P(None, "dp"),
        P(),
        P(),
        P(),
        P(),
        P(),
        P(),
        P(None, None, "tp"),
        P(None, "tp", None),
        P("tp", "dp", None),
    )
    out_specs = (
        P("tp", "dp", None),
        P("tp", "dp", None),
        P(),
        P(),
        P(),
        P(),
        P(),
        P(),
        P(None, "dp", "tp"),
        P(None, "tp", "dp"),
    )
    return jax.shard_map(
        on_device, mesh=mesh, in_specs=in_specs, out_specs=out_specs, check_vma=False
    )
```

```python
import functools

import jax
import jax.numpy as jnp
from jax import lax
from jax.experimental import pallas as pl
from jax.experimental.pallas import tpu as pltpu
from jax.sharding import PartitionSpec as P

LAYERS = 2
EPSILON = 1e-06
NEGATIVE = -1e30
LOG2E = 1.4426950408889634
GROUPS = 4
PIECES = 8
GP = 4
GB = 4
VMEM = 60 * 1024 * 1024
SMALL = 18 * 1024 * 1024
F32 = jnp.float32
BF16 = jnp.bfloat16


def dot_nn(a, b):
    return lax.dot_general(a, b, (((1,), (0,)), ((), ())), preferred_element_type=F32)


def dot_nt(a, b):
    return lax.dot_general(a, b, (((1,), (1,)), ((), ())), preferred_element_type=F32)


def dot_tn(a, b):
    return lax.dot_general(a, b, (((0,), (0,)), ((), ())), preferred_element_type=F32)


def rms(values, gain):
    return values * lax.rsqrt(jnp.mean(values * values, -1, keepdims=True) + EPSILON) * gain


def rms_back(grad, values, gain):
    inv = lax.rsqrt(jnp.mean(values * values, -1, keepdims=True) + EPSILON)
    unit = values * inv
    scaled = grad * gain
    grad_values = (scaled - unit * jnp.mean(scaled * unit, -1, keepdims=True)) * inv
    return grad_values, jnp.sum(grad * unit, axis=0)


def whole(shape):
    return pl.BlockSpec(shape, lambda *_: (0,) * len(shape))


def layer_of(array, layer):
    shape = array.shape[1:]
    return pl.BlockSpec((1,) + shape, lambda *_: (layer,) + (0,) * len(shape))


def attn_fwd_body(blocks, heads, layer, plain, *refs):
    n_refs = refs[:blocks]
    x_hbm, wqkv_hbm, wout_hbm, tab_ref, gain_ref, qinfo_ref, kinfo_ref, at_ref = refs[blocks : blocks + 8]
    p_ref, u_ref, q_ref, k_hbm, v_hbm, ot_ref, n1t_hbm, xm_ref, n2_ref = refs[blocks + 8 : blocks + 17]
    bias_ref, acc_ref, k_ref, v_ref, n1t_ref, x_ref, wqkv_ref, wout_ref, sems = refs[blocks + 17 :]
    step = pl.program_id(0)
    rows, width = x_ref.shape
    q_cols, k_cols, v_cols = [slice(i * width, (i + 1) * width) for i in range(3)]
    weights = [
        pltpu.make_async_copy(wqkv_hbm.at[layer, :, cols], wqkv_ref.at[i], sems.at[i])
        for i, cols in enumerate((k_cols, v_cols, q_cols))
    ]
    last_used = [
        pltpu.make_async_copy(wout_hbm.at[layer], wout_ref, sems.at[3]),
        pltpu.make_async_copy(x_hbm, x_ref, sems.at[4]),
    ]
    early = [
        pltpu.make_async_copy(k_ref, k_hbm, sems.at[5]),
        pltpu.make_async_copy(v_ref, v_hbm, sems.at[6]),
    ]
    turned = pltpu.make_async_copy(n1t_ref, n1t_hbm, sems.at[7])
    half = rows // 2
    at = at_ref[0]

    def place(r, second):
        block = chunk_of(at ^ r, second, blocks, plain)
        return pl.ds(pl.multiple_of(block * half, half), half)

    @pl.when(step == 0)
    def _():
        for copy in weights + last_used:
            copy.start()
        for i, ref in enumerate((k_ref, v_ref)):
            weights[i].wait()
            for r in range(blocks):
                value = dot_nn(n_refs[r][...], wqkv_ref[i]).astype(BF16)
                ref[place(r, 0), :] = value[:half]
                ref[place(r, 1), :] = value[half:]
            early[i].start()
        weights[2].wait()
        n_second = n_refs[blocks - 1 if plain else 0]
        q_ref[:half] = dot_nn(n_refs[0][:half], wqkv_ref[2]).astype(BF16)
        q_ref[half:] = dot_nn(n_second[half:], wqkv_ref[2]).astype(BF16)
        ok = (qinfo_ref[:, 1:2] == kinfo_ref[1:2, :]) & (kinfo_ref[0:1, :] <= qinfo_ref[:, 0:1])
        bias_ref[...] = jnp.where(ok, 0.0, NEGATIVE)
        acc_ref[...] = jnp.zeros_like(acc_ref)

    def work(second, keys):
        here = pl.ds(pl.multiple_of(second * half, half), half)
        q = q_ref[here, :].astype(F32)
        gs = [step * GP + u for u in range(GP)]
        qm = jnp.concatenate([(q * (tab_ref[0, pl.ds(g, 1), :] * LOG2E)).astype(BF16) for g in gs], 0)
        m = dot_nt(qm, k_ref[:keys, :])
        bias = bias_ref[here, :keys]
        ps = []
        for u in range(GP):
            mu = m[u * half : (u + 1) * half] + bias
            e = jnp.exp2(mu - jnp.max(mu, -1, keepdims=True))
            p = (e * (1.0 / jnp.sum(e, -1, keepdims=True))).astype(BF16)
            p_ref[u, here, :keys] = p
            ps.append(p)
        ctx = dot_nn(jnp.concatenate(ps, 0), v_ref[:keys, :])
        total = acc_ref[here, :]
        for u in range(GP):
            cu = ctx[u * half : (u + 1) * half]
            u_ref[u, here, :] = cu.astype(BF16)
            total = total + cu * tab_ref[0, pl.ds(heads + gs[u], 1), :]
        acc_ref[here, :] = total

    for pairs in range(1, blocks + 1):
        late = at == blocks - pairs

        @pl.when(late | (at == pairs - 1))
        def _(pairs=pairs, late=late):
            work(late.astype(jnp.int32), 2 * pairs * half)

    @pl.when(step == 0)
    def _():
        for r in range(blocks):
            for second in range(2):
                n1t_ref[:, place(r, second)] = n_refs[r][second * half : (second + 1) * half, :].T
        turned.start()

    @pl.when(step == pl.num_programs(0) - 1)
    def _():
        o = acc_ref[...].astype(BF16)
        ot_ref[...] = o.T
        for copy in last_used + early + [turned]:
            copy.wait()
        xm = x_ref[...] + dot_nn(o, wout_ref[...])
        xm_ref[...] = xm
        n2_ref[...] = rms(xm, gain_ref[pl.ds(layer, 1), :]).astype(BF16)


def chunk_of(device, second, devices, plain):
    if not second:
        return 2 * device
    return 2 * device + 1 if plain else 2 * (devices - 1 - device) + 1


def attn_fwd(layer, plain, n_blocks, x, w_qkv, w_out, tab, gain, where):
    rows, width = x.shape
    blocks = len(n_blocks)
    heads = tab.shape[1] // 2
    keys = rows * blocks
    args = (*n_blocks, x, w_qkv, w_out, tab, gain, *where)
    in_specs = [whole(a.shape) for a in args]
    in_specs[blocks : blocks + 3] = [pl.BlockSpec(memory_space=pl.ANY)] * 3
    in_specs[blocks + 3] = layer_of(tab, layer)
    in_specs[-1] = pl.BlockSpec(memory_space=pltpu.SMEM)
    out = [
        ((heads, rows, keys), BF16),
        ((heads, rows, width), BF16),
        ((rows, width), BF16),
        ((keys, width), BF16),
        ((keys, width), BF16),
        ((width, rows), BF16),
        ((width, keys), BF16),
        ((rows, width), F32),
        ((rows, width), BF16),
    ]
    out_specs = [whole(s) for s, _ in out]
    out_specs[0] = pl.BlockSpec((GP, rows, keys), lambda i: (i, 0, 0))
    out_specs[1] = pl.BlockSpec((GP, rows, width), lambda i: (i, 0, 0))
    for i in (3, 4, 6):
        out_specs[i] = pl.BlockSpec(memory_space=pltpu.HBM)
    return pl.pallas_call(
        functools.partial(attn_fwd_body, blocks, heads, layer, plain),
        grid=(heads // GP,),
        in_specs=in_specs,
        out_specs=out_specs,
        out_shape=[jax.ShapeDtypeStruct(s, d) for s, d in out],
        scratch_shapes=[
            pltpu.VMEM((rows, keys), F32),
            pltpu.VMEM((rows, width), F32),
            pltpu.VMEM((keys, width), BF16),
            pltpu.VMEM((keys, width), BF16),
            pltpu.VMEM((width, keys), BF16),
            pltpu.VMEM((rows, width), F32),
            pltpu.VMEM((3, width, width), BF16),
            pltpu.VMEM((width, width), BF16),
            pltpu.SemaphoreType.DMA((8,)),
        ],
        compiler_params=pltpu.CompilerParams(vmem_limit_bytes=VMEM),
        cost_estimate=pl.CostEstimate(
            flops=2 * rows * keys * width * heads * 2, bytes_accessed=20_000_000, transcendentals=rows * keys * heads
        ),
        name="attn_fwd",
    )(*args)


def attn_bwd_body(heads, blocks, layer, parts, *refs):
    (ga_ref, wout_ref, q_ref, k_ref, v_ref, p_ref, u_ref, tab_ref, tabt_ref, place_ref) = refs[:10]
    wqkv_hbm, n1t_hbm, ot_hbm = refs[10:13]
    gn1_refs = refs[13 : 13 + blocks]
    grad_refs = refs[13 + blocks : 13 + blocks + 2 * parts]
    zpre_ref, zpost_ref = refs[13 + blocks + 2 * parts : 15 + blocks + 2 * parts]
    go_ref, got_ref, qt_ref, gq_acc, gk_acc, gv_acc, wqkv_ref, n1t_ref, ot_ref, sems = refs[15 + blocks + 2 * parts :]
    step = pl.program_id(0)
    rows, width = q_ref.shape

    late = [
        pltpu.make_async_copy(wqkv_hbm.at[layer], wqkv_ref, sems.at[0]),
        pltpu.make_async_copy(n1t_hbm, n1t_ref, sems.at[1]),
        pltpu.make_async_copy(ot_hbm, ot_ref, sems.at[2]),
    ]

    @pl.when(step == 0)
    def _():
        for copy in late:
            copy.start()
        go = dot_nt(ga_ref[...], wout_ref[0]).astype(BF16).astype(F32)
        go_ref[...] = go
        got_ref[...] = go.T
        qt_ref[...] = q_ref[...].astype(F32).T
        gq_acc[...] = jnp.zeros_like(gq_acc)
        gk_acc[...] = jnp.zeros_like(gk_acc)
        gv_acc[...] = jnp.zeros_like(gv_acc)
        zpre_ref[...] = jnp.zeros_like(zpre_ref)
        zpost_ref[...] = jnp.zeros_like(zpost_ref)

    half = rows // 2
    at = place_ref[1 + parts]
    lane = lax.broadcasted_iota(jnp.int32, tabt_ref.shape[1:], 1)
    gs = [step * GB + u for u in range(GB)]
    cols = []
    for g in gs:
        pre_col = jnp.sum(jnp.where(lane == g, tabt_ref[0], 0.0), 1, keepdims=True)
        post_col = jnp.sum(jnp.where(lane == heads + g, tabt_ref[0], 0.0), 1, keepdims=True)
        cols.append((pre_col, post_col))

    def work(second, keys):
        here = pl.ds(pl.multiple_of(second * half, half), half)
        go = go_ref[here, :]
        q = q_ref[here, :].astype(F32)
        mixed = [go * tab_ref[0, pl.ds(heads + g, 1), :] for g in gs]
        gp = dot_nt(jnp.concatenate([x.astype(BF16) for x in mixed], 0), v_ref[:keys, :])
        gms, ps, zposts = [], [], []
        for u in range(GB):
            ctx = u_ref[u, here, :].astype(F32)
            zposts.append(jnp.sum(ctx * go, axis=0, keepdims=True))
            delta = jnp.sum(ctx * mixed[u], axis=1, keepdims=True)
            p = p_ref[u, here, :keys]
            gms.append((p.astype(F32) * (gp[u * half : (u + 1) * half] - delta)).astype(BF16))
            ps.append(p)
        gm = jnp.concatenate(gms, 0)
        t = dot_nn(gm, k_ref[:keys, :])
        total = gq_acc[here, :]
        zpres = []
        for u in range(GB):
            tu = t[u * half : (u + 1) * half]
            zpres.append(jnp.sum(tu * q, axis=0, keepdims=True))
            total = total + tu * tab_ref[0, pl.ds(gs[u], 1), :]
        gq_acc[here, :] = total
        qm = jnp.concatenate([(qt_ref[:, here] * pre).astype(BF16) for pre, _ in cols], 1)
        gk_acc[:, :keys] += dot_nn(qm, gm)
        gm2 = jnp.concatenate([(got_ref[:, here] * post).astype(BF16) for _, post in cols], 1)
        gv_acc[:, :keys] += dot_nn(gm2, jnp.concatenate(ps, 0))
        return zpres, zposts

    for pairs in range(1, blocks + 1):
        is_late = at == blocks - pairs

        @pl.when(is_late | (at == pairs - 1))
        def _(pairs=pairs, is_late=is_late):
            zpres, zposts = work(is_late.astype(jnp.int32), 2 * pairs * half)
            for u, g in enumerate(gs):
                zpre_ref[pl.ds(g, 1), :] += zpres[u]
                zpost_ref[pl.ds(g, 1), :] += zposts[u]

    @pl.when(step == pl.num_programs(0) - 1)
    def _():
        for copy in late:
            copy.wait()
        gq = gq_acc[...].astype(BF16)
        gkt = gk_acc[...].astype(BF16)
        gvt = gv_acc[...].astype(BF16)
        ga = ga_ref[...]
        for r in range(blocks):
            there = [pl.ds(pl.multiple_of(chunk_of(at ^ r, x, blocks, False) * half, half), half) for x in range(2)]
            gk = jnp.concatenate([gk_acc[:, x].T.astype(BF16) for x in there], 0)
            gv = jnp.concatenate([gv_acc[:, x].T.astype(BF16) for x in there], 0)
            gn1 = dot_nt(gk, wqkv_ref[:, width : 2 * width]) + dot_nt(gv, wqkv_ref[:, 2 * width :])
            if r == 0:
                gn1 = gn1 + dot_nt(gq, wqkv_ref[:, :width])
            gn1_refs[r][...] = gn1.astype(BF16)
        hand = width // 2
        per = hand // PIECES
        own = [pl.ds(pl.multiple_of(chunk_of(at, x, blocks, False) * half, half), half) for x in range(2)]
        for side in range(2):
            core = place_ref[0] if side == 0 else 1 - place_ref[0]
            mine = pl.ds(pl.multiple_of(core * hand, hand), hand)
            n1t = n1t_ref[mine, :]
            n1t_own = jnp.concatenate([n1t_ref[mine, x] for x in own], 1)
            grads = (
                lambda: dot_nn(n1t_own, gq),
                lambda: dot_nt(n1t, gkt),
                lambda: dot_nt(n1t, gvt),
                lambda: dot_nn(ot_ref[mine, :], ga),
            )
            for index, grad in enumerate(grads):
                part = index * parts // len(grads)
                column = (index - part * (len(grads) // parts)) * width
                value = grad().astype(BF16)
                for piece in range(PIECES):
                    there = pl.multiple_of((piece ^ place_ref[1 + part]) * per, per)
                    grad_refs[2 * part + side][pl.ds(there, per), column : column + width] = value[
                        piece * per : (piece + 1) * per
                    ]


def attn_bwd(layer, blocks, ga, w_out, q, k, v, p, u, tab, tabt, place, w_qkv, n1t, ot):
    rows, width = q.shape
    keys = k.shape[0]
    heads = p.shape[0]
    parts = place.shape[0] - 2
    args = (ga, w_out, q, k, v, p, u, tab, tabt, place, w_qkv, n1t, ot)
    in_specs = [whole(a.shape) for a in args]
    in_specs[1] = layer_of(w_out, layer)
    in_specs[5] = pl.BlockSpec((GB, rows, keys), lambda i: (i, 0, 0))
    in_specs[6] = pl.BlockSpec((GB, rows, width), lambda i: (i, 0, 0))
    in_specs[7] = layer_of(tab, layer)
    in_specs[8] = layer_of(tabt, layer)
    in_specs[9] = pl.BlockSpec(memory_space=pltpu.SMEM)
    in_specs[10:13] = [pl.BlockSpec(memory_space=pl.ANY)] * 3
    out = (
        [((rows, width), BF16)] * blocks
        + [((width // 2, 4 // parts * width), BF16)] * (2 * parts)
        + [((heads, width), F32)] * 2
    )
    res = pl.pallas_call(
        functools.partial(attn_bwd_body, heads, blocks, layer, parts),
        grid=(heads // GB,),
        in_specs=in_specs,
        out_specs=[whole(s) for s, _ in out],
        out_shape=[jax.ShapeDtypeStruct(s, d) for s, d in out],
        scratch_shapes=[
            pltpu.VMEM((rows, width), F32),
            pltpu.VMEM((width, rows), F32),
            pltpu.VMEM((width, rows), F32),
            pltpu.VMEM((rows, width), F32),
            pltpu.VMEM((width, keys), F32),
            pltpu.VMEM((width, keys), F32),
            pltpu.VMEM(w_qkv.shape[1:], BF16),
            pltpu.VMEM(n1t.shape, BF16),
            pltpu.VMEM(ot.shape, BF16),
            pltpu.SemaphoreType.DMA((3,)),
        ],
        compiler_params=pltpu.CompilerParams(vmem_limit_bytes=VMEM),
        cost_estimate=pl.CostEstimate(
            flops=2 * rows * keys * width * heads * 4 * 2, bytes_accessed=20_000_000, transcendentals=0
        ),
        name="attn_bwd",
    )(*args)
    return res[:blocks], res[blocks:-2], res[-2], res[-1]


def expand_body(parts, place_ref, *refs):
    qkv_ref, out_ref = refs[-2:]
    width3 = qkv_ref.shape[2]
    inner = PIECES // GROUPS
    per = qkv_ref.shape[1] // inner
    column = 0
    for part, ref in enumerate(refs[:parts]):
        end = column + ref.shape[1]
        cut = min(end, width3)
        for piece in range(inner):
            here = slice(piece * per, (piece + 1) * per)
            there = piece ^ lax.rem(place_ref[1 + part], inner)
            value = ref[pl.ds(pl.multiple_of(there * per, per), per), :].astype(F32)
            qkv_ref[0, here, column:cut] = value[:, : cut - column]
            if end > width3:
                out_ref[0, here, :] = value[:, cut - column :]
        column = end


def expand(layer, side, place, halves, before=()):
    half = halves[0].shape[0]
    width = sum(h.shape[1] for h in halves) // 4
    per = half // GROUPS
    in_specs = []
    for part, array in enumerate(halves):

        def piece(i, place, part=part):
            return i ^ (place[1 + part] // (PIECES // GROUPS)), 0

        in_specs.append(pl.BlockSpec((per, array.shape[1]), piece))
    first = 1 + len(halves)
    in_specs += [pl.BlockSpec(memory_space=pl.ANY)] * len(before)

    def there(i, place):
        return layer, (place[0] ^ side) * GROUPS + i, 0

    return pl.pallas_call(
        functools.partial(expand_body, len(halves)),
        grid_spec=pltpu.PrefetchScalarGridSpec(
            num_scalar_prefetch=1,
            grid=(GROUPS,),
            in_specs=in_specs,
            out_specs=[pl.BlockSpec((1, per, 3 * width), there), pl.BlockSpec((1, per, width), there)],
        ),
        out_shape=[
            jax.ShapeDtypeStruct((LAYERS, 2 * half, 3 * width), F32),
            jax.ShapeDtypeStruct((LAYERS, 2 * half, width), F32),
        ],
        input_output_aliases={first + i: i for i in range(len(before))},
        compiler_params=pltpu.CompilerParams(vmem_limit_bytes=SMALL),
        cost_estimate=pl.CostEstimate(flops=0, bytes_accessed=7_000_000, transcendentals=0),
        name="expand",
    )(place, *halves, *before)


def ffn_fwd_body(blocks, *refs):
    n_refs = refs[:blocks]
    win_ref, wdown_ref = refs[blocks : blocks + 2]
    out_refs = refs[blocks + 2 : 2 * blocks + 2]
    hid_ref, dgelu_ref = refs[2 * blocks + 2 :]
    rows = n_refs[0].shape[0]
    for r in range(blocks):
        here = pl.ds(r * rows, rows)
        pre = dot_nn(n_refs[r][...], win_ref[0])
        cdf = 0.5 + 0.5 * lax.erf(pre * (0.5**0.5))
        hid = (pre * cdf).astype(BF16)
        hid_ref[here, :] = hid
        density = jnp.exp2(pre * pre * (-0.5 * LOG2E)) * 0.3989422804014327
        dgelu_ref[here, :] = (cdf + pre * density).astype(BF16)
        out_refs[r][...] = dot_nn(hid, wdown_ref[0]).astype(BF16)


def ffn_fwd(layer, n_blocks, w_in, w_down):
    blocks = len(n_blocks)
    rows, width = n_blocks[0].shape
    hidden = w_in.shape[2]
    args = (*n_blocks, w_in, w_down)
    in_specs = [whole(a.shape) for a in args]
    in_specs[blocks] = layer_of(w_in, layer)
    in_specs[blocks + 1] = layer_of(w_down, layer)
    out = [((rows, width), BF16)] * blocks + [((rows * blocks, hidden), BF16)] * 2
    res = pl.pallas_call(
        functools.partial(ffn_fwd_body, blocks),
        grid=(1,),
        in_specs=in_specs,
        out_specs=[whole(s) for s, _ in out],
        out_shape=[jax.ShapeDtypeStruct(s, d) for s, d in out],
        compiler_params=pltpu.CompilerParams(vmem_limit_bytes=SMALL),
        cost_estimate=pl.CostEstimate(
            flops=4 * rows * blocks * width * hidden, bytes_accessed=6_000_000, transcendentals=rows * blocks * hidden
        ),
        name="ffn_fwd",
    )(*args)
    return res[:blocks], res[blocks], res[blocks + 1]


def ffn_bwd_body(blocks, *refs):
    g_refs = refs[:blocks]
    dgelu_ref, win_ref, wdown_ref = refs[blocks : blocks + 3]
    out_refs = refs[blocks + 3 : 2 * blocks + 3]
    gpre_ref = refs[2 * blocks + 3]
    rows = g_refs[0].shape[0]
    for r in range(blocks):
        here = pl.ds(r * rows, rows)
        gh = dot_nt(g_refs[r][...], wdown_ref[0])
        gpre = (gh * dgelu_ref[here, :].astype(F32)).astype(BF16)
        gpre_ref[here, :] = gpre
        out_refs[r][...] = dot_nt(gpre, win_ref[0]).astype(BF16)


def ffn_bwd(layer, g_blocks, dgelu, w_in, w_down):
    blocks = len(g_blocks)
    rows, width = g_blocks[0].shape
    hidden = w_in.shape[2]
    args = (*g_blocks, dgelu, w_in, w_down)
    in_specs = [whole(a.shape) for a in args]
    in_specs[blocks + 1] = layer_of(w_in, layer)
    in_specs[blocks + 2] = layer_of(w_down, layer)
    out = [((rows, width), BF16)] * blocks + [((rows * blocks, hidden), BF16)]
    res = pl.pallas_call(
        functools.partial(ffn_bwd_body, blocks),
        grid=(1,),
        in_specs=in_specs,
        out_specs=[whole(s) for s, _ in out],
        out_shape=[jax.ShapeDtypeStruct(s, d) for s, d in out],
        compiler_params=pltpu.CompilerParams(vmem_limit_bytes=SMALL),
        cost_estimate=pl.CostEstimate(
            flops=4 * rows * blocks * width * hidden, bytes_accessed=6_000_000, transcendentals=0
        ),
        name="ffn_bwd",
    )(*args)
    return res[:blocks], res[blocks]


def ffn_grads_body(blocks, chunks, *refs):
    n_refs, g_refs = refs[:blocks], refs[blocks : 2 * blocks]
    hid_refs, gpre_refs = refs[2 * blocks : 2 * blocks + 2], refs[2 * blocks + 2 : 2 * blocks + 4]
    out_ref = refs[-1]
    rows, width = n_refs[0].shape
    per = width // chunks
    for part, (left_refs, right_refs) in enumerate(((n_refs, gpre_refs), (g_refs, hid_refs))):
        left = jnp.concatenate([ref[...].T for ref in left_refs], 1)
        right = jnp.concatenate([ref[...] for ref in right_refs], 0)
        grad = dot_nn(left, right).astype(BF16)
        for c in range(chunks):
            place = 2 * sum(((c >> i) & 1) * (chunks >> (i + 1)) for i in range(chunks.bit_length() - 1)) + part
            out_ref[place * per : (place + 1) * per, :] = grad[c * per : (c + 1) * per]


def ffn_grads(n_blocks, g_blocks, hids, gpres, chunks):
    blocks = len(n_blocks)
    rows, width = n_blocks[0].shape
    hidden = hids[0].shape[1]
    args = (*n_blocks, *g_blocks, *hids, *gpres)
    return pl.pallas_call(
        functools.partial(ffn_grads_body, blocks, chunks),
        grid=(1,),
        in_specs=[whole(a.shape) for a in args],
        out_specs=whole((2 * width, hidden)),
        out_shape=jax.ShapeDtypeStruct((2 * width, hidden), BF16),
        compiler_params=pltpu.CompilerParams(vmem_limit_bytes=VMEM),
        cost_estimate=pl.CostEstimate(
            flops=4 * rows * blocks * width * hidden, bytes_accessed=9_000_000, transcendentals=0
        ),
        name="ffn_grads",
    )(*args)


def swap(value, axis, bit):
    size = lax.axis_size(axis)
    return lax.ppermute(value, axis, [(i, i ^ bit) for i in range(size)])


def after(values, *done):
    return lax.optimization_barrier((values, done))[0]


def gather_near(value):
    half = lax.axis_size("tp") // 2
    far = swap(value, "tp", half)
    near = [value]
    bit = 1
    while bit < half:
        near += [swap(b, "tp", bit) for b in near]
        bit *= 2
    return near, far


def gather_far(far):
    half = lax.axis_size("tp") // 2
    blocks = [far]
    bit = 1
    while bit < half:
        blocks += [swap(b, "tp", bit) for b in blocks]
        bit *= 2
    return blocks


def gather_blocks(value):
    near, far = gather_near(value)
    return near + gather_far(far)


def scatter_begin(blocks):
    blocks = list(blocks)
    bit = 1
    while bit < lax.axis_size("tp") // 2:
        size = len(blocks)
        keep = [blocks[r] for r in range(size) if not r & 1]
        sent = [swap(blocks[r], "tp", bit) for r in range(size) if r & 1]
        blocks = [a.astype(F32) + b.astype(F32) for a, b in zip(keep, sent)]
        bit *= 2
        blocks = [blocks[0]] + [b.astype(BF16) for b in blocks[1:]]
    return blocks[0].astype(F32), swap(blocks[1], "tp", bit)


def halve_begin(part, axis, bit):
    mine = (lax.axis_index(axis) // bit) & 1
    pair = part.reshape(2, part.shape[0] // 2, part.shape[1])
    sent = lax.dynamic_index_in_dim(pair, 1 - mine, 0, keepdims=False)
    kept = lax.dynamic_index_in_dim(pair, mine, 0, keepdims=False)
    return kept, swap(sent, axis, bit)


def halve_end(kept, got):
    return (kept.astype(F32) + got.astype(F32)).astype(BF16)


class Scatter:
    def __init__(self, parts, steps):
        self.steps = list(steps)
        self.begin(parts)

    def begin(self, parts):
        step = self.steps.pop(0)
        self.kept, self.got = zip(*[halve_begin(part, *step) for part in parts])

    def advance(self, *done):
        if self.steps:
            got = after(self.got, *done)
            self.begin([halve_end(a, b) for a, b in zip(self.kept, got)])

    def finish(self, *done):
        while self.steps:
            self.advance(*done)
        return [a.astype(F32) + b.astype(F32) for a, b in zip(self.kept, after(self.got, *done))]


def steps_of(axis):
    return [(axis, 1 << i) for i in range(lax.axis_size(axis).bit_length() - 1)]


HALVINGS = PIECES.bit_length() - 1


def place_of(order):
    number = 0
    for axis, bit in order[:HALVINGS]:
        number = 2 * number + ((lax.axis_index(axis) // bit) & 1)
    return number


def sum_start(part, order, stage):
    if stage < HALVINGS:
        rows = part.shape[0] // 2
        return part[:rows], swap(part[rows:], *order[stage])
    return part, swap(part, *order[stage])


def spread(part, got):
    return jnp.concatenate([part, got], 0)


class Butterfly:
    def __init__(self, value):
        self.value = value
        self.steps = steps_of("tp") + steps_of("dp")
        self.got = None

    def start(self):
        if self.steps:
            self.got = swap(self.value, *self.steps.pop(0))
            return [self.got]
        return []

    def end(self, got):
        for g in got:
            self.value = self.value + g


def on_device(
    x_in, segments, w_qkv, w_out, mix_pre, mix_post, gain_attn, gain_ffn, w_in, w_down, cotangent
):
    rows, _, width = x_in.shape
    heads = mix_pre.shape[1]
    head_size = width // heads
    tp_size = lax.axis_size("tp")
    dp_size = lax.axis_size("dp")
    tp_index = lax.axis_index("tp")
    seg = segments[:, 0]
    side = rows // 2
    span = jnp.arange(side, dtype=jnp.int32)
    starts = [chunk_of(tp_index, x, tp_size, False) * side for x in range(2)]
    qpos = jnp.concatenate([start + span for start in starts])
    qseg = jnp.concatenate([lax.dynamic_slice_in_dim(seg, start, side, 0) for start in starts])
    qinfo = jnp.stack([qpos, qseg] + [qpos] * 6, 1)
    kinfo = jnp.pad(jnp.stack([jnp.arange(seg.shape[0], dtype=jnp.int32), seg]), ((0, 6), (0, 0)))
    where = (qinfo, kinfo, tp_index[None])

    def mirror(value):
        moved = lax.ppermute(value[side:], "tp", [(i, tp_size - 1 - i) for i in range(tp_size)])
        return value[:side], moved

    tab = jnp.concatenate([jnp.swapaxes(mix_pre, 1, 2) * (head_size**-0.5), mix_post], 1)
    tabt = jnp.pad(jnp.repeat(jnp.swapaxes(tab, 1, 2), head_size, axis=1), ((0, 0), (0, 0), (0, 128 - 2 * heads)))
    tab = jnp.repeat(tab, head_size, axis=2)

    stream = x_in[:, 0].astype(F32)
    x_folded = jnp.concatenate(mirror(x_in[:, 0]), 0).astype(F32)
    kept = []
    half = tp_size // 2
    for layer in range(LAYERS):
        last = layer == LAYERS - 1
        n1_blocks = gather_blocks(rms(stream, gain_attn[layer]).astype(BF16))
        if last:
            low, n1_blocks[half] = after((cotangent[:, 0], n1_blocks[half]))
            grad_near, grad_far = gather_near(low)
        else:
            stream = x_folded
        p, u, q, k, v, ot, n1t, middle, n2 = attn_fwd(
            layer,
            layer == 0,
            n1_blocks,
            stream,
            w_qkv,
            w_out,
            tab,
            gain_ffn,
            where,
        )
        if last:
            n2, grad_near, grad_far = after((n2, grad_near, grad_far))
        near, far = gather_near(n2)
        out_a, hid_a, dgelu_a = ffn_fwd(layer, near, w_in, w_down)
        if last:
            given = grad_near + gather_far(grad_far)
            gf_blocks = [jnp.concatenate([given[r][:side], given[tp_size - 1 - r][side:]], 0) for r in range(tp_size)]
            gn2_a, gpre_a = ffn_bwd(layer, gf_blocks[:half], dgelu_a, w_in, w_down)
            far, gpre_a = after((far, gpre_a))
        far, hid_a = after((far, hid_a))
        n2_blocks = near + gather_far(far)
        out_b, hid_b, dgelu_b = ffn_fwd(layer, n2_blocks[half:], w_in, w_down)
        kept.append((stream, n1t, p, u, q, k, v, ot, middle, n2_blocks, hid_a, hid_b, dgelu_a, dgelu_b))
        if not last:
            own, far = scatter_begin([*out_a, *out_b])
            stream = middle + (own + far.astype(F32))

    grad_flow = gf_blocks[0].astype(F32)
    per = width // dp_size
    small = [None] * LAYERS
    sharded = [None] * LAYERS
    for layer in range(LAYERS - 1, -1, -1):
        last = layer == LAYERS - 1
        stream, n1t, p, u, q, k, v, ot, middle, n2_blocks, hid_a, hid_b, dgelu_a, dgelu_b = kept[layer]
        if not last:
            near, far = gather_near(grad_flow.astype(BF16))
            gn2_a, gpre_a = ffn_bwd(layer, near, dgelu_a, w_in, w_down)
            far, gpre_a = after((far, gpre_a))
            gf_blocks = near + gather_far(far)
        gn2_b, gpre_b = ffn_bwd(layer, gf_blocks[half:], dgelu_b, w_in, w_down)
        if not last:
            total_got, gpre_b = after((total_got, gpre_b))
            total = halve_end(total_kept, total_got)
            total_kept, total_got = sum_start(total, total_order, 1)
        own, far = scatter_begin([*gn2_a, *gn2_b])
        packed = ffn_grads(n2_blocks, gf_blocks, (hid_a, hid_b), (gpre_a, gpre_b), dp_size)
        far, packed = after((far, packed))
        if not last:
            total_got, packed = after((total_got, packed))
            total = halve_end(total_kept, total_got)
            total_kept, total_got = sum_start(total, total_order, 2)
        if not last:
            previous = moving
        moving = Scatter([packed], steps_of("dp"))
        gn2 = (own + far.astype(F32)).astype(BF16).astype(F32)
        grad_norm, grad_gffn = rms_back(gn2, middle, gain_ffn[layer])
        grad_middle = grad_flow + grad_norm
        ga = grad_middle.astype(BF16)
        if last:
            orders = [steps_of("dp") + steps_of("tp")[1:]]
        else:
            (y_step, *dp_rest), x_steps = steps_of("dp"), steps_of("tp")[1:]
            orders = [x_steps + [y_step] + dp_rest, [y_step] + x_steps + dp_rest]
        place = jnp.stack([tp_index & 1] + [place_of(order) for order in orders] + [tp_index])
        parts, grads, zpre, zpost = attn_bwd(
            layer, tp_size, ga, w_out, q, k, v, p, u, tab, tabt, place, w_qkv, n1t, ot
        )
        core_step = steps_of("tp")[0]
        if last:
            parts, grads, moving.got = after((parts, grads, moving.got))
            y_middle = middle
            keep, send = grads
            total = halve_end(keep, swap(send, *core_step))
            own, far = scatter_begin(parts)
            moving.advance()
            far, moving.got = after((far, moving.got), total)
            moving.advance()
            (total_order,), total_place = orders, place
            total_kept, total_got = sum_start(total, total_order, 0)
        else:
            parts, grads, moving.got, total_got, previous.got = after(
                (parts, grads, moving.got, total_got, previous.got)
            )
            (summed,) = previous.finish()
            sharded[layer + 1] = (summed[:per], summed[per:].T)
        if not last:
            break
        gn1 = (own + far.astype(F32)).astype(BF16).astype(F32)
        grad_norm, grad_gattn = rms_back(gn1, stream, gain_attn[layer])
        grad_flow = grad_middle + grad_norm
        grad_mpre = jnp.sum(zpre.reshape(heads, heads, head_size), -1).T * (head_size**-0.5)
        grad_mpost = jnp.sum(zpost.reshape(heads, heads, head_size), -1)
        small[layer] = (grad_mpre, grad_mpost, grad_gattn, grad_gffn)

    total = halve_end(total_kept, total_got)
    grads, total = after((grads, total))
    got = [swap(send, *core_step) for send in grads[1::2]]
    pieces = [halve_end(keep, g) for keep, g in zip(grads[::2], got)]
    for stage in range(HALVINGS, len(total_order)):
        total_got = swap(total, *total_order[stage])
        pieces, total_got = after((pieces, total_got))
        total = halve_end(total, total_got)
    for stage in range(HALVINGS):
        kept, got = zip(*[sum_start(part, order, stage) for part, order in zip(pieces, orders)])
        total_got = swap(total, *total_order[HALVINGS - 1 - stage])
        if stage < HALVINGS - 1:
            got, total_got = after((got, total_got))
            total = spread(total, total_got)
        if stage == HALVINGS - 1:
            got, far = after((got, far))
        pieces = [halve_end(a, b) for a, b in zip(kept, after(got))]
        if stage == HALVINGS - 1:
            gn1 = (own + far.astype(F32)).astype(BF16).astype(F32)
            grad_norm, grad_gattn = rms_back(gn1, stream, gain_attn[layer])
            grad_flow = grad_middle + grad_norm
            grad_mpre = jnp.sum(zpre.reshape(heads, heads, head_size), -1).T * (head_size**-0.5)
            grad_mpost = jnp.sum(zpost.reshape(heads, heads, head_size), -1)
            small[layer] = (grad_mpre, grad_mpost, grad_gattn, grad_gffn)
            mixes = jnp.concatenate([a.reshape(-1) for s in small for a in s[:2]])
            count = mixes.shape[0]
            mix_rows = -(-count // width)
            flat = jnp.concatenate(
                [jnp.pad(mixes, (0, mix_rows * width - count)).reshape(mix_rows, width)]
                + [g[None] for s in small for g in s[2:]]
            )
            flat = jnp.pad(flat, ((0, -flat.shape[0] % 8), (0, 0)))
            flat = Butterfly(flat)
        if stage == 1:
            moving.advance(*pieces)
            y_parts, parts, pieces = after(([*out_a, *out_b], parts, pieces))
            own, far = scatter_begin(parts)
            own_y, far_y = scatter_begin(y_parts)
    for stage in range(HALVINGS, len(orders[0])):
        got = [swap(part, *order[stage]) for part, order in zip(pieces, orders)]
        if stage == HALVINGS:
            flat.end(flat.start())
        flat_got = flat.start()
        if stage == HALVINGS:
            first_rows, second_rows = mirror(grad_flow)
            got, second_rows, total_got, moving.got, far_y = after((got, second_rows, total_got, moving.got, far_y))
            y_out = (y_middle + (own_y + far_y.astype(F32))).astype(BF16)
            y_first, y_second = mirror(y_out)
            grad_x = jnp.concatenate([first_rows, second_rows], 0)
            total = spread(total, total_got)
            moving.advance()
        got, flat_got = after((got, flat_got))
        flat.end(flat_got)
        pieces = [halve_end(a, b) for a, b in zip(pieces, got)]
    total_other = swap(total, *core_step)
    replicated = ()
    for stage in range(HALVINGS - 1, -1, -1):
        got = [swap(part, *order[stage]) for part, order in zip(pieces, orders)]
        flat_got = flat.start()
        if stage == HALVINGS - 1:
            got, total_other = after((got, total_other))
        elif stage == HALVINGS - 2:
            replicated = expand(1, 0, total_place, [total])
            got, replicated, moving.got, y_second = after((got, replicated, moving.got, y_second))
            y_out = jnp.concatenate([y_first, y_second], 0)
        elif stage == 0:
            replicated = expand(1, 1, total_place, [total_other], replicated)
            got, replicated = after((got, replicated))
        got, flat_got = after((got, flat_got))
        flat.end(flat_got)
        pieces = [spread(a, b) for a, b in zip(pieces, got)]
    got = [swap(part, *core_step) for part in pieces]
    while flat.steps:
        flat.end(flat.start())
    flat = flat.value
    (summed,) = moving.finish()
    sharded[0] = (summed[:per], summed[per:].T)
    replicated = expand(0, 0, place, pieces, replicated)
    got, replicated, sharded = after((got, replicated, sharded))
    replicated = expand(0, 1, place, got, replicated)
    mixes = flat[:mix_rows].reshape(-1)[:count].reshape(LAYERS, 2, heads, heads)
    gains = flat[mix_rows : mix_rows + 2 * LAYERS].reshape(LAYERS, 2, width)
    return (
        y_out[:, None],
        grad_x[:, None],
        *replicated,
        mixes[:, 0],
        mixes[:, 1],
        gains[:, 0],
        gains[:, 1],
        jnp.stack([s[0] for s in sharded]),
        jnp.stack([s[1] for s in sharded]),
    )


def solution(mesh):
    in_specs = (
        P("tp", "dp", None),
        P(None, "dp"),
        P(),
        P(),
        P(),
        P(),
        P(),
        P(),
        P(None, None, "tp"),
        P(None, "tp", None),
        P("tp", "dp", None),
    )
    out_specs = (
        P("tp", "dp", None),
        P("tp", "dp", None),
        P(),
        P(),
        P(),
        P(),
        P(),
        P(),
        P(None, "dp", "tp"),
        P(None, "tp", "dp"),
    )
    return jax.shard_map(
        on_device, mesh=mesh, in_specs=in_specs, out_specs=out_specs, check_vma=False
    )
```

```python
import functools

import jax
import jax.numpy as jnp
from jax import lax
from jax.experimental import pallas as pl
from jax.experimental.pallas import tpu as pltpu
from jax.sharding import PartitionSpec as P

LAYERS = 2
EPSILON = 1e-06
NEGATIVE = -1e30
LOG2E = 1.4426950408889634
GROUPS = 4
PIECES = 8
GP = 4
GB = 4
VMEM = 60 * 1024 * 1024
SMALL = 18 * 1024 * 1024
F32 = jnp.float32
BF16 = jnp.bfloat16


def dot_nn(a, b):
    return lax.dot_general(a, b, (((1,), (0,)), ((), ())), preferred_element_type=F32)


def dot_nt(a, b):
    return lax.dot_general(a, b, (((1,), (1,)), ((), ())), preferred_element_type=F32)


def dot_tn(a, b):
    return lax.dot_general(a, b, (((0,), (0,)), ((), ())), preferred_element_type=F32)


def rms(values, gain):
    return values * lax.rsqrt(jnp.mean(values * values, -1, keepdims=True) + EPSILON) * gain


def rms_back(grad, values, gain):
    inv = lax.rsqrt(jnp.mean(values * values, -1, keepdims=True) + EPSILON)
    unit = values * inv
    scaled = grad * gain
    grad_values = (scaled - unit * jnp.mean(scaled * unit, -1, keepdims=True)) * inv
    return grad_values, jnp.sum(grad * unit, axis=0)


def whole(shape):
    return pl.BlockSpec(shape, lambda *_: (0,) * len(shape))


def layer_of(array, layer):
    shape = array.shape[1:]
    return pl.BlockSpec((1,) + shape, lambda *_: (layer,) + (0,) * len(shape))


def attn_fwd_body(blocks, heads, layer, plain, *refs):
    n_refs = refs[:blocks]
    x_hbm, wqkv_hbm, wout_hbm, tab_ref, gain_ref, qinfo_ref, kinfo_ref, at_ref = refs[blocks : blocks + 8]
    p_ref, u_ref, q_ref, k_hbm, v_hbm, ot_ref, n1t_hbm, xm_ref, n2_ref = refs[blocks + 8 : blocks + 17]
    bias_ref, acc_ref, k_ref, v_ref, n1t_ref, x_ref, wqkv_ref, wout_ref, sems = refs[blocks + 17 :]
    step = pl.program_id(0)
    rows, width = x_ref.shape
    q_cols, k_cols, v_cols = [slice(i * width, (i + 1) * width) for i in range(3)]
    weights = [
        pltpu.make_async_copy(wqkv_hbm.at[layer, :, cols], wqkv_ref.at[i], sems.at[i])
        for i, cols in enumerate((k_cols, v_cols, q_cols))
    ]
    last_used = [
        pltpu.make_async_copy(wout_hbm.at[layer], wout_ref, sems.at[3]),
        pltpu.make_async_copy(x_hbm, x_ref, sems.at[4]),
    ]
    early = [
        pltpu.make_async_copy(k_ref, k_hbm, sems.at[5]),
        pltpu.make_async_copy(v_ref, v_hbm, sems.at[6]),
    ]
    turned = pltpu.make_async_copy(n1t_ref, n1t_hbm, sems.at[7])
    half = rows // 2
    at = at_ref[0]

    def place(r, second):
        block = chunk_of(at ^ r, second, blocks, plain)
        return pl.ds(pl.multiple_of(block * half, half), half)

    @pl.when(step == 0)
    def _():
        for copy in weights + last_used:
            copy.start()
        for i, ref in enumerate((k_ref, v_ref)):
            weights[i].wait()
            for r in range(blocks):
                value = dot_nn(n_refs[r][...], wqkv_ref[i]).astype(BF16)
                ref[place(r, 0), :] = value[:half]
                ref[place(r, 1), :] = value[half:]
            early[i].start()
        weights[2].wait()
        n_second = n_refs[blocks - 1 if plain else 0]
        q_ref[:half] = dot_nn(n_refs[0][:half], wqkv_ref[2]).astype(BF16)
        q_ref[half:] = dot_nn(n_second[half:], wqkv_ref[2]).astype(BF16)
        ok = (qinfo_ref[:, 1:2] == kinfo_ref[1:2, :]) & (kinfo_ref[0:1, :] <= qinfo_ref[:, 0:1])
        bias_ref[...] = jnp.where(ok, 0.0, NEGATIVE)
        acc_ref[...] = jnp.zeros_like(acc_ref)

    def work(second, keys):
        here = pl.ds(pl.multiple_of(second * half, half), half)
        q = q_ref[here, :].astype(F32)
        gs = [step * GP + u for u in range(GP)]
        qm = jnp.concatenate([(q * (tab_ref[0, pl.ds(g, 1), :] * LOG2E)).astype(BF16) for g in gs], 0)
        m = dot_nt(qm, k_ref[:keys, :])
        bias = bias_ref[here, :keys]
        ps = []
        for u in range(GP):
            mu = m[u * half : (u + 1) * half] + bias
            e = jnp.exp2(mu - jnp.max(mu, -1, keepdims=True))
            p = (e * (1.0 / jnp.sum(e, -1, keepdims=True))).astype(BF16)
            p_ref[u, here, :keys] = p
            ps.append(p)
        ctx = dot_nn(jnp.concatenate(ps, 0), v_ref[:keys, :])
        total = acc_ref[here, :]
        for u in range(GP):
            cu = ctx[u * half : (u + 1) * half]
            u_ref[u, here, :] = cu.astype(BF16)
            total = total + cu * tab_ref[0, pl.ds(heads + gs[u], 1), :]
        acc_ref[here, :] = total

    for pairs in range(1, blocks + 1):
        late = at == blocks - pairs

        @pl.when(late | (at == pairs - 1))
        def _(pairs=pairs, late=late):
            work(late.astype(jnp.int32), 2 * pairs * half)

    @pl.when(step == 0)
    def _():
        for r in range(blocks):
            for second in range(2):
                n1t_ref[:, place(r, second)] = n_refs[r][second * half : (second + 1) * half, :].T
        turned.start()

    @pl.when(step == pl.num_programs(0) - 1)
    def _():
        o = acc_ref[...].astype(BF16)
        ot_ref[...] = o.T
        for copy in last_used + early + [turned]:
            copy.wait()
        xm = x_ref[...] + dot_nn(o, wout_ref[...])
        xm_ref[...] = xm
        n2_ref[...] = rms(xm, gain_ref[pl.ds(layer, 1), :]).astype(BF16)


def chunk_of(device, second, devices, plain):
    if not second:
        return 2 * device
    return 2 * device + 1 if plain else 2 * (devices - 1 - device) + 1


def attn_fwd(layer, plain, n_blocks, x, w_qkv, w_out, tab, gain, where):
    rows, width = x.shape
    blocks = len(n_blocks)
    heads = tab.shape[1] // 2
    keys = rows * blocks
    args = (*n_blocks, x, w_qkv, w_out, tab, gain, *where)
    in_specs = [whole(a.shape) for a in args]
    in_specs[blocks : blocks + 3] = [pl.BlockSpec(memory_space=pl.ANY)] * 3
    in_specs[blocks + 3] = layer_of(tab, layer)
    in_specs[-1] = pl.BlockSpec(memory_space=pltpu.SMEM)
    out = [
        ((heads, rows, keys), BF16),
        ((heads, rows, width), BF16),
        ((rows, width), BF16),
        ((keys, width), BF16),
        ((keys, width), BF16),
        ((width, rows), BF16),
        ((width, keys), BF16),
        ((rows, width), F32),
        ((rows, width), BF16),
    ]
    out_specs = [whole(s) for s, _ in out]
    out_specs[0] = pl.BlockSpec((GP, rows, keys), lambda i: (i, 0, 0))
    out_specs[1] = pl.BlockSpec((GP, rows, width), lambda i: (i, 0, 0))
    for i in (3, 4, 6):
        out_specs[i] = pl.BlockSpec(memory_space=pltpu.HBM)
    return pl.pallas_call(
        functools.partial(attn_fwd_body, blocks, heads, layer, plain),
        grid=(heads // GP,),
        in_specs=in_specs,
        out_specs=out_specs,
        out_shape=[jax.ShapeDtypeStruct(s, d) for s, d in out],
        scratch_shapes=[
            pltpu.VMEM((rows, keys), F32),
            pltpu.VMEM((rows, width), F32),
            pltpu.VMEM((keys, width), BF16),
            pltpu.VMEM((keys, width), BF16),
            pltpu.VMEM((width, keys), BF16),
            pltpu.VMEM((rows, width), F32),
            pltpu.VMEM((3, width, width), BF16),
            pltpu.VMEM((width, width), BF16),
            pltpu.SemaphoreType.DMA((8,)),
        ],
        compiler_params=pltpu.CompilerParams(vmem_limit_bytes=VMEM),
        cost_estimate=pl.CostEstimate(
            flops=2 * rows * keys * width * heads * 2, bytes_accessed=20_000_000, transcendentals=rows * keys * heads
        ),
        name="attn_fwd",
    )(*args)


def attn_bwd_body(heads, blocks, layer, parts, *refs):
    (ga_ref, wout_ref, q_ref, k_ref, v_ref, p_ref, u_ref, tab_ref, tabt_ref, place_ref) = refs[:10]
    wqkv_hbm, n1t_hbm, ot_hbm = refs[10:13]
    gn1_refs = refs[13 : 13 + blocks]
    grad_refs = refs[13 + blocks : 13 + blocks + 2 * parts]
    zpre_ref, zpost_ref = refs[13 + blocks + 2 * parts : 15 + blocks + 2 * parts]
    go_ref, got_ref, qt_ref, gq_acc, gk_acc, gv_acc, wqkv_ref, n1t_ref, ot_ref, sems = refs[15 + blocks + 2 * parts :]
    step = pl.program_id(0)
    rows, width = q_ref.shape

    late = [
        pltpu.make_async_copy(wqkv_hbm.at[layer], wqkv_ref, sems.at[0]),
        pltpu.make_async_copy(n1t_hbm, n1t_ref, sems.at[1]),
        pltpu.make_async_copy(ot_hbm, ot_ref, sems.at[2]),
    ]

    @pl.when(step == 0)
    def _():
        for copy in late:
            copy.start()
        go = dot_nt(ga_ref[...], wout_ref[0]).astype(BF16).astype(F32)
        go_ref[...] = go
        got_ref[...] = go.T
        qt_ref[...] = q_ref[...].astype(F32).T
        gq_acc[...] = jnp.zeros_like(gq_acc)
        gk_acc[...] = jnp.zeros_like(gk_acc)
        gv_acc[...] = jnp.zeros_like(gv_acc)
        zpre_ref[...] = jnp.zeros_like(zpre_ref)
        zpost_ref[...] = jnp.zeros_like(zpost_ref)

    half = rows // 2
    at = place_ref[1 + parts]
    lane = lax.broadcasted_iota(jnp.int32, tabt_ref.shape[1:], 1)
    gs = [step * GB + u for u in range(GB)]
    cols = []
    for g in gs:
        pre_col = jnp.sum(jnp.where(lane == g, tabt_ref[0], 0.0), 1, keepdims=True)
        post_col = jnp.sum(jnp.where(lane == heads + g, tabt_ref[0], 0.0), 1, keepdims=True)
        cols.append((pre_col, post_col))

    def work(second, keys):
        here = pl.ds(pl.multiple_of(second * half, half), half)
        go = go_ref[here, :]
        q = q_ref[here, :].astype(F32)
        mixed = [go * tab_ref[0, pl.ds(heads + g, 1), :] for g in gs]
        gp = dot_nt(jnp.concatenate([x.astype(BF16) for x in mixed], 0), v_ref[:keys, :])
        gms, ps, zposts = [], [], []
        for u in range(GB):
            ctx = u_ref[u, here, :].astype(F32)
            zposts.append(jnp.sum(ctx * go, axis=0, keepdims=True))
            delta = jnp.sum(ctx * mixed[u], axis=1, keepdims=True)
            p = p_ref[u, here, :keys]
            gms.append((p.astype(F32) * (gp[u * half : (u + 1) * half] - delta)).astype(BF16))
            ps.append(p)
        gm = jnp.concatenate(gms, 0)
        t = dot_nn(gm, k_ref[:keys, :])
        total = gq_acc[here, :]
        zpres = []
        for u in range(GB):
            tu = t[u * half : (u + 1) * half]
            zpres.append(jnp.sum(tu * q, axis=0, keepdims=True))
            total = total + tu * tab_ref[0, pl.ds(gs[u], 1), :]
        gq_acc[here, :] = total
        qm = jnp.concatenate([(qt_ref[:, here] * pre).astype(BF16) for pre, _ in cols], 1)
        gk_acc[:, :keys] += dot_nn(qm, gm)
        gm2 = jnp.concatenate([(got_ref[:, here] * post).astype(BF16) for _, post in cols], 1)
        gv_acc[:, :keys] += dot_nn(gm2, jnp.concatenate(ps, 0))
        return zpres, zposts

    for pairs in range(1, blocks + 1):
        is_late = at == blocks - pairs

        @pl.when(is_late | (at == pairs - 1))
        def _(pairs=pairs, is_late=is_late):
            zpres, zposts = work(is_late.astype(jnp.int32), 2 * pairs * half)
            for u, g in enumerate(gs):
                zpre_ref[pl.ds(g, 1), :] += zpres[u]
                zpost_ref[pl.ds(g, 1), :] += zposts[u]

    @pl.when(step == pl.num_programs(0) - 1)
    def _():
        for copy in late:
            copy.wait()
        gq = gq_acc[...].astype(BF16)
        gkt = gk_acc[...].astype(BF16)
        gvt = gv_acc[...].astype(BF16)
        ga = ga_ref[...]
        for r in range(blocks):
            there = [pl.ds(pl.multiple_of(chunk_of(at ^ r, x, blocks, False) * half, half), half) for x in range(2)]
            gk = jnp.concatenate([gk_acc[:, x].T.astype(BF16) for x in there], 0)
            gv = jnp.concatenate([gv_acc[:, x].T.astype(BF16) for x in there], 0)
            gn1 = dot_nt(gk, wqkv_ref[:, width : 2 * width]) + dot_nt(gv, wqkv_ref[:, 2 * width :])
            if r == 0:
                gn1 = gn1 + dot_nt(gq, wqkv_ref[:, :width])
            gn1_refs[r][...] = gn1.astype(BF16)
        hand = width // 2
        per = hand // PIECES
        own = [pl.ds(pl.multiple_of(chunk_of(at, x, blocks, False) * half, half), half) for x in range(2)]
        for side in range(2):
            core = place_ref[0] if side == 0 else 1 - place_ref[0]
            mine = pl.ds(pl.multiple_of(core * hand, hand), hand)
            n1t = n1t_ref[mine, :]
            n1t_own = jnp.concatenate([n1t_ref[mine, x] for x in own], 1)
            grads = (
                lambda: dot_nn(n1t_own, gq),
                lambda: dot_nt(n1t, gkt),
                lambda: dot_nt(n1t, gvt),
                lambda: dot_nn(ot_ref[mine, :], ga),
            )
            for index, grad in enumerate(grads):
                part = index * parts // len(grads)
                column = (index - part * (len(grads) // parts)) * width
                value = grad().astype(BF16)
                for piece in range(PIECES):
                    there = pl.multiple_of((piece ^ place_ref[1 + part]) * per, per)
                    grad_refs[2 * part + side][pl.ds(there, per), column : column + width] = value[
                        piece * per : (piece + 1) * per
                    ]


def attn_bwd(layer, blocks, ga, w_out, q, k, v, p, u, tab, tabt, place, w_qkv, n1t, ot):
    rows, width = q.shape
    keys = k.shape[0]
    heads = p.shape[0]
    parts = place.shape[0] - 2
    args = (ga, w_out, q, k, v, p, u, tab, tabt, place, w_qkv, n1t, ot)
    in_specs = [whole(a.shape) for a in args]
    in_specs[1] = layer_of(w_out, layer)
    in_specs[5] = pl.BlockSpec((GB, rows, keys), lambda i: (i, 0, 0))
    in_specs[6] = pl.BlockSpec((GB, rows, width), lambda i: (i, 0, 0))
    in_specs[7] = layer_of(tab, layer)
    in_specs[8] = layer_of(tabt, layer)
    in_specs[9] = pl.BlockSpec(memory_space=pltpu.SMEM)
    in_specs[10:13] = [pl.BlockSpec(memory_space=pl.ANY)] * 3
    out = (
        [((rows, width), BF16)] * blocks
        + [((width // 2, 4 // parts * width), BF16)] * (2 * parts)
        + [((heads, width), F32)] * 2
    )
    res = pl.pallas_call(
        functools.partial(attn_bwd_body, heads, blocks, layer, parts),
        grid=(heads // GB,),
        in_specs=in_specs,
        out_specs=[whole(s) for s, _ in out],
        out_shape=[jax.ShapeDtypeStruct(s, d) for s, d in out],
        scratch_shapes=[
            pltpu.VMEM((rows, width), F32),
            pltpu.VMEM((width, rows), F32),
            pltpu.VMEM((width, rows), F32),
            pltpu.VMEM((rows, width), F32),
            pltpu.VMEM((width, keys), F32),
            pltpu.VMEM((width, keys), F32),
            pltpu.VMEM(w_qkv.shape[1:], BF16),
            pltpu.VMEM(n1t.shape, BF16),
            pltpu.VMEM(ot.shape, BF16),
            pltpu.SemaphoreType.DMA((3,)),
        ],
        compiler_params=pltpu.CompilerParams(vmem_limit_bytes=VMEM),
        cost_estimate=pl.CostEstimate(
            flops=2 * rows * keys * width * heads * 4 * 2, bytes_accessed=20_000_000, transcendentals=0
        ),
        name="attn_bwd",
    )(*args)
    return res[:blocks], res[blocks:-2], res[-2], res[-1]


def expand_body(parts, place_ref, *refs):
    qkv_ref, out_ref = refs[-2:]
    width3 = qkv_ref.shape[2]
    inner = PIECES // GROUPS
    per = qkv_ref.shape[1] // inner
    column = 0
    for part, ref in enumerate(refs[:parts]):
        end = column + ref.shape[1]
        cut = min(end, width3)
        for piece in range(inner):
            here = slice(piece * per, (piece + 1) * per)
            there = piece ^ lax.rem(place_ref[1 + part], inner)
            value = ref[pl.ds(pl.multiple_of(there * per, per), per), :].astype(F32)
            qkv_ref[0, here, column:cut] = value[:, : cut - column]
            if end > width3:
                out_ref[0, here, :] = value[:, cut - column :]
        column = end


def expand(layer, side, place, halves, before=()):
    half = halves[0].shape[0]
    width = sum(h.shape[1] for h in halves) // 4
    per = half // GROUPS
    in_specs = []
    for part, array in enumerate(halves):

        def piece(i, place, part=part):
            return i ^ (place[1 + part] // (PIECES // GROUPS)), 0

        in_specs.append(pl.BlockSpec((per, array.shape[1]), piece))
    first = 1 + len(halves)
    in_specs += [pl.BlockSpec(memory_space=pl.ANY)] * len(before)

    def there(i, place):
        return layer, (place[0] ^ side) * GROUPS + i, 0

    return pl.pallas_call(
        functools.partial(expand_body, len(halves)),
        grid_spec=pltpu.PrefetchScalarGridSpec(
            num_scalar_prefetch=1,
            grid=(GROUPS,),
            in_specs=in_specs,
            out_specs=[pl.BlockSpec((1, per, 3 * width), there), pl.BlockSpec((1, per, width), there)],
        ),
        out_shape=[
            jax.ShapeDtypeStruct((LAYERS, 2 * half, 3 * width), F32),
            jax.ShapeDtypeStruct((LAYERS, 2 * half, width), F32),
        ],
        input_output_aliases={first + i: i for i in range(len(before))},
        compiler_params=pltpu.CompilerParams(vmem_limit_bytes=SMALL),
        cost_estimate=pl.CostEstimate(flops=0, bytes_accessed=7_000_000, transcendentals=0),
        name="expand",
    )(place, *halves, *before)


def ffn_fwd_body(blocks, *refs):
    n_refs = refs[:blocks]
    win_ref, wdown_ref = refs[blocks : blocks + 2]
    out_refs = refs[blocks + 2 : 2 * blocks + 2]
    hid_ref, dgelu_ref = refs[2 * blocks + 2 :]
    rows = n_refs[0].shape[0]
    for r in range(blocks):
        here = pl.ds(r * rows, rows)
        pre = dot_nn(n_refs[r][...], win_ref[0])
        cdf = 0.5 + 0.5 * lax.erf(pre * (0.5**0.5))
        hid = (pre * cdf).astype(BF16)
        hid_ref[here, :] = hid
        density = jnp.exp2(pre * pre * (-0.5 * LOG2E)) * 0.3989422804014327
        dgelu_ref[here, :] = (cdf + pre * density).astype(BF16)
        out_refs[r][...] = dot_nn(hid, wdown_ref[0]).astype(BF16)


def ffn_fwd(layer, n_blocks, w_in, w_down):
    blocks = len(n_blocks)
    rows, width = n_blocks[0].shape
    hidden = w_in.shape[2]
    args = (*n_blocks, w_in, w_down)
    in_specs = [whole(a.shape) for a in args]
    in_specs[blocks] = layer_of(w_in, layer)
    in_specs[blocks + 1] = layer_of(w_down, layer)
    out = [((rows, width), BF16)] * blocks + [((rows * blocks, hidden), BF16)] * 2
    res = pl.pallas_call(
        functools.partial(ffn_fwd_body, blocks),
        grid=(1,),
        in_specs=in_specs,
        out_specs=[whole(s) for s, _ in out],
        out_shape=[jax.ShapeDtypeStruct(s, d) for s, d in out],
        compiler_params=pltpu.CompilerParams(vmem_limit_bytes=SMALL),
        cost_estimate=pl.CostEstimate(
            flops=4 * rows * blocks * width * hidden, bytes_accessed=6_000_000, transcendentals=rows * blocks * hidden
        ),
        name="ffn_fwd",
    )(*args)
    return res[:blocks], res[blocks], res[blocks + 1]


def ffn_bwd_body(blocks, *refs):
    g_refs = refs[:blocks]
    dgelu_ref, win_ref, wdown_ref = refs[blocks : blocks + 3]
    out_refs = refs[blocks + 3 : 2 * blocks + 3]
    gpre_ref = refs[2 * blocks + 3]
    rows = g_refs[0].shape[0]
    for r in range(blocks):
        here = pl.ds(r * rows, rows)
        gh = dot_nt(g_refs[r][...], wdown_ref[0])
        gpre = (gh * dgelu_ref[here, :].astype(F32)).astype(BF16)
        gpre_ref[here, :] = gpre
        out_refs[r][...] = dot_nt(gpre, win_ref[0]).astype(BF16)


def ffn_bwd(layer, g_blocks, dgelu, w_in, w_down):
    blocks = len(g_blocks)
    rows, width = g_blocks[0].shape
    hidden = w_in.shape[2]
    args = (*g_blocks, dgelu, w_in, w_down)
    in_specs = [whole(a.shape) for a in args]
    in_specs[blocks + 1] = layer_of(w_in, layer)
    in_specs[blocks + 2] = layer_of(w_down, layer)
    out = [((rows, width), BF16)] * blocks + [((rows * blocks, hidden), BF16)]
    res = pl.pallas_call(
        functools.partial(ffn_bwd_body, blocks),
        grid=(1,),
        in_specs=in_specs,
        out_specs=[whole(s) for s, _ in out],
        out_shape=[jax.ShapeDtypeStruct(s, d) for s, d in out],
        compiler_params=pltpu.CompilerParams(vmem_limit_bytes=SMALL),
        cost_estimate=pl.CostEstimate(
            flops=4 * rows * blocks * width * hidden, bytes_accessed=6_000_000, transcendentals=0
        ),
        name="ffn_bwd",
    )(*args)
    return res[:blocks], res[blocks]


def ffn_grads_body(blocks, chunks, *refs):
    n_refs, g_refs = refs[:blocks], refs[blocks : 2 * blocks]
    hid_refs, gpre_refs = refs[2 * blocks : 2 * blocks + 2], refs[2 * blocks + 2 : 2 * blocks + 4]
    out_ref = refs[-1]
    rows, width = n_refs[0].shape
    per = width // chunks
    for part, (left_refs, right_refs) in enumerate(((n_refs, gpre_refs), (g_refs, hid_refs))):
        left = jnp.concatenate([ref[...].T for ref in left_refs], 1)
        right = jnp.concatenate([ref[...] for ref in right_refs], 0)
        grad = dot_nn(left, right).astype(BF16)
        for c in range(chunks):
            place = 2 * sum(((c >> i) & 1) * (chunks >> (i + 1)) for i in range(chunks.bit_length() - 1)) + part
            out_ref[place * per : (place + 1) * per, :] = grad[c * per : (c + 1) * per]


def ffn_grads(n_blocks, g_blocks, hids, gpres, chunks):
    blocks = len(n_blocks)
    rows, width = n_blocks[0].shape
    hidden = hids[0].shape[1]
    args = (*n_blocks, *g_blocks, *hids, *gpres)
    return pl.pallas_call(
        functools.partial(ffn_grads_body, blocks, chunks),
        grid=(1,),
        in_specs=[whole(a.shape) for a in args],
        out_specs=whole((2 * width, hidden)),
        out_shape=jax.ShapeDtypeStruct((2 * width, hidden), BF16),
        compiler_params=pltpu.CompilerParams(vmem_limit_bytes=VMEM),
        cost_estimate=pl.CostEstimate(
            flops=4 * rows * blocks * width * hidden, bytes_accessed=9_000_000, transcendentals=0
        ),
        name="ffn_grads",
    )(*args)


def swap(value, axis, bit):
    size = lax.axis_size(axis)
    return lax.ppermute(value, axis, [(i, i ^ bit) for i in range(size)])


def after(values, *done):
    return lax.optimization_barrier((values, done))[0]


def gather_near(value):
    half = lax.axis_size("tp") // 2
    far = swap(value, "tp", half)
    near = [value]
    bit = 1
    while bit < half:
        near += [swap(b, "tp", bit) for b in near]
        bit *= 2
    return near, far


def gather_far(far):
    half = lax.axis_size("tp") // 2
    blocks = [far]
    bit = 1
    while bit < half:
        blocks += [swap(b, "tp", bit) for b in blocks]
        bit *= 2
    return blocks


def gather_blocks(value):
    near, far = gather_near(value)
    return near + gather_far(far)


def scatter_begin(blocks):
    blocks = list(blocks)
    bit = 1
    while bit < lax.axis_size("tp") // 2:
        size = len(blocks)
        keep = [blocks[r] for r in range(size) if not r & 1]
        sent = [swap(blocks[r], "tp", bit) for r in range(size) if r & 1]
        blocks = [a.astype(F32) + b.astype(F32) for a, b in zip(keep, sent)]
        bit *= 2
        blocks = [blocks[0]] + [b.astype(BF16) for b in blocks[1:]]
    return blocks[0].astype(F32), swap(blocks[1], "tp", bit)


def halve_begin(part, axis, bit):
    mine = (lax.axis_index(axis) // bit) & 1
    pair = part.reshape(2, part.shape[0] // 2, part.shape[1])
    sent = lax.dynamic_index_in_dim(pair, 1 - mine, 0, keepdims=False)
    kept = lax.dynamic_index_in_dim(pair, mine, 0, keepdims=False)
    return kept, swap(sent, axis, bit)


def halve_end(kept, got):
    return (kept.astype(F32) + got.astype(F32)).astype(BF16)


class Scatter:
    def __init__(self, parts, steps):
        self.steps = list(steps)
        self.begin(parts)

    def begin(self, parts):
        step = self.steps.pop(0)
        self.kept, self.got = zip(*[halve_begin(part, *step) for part in parts])

    def advance(self, *done):
        if self.steps:
            got = after(self.got, *done)
            self.begin([halve_end(a, b) for a, b in zip(self.kept, got)])

    def finish(self, *done):
        while self.steps:
            self.advance(*done)
        return [a.astype(F32) + b.astype(F32) for a, b in zip(self.kept, after(self.got, *done))]


def steps_of(axis):
    return [(axis, 1 << i) for i in range(lax.axis_size(axis).bit_length() - 1)]


HALVINGS = PIECES.bit_length() - 1


def place_of(order):
    number = 0
    for axis, bit in order[:HALVINGS]:
        number = 2 * number + ((lax.axis_index(axis) // bit) & 1)
    return number


def sum_start(part, order, stage):
    if stage < HALVINGS:
        rows = part.shape[0] // 2
        return part[:rows], swap(part[rows:], *order[stage])
    return part, swap(part, *order[stage])


def spread(part, got):
    return jnp.concatenate([part, got], 0)


class Butterfly:
    def __init__(self, value):
        self.value = value
        self.steps = steps_of("tp") + steps_of("dp")
        self.got = None

    def start(self):
        if self.steps:
            self.got = swap(self.value, *self.steps.pop(0))
            return [self.got]
        return []

    def end(self, got):
        for g in got:
            self.value = self.value + g


def on_device(
    x_in, segments, w_qkv, w_out, mix_pre, mix_post, gain_attn, gain_ffn, w_in, w_down, cotangent
):
    rows, _, width = x_in.shape
    heads = mix_pre.shape[1]
    head_size = width // heads
    tp_size = lax.axis_size("tp")
    dp_size = lax.axis_size("dp")
    tp_index = lax.axis_index("tp")
    seg = segments[:, 0]
    side = rows // 2
    span = jnp.arange(side, dtype=jnp.int32)
    starts = [chunk_of(tp_index, x, tp_size, False) * side for x in range(2)]
    qpos = jnp.concatenate([start + span for start in starts])
    qseg = jnp.concatenate([lax.dynamic_slice_in_dim(seg, start, side, 0) for start in starts])
    qinfo = jnp.stack([qpos, qseg] + [qpos] * 6, 1)
    kinfo = jnp.pad(jnp.stack([jnp.arange(seg.shape[0], dtype=jnp.int32), seg]), ((0, 6), (0, 0)))
    where = (qinfo, kinfo, tp_index[None])

    def mirror(value):
        moved = lax.ppermute(value[side:], "tp", [(i, tp_size - 1 - i) for i in range(tp_size)])
        return value[:side], moved

    tab = jnp.concatenate([jnp.swapaxes(mix_pre, 1, 2) * (head_size**-0.5), mix_post], 1)
    tabt = jnp.pad(jnp.repeat(jnp.swapaxes(tab, 1, 2), head_size, axis=1), ((0, 0), (0, 0), (0, 128 - 2 * heads)))
    tab = jnp.repeat(tab, head_size, axis=2)

    stream = x_in[:, 0].astype(F32)
    x_folded = jnp.concatenate(mirror(x_in[:, 0]), 0).astype(F32)
    kept = []
    half = tp_size // 2
    for layer in range(LAYERS):
        last = layer == LAYERS - 1
        n1_blocks = gather_blocks(rms(stream, gain_attn[layer]).astype(BF16))
        if last:
            low, n1_blocks[half] = after((cotangent[:, 0], n1_blocks[half]))
            grad_near, grad_far = gather_near(low)
        else:
            stream = x_folded
        p, u, q, k, v, ot, n1t, middle, n2 = attn_fwd(
            layer,
            layer == 0,
            n1_blocks,
            stream,
            w_qkv,
            w_out,
            tab,
            gain_ffn,
            where,
        )
        if last:
            n2, grad_near, grad_far = after((n2, grad_near, grad_far))
        near, far = gather_near(n2)
        out_a, hid_a, dgelu_a = ffn_fwd(layer, near, w_in, w_down)
        if last:
            given = grad_near + gather_far(grad_far)
            gf_blocks = [jnp.concatenate([given[r][:side], given[tp_size - 1 - r][side:]], 0) for r in range(tp_size)]
            gn2_a, gpre_a = ffn_bwd(layer, gf_blocks[:half], dgelu_a, w_in, w_down)
            far, gpre_a = after((far, gpre_a))
        far, hid_a = after((far, hid_a))
        n2_blocks = near + gather_far(far)
        out_b, hid_b, dgelu_b = ffn_fwd(layer, n2_blocks[half:], w_in, w_down)
        kept.append((stream, n1t, p, u, q, k, v, ot, middle, n2_blocks, hid_a, hid_b, dgelu_a, dgelu_b))
        if not last:
            own, far = scatter_begin([*out_a, *out_b])
            stream = middle + (own + far.astype(F32))

    grad_flow = gf_blocks[0].astype(F32)
    per = width // dp_size
    small = [None] * LAYERS
    sharded = [None] * LAYERS
    for layer in range(LAYERS - 1, -1, -1):
        last = layer == LAYERS - 1
        stream, n1t, p, u, q, k, v, ot, middle, n2_blocks, hid_a, hid_b, dgelu_a, dgelu_b = kept[layer]
        if not last:
            near, far = gather_near(grad_flow.astype(BF16))
            gn2_a, gpre_a = ffn_bwd(layer, near, dgelu_a, w_in, w_down)
            far, gpre_a, total_second = after((far, gpre_a, total_second))
            gf_blocks = near + gather_far(far)
        gn2_b, gpre_b = ffn_bwd(layer, gf_blocks[half:], dgelu_b, w_in, w_down)
        if not last:
            total_third, gpre_b = after((total_third, gpre_b))
            total = halve_end(total_kept, jnp.concatenate([total_first, total_second, total_third], 0))
            total_kept, total_got = sum_start(total, total_order, 1)
        own, far = scatter_begin([*gn2_a, *gn2_b])
        packed = ffn_grads(n2_blocks, gf_blocks, (hid_a, hid_b), (gpre_a, gpre_b), dp_size)
        far, packed = after((far, packed))
        if not last:
            total_got, packed = after((total_got, packed))
            total = halve_end(total_kept, total_got)
            total_kept, total_got = sum_start(total, total_order, 2)
        if not last:
            previous = moving
        moving = Scatter([packed], steps_of("dp"))
        gn2 = (own + far.astype(F32)).astype(BF16).astype(F32)
        grad_norm, grad_gffn = rms_back(gn2, middle, gain_ffn[layer])
        grad_middle = grad_flow + grad_norm
        ga = grad_middle.astype(BF16)
        if last:
            orders = [steps_of("dp") + steps_of("tp")[1:]]
        else:
            (y_step, *dp_rest), x_steps = steps_of("dp"), steps_of("tp")[1:]
            orders = [x_steps + [y_step] + dp_rest, [y_step] + x_steps + dp_rest]
        place = jnp.stack([tp_index & 1] + [place_of(order) for order in orders] + [tp_index])
        parts, grads, zpre, zpost = attn_bwd(
            layer, tp_size, ga, w_out, q, k, v, p, u, tab, tabt, place, w_qkv, n1t, ot
        )
        core_step = steps_of("tp")[0]
        if last:
            parts, grads, moving.got = after((parts, grads, moving.got))
            y_middle = middle
            keep, send = grads
            total = halve_end(keep, swap(send, *core_step))
            own, far = scatter_begin(parts)
            moving.advance()
            total_kept, rest = jnp.split(total, 2)
            cuts = [0, rest.shape[0] // 4, rest.shape[0] * 5 // 8, rest.shape[0]]
            total_first, total_second, total_third = [
                swap(rest[a:b], *orders[0][0]) for a, b in zip(cuts, cuts[1:])
            ]
            far, moving.got, total_first = after((far, moving.got, total_first), total)
            moving.advance()
            (total_order,), total_place = orders, place
        else:
            parts, grads, moving.got, total_got, previous.got = after(
                (parts, grads, moving.got, total_got, previous.got)
            )
            (summed,) = previous.finish()
            sharded[layer + 1] = (summed[:per], summed[per:].T)
        if not last:
            break
        gn1 = (own + far.astype(F32)).astype(BF16).astype(F32)
        grad_norm, grad_gattn = rms_back(gn1, stream, gain_attn[layer])
        grad_flow = grad_middle + grad_norm
        grad_mpre = jnp.sum(zpre.reshape(heads, heads, head_size), -1).T * (head_size**-0.5)
        grad_mpost = jnp.sum(zpost.reshape(heads, heads, head_size), -1)
        small[layer] = (grad_mpre, grad_mpost, grad_gattn, grad_gffn)

    total = halve_end(total_kept, total_got)
    grads, total = after((grads, total))
    got = [swap(send, *core_step) for send in grads[1::2]]
    pieces = [halve_end(keep, g) for keep, g in zip(grads[::2], got)]
    for stage in range(HALVINGS, len(total_order)):
        total_got = swap(total, *total_order[stage])
        pieces, total_got = after((pieces, total_got))
        total = halve_end(total, total_got)
    for stage in range(HALVINGS):
        kept, got = zip(*[sum_start(part, order, stage) for part, order in zip(pieces, orders)])
        if stage == 0:
            by_last, by_middle = [swap(total, *step) for step in total_order[HALVINGS - 1 : 0 : -1]]
            got, by_last, by_middle = after((got, by_last, by_middle))
            near_rows = spread(total, by_last)
        elif stage == 1:
            near_got = swap(near_rows, *total_order[0])
            by_both = swap(by_last, *total_order[1])
            got, by_both = after((got, by_both))
            far_rows = spread(by_middle, by_both)
        else:
            total_got = swap(far_rows, *total_order[0])
            got, near_got = after((got, near_got))
        if stage == HALVINGS - 1:
            got, far = after((got, far))
        pieces = [halve_end(a, b) for a, b in zip(kept, after(got))]
        if stage == HALVINGS - 1:
            gn1 = (own + far.astype(F32)).astype(BF16).astype(F32)
            grad_norm, grad_gattn = rms_back(gn1, stream, gain_attn[layer])
            grad_flow = grad_middle + grad_norm
            grad_mpre = jnp.sum(zpre.reshape(heads, heads, head_size), -1).T * (head_size**-0.5)
            grad_mpost = jnp.sum(zpost.reshape(heads, heads, head_size), -1)
            small[layer] = (grad_mpre, grad_mpost, grad_gattn, grad_gffn)
            mixes = jnp.concatenate([a.reshape(-1) for s in small for a in s[:2]])
            count = mixes.shape[0]
            mix_rows = -(-count // width)
            flat = jnp.concatenate(
                [jnp.pad(mixes, (0, mix_rows * width - count)).reshape(mix_rows, width)]
                + [g[None] for s in small for g in s[2:]]
            )
            flat = jnp.pad(flat, ((0, -flat.shape[0] % 8), (0, 0)))
            flat = Butterfly(flat)
        if stage == 1:
            moving.advance(*pieces)
            y_parts, parts, pieces = after(([*out_a, *out_b], parts, pieces))
            own, far = scatter_begin(parts)
            own_y, far_y = scatter_begin(y_parts)
    for stage in range(HALVINGS, len(orders[0])):
        got = [swap(part, *order[stage]) for part, order in zip(pieces, orders)]
        if stage == HALVINGS:
            flat.end(flat.start())
        flat_got = flat.start()
        if stage == HALVINGS:
            first_rows, second_rows = mirror(grad_flow)
            got, second_rows, total_got, moving.got, far_y = after((got, second_rows, total_got, moving.got, far_y))
            y_out = (y_middle + (own_y + far_y.astype(F32))).astype(BF16)
            y_first, y_second = mirror(y_out)
            grad_x = jnp.concatenate([first_rows, second_rows], 0)
            total = jnp.concatenate([near_rows, far_rows, near_got, total_got], 0)
            moving.advance()
        got, flat_got = after((got, flat_got))
        flat.end(flat_got)
        pieces = [halve_end(a, b) for a, b in zip(pieces, got)]
    total_other = swap(total, *core_step)
    replicated = ()
    for stage in range(HALVINGS - 1, -1, -1):
        got = [swap(part, *order[stage]) for part, order in zip(pieces, orders)]
        flat_got = flat.start()
        if stage == HALVINGS - 1:
            got, total_other = after((got, total_other))
        elif stage == HALVINGS - 2:
            replicated = expand(1, 0, total_place, [total])
            got, replicated, moving.got, y_second = after((got, replicated, moving.got, y_second))
            y_out = jnp.concatenate([y_first, y_second], 0)
        elif stage == 0:
            replicated = expand(1, 1, total_place, [total_other], replicated)
            got, replicated = after((got, replicated))
        got, flat_got = after((got, flat_got))
        flat.end(flat_got)
        pieces = [spread(a, b) for a, b in zip(pieces, got)]
    got = [swap(part, *core_step) for part in pieces]
    while flat.steps:
        flat.end(flat.start())
    flat = flat.value
    (summed,) = moving.finish()
    sharded[0] = (summed[:per], summed[per:].T)
    replicated = expand(0, 0, place, pieces, replicated)
    got, replicated, sharded = after((got, replicated, sharded))
    replicated = expand(0, 1, place, got, replicated)
    mixes = flat[:mix_rows].reshape(-1)[:count].reshape(LAYERS, 2, heads, heads)
    gains = flat[mix_rows : mix_rows + 2 * LAYERS].reshape(LAYERS, 2, width)
    return (
        y_out[:, None],
        grad_x[:, None],
        *replicated,
        mixes[:, 0],
        mixes[:, 1],
        gains[:, 0],
        gains[:, 1],
        jnp.stack([s[0] for s in sharded]),
        jnp.stack([s[1] for s in sharded]),
    )


def solution(mesh):
    in_specs = (
        P("tp", "dp", None),
        P(None, "dp"),
        P(),
        P(),
        P(),
        P(),
        P(),
        P(),
        P(None, None, "tp"),
        P(None, "tp", None),
        P("tp", "dp", None),
    )
    out_specs = (
        P("tp", "dp", None),
        P("tp", "dp", None),
        P(),
        P(),
        P(),
        P(),
        P(),
        P(),
        P(None, "dp", "tp"),
        P(None, "tp", "dp"),
    )
    return jax.shard_map(
        on_device, mesh=mesh, in_specs=in_specs, out_specs=out_specs, check_vma=False
    )
```

```python
import functools

import jax
import jax.numpy as jnp
from jax import lax
from jax.experimental import pallas as pl
from jax.experimental.pallas import tpu as pltpu
from jax.sharding import PartitionSpec as P

LAYERS = 2
EPSILON = 1e-06
NEGATIVE = -1e30
LOG2E = 1.4426950408889634
GROUPS = 4
PIECES = 8
GP = 4
GB = 4
VMEM = 60 * 1024 * 1024
SMALL = 18 * 1024 * 1024
F32 = jnp.float32
BF16 = jnp.bfloat16


def dot_nn(a, b):
    return lax.dot_general(a, b, (((1,), (0,)), ((), ())), preferred_element_type=F32)


def dot_nt(a, b):
    return lax.dot_general(a, b, (((1,), (1,)), ((), ())), preferred_element_type=F32)


def dot_tn(a, b):
    return lax.dot_general(a, b, (((0,), (0,)), ((), ())), preferred_element_type=F32)


def rms(values, gain):
    return values * lax.rsqrt(jnp.mean(values * values, -1, keepdims=True) + EPSILON) * gain


def rms_back(grad, values, gain):
    inv = lax.rsqrt(jnp.mean(values * values, -1, keepdims=True) + EPSILON)
    unit = values * inv
    scaled = grad * gain
    grad_values = (scaled - unit * jnp.mean(scaled * unit, -1, keepdims=True)) * inv
    return grad_values, jnp.sum(grad * unit, axis=0)


def whole(shape):
    return pl.BlockSpec(shape, lambda *_: (0,) * len(shape))


def layer_of(array, layer):
    shape = array.shape[1:]
    return pl.BlockSpec((1,) + shape, lambda *_: (layer,) + (0,) * len(shape))


def attn_fwd_body(blocks, heads, layer, plain, *refs):
    n_refs = refs[:blocks]
    x_hbm, wqkv_hbm, wout_hbm, tab_ref, gain_ref, qinfo_ref, kinfo_ref, at_ref = refs[blocks : blocks + 8]
    p_ref, u_ref, q_ref, k_hbm, v_hbm, ot_ref, n1t_hbm, xm_ref, n2_ref = refs[blocks + 8 : blocks + 17]
    bias_ref, acc_ref, k_ref, v_ref, n1t_ref, x_ref, wqkv_ref, wout_ref, sems = refs[blocks + 17 :]
    step = pl.program_id(0)
    rows, width = x_ref.shape
    q_cols, k_cols, v_cols = [slice(i * width, (i + 1) * width) for i in range(3)]
    weights = [
        pltpu.make_async_copy(wqkv_hbm.at[layer, :, cols], wqkv_ref.at[i], sems.at[i])
        for i, cols in enumerate((k_cols, v_cols, q_cols))
    ]
    last_used = [
        pltpu.make_async_copy(wout_hbm.at[layer], wout_ref, sems.at[3]),
        pltpu.make_async_copy(x_hbm, x_ref, sems.at[4]),
    ]
    early = [
        pltpu.make_async_copy(k_ref, k_hbm, sems.at[5]),
        pltpu.make_async_copy(v_ref, v_hbm, sems.at[6]),
    ]
    turned = pltpu.make_async_copy(n1t_ref, n1t_hbm, sems.at[7])
    half = rows // 2
    at = at_ref[0]

    def place(r, second):
        block = chunk_of(at ^ r, second, blocks, plain)
        return pl.ds(pl.multiple_of(block * half, half), half)

    @pl.when(step == 0)
    def _():
        for copy in weights + last_used:
            copy.start()
        for i, ref in enumerate((k_ref, v_ref)):
            weights[i].wait()
            for r in range(blocks):
                value = dot_nn(n_refs[r][...], wqkv_ref[i]).astype(BF16)
                ref[place(r, 0), :] = value[:half]
                ref[place(r, 1), :] = value[half:]
            early[i].start()
        weights[2].wait()
        n_second = n_refs[blocks - 1 if plain else 0]
        q_ref[:half] = dot_nn(n_refs[0][:half], wqkv_ref[2]).astype(BF16)
        q_ref[half:] = dot_nn(n_second[half:], wqkv_ref[2]).astype(BF16)
        ok = (qinfo_ref[:, 1:2] == kinfo_ref[1:2, :]) & (kinfo_ref[0:1, :] <= qinfo_ref[:, 0:1])
        bias_ref[...] = jnp.where(ok, 0.0, NEGATIVE)
        acc_ref[...] = jnp.zeros_like(acc_ref)

    def work(second, keys):
        here = pl.ds(pl.multiple_of(second * half, half), half)
        q = q_ref[here, :].astype(F32)
        gs = [step * GP + u for u in range(GP)]
        qm = jnp.concatenate([(q * (tab_ref[0, pl.ds(g, 1), :] * LOG2E)).astype(BF16) for g in gs], 0)
        m = dot_nt(qm, k_ref[:keys, :])
        bias = bias_ref[here, :keys]
        ps = []
        for u in range(GP):
            mu = m[u * half : (u + 1) * half] + bias
            e = jnp.exp2(mu - jnp.max(mu, -1, keepdims=True))
            p = (e * (1.0 / jnp.sum(e, -1, keepdims=True))).astype(BF16)
            p_ref[u, here, :keys] = p
            ps.append(p)
        ctx = dot_nn(jnp.concatenate(ps, 0), v_ref[:keys, :])
        total = acc_ref[here, :]
        for u in range(GP):
            cu = ctx[u * half : (u + 1) * half]
            u_ref[u, here, :] = cu.astype(BF16)
            total = total + cu * tab_ref[0, pl.ds(heads + gs[u], 1), :]
        acc_ref[here, :] = total

    for pairs in range(1, blocks + 1):
        late = at == blocks - pairs

        @pl.when(late | (at == pairs - 1))
        def _(pairs=pairs, late=late):
            work(late.astype(jnp.int32), 2 * pairs * half)

    @pl.when(step == 0)
    def _():
        for r in range(blocks):
            for second in range(2):
                n1t_ref[:, place(r, second)] = n_refs[r][second * half : (second + 1) * half, :].T
        turned.start()

    @pl.when(step == pl.num_programs(0) - 1)
    def _():
        o = acc_ref[...].astype(BF16)
        ot_ref[...] = o.T
        for copy in last_used + early + [turned]:
            copy.wait()
        xm = x_ref[...] + dot_nn(o, wout_ref[...])
        xm_ref[...] = xm
        n2_ref[...] = rms(xm, gain_ref[pl.ds(layer, 1), :]).astype(BF16)


def chunk_of(device, second, devices, plain):
    if not second:
        return 2 * device
    return 2 * device + 1 if plain else 2 * (devices - 1 - device) + 1


def attn_fwd(layer, plain, n_blocks, x, w_qkv, w_out, tab, gain, where):
    rows, width = x.shape
    blocks = len(n_blocks)
    heads = tab.shape[1] // 2
    keys = rows * blocks
    args = (*n_blocks, x, w_qkv, w_out, tab, gain, *where)
    in_specs = [whole(a.shape) for a in args]
    in_specs[blocks : blocks + 3] = [pl.BlockSpec(memory_space=pl.ANY)] * 3
    in_specs[blocks + 3] = layer_of(tab, layer)
    in_specs[-1] = pl.BlockSpec(memory_space=pltpu.SMEM)
    out = [
        ((heads, rows, keys), BF16),
        ((heads, rows, width), BF16),
        ((rows, width), BF16),
        ((keys, width), BF16),
        ((keys, width), BF16),
        ((width, rows), BF16),
        ((width, keys), BF16),
        ((rows, width), F32),
        ((rows, width), BF16),
    ]
    out_specs = [whole(s) for s, _ in out]
    out_specs[0] = pl.BlockSpec((GP, rows, keys), lambda i: (i, 0, 0))
    out_specs[1] = pl.BlockSpec((GP, rows, width), lambda i: (i, 0, 0))
    for i in (3, 4, 6):
        out_specs[i] = pl.BlockSpec(memory_space=pltpu.HBM)
    return pl.pallas_call(
        functools.partial(attn_fwd_body, blocks, heads, layer, plain),
        grid=(heads // GP,),
        in_specs=in_specs,
        out_specs=out_specs,
        out_shape=[jax.ShapeDtypeStruct(s, d) for s, d in out],
        scratch_shapes=[
            pltpu.VMEM((rows, keys), F32),
            pltpu.VMEM((rows, width), F32),
            pltpu.VMEM((keys, width), BF16),
            pltpu.VMEM((keys, width), BF16),
            pltpu.VMEM((width, keys), BF16),
            pltpu.VMEM((rows, width), F32),
            pltpu.VMEM((3, width, width), BF16),
            pltpu.VMEM((width, width), BF16),
            pltpu.SemaphoreType.DMA((8,)),
        ],
        compiler_params=pltpu.CompilerParams(vmem_limit_bytes=VMEM),
        cost_estimate=pl.CostEstimate(
            flops=2 * rows * keys * width * heads * 2, bytes_accessed=20_000_000, transcendentals=rows * keys * heads
        ),
        name="attn_fwd",
    )(*args)


def attn_bwd_body(heads, blocks, layer, parts, *refs):
    (ga_ref, wout_ref, q_ref, k_ref, v_ref, p_ref, u_ref, tab_ref, tabt_ref, place_ref) = refs[:10]
    wqkv_hbm, n1t_hbm, ot_hbm = refs[10:13]
    gn1_refs = refs[13 : 13 + blocks]
    grad_refs = refs[13 + blocks : 13 + blocks + 2 * parts]
    zpre_ref, zpost_ref = refs[13 + blocks + 2 * parts : 15 + blocks + 2 * parts]
    go_ref, got_ref, qt_ref, gq_acc, gk_acc, gv_acc, wqkv_ref, n1t_ref, ot_ref, sems = refs[15 + blocks + 2 * parts :]
    step = pl.program_id(0)
    rows, width = q_ref.shape

    late = [
        pltpu.make_async_copy(wqkv_hbm.at[layer], wqkv_ref, sems.at[0]),
        pltpu.make_async_copy(n1t_hbm, n1t_ref, sems.at[1]),
        pltpu.make_async_copy(ot_hbm, ot_ref, sems.at[2]),
    ]

    @pl.when(step == 0)
    def _():
        for copy in late:
            copy.start()
        go = dot_nt(ga_ref[...], wout_ref[0]).astype(BF16).astype(F32)
        go_ref[...] = go
        got_ref[...] = go.T
        qt_ref[...] = q_ref[...].astype(F32).T
        gq_acc[...] = jnp.zeros_like(gq_acc)
        gk_acc[...] = jnp.zeros_like(gk_acc)
        gv_acc[...] = jnp.zeros_like(gv_acc)
        zpre_ref[...] = jnp.zeros_like(zpre_ref)
        zpost_ref[...] = jnp.zeros_like(zpost_ref)

    half = rows // 2
    at = place_ref[1 + parts]
    lane = lax.broadcasted_iota(jnp.int32, tabt_ref.shape[1:], 1)
    gs = [step * GB + u for u in range(GB)]
    cols = []
    for g in gs:
        pre_col = jnp.sum(jnp.where(lane == g, tabt_ref[0], 0.0), 1, keepdims=True)
        post_col = jnp.sum(jnp.where(lane == heads + g, tabt_ref[0], 0.0), 1, keepdims=True)
        cols.append((pre_col, post_col))

    def work(second, keys):
        here = pl.ds(pl.multiple_of(second * half, half), half)
        go = go_ref[here, :]
        q = q_ref[here, :].astype(F32)
        mixed = [go * tab_ref[0, pl.ds(heads + g, 1), :] for g in gs]
        gp = dot_nt(jnp.concatenate([x.astype(BF16) for x in mixed], 0), v_ref[:keys, :])
        gms, ps, zposts = [], [], []
        for u in range(GB):
            ctx = u_ref[u, here, :].astype(F32)
            zposts.append(jnp.sum(ctx * go, axis=0, keepdims=True))
            delta = jnp.sum(ctx * mixed[u], axis=1, keepdims=True)
            p = p_ref[u, here, :keys]
            gms.append((p.astype(F32) * (gp[u * half : (u + 1) * half] - delta)).astype(BF16))
            ps.append(p)
        gm = jnp.concatenate(gms, 0)
        t = dot_nn(gm, k_ref[:keys, :])
        total = gq_acc[here, :]
        zpres = []
        for u in range(GB):
            tu = t[u * half : (u + 1) * half]
            zpres.append(jnp.sum(tu * q, axis=0, keepdims=True))
            total = total + tu * tab_ref[0, pl.ds(gs[u], 1), :]
        gq_acc[here, :] = total
        qm = jnp.concatenate([(qt_ref[:, here] * pre).astype(BF16) for pre, _ in cols], 1)
        gk_acc[:, :keys] += dot_nn(qm, gm)
        gm2 = jnp.concatenate([(got_ref[:, here] * post).astype(BF16) for _, post in cols], 1)
        gv_acc[:, :keys] += dot_nn(gm2, jnp.concatenate(ps, 0))
        return zpres, zposts

    for pairs in range(1, blocks + 1):
        is_late = at == blocks - pairs

        @pl.when(is_late | (at == pairs - 1))
        def _(pairs=pairs, is_late=is_late):
            zpres, zposts = work(is_late.astype(jnp.int32), 2 * pairs * half)
            for u, g in enumerate(gs):
                zpre_ref[pl.ds(g, 1), :] += zpres[u]
                zpost_ref[pl.ds(g, 1), :] += zposts[u]

    @pl.when(step == pl.num_programs(0) - 1)
    def _():
        for copy in late:
            copy.wait()
        gq = gq_acc[...].astype(BF16)
        gkt = gk_acc[...].astype(BF16)
        gvt = gv_acc[...].astype(BF16)
        ga = ga_ref[...]
        for r in range(blocks):
            there = [pl.ds(pl.multiple_of(chunk_of(at ^ r, x, blocks, False) * half, half), half) for x in range(2)]
            gk = jnp.concatenate([gk_acc[:, x].T.astype(BF16) for x in there], 0)
            gv = jnp.concatenate([gv_acc[:, x].T.astype(BF16) for x in there], 0)
            gn1 = dot_nt(gk, wqkv_ref[:, width : 2 * width]) + dot_nt(gv, wqkv_ref[:, 2 * width :])
            if r == 0:
                gn1 = gn1 + dot_nt(gq, wqkv_ref[:, :width])
            gn1_refs[r][...] = gn1.astype(BF16)
        hand = width // 2
        per = hand // PIECES
        own = [pl.ds(pl.multiple_of(chunk_of(at, x, blocks, False) * half, half), half) for x in range(2)]
        for side in range(2):
            core = place_ref[0] if side == 0 else 1 - place_ref[0]
            mine = pl.ds(pl.multiple_of(core * hand, hand), hand)
            n1t = n1t_ref[mine, :]
            n1t_own = jnp.concatenate([n1t_ref[mine, x] for x in own], 1)
            grads = (
                lambda: dot_nn(n1t_own, gq),
                lambda: dot_nt(n1t, gkt),
                lambda: dot_nt(n1t, gvt),
                lambda: dot_nn(ot_ref[mine, :], ga),
            )
            for index, grad in enumerate(grads):
                part = index * parts // len(grads)
                column = (index - part * (len(grads) // parts)) * width
                value = grad().astype(BF16)
                for piece in range(PIECES):
                    there = pl.multiple_of((piece ^ place_ref[1 + part]) * per, per)
                    grad_refs[2 * part + side][pl.ds(there, per), column : column + width] = value[
                        piece * per : (piece + 1) * per
                    ]


def attn_bwd(layer, blocks, ga, w_out, q, k, v, p, u, tab, tabt, place, w_qkv, n1t, ot):
    rows, width = q.shape
    keys = k.shape[0]
    heads = p.shape[0]
    parts = place.shape[0] - 2
    args = (ga, w_out, q, k, v, p, u, tab, tabt, place, w_qkv, n1t, ot)
    in_specs = [whole(a.shape) for a in args]
    in_specs[1] = layer_of(w_out, layer)
    in_specs[5] = pl.BlockSpec((GB, rows, keys), lambda i: (i, 0, 0))
    in_specs[6] = pl.BlockSpec((GB, rows, width), lambda i: (i, 0, 0))
    in_specs[7] = layer_of(tab, layer)
    in_specs[8] = layer_of(tabt, layer)
    in_specs[9] = pl.BlockSpec(memory_space=pltpu.SMEM)
    in_specs[10:13] = [pl.BlockSpec(memory_space=pl.ANY)] * 3
    out = (
        [((rows, width), BF16)] * blocks
        + [((width // 2, 4 // parts * width), BF16)] * (2 * parts)
        + [((heads, width), F32)] * 2
    )
    res = pl.pallas_call(
        functools.partial(attn_bwd_body, heads, blocks, layer, parts),
        grid=(heads // GB,),
        in_specs=in_specs,
        out_specs=[whole(s) for s, _ in out],
        out_shape=[jax.ShapeDtypeStruct(s, d) for s, d in out],
        scratch_shapes=[
            pltpu.VMEM((rows, width), F32),
            pltpu.VMEM((width, rows), F32),
            pltpu.VMEM((width, rows), F32),
            pltpu.VMEM((rows, width), F32),
            pltpu.VMEM((width, keys), F32),
            pltpu.VMEM((width, keys), F32),
            pltpu.VMEM(w_qkv.shape[1:], BF16),
            pltpu.VMEM(n1t.shape, BF16),
            pltpu.VMEM(ot.shape, BF16),
            pltpu.SemaphoreType.DMA((3,)),
        ],
        compiler_params=pltpu.CompilerParams(vmem_limit_bytes=VMEM),
        cost_estimate=pl.CostEstimate(
            flops=2 * rows * keys * width * heads * 4 * 2, bytes_accessed=20_000_000, transcendentals=0
        ),
        name="attn_bwd",
    )(*args)
    return res[:blocks], res[blocks:-2], res[-2], res[-1]


def expand_body(parts, place_ref, *refs):
    qkv_ref, out_ref = refs[-2:]
    width3 = qkv_ref.shape[2]
    inner = PIECES // GROUPS
    per = qkv_ref.shape[1] // inner
    column = 0
    for part, ref in enumerate(refs[:parts]):
        end = column + ref.shape[1]
        cut = min(end, width3)
        for piece in range(inner):
            here = slice(piece * per, (piece + 1) * per)
            there = piece ^ lax.rem(place_ref[1 + part], inner)
            value = ref[pl.ds(pl.multiple_of(there * per, per), per), :].astype(F32)
            qkv_ref[0, here, column:cut] = value[:, : cut - column]
            if end > width3:
                out_ref[0, here, :] = value[:, cut - column :]
        column = end


def expand(layer, side, place, halves, before=()):
    half = halves[0].shape[0]
    width = sum(h.shape[1] for h in halves) // 4
    per = half // GROUPS
    in_specs = []
    for part, array in enumerate(halves):

        def piece(i, place, part=part):
            return i ^ (place[1 + part] // (PIECES // GROUPS)), 0

        in_specs.append(pl.BlockSpec((per, array.shape[1]), piece))
    first = 1 + len(halves)
    in_specs += [pl.BlockSpec(memory_space=pl.ANY)] * len(before)

    def there(i, place):
        return layer, (place[0] ^ side) * GROUPS + i, 0

    return pl.pallas_call(
        functools.partial(expand_body, len(halves)),
        grid_spec=pltpu.PrefetchScalarGridSpec(
            num_scalar_prefetch=1,
            grid=(GROUPS,),
            in_specs=in_specs,
            out_specs=[pl.BlockSpec((1, per, 3 * width), there), pl.BlockSpec((1, per, width), there)],
        ),
        out_shape=[
            jax.ShapeDtypeStruct((LAYERS, 2 * half, 3 * width), F32),
            jax.ShapeDtypeStruct((LAYERS, 2 * half, width), F32),
        ],
        input_output_aliases={first + i: i for i in range(len(before))},
        compiler_params=pltpu.CompilerParams(vmem_limit_bytes=SMALL),
        cost_estimate=pl.CostEstimate(flops=0, bytes_accessed=7_000_000, transcendentals=0),
        name="expand",
    )(place, *halves, *before)


def ffn_fwd_body(blocks, *refs):
    n_refs = refs[:blocks]
    win_ref, wdown_ref = refs[blocks : blocks + 2]
    out_refs = refs[blocks + 2 : 2 * blocks + 2]
    hid_ref, dgelu_ref = refs[2 * blocks + 2 :]
    rows = n_refs[0].shape[0]
    for r in range(blocks):
        here = pl.ds(r * rows, rows)
        pre = dot_nn(n_refs[r][...], win_ref[0])
        cdf = 0.5 + 0.5 * lax.erf(pre * (0.5**0.5))
        hid = (pre * cdf).astype(BF16)
        hid_ref[here, :] = hid
        density = jnp.exp2(pre * pre * (-0.5 * LOG2E)) * 0.3989422804014327
        dgelu_ref[here, :] = (cdf + pre * density).astype(BF16)
        out_refs[r][...] = dot_nn(hid, wdown_ref[0]).astype(BF16)


def ffn_fwd(layer, n_blocks, w_in, w_down):
    blocks = len(n_blocks)
    rows, width = n_blocks[0].shape
    hidden = w_in.shape[2]
    args = (*n_blocks, w_in, w_down)
    in_specs = [whole(a.shape) for a in args]
    in_specs[blocks] = layer_of(w_in, layer)
    in_specs[blocks + 1] = layer_of(w_down, layer)
    out = [((rows, width), BF16)] * blocks + [((rows * blocks, hidden), BF16)] * 2
    res = pl.pallas_call(
        functools.partial(ffn_fwd_body, blocks),
        grid=(1,),
        in_specs=in_specs,
        out_specs=[whole(s) for s, _ in out],
        out_shape=[jax.ShapeDtypeStruct(s, d) for s, d in out],
        compiler_params=pltpu.CompilerParams(vmem_limit_bytes=SMALL),
        cost_estimate=pl.CostEstimate(
            flops=4 * rows * blocks * width * hidden, bytes_accessed=6_000_000, transcendentals=rows * blocks * hidden
        ),
        name="ffn_fwd",
    )(*args)
    return res[:blocks], res[blocks], res[blocks + 1]


def ffn_bwd_body(blocks, *refs):
    g_refs = refs[:blocks]
    dgelu_ref, win_ref, wdown_ref = refs[blocks : blocks + 3]
    out_refs = refs[blocks + 3 : 2 * blocks + 3]
    gpre_ref = refs[2 * blocks + 3]
    rows = g_refs[0].shape[0]
    for r in range(blocks):
        here = pl.ds(r * rows, rows)
        gh = dot_nt(g_refs[r][...], wdown_ref[0])
        gpre = (gh * dgelu_ref[here, :].astype(F32)).astype(BF16)
        gpre_ref[here, :] = gpre
        out_refs[r][...] = dot_nt(gpre, win_ref[0]).astype(BF16)


def ffn_bwd(layer, g_blocks, dgelu, w_in, w_down):
    blocks = len(g_blocks)
    rows, width = g_blocks[0].shape
    hidden = w_in.shape[2]
    args = (*g_blocks, dgelu, w_in, w_down)
    in_specs = [whole(a.shape) for a in args]
    in_specs[blocks + 1] = layer_of(w_in, layer)
    in_specs[blocks + 2] = layer_of(w_down, layer)
    out = [((rows, width), BF16)] * blocks + [((rows * blocks, hidden), BF16)]
    res = pl.pallas_call(
        functools.partial(ffn_bwd_body, blocks),
        grid=(1,),
        in_specs=in_specs,
        out_specs=[whole(s) for s, _ in out],
        out_shape=[jax.ShapeDtypeStruct(s, d) for s, d in out],
        compiler_params=pltpu.CompilerParams(vmem_limit_bytes=SMALL),
        cost_estimate=pl.CostEstimate(
            flops=4 * rows * blocks * width * hidden, bytes_accessed=6_000_000, transcendentals=0
        ),
        name="ffn_bwd",
    )(*args)
    return res[:blocks], res[blocks]


def ffn_grads_body(blocks, chunks, *refs):
    n_refs, g_refs = refs[:blocks], refs[blocks : 2 * blocks]
    hid_refs, gpre_refs = refs[2 * blocks : 2 * blocks + 2], refs[2 * blocks + 2 : 2 * blocks + 4]
    out_ref = refs[-1]
    rows, width = n_refs[0].shape
    per = width // chunks
    for part, (left_refs, right_refs) in enumerate(((n_refs, gpre_refs), (g_refs, hid_refs))):
        left = jnp.concatenate([ref[...].T for ref in left_refs], 1)
        right = jnp.concatenate([ref[...] for ref in right_refs], 0)
        grad = dot_nn(left, right).astype(BF16)
        for c in range(chunks):
            place = 2 * sum(((c >> i) & 1) * (chunks >> (i + 1)) for i in range(chunks.bit_length() - 1)) + part
            out_ref[place * per : (place + 1) * per, :] = grad[c * per : (c + 1) * per]


def ffn_grads(n_blocks, g_blocks, hids, gpres, chunks):
    blocks = len(n_blocks)
    rows, width = n_blocks[0].shape
    hidden = hids[0].shape[1]
    args = (*n_blocks, *g_blocks, *hids, *gpres)
    return pl.pallas_call(
        functools.partial(ffn_grads_body, blocks, chunks),
        grid=(1,),
        in_specs=[whole(a.shape) for a in args],
        out_specs=whole((2 * width, hidden)),
        out_shape=jax.ShapeDtypeStruct((2 * width, hidden), BF16),
        compiler_params=pltpu.CompilerParams(vmem_limit_bytes=VMEM),
        cost_estimate=pl.CostEstimate(
            flops=4 * rows * blocks * width * hidden, bytes_accessed=9_000_000, transcendentals=0
        ),
        name="ffn_grads",
    )(*args)


def swap(value, axis, bit):
    size = lax.axis_size(axis)
    return lax.ppermute(value, axis, [(i, i ^ bit) for i in range(size)])


def after(values, *done):
    return lax.optimization_barrier((values, done))[0]


def gather_near(value):
    half = lax.axis_size("tp") // 2
    far = swap(value, "tp", half)
    near = [value]
    bit = 1
    while bit < half:
        near += [swap(b, "tp", bit) for b in near]
        bit *= 2
    return near, far


def gather_far(far):
    half = lax.axis_size("tp") // 2
    blocks = [far]
    bit = 1
    while bit < half:
        blocks += [swap(b, "tp", bit) for b in blocks]
        bit *= 2
    return blocks


def gather_blocks(value):
    near, far = gather_near(value)
    return near + gather_far(far)


def scatter_begin(blocks):
    blocks = list(blocks)
    bit = 1
    while bit < lax.axis_size("tp") // 2:
        size = len(blocks)
        keep = [blocks[r] for r in range(size) if not r & 1]
        sent = [swap(blocks[r], "tp", bit) for r in range(size) if r & 1]
        blocks = [a.astype(F32) + b.astype(F32) for a, b in zip(keep, sent)]
        bit *= 2
        blocks = [blocks[0]] + [b.astype(BF16) for b in blocks[1:]]
    return blocks[0].astype(F32), swap(blocks[1], "tp", bit)


def halve_begin(part, axis, bit):
    mine = (lax.axis_index(axis) // bit) & 1
    pair = part.reshape(2, part.shape[0] // 2, part.shape[1])
    sent = lax.dynamic_index_in_dim(pair, 1 - mine, 0, keepdims=False)
    kept = lax.dynamic_index_in_dim(pair, mine, 0, keepdims=False)
    return kept, swap(sent, axis, bit)


def halve_end(kept, got):
    return (kept.astype(F32) + got.astype(F32)).astype(BF16)


class Scatter:
    def __init__(self, parts, steps):
        self.steps = list(steps)
        self.begin(parts)

    def begin(self, parts):
        step = self.steps.pop(0)
        self.kept, self.got = zip(*[halve_begin(part, *step) for part in parts])

    def advance(self, *done):
        if self.steps:
            got = after(self.got, *done)
            self.begin([halve_end(a, b) for a, b in zip(self.kept, got)])

    def finish(self, *done):
        while self.steps:
            self.advance(*done)
        return [a.astype(F32) + b.astype(F32) for a, b in zip(self.kept, after(self.got, *done))]


def steps_of(axis):
    return [(axis, 1 << i) for i in range(lax.axis_size(axis).bit_length() - 1)]


HALVINGS = PIECES.bit_length() - 1


def place_of(order):
    number = 0
    for axis, bit in order[:HALVINGS]:
        number = 2 * number + ((lax.axis_index(axis) // bit) & 1)
    return number


def sum_start(part, order, stage):
    if stage < HALVINGS:
        rows = part.shape[0] // 2
        return part[:rows], swap(part[rows:], *order[stage])
    return part, swap(part, *order[stage])


def spread(part, got):
    return jnp.concatenate([part, got], 0)


class Butterfly:
    def __init__(self, value):
        self.value = value
        self.steps = steps_of("tp") + steps_of("dp")
        self.got = None

    def start(self):
        if self.steps:
            self.got = swap(self.value, *self.steps.pop(0))
            return [self.got]
        return []

    def end(self, got):
        for g in got:
            self.value = self.value + g


def on_device(
    x_in, segments, w_qkv, w_out, mix_pre, mix_post, gain_attn, gain_ffn, w_in, w_down, cotangent
):
    rows, _, width = x_in.shape
    heads = mix_pre.shape[1]
    head_size = width // heads
    tp_size = lax.axis_size("tp")
    dp_size = lax.axis_size("dp")
    tp_index = lax.axis_index("tp")
    seg = segments[:, 0]
    side = rows // 2
    span = jnp.arange(side, dtype=jnp.int32)
    starts = [chunk_of(tp_index, x, tp_size, False) * side for x in range(2)]
    qpos = jnp.concatenate([start + span for start in starts])
    qseg = jnp.concatenate([lax.dynamic_slice_in_dim(seg, start, side, 0) for start in starts])
    qinfo = jnp.stack([qpos, qseg] + [qpos] * 6, 1)
    kinfo = jnp.pad(jnp.stack([jnp.arange(seg.shape[0], dtype=jnp.int32), seg]), ((0, 6), (0, 0)))
    where = (qinfo, kinfo, tp_index[None])

    def mirror(value):
        moved = lax.ppermute(value[side:], "tp", [(i, tp_size - 1 - i) for i in range(tp_size)])
        return value[:side], moved

    tab = jnp.concatenate([jnp.swapaxes(mix_pre, 1, 2) * (head_size**-0.5), mix_post], 1)
    tabt = jnp.pad(jnp.repeat(jnp.swapaxes(tab, 1, 2), head_size, axis=1), ((0, 0), (0, 0), (0, 128 - 2 * heads)))
    tab = jnp.repeat(tab, head_size, axis=2)

    stream = x_in[:, 0].astype(F32)
    x_folded = jnp.concatenate(mirror(x_in[:, 0]), 0).astype(F32)
    kept = []
    half = tp_size // 2
    for layer in range(LAYERS):
        last = layer == LAYERS - 1
        n1_blocks = gather_blocks(rms(stream, gain_attn[layer]).astype(BF16))
        if last:
            low, n1_blocks[half] = after((cotangent[:, 0], n1_blocks[half]))
            grad_near, grad_far = gather_near(low)
        else:
            stream = x_folded
        p, u, q, k, v, ot, n1t, middle, n2 = attn_fwd(
            layer,
            layer == 0,
            n1_blocks,
            stream,
            w_qkv,
            w_out,
            tab,
            gain_ffn,
            where,
        )
        if last:
            n2, grad_near, grad_far = after((n2, grad_near, grad_far))
        near, far = gather_near(n2)
        out_a, hid_a, dgelu_a = ffn_fwd(layer, near, w_in, w_down)
        if last:
            given = grad_near + gather_far(grad_far)
            gf_blocks = [jnp.concatenate([given[r][:side], given[tp_size - 1 - r][side:]], 0) for r in range(tp_size)]
            gn2_a, gpre_a = ffn_bwd(layer, gf_blocks[:half], dgelu_a, w_in, w_down)
            far, gpre_a = after((far, gpre_a))
        far, hid_a = after((far, hid_a))
        n2_blocks = near + gather_far(far)
        out_b, hid_b, dgelu_b = ffn_fwd(layer, n2_blocks[half:], w_in, w_down)
        kept.append((stream, n1t, p, u, q, k, v, ot, middle, n2_blocks, hid_a, hid_b, dgelu_a, dgelu_b))
        if not last:
            own, far = scatter_begin([*out_a, *out_b])
            stream = middle + (own + far.astype(F32))

    grad_flow = gf_blocks[0].astype(F32)
    per = width // dp_size
    small = [None] * LAYERS
    sharded = [None] * LAYERS
    for layer in range(LAYERS - 1, -1, -1):
        last = layer == LAYERS - 1
        stream, n1t, p, u, q, k, v, ot, middle, n2_blocks, hid_a, hid_b, dgelu_a, dgelu_b = kept[layer]
        if not last:
            near, far = gather_near(grad_flow.astype(BF16))
            gn2_a, gpre_a = ffn_bwd(layer, near, dgelu_a, w_in, w_down)
            far, gpre_a = after((far, gpre_a))
            gf_blocks = near + gather_far(far)
        gn2_b, gpre_b = ffn_bwd(layer, gf_blocks[half:], dgelu_b, w_in, w_down)
        if not last:
            total_got, gpre_b = after((total_got, gpre_b))
            total = halve_end(total_kept, total_got)
            total_kept, total_got = sum_start(total, total_order, 1)
        own, far = scatter_begin([*gn2_a, *gn2_b])
        packed = ffn_grads(n2_blocks, gf_blocks, (hid_a, hid_b), (gpre_a, gpre_b), dp_size)
        far, packed = after((far, packed))
        if not last:
            total_got, packed = after((total_got, packed))
            total = halve_end(total_kept, total_got)
            total_kept, total_got = sum_start(total, total_order, 2)
        if not last:
            previous = moving
        moving = Scatter([packed], steps_of("dp"))
        gn2 = (own + far.astype(F32)).astype(BF16).astype(F32)
        grad_norm, grad_gffn = rms_back(gn2, middle, gain_ffn[layer])
        grad_middle = grad_flow + grad_norm
        ga = grad_middle.astype(BF16)
        if last:
            orders = [steps_of("dp") + steps_of("tp")[1:]]
        else:
            (y_step, *dp_rest), x_steps = steps_of("dp"), steps_of("tp")[1:]
            orders = [x_steps + [y_step] + dp_rest, [y_step] + x_steps + dp_rest]
        place = jnp.stack([tp_index & 1] + [place_of(order) for order in orders] + [tp_index])
        parts, grads, zpre, zpost = attn_bwd(
            layer, tp_size, ga, w_out, q, k, v, p, u, tab, tabt, place, w_qkv, n1t, ot
        )
        core_step = steps_of("tp")[0]
        if last:
            parts, grads, moving.got = after((parts, grads, moving.got))
            y_middle = middle
            keep, send = grads
            total = halve_end(keep, swap(send, *core_step))
            own, far = scatter_begin(parts)
            moving.advance()
            far, moving.got = after((far, moving.got), total)
            moving.advance()
            (total_order,), total_place = orders, place
            total_kept, total_got = sum_start(total, total_order, 0)
        else:
            parts, grads, moving.got, total_got, previous.got = after(
                (parts, grads, moving.got, total_got, previous.got)
            )
            (summed,) = previous.finish()
            sharded[layer + 1] = (summed[:per], summed[per:].T)
        if not last:
            break
        gn1 = (own + far.astype(F32)).astype(BF16).astype(F32)
        grad_norm, grad_gattn = rms_back(gn1, stream, gain_attn[layer])
        grad_flow = grad_middle + grad_norm
        grad_mpre = jnp.sum(zpre.reshape(heads, heads, head_size), -1).T * (head_size**-0.5)
        grad_mpost = jnp.sum(zpost.reshape(heads, heads, head_size), -1)
        small[layer] = (grad_mpre, grad_mpost, grad_gattn, grad_gffn)

    total = halve_end(total_kept, total_got)
    grads, total = after((grads, total))
    got = [swap(send, *core_step) for send in grads[1::2]]
    pieces = [halve_end(keep, g) for keep, g in zip(grads[::2], got)]
    for stage in range(HALVINGS, len(total_order)):
        total_got = swap(total, *total_order[stage])
        pieces, total_got = after((pieces, total_got))
        total = halve_end(total, total_got)
    for stage in range(HALVINGS):
        kept, got = zip(*[sum_start(part, order, stage) for part, order in zip(pieces, orders)])
        if stage == 0:
            by_last, by_middle = [swap(total, *step) for step in total_order[HALVINGS - 1 : 0 : -1]]
            got, by_last, by_middle = after((got, by_last, by_middle))
            near_rows = spread(total, by_last)
        elif stage == 1:
            near_got = swap(near_rows, *total_order[0])
            by_both = swap(by_last, *total_order[1])
            got, by_both = after((got, by_both))
            far_rows = spread(by_middle, by_both)
        else:
            total_got = swap(far_rows, *total_order[0])
            got, near_got = after((got, near_got))
        if stage == HALVINGS - 1:
            got, far = after((got, far))
        pieces = [halve_end(a, b) for a, b in zip(kept, after(got))]
        if stage == HALVINGS - 1:
            gn1 = (own + far.astype(F32)).astype(BF16).astype(F32)
            grad_norm, grad_gattn = rms_back(gn1, stream, gain_attn[layer])
            grad_flow = grad_middle + grad_norm
            grad_mpre = jnp.sum(zpre.reshape(heads, heads, head_size), -1).T * (head_size**-0.5)
            grad_mpost = jnp.sum(zpost.reshape(heads, heads, head_size), -1)
            small[layer] = (grad_mpre, grad_mpost, grad_gattn, grad_gffn)
            mixes = jnp.concatenate([a.reshape(-1) for s in small for a in s[:2]])
            count = mixes.shape[0]
            mix_rows = -(-count // width)
            flat = jnp.concatenate(
                [jnp.pad(mixes, (0, mix_rows * width - count)).reshape(mix_rows, width)]
                + [g[None] for s in small for g in s[2:]]
            )
            flat = jnp.pad(flat, ((0, -flat.shape[0] % 8), (0, 0)))
            flat = Butterfly(flat)
        if stage == 1:
            moving.advance(*pieces)
            y_parts, parts, pieces = after(([*out_a, *out_b], parts, pieces))
            own, far = scatter_begin(parts)
            own_y, far_y = scatter_begin(y_parts)
    for stage in range(HALVINGS, len(orders[0])):
        got = [swap(part, *order[stage]) for part, order in zip(pieces, orders)]
        if stage == HALVINGS:
            flat.end(flat.start())
        flat_got = flat.start()
        if stage == HALVINGS:
            first_rows, second_rows = mirror(grad_flow)
            got, second_rows, total_got, moving.got, far_y = after((got, second_rows, total_got, moving.got, far_y))
            y_out = (y_middle + (own_y + far_y.astype(F32))).astype(BF16)
            y_first, y_second = mirror(y_out)
            grad_x = jnp.concatenate([first_rows, second_rows], 0)
            total = jnp.concatenate([near_rows, far_rows, near_got, total_got], 0)
            moving.advance()
        got, flat_got = after((got, flat_got))
        flat.end(flat_got)
        pieces = [halve_end(a, b) for a, b in zip(pieces, got)]
    total_other = swap(total, *core_step)
    replicated = ()
    for stage in range(HALVINGS - 1, -1, -1):
        got = [swap(part, *order[stage]) for part, order in zip(pieces, orders)]
        flat_got = flat.start()
        if stage == HALVINGS - 1:
            got, total_other = after((got, total_other))
        elif stage == HALVINGS - 2:
            replicated = expand(1, 0, total_place, [total])
            got, replicated, moving.got, y_second = after((got, replicated, moving.got, y_second))
            y_out = jnp.concatenate([y_first, y_second], 0)[:, None]
            (summed,) = moving.finish()
            sharded[0] = (summed[:per], summed[per:].T)
            sharded = [jnp.stack(members) for members in zip(*sharded)]
            grad_x = grad_x[:, None]
        elif stage == 0:
            replicated = expand(1, 1, total_place, [total_other], replicated)
            got, replicated, sharded, grad_x, y_out = after((got, replicated, sharded, grad_x, y_out))
        got, flat_got = after((got, flat_got))
        flat.end(flat_got)
        pieces = [spread(a, b) for a, b in zip(pieces, got)]
    got = [swap(part, *core_step) for part in pieces]
    while flat.steps:
        flat.end(flat.start())
    flat = flat.value
    replicated = expand(0, 0, place, pieces, replicated)
    got, replicated = after((got, replicated))
    replicated = expand(0, 1, place, got, replicated)
    mixes = flat[:mix_rows].reshape(-1)[:count].reshape(LAYERS, 2, heads, heads)
    gains = flat[mix_rows : mix_rows + 2 * LAYERS].reshape(LAYERS, 2, width)
    return (
        y_out,
        grad_x,
        *replicated,
        mixes[:, 0],
        mixes[:, 1],
        gains[:, 0],
        gains[:, 1],
        *sharded,
    )


def solution(mesh):
    in_specs = (
        P("tp", "dp", None),
        P(None, "dp"),
        P(),
        P(),
        P(),
        P(),
        P(),
        P(),
        P(None, None, "tp"),
        P(None, "tp", None),
        P("tp", "dp", None),
    )
    out_specs = (
        P("tp", "dp", None),
        P("tp", "dp", None),
        P(),
        P(),
        P(),
        P(),
        P(),
        P(),
        P(None, "dp", "tp"),
        P(None, "tp", "dp"),
    )
    return jax.shard_map(
        on_device, mesh=mesh, in_specs=in_specs, out_specs=out_specs, check_vma=False
    )
```

```python
import functools

import jax
import jax.numpy as jnp
from jax import lax
from jax.experimental import pallas as pl
from jax.experimental.pallas import tpu as pltpu
from jax.sharding import PartitionSpec as P

LAYERS = 2
EPSILON = 1e-06
NEGATIVE = -1e30
LOG2E = 1.4426950408889634
GROUPS = 4
PIECES = 8
GP = 4
GB = 4
VMEM = 60 * 1024 * 1024
SMALL = 18 * 1024 * 1024
F32 = jnp.float32
BF16 = jnp.bfloat16


def dot_nn(a, b):
    return lax.dot_general(a, b, (((1,), (0,)), ((), ())), preferred_element_type=F32)


def dot_nt(a, b):
    return lax.dot_general(a, b, (((1,), (1,)), ((), ())), preferred_element_type=F32)


def dot_tn(a, b):
    return lax.dot_general(a, b, (((0,), (0,)), ((), ())), preferred_element_type=F32)


def rms(values, gain):
    return values * lax.rsqrt(jnp.mean(values * values, -1, keepdims=True) + EPSILON) * gain


def rms_back(grad, values, gain):
    inv = lax.rsqrt(jnp.mean(values * values, -1, keepdims=True) + EPSILON)
    unit = values * inv
    scaled = grad * gain
    grad_values = (scaled - unit * jnp.mean(scaled * unit, -1, keepdims=True)) * inv
    return grad_values, jnp.sum(grad * unit, axis=0)


def whole(shape):
    return pl.BlockSpec(shape, lambda *_: (0,) * len(shape))


def layer_of(array, layer):
    shape = array.shape[1:]
    return pl.BlockSpec((1,) + shape, lambda *_: (layer,) + (0,) * len(shape))


def attn_fwd_body(blocks, heads, layer, plain, *refs):
    n_refs = refs[:blocks]
    x_hbm, wqkv_hbm, wout_hbm, tab_ref, gain_ref, qinfo_ref, kinfo_ref, at_ref = refs[blocks : blocks + 8]
    p_ref, u_ref, q_ref, k_hbm, v_hbm, ot_ref, n1t_hbm, xm_ref, n2_ref = refs[blocks + 8 : blocks + 17]
    bias_ref, acc_ref, k_ref, v_ref, n1t_ref, x_ref, wqkv_ref, wout_ref, sems = refs[blocks + 17 :]
    step = pl.program_id(0)
    rows, width = x_ref.shape
    q_cols, k_cols, v_cols = [slice(i * width, (i + 1) * width) for i in range(3)]
    weights = [
        pltpu.make_async_copy(wqkv_hbm.at[layer, :, cols], wqkv_ref.at[i], sems.at[i])
        for i, cols in enumerate((k_cols, v_cols, q_cols))
    ]
    last_used = [
        pltpu.make_async_copy(wout_hbm.at[layer], wout_ref, sems.at[3]),
        pltpu.make_async_copy(x_hbm, x_ref, sems.at[4]),
    ]
    early = [
        pltpu.make_async_copy(k_ref, k_hbm, sems.at[5]),
        pltpu.make_async_copy(v_ref, v_hbm, sems.at[6]),
    ]
    turned = pltpu.make_async_copy(n1t_ref, n1t_hbm, sems.at[7])
    half = rows // 2
    at = at_ref[0]

    def place(r, second):
        block = chunk_of(at ^ r, second, blocks, plain)
        return pl.ds(pl.multiple_of(block * half, half), half)

    @pl.when(step == 0)
    def _():
        for copy in weights + last_used:
            copy.start()
        for i, ref in enumerate((k_ref, v_ref)):
            weights[i].wait()
            for r in range(blocks):
                value = dot_nn(n_refs[r][...], wqkv_ref[i]).astype(BF16)
                ref[place(r, 0), :] = value[:half]
                ref[place(r, 1), :] = value[half:]
            early[i].start()
        weights[2].wait()
        n_second = n_refs[blocks - 1 if plain else 0]
        q_ref[:half] = dot_nn(n_refs[0][:half], wqkv_ref[2]).astype(BF16)
        q_ref[half:] = dot_nn(n_second[half:], wqkv_ref[2]).astype(BF16)
        ok = (qinfo_ref[:, 1:2] == kinfo_ref[1:2, :]) & (kinfo_ref[0:1, :] <= qinfo_ref[:, 0:1])
        bias_ref[...] = jnp.where(ok, 0.0, NEGATIVE)
        acc_ref[...] = jnp.zeros_like(acc_ref)

    def work(second, keys):
        here = pl.ds(pl.multiple_of(second * half, half), half)
        q = q_ref[here, :].astype(F32)
        gs = [step * GP + u for u in range(GP)]
        qm = jnp.concatenate([(q * (tab_ref[0, pl.ds(g, 1), :] * LOG2E)).astype(BF16) for g in gs], 0)
        m = dot_nt(qm, k_ref[:keys, :])
        bias = bias_ref[here, :keys]
        ps = []
        for u in range(GP):
            mu = m[u * half : (u + 1) * half] + bias
            e = jnp.exp2(mu - jnp.max(mu, -1, keepdims=True))
            p = (e * (1.0 / jnp.sum(e, -1, keepdims=True))).astype(BF16)
            p_ref[u, here, :keys] = p
            ps.append(p)
        ctx = dot_nn(jnp.concatenate(ps, 0), v_ref[:keys, :])
        total = acc_ref[here, :]
        for u in range(GP):
            cu = ctx[u * half : (u + 1) * half]
            u_ref[u, here, :] = cu.astype(BF16)
            total = total + cu * tab_ref[0, pl.ds(heads + gs[u], 1), :]
        acc_ref[here, :] = total

    for pairs in range(1, blocks + 1):
        late = at == blocks - pairs

        @pl.when(late | (at == pairs - 1))
        def _(pairs=pairs, late=late):
            work(late.astype(jnp.int32), 2 * pairs * half)

    @pl.when(step == 0)
    def _():
        for r in range(blocks):
            for second in range(2):
                n1t_ref[:, place(r, second)] = n_refs[r][second * half : (second + 1) * half, :].T
        turned.start()

    @pl.when(step == pl.num_programs(0) - 1)
    def _():
        o = acc_ref[...].astype(BF16)
        ot_ref[...] = o.T
        for copy in last_used + early + [turned]:
            copy.wait()
        xm = x_ref[...] + dot_nn(o, wout_ref[...])
        xm_ref[...] = xm
        n2_ref[...] = rms(xm, gain_ref[pl.ds(layer, 1), :]).astype(BF16)


def chunk_of(device, second, devices, plain):
    if not second:
        return 2 * device
    return 2 * device + 1 if plain else 2 * (devices - 1 - device) + 1


def attn_fwd(layer, plain, n_blocks, x, w_qkv, w_out, tab, gain, where):
    rows, width = x.shape
    blocks = len(n_blocks)
    heads = tab.shape[1] // 2
    keys = rows * blocks
    args = (*n_blocks, x, w_qkv, w_out, tab, gain, *where)
    in_specs = [whole(a.shape) for a in args]
    in_specs[blocks : blocks + 3] = [pl.BlockSpec(memory_space=pl.ANY)] * 3
    in_specs[blocks + 3] = layer_of(tab, layer)
    in_specs[-1] = pl.BlockSpec(memory_space=pltpu.SMEM)
    out = [
        ((heads, rows, keys), BF16),
        ((heads, rows, width), BF16),
        ((rows, width), BF16),
        ((keys, width), BF16),
        ((keys, width), BF16),
        ((width, rows), BF16),
        ((width, keys), BF16),
        ((rows, width), F32),
        ((rows, width), BF16),
    ]
    out_specs = [whole(s) for s, _ in out]
    out_specs[0] = pl.BlockSpec((GP, rows, keys), lambda i: (i, 0, 0))
    out_specs[1] = pl.BlockSpec((GP, rows, width), lambda i: (i, 0, 0))
    for i in (3, 4, 6):
        out_specs[i] = pl.BlockSpec(memory_space=pltpu.HBM)
    return pl.pallas_call(
        functools.partial(attn_fwd_body, blocks, heads, layer, plain),
        grid=(heads // GP,),
        in_specs=in_specs,
        out_specs=out_specs,
        out_shape=[jax.ShapeDtypeStruct(s, d) for s, d in out],
        scratch_shapes=[
            pltpu.VMEM((rows, keys), F32),
            pltpu.VMEM((rows, width), F32),
            pltpu.VMEM((keys, width), BF16),
            pltpu.VMEM((keys, width), BF16),
            pltpu.VMEM((width, keys), BF16),
            pltpu.VMEM((rows, width), F32),
            pltpu.VMEM((3, width, width), BF16),
            pltpu.VMEM((width, width), BF16),
            pltpu.SemaphoreType.DMA((8,)),
        ],
        compiler_params=pltpu.CompilerParams(vmem_limit_bytes=VMEM),
        cost_estimate=pl.CostEstimate(
            flops=2 * rows * keys * width * heads * 2, bytes_accessed=20_000_000, transcendentals=rows * keys * heads
        ),
        name="attn_fwd",
    )(*args)


def attn_bwd_body(heads, blocks, layer, parts, *refs):
    (ga_ref, wout_ref, q_ref, k_ref, v_ref, p_ref, u_ref, tab_ref, tabt_ref, place_ref) = refs[:10]
    wqkv_hbm, n1t_hbm, ot_hbm = refs[10:13]
    gn1_refs = refs[13 : 13 + blocks]
    grad_refs = refs[13 + blocks : 13 + blocks + 2 * parts]
    zpre_ref, zpost_ref = refs[13 + blocks + 2 * parts : 15 + blocks + 2 * parts]
    go_ref, got_ref, qt_ref, gq_acc, gk_acc, gv_acc, wqkv_ref, n1t_ref, ot_ref, sems = refs[15 + blocks + 2 * parts :]
    step = pl.program_id(0)
    rows, width = q_ref.shape

    late = [
        pltpu.make_async_copy(wqkv_hbm.at[layer], wqkv_ref, sems.at[0]),
        pltpu.make_async_copy(n1t_hbm, n1t_ref, sems.at[1]),
        pltpu.make_async_copy(ot_hbm, ot_ref, sems.at[2]),
    ]

    @pl.when(step == 0)
    def _():
        for copy in late:
            copy.start()
        go = dot_nt(ga_ref[...], wout_ref[0]).astype(BF16).astype(F32)
        go_ref[...] = go
        got_ref[...] = go.T
        qt_ref[...] = q_ref[...].astype(F32).T
        gq_acc[...] = jnp.zeros_like(gq_acc)
        gk_acc[...] = jnp.zeros_like(gk_acc)
        gv_acc[...] = jnp.zeros_like(gv_acc)
        zpre_ref[...] = jnp.zeros_like(zpre_ref)
        zpost_ref[...] = jnp.zeros_like(zpost_ref)

    half = rows // 2
    at = place_ref[1 + parts]
    lane = lax.broadcasted_iota(jnp.int32, tabt_ref.shape[1:], 1)
    gs = [step * GB + u for u in range(GB)]
    cols = []
    for g in gs:
        pre_col = jnp.sum(jnp.where(lane == g, tabt_ref[0], 0.0), 1, keepdims=True)
        post_col = jnp.sum(jnp.where(lane == heads + g, tabt_ref[0], 0.0), 1, keepdims=True)
        cols.append((pre_col, post_col))

    def work(second, keys):
        here = pl.ds(pl.multiple_of(second * half, half), half)
        go = go_ref[here, :]
        q = q_ref[here, :].astype(F32)
        mixed = [go * tab_ref[0, pl.ds(heads + g, 1), :] for g in gs]
        gp = dot_nt(jnp.concatenate([x.astype(BF16) for x in mixed], 0), v_ref[:keys, :])
        gms, ps, zposts = [], [], []
        for u in range(GB):
            ctx = u_ref[u, here, :].astype(F32)
            zposts.append(jnp.sum(ctx * go, axis=0, keepdims=True))
            delta = jnp.sum(ctx * mixed[u], axis=1, keepdims=True)
            p = p_ref[u, here, :keys]
            gms.append((p.astype(F32) * (gp[u * half : (u + 1) * half] - delta)).astype(BF16))
            ps.append(p)
        gm = jnp.concatenate(gms, 0)
        t = dot_nn(gm, k_ref[:keys, :])
        total = gq_acc[here, :]
        zpres = []
        for u in range(GB):
            tu = t[u * half : (u + 1) * half]
            zpres.append(jnp.sum(tu * q, axis=0, keepdims=True))
            total = total + tu * tab_ref[0, pl.ds(gs[u], 1), :]
        gq_acc[here, :] = total
        qm = jnp.concatenate([(qt_ref[:, here] * pre).astype(BF16) for pre, _ in cols], 1)
        gk_acc[:, :keys] += dot_nn(qm, gm)
        gm2 = jnp.concatenate([(got_ref[:, here] * post).astype(BF16) for _, post in cols], 1)
        gv_acc[:, :keys] += dot_nn(gm2, jnp.concatenate(ps, 0))
        return zpres, zposts

    for pairs in range(1, blocks + 1):
        is_late = at == blocks - pairs

        @pl.when(is_late | (at == pairs - 1))
        def _(pairs=pairs, is_late=is_late):
            zpres, zposts = work(is_late.astype(jnp.int32), 2 * pairs * half)
            for u, g in enumerate(gs):
                zpre_ref[pl.ds(g, 1), :] += zpres[u]
                zpost_ref[pl.ds(g, 1), :] += zposts[u]

    @pl.when(step == pl.num_programs(0) - 1)
    def _():
        for copy in late:
            copy.wait()
        gq = gq_acc[...].astype(BF16)
        gkt = gk_acc[...].astype(BF16)
        gvt = gv_acc[...].astype(BF16)
        ga = ga_ref[...]
        for r in range(blocks):
            there = [pl.ds(pl.multiple_of(chunk_of(at ^ r, x, blocks, False) * half, half), half) for x in range(2)]
            gk = jnp.concatenate([gk_acc[:, x].T.astype(BF16) for x in there], 0)
            gv = jnp.concatenate([gv_acc[:, x].T.astype(BF16) for x in there], 0)
            gn1 = dot_nt(gk, wqkv_ref[:, width : 2 * width]) + dot_nt(gv, wqkv_ref[:, 2 * width :])
            if r == 0:
                gn1 = gn1 + dot_nt(gq, wqkv_ref[:, :width])
            gn1_refs[r][...] = gn1.astype(BF16)
        hand = width // 2
        per = hand // PIECES
        own = [pl.ds(pl.multiple_of(chunk_of(at, x, blocks, False) * half, half), half) for x in range(2)]
        for side in range(2):
            core = place_ref[0] if side == 0 else 1 - place_ref[0]
            mine = pl.ds(pl.multiple_of(core * hand, hand), hand)
            n1t = n1t_ref[mine, :]
            n1t_own = jnp.concatenate([n1t_ref[mine, x] for x in own], 1)
            grads = (
                lambda: dot_nn(n1t_own, gq),
                lambda: dot_nt(n1t, gkt),
                lambda: dot_nt(n1t, gvt),
                lambda: dot_nn(ot_ref[mine, :], ga),
            )
            for index, grad in enumerate(grads):
                part = index * parts // len(grads)
                column = (index - part * (len(grads) // parts)) * width
                value = grad().astype(BF16)
                for piece in range(PIECES):
                    there = pl.multiple_of((piece ^ place_ref[1 + part]) * per, per)
                    grad_refs[2 * part + side][pl.ds(there, per), column : column + width] = value[
                        piece * per : (piece + 1) * per
                    ]


def attn_bwd(layer, blocks, ga, w_out, q, k, v, p, u, tab, tabt, place, w_qkv, n1t, ot):
    rows, width = q.shape
    keys = k.shape[0]
    heads = p.shape[0]
    parts = place.shape[0] - 2
    args = (ga, w_out, q, k, v, p, u, tab, tabt, place, w_qkv, n1t, ot)
    in_specs = [whole(a.shape) for a in args]
    in_specs[1] = layer_of(w_out, layer)
    in_specs[5] = pl.BlockSpec((GB, rows, keys), lambda i: (i, 0, 0))
    in_specs[6] = pl.BlockSpec((GB, rows, width), lambda i: (i, 0, 0))
    in_specs[7] = layer_of(tab, layer)
    in_specs[8] = layer_of(tabt, layer)
    in_specs[9] = pl.BlockSpec(memory_space=pltpu.SMEM)
    in_specs[10:13] = [pl.BlockSpec(memory_space=pl.ANY)] * 3
    out = (
        [((rows, width), BF16)] * blocks
        + [((width // 2, 4 // parts * width), BF16)] * (2 * parts)
        + [((heads, width), F32)] * 2
    )
    res = pl.pallas_call(
        functools.partial(attn_bwd_body, heads, blocks, layer, parts),
        grid=(heads // GB,),
        in_specs=in_specs,
        out_specs=[whole(s) for s, _ in out],
        out_shape=[jax.ShapeDtypeStruct(s, d) for s, d in out],
        scratch_shapes=[
            pltpu.VMEM((rows, width), F32),
            pltpu.VMEM((width, rows), F32),
            pltpu.VMEM((width, rows), F32),
            pltpu.VMEM((rows, width), F32),
            pltpu.VMEM((width, keys), F32),
            pltpu.VMEM((width, keys), F32),
            pltpu.VMEM(w_qkv.shape[1:], BF16),
            pltpu.VMEM(n1t.shape, BF16),
            pltpu.VMEM(ot.shape, BF16),
            pltpu.SemaphoreType.DMA((3,)),
        ],
        compiler_params=pltpu.CompilerParams(vmem_limit_bytes=VMEM),
        cost_estimate=pl.CostEstimate(
            flops=2 * rows * keys * width * heads * 4 * 2, bytes_accessed=20_000_000, transcendentals=0
        ),
        name="attn_bwd",
    )(*args)
    return res[:blocks], res[blocks:-2], res[-2], res[-1]


def expand_body(parts, place_ref, *refs):
    qkv_ref, out_ref = refs[-2:]
    width3 = qkv_ref.shape[2]
    inner = PIECES // GROUPS
    per = qkv_ref.shape[1] // inner
    column = 0
    for part, ref in enumerate(refs[:parts]):
        end = column + ref.shape[1]
        cut = min(end, width3)
        for piece in range(inner):
            here = slice(piece * per, (piece + 1) * per)
            there = piece ^ lax.rem(place_ref[1 + part], inner)
            value = ref[pl.ds(pl.multiple_of(there * per, per), per), :].astype(F32)
            qkv_ref[0, here, column:cut] = value[:, : cut - column]
            if end > width3:
                out_ref[0, here, :] = value[:, cut - column :]
        column = end


def expand(layer, side, place, halves, before=()):
    half = halves[0].shape[0]
    width = sum(h.shape[1] for h in halves) // 4
    per = half // GROUPS
    in_specs = []
    for part, array in enumerate(halves):

        def piece(i, place, part=part):
            return i ^ (place[1 + part] // (PIECES // GROUPS)), 0

        in_specs.append(pl.BlockSpec((per, array.shape[1]), piece))
    first = 1 + len(halves)
    in_specs += [pl.BlockSpec(memory_space=pl.ANY)] * len(before)

    def there(i, place):
        return layer, (place[0] ^ side) * GROUPS + i, 0

    return pl.pallas_call(
        functools.partial(expand_body, len(halves)),
        grid_spec=pltpu.PrefetchScalarGridSpec(
            num_scalar_prefetch=1,
            grid=(GROUPS,),
            in_specs=in_specs,
            out_specs=[pl.BlockSpec((1, per, 3 * width), there), pl.BlockSpec((1, per, width), there)],
        ),
        out_shape=[
            jax.ShapeDtypeStruct((LAYERS, 2 * half, 3 * width), F32),
            jax.ShapeDtypeStruct((LAYERS, 2 * half, width), F32),
        ],
        input_output_aliases={first + i: i for i in range(len(before))},
        compiler_params=pltpu.CompilerParams(vmem_limit_bytes=SMALL),
        cost_estimate=pl.CostEstimate(flops=0, bytes_accessed=7_000_000, transcendentals=0),
        name="expand",
    )(place, *halves, *before)


def ffn_fwd_body(blocks, *refs):
    n_refs = refs[:blocks]
    win_ref, wdown_ref = refs[blocks : blocks + 2]
    out_refs = refs[blocks + 2 : 2 * blocks + 2]
    hid_ref, dgelu_ref = refs[2 * blocks + 2 :]
    rows = n_refs[0].shape[0]
    for r in range(blocks):
        here = pl.ds(r * rows, rows)
        pre = dot_nn(n_refs[r][...], win_ref[0])
        cdf = 0.5 + 0.5 * lax.erf(pre * (0.5**0.5))
        hid = (pre * cdf).astype(BF16)
        hid_ref[here, :] = hid
        density = jnp.exp2(pre * pre * (-0.5 * LOG2E)) * 0.3989422804014327
        dgelu_ref[here, :] = (cdf + pre * density).astype(BF16)
        out_refs[r][...] = dot_nn(hid, wdown_ref[0]).astype(BF16)


def ffn_fwd(layer, n_blocks, w_in, w_down):
    blocks = len(n_blocks)
    rows, width = n_blocks[0].shape
    hidden = w_in.shape[2]
    args = (*n_blocks, w_in, w_down)
    in_specs = [whole(a.shape) for a in args]
    in_specs[blocks] = layer_of(w_in, layer)
    in_specs[blocks + 1] = layer_of(w_down, layer)
    out = [((rows, width), BF16)] * blocks + [((rows * blocks, hidden), BF16)] * 2
    res = pl.pallas_call(
        functools.partial(ffn_fwd_body, blocks),
        grid=(1,),
        in_specs=in_specs,
        out_specs=[whole(s) for s, _ in out],
        out_shape=[jax.ShapeDtypeStruct(s, d) for s, d in out],
        compiler_params=pltpu.CompilerParams(vmem_limit_bytes=SMALL),
        cost_estimate=pl.CostEstimate(
            flops=4 * rows * blocks * width * hidden, bytes_accessed=6_000_000, transcendentals=rows * blocks * hidden
        ),
        name="ffn_fwd",
    )(*args)
    return res[:blocks], res[blocks], res[blocks + 1]


def ffn_bwd_body(blocks, *refs):
    g_refs = refs[:blocks]
    dgelu_ref, win_ref, wdown_ref = refs[blocks : blocks + 3]
    out_refs = refs[blocks + 3 : 2 * blocks + 3]
    gpre_ref = refs[2 * blocks + 3]
    rows = g_refs[0].shape[0]
    for r in range(blocks):
        here = pl.ds(r * rows, rows)
        gh = dot_nt(g_refs[r][...], wdown_ref[0])
        gpre = (gh * dgelu_ref[here, :].astype(F32)).astype(BF16)
        gpre_ref[here, :] = gpre
        out_refs[r][...] = dot_nt(gpre, win_ref[0]).astype(BF16)


def ffn_bwd(layer, g_blocks, dgelu, w_in, w_down):
    blocks = len(g_blocks)
    rows, width = g_blocks[0].shape
    hidden = w_in.shape[2]
    args = (*g_blocks, dgelu, w_in, w_down)
    in_specs = [whole(a.shape) for a in args]
    in_specs[blocks + 1] = layer_of(w_in, layer)
    in_specs[blocks + 2] = layer_of(w_down, layer)
    out = [((rows, width), BF16)] * blocks + [((rows * blocks, hidden), BF16)]
    res = pl.pallas_call(
        functools.partial(ffn_bwd_body, blocks),
        grid=(1,),
        in_specs=in_specs,
        out_specs=[whole(s) for s, _ in out],
        out_shape=[jax.ShapeDtypeStruct(s, d) for s, d in out],
        compiler_params=pltpu.CompilerParams(vmem_limit_bytes=SMALL),
        cost_estimate=pl.CostEstimate(
            flops=4 * rows * blocks * width * hidden, bytes_accessed=6_000_000, transcendentals=0
        ),
        name="ffn_bwd",
    )(*args)
    return res[:blocks], res[blocks]


def ffn_grads_body(blocks, chunks, *refs):
    n_refs, g_refs = refs[:blocks], refs[blocks : 2 * blocks]
    hid_refs, gpre_refs = refs[2 * blocks : 2 * blocks + 2], refs[2 * blocks + 2 : 2 * blocks + 4]
    out_ref = refs[-1]
    rows, width = n_refs[0].shape
    per = width // chunks
    for part, (left_refs, right_refs) in enumerate(((n_refs, gpre_refs), (g_refs, hid_refs))):
        left = jnp.concatenate([ref[...].T for ref in left_refs], 1)
        right = jnp.concatenate([ref[...] for ref in right_refs], 0)
        grad = dot_nn(left, right).astype(BF16)
        for c in range(chunks):
            place = 2 * sum(((c >> i) & 1) * (chunks >> (i + 1)) for i in range(chunks.bit_length() - 1)) + part
            out_ref[place * per : (place + 1) * per, :] = grad[c * per : (c + 1) * per]


def ffn_grads(n_blocks, g_blocks, hids, gpres, chunks):
    blocks = len(n_blocks)
    rows, width = n_blocks[0].shape
    hidden = hids[0].shape[1]
    args = (*n_blocks, *g_blocks, *hids, *gpres)
    return pl.pallas_call(
        functools.partial(ffn_grads_body, blocks, chunks),
        grid=(1,),
        in_specs=[whole(a.shape) for a in args],
        out_specs=whole((2 * width, hidden)),
        out_shape=jax.ShapeDtypeStruct((2 * width, hidden), BF16),
        compiler_params=pltpu.CompilerParams(vmem_limit_bytes=VMEM),
        cost_estimate=pl.CostEstimate(
            flops=4 * rows * blocks * width * hidden, bytes_accessed=9_000_000, transcendentals=0
        ),
        name="ffn_grads",
    )(*args)


def swap(value, axis, bit):
    size = lax.axis_size(axis)
    return lax.ppermute(value, axis, [(i, i ^ bit) for i in range(size)])


def after(values, *done):
    return lax.optimization_barrier((values, done))[0]


def gather_near(value):
    half = lax.axis_size("tp") // 2
    far = swap(value, "tp", half)
    near = [value]
    bit = 1
    while bit < half:
        near += [swap(b, "tp", bit) for b in near]
        bit *= 2
    return near, far


def gather_far(far):
    half = lax.axis_size("tp") // 2
    blocks = [far]
    bit = 1
    while bit < half:
        blocks += [swap(b, "tp", bit) for b in blocks]
        bit *= 2
    return blocks


def gather_blocks(value):
    near, far = gather_near(value)
    return near + gather_far(far)


def scatter_begin(blocks):
    blocks = list(blocks)
    bit = 1
    while bit < lax.axis_size("tp") // 2:
        size = len(blocks)
        keep = [blocks[r] for r in range(size) if not r & 1]
        sent = [swap(blocks[r], "tp", bit) for r in range(size) if r & 1]
        blocks = [a.astype(F32) + b.astype(F32) for a, b in zip(keep, sent)]
        bit *= 2
        blocks = [blocks[0]] + [b.astype(BF16) for b in blocks[1:]]
    return blocks[0].astype(F32), swap(blocks[1], "tp", bit)


def halve_begin(part, axis, bit):
    mine = (lax.axis_index(axis) // bit) & 1
    pair = part.reshape(2, part.shape[0] // 2, part.shape[1])
    sent = lax.dynamic_index_in_dim(pair, 1 - mine, 0, keepdims=False)
    kept = lax.dynamic_index_in_dim(pair, mine, 0, keepdims=False)
    return kept, swap(sent, axis, bit)


def halve_end(kept, got):
    return (kept.astype(F32) + got.astype(F32)).astype(BF16)


class Scatter:
    def __init__(self, parts, steps):
        self.steps = list(steps)
        self.begin(parts)

    def begin(self, parts):
        step = self.steps.pop(0)
        self.kept, self.got = zip(*[halve_begin(part, *step) for part in parts])

    def advance(self, *done):
        if self.steps:
            got = after(self.got, *done)
            self.begin([halve_end(a, b) for a, b in zip(self.kept, got)])

    def finish(self, *done):
        while self.steps:
            self.advance(*done)
        return [a.astype(F32) + b.astype(F32) for a, b in zip(self.kept, after(self.got, *done))]


def steps_of(axis):
    return [(axis, 1 << i) for i in range(lax.axis_size(axis).bit_length() - 1)]


HALVINGS = PIECES.bit_length() - 1


def place_of(order):
    number = 0
    for axis, bit in order[:HALVINGS]:
        number = 2 * number + ((lax.axis_index(axis) // bit) & 1)
    return number


def sum_start(part, order, stage):
    if stage < HALVINGS:
        rows = part.shape[0] // 2
        return part[:rows], swap(part[rows:], *order[stage])
    return part, swap(part, *order[stage])


def spread(part, got):
    return jnp.concatenate([part, got], 0)


class Butterfly:
    def __init__(self, value):
        self.value = value
        self.steps = steps_of("tp") + steps_of("dp")
        self.got = None

    def start(self):
        if self.steps:
            self.got = swap(self.value, *self.steps.pop(0))
            return [self.got]
        return []

    def end(self, got):
        for g in got:
            self.value = self.value + g


def on_device(
    x_in, segments, w_qkv, w_out, mix_pre, mix_post, gain_attn, gain_ffn, w_in, w_down, cotangent
):
    rows, _, width = x_in.shape
    heads = mix_pre.shape[1]
    head_size = width // heads
    tp_size = lax.axis_size("tp")
    dp_size = lax.axis_size("dp")
    tp_index = lax.axis_index("tp")
    seg = segments[:, 0]
    side = rows // 2
    span = jnp.arange(side, dtype=jnp.int32)
    starts = [chunk_of(tp_index, x, tp_size, False) * side for x in range(2)]
    qpos = jnp.concatenate([start + span for start in starts])
    qseg = jnp.concatenate([lax.dynamic_slice_in_dim(seg, start, side, 0) for start in starts])
    qinfo = jnp.stack([qpos, qseg] + [qpos] * 6, 1)
    kinfo = jnp.pad(jnp.stack([jnp.arange(seg.shape[0], dtype=jnp.int32), seg]), ((0, 6), (0, 0)))
    where = (qinfo, kinfo, tp_index[None])

    def mirror(value):
        moved = lax.ppermute(value[side:], "tp", [(i, tp_size - 1 - i) for i in range(tp_size)])
        return value[:side], moved

    tab = jnp.concatenate([jnp.swapaxes(mix_pre, 1, 2) * (head_size**-0.5), mix_post], 1)
    tabt = jnp.pad(jnp.repeat(jnp.swapaxes(tab, 1, 2), head_size, axis=1), ((0, 0), (0, 0), (0, 128 - 2 * heads)))
    tab = jnp.repeat(tab, head_size, axis=2)

    stream = x_in[:, 0].astype(F32)
    x_folded = jnp.concatenate(mirror(x_in[:, 0]), 0).astype(F32)
    kept = []
    half = tp_size // 2
    for layer in range(LAYERS):
        last = layer == LAYERS - 1
        n1_blocks = gather_blocks(rms(stream, gain_attn[layer]).astype(BF16))
        if last:
            low, n1_blocks[half] = after((cotangent[:, 0], n1_blocks[half]))
            grad_near, grad_far = gather_near(low)
        else:
            stream = x_folded
        p, u, q, k, v, ot, n1t, middle, n2 = attn_fwd(
            layer,
            layer == 0,
            n1_blocks,
            stream,
            w_qkv,
            w_out,
            tab,
            gain_ffn,
            where,
        )
        if last:
            n2, grad_near, grad_far = after((n2, grad_near, grad_far))
        near, far = gather_near(n2)
        out_a, hid_a, dgelu_a = ffn_fwd(layer, near, w_in, w_down)
        if last:
            given = grad_near + gather_far(grad_far)
            gf_blocks = [jnp.concatenate([given[r][:side], given[tp_size - 1 - r][side:]], 0) for r in range(tp_size)]
            gn2_a, gpre_a = ffn_bwd(layer, gf_blocks[:half], dgelu_a, w_in, w_down)
            far, gpre_a = after((far, gpre_a))
        far, hid_a = after((far, hid_a))
        n2_blocks = near + gather_far(far)
        out_b, hid_b, dgelu_b = ffn_fwd(layer, n2_blocks[half:], w_in, w_down)
        kept.append((stream, n1t, p, u, q, k, v, ot, middle, n2_blocks, hid_a, hid_b, dgelu_a, dgelu_b))
        if not last:
            own, far = scatter_begin([*out_a, *out_b])
            stream = middle + (own + far.astype(F32))

    grad_flow = gf_blocks[0].astype(F32)
    per = width // dp_size
    small = [None] * LAYERS
    sharded = [None] * LAYERS
    for layer in range(LAYERS - 1, -1, -1):
        last = layer == LAYERS - 1
        stream, n1t, p, u, q, k, v, ot, middle, n2_blocks, hid_a, hid_b, dgelu_a, dgelu_b = kept[layer]
        if not last:
            near, far = gather_near(grad_flow.astype(BF16))
            gn2_a, gpre_a = ffn_bwd(layer, near, dgelu_a, w_in, w_down)
            far, gpre_a, moving.got = after((far, gpre_a, moving.got))
            moving.advance()
            gf_blocks = near + gather_far(far)
        gn2_b, gpre_b = ffn_bwd(layer, gf_blocks[half:], dgelu_b, w_in, w_down)
        if not last:
            total_got, gpre_b = after((total_got, gpre_b))
            total = halve_end(total_kept, total_got)
            total_kept, total_got = sum_start(total, total_order, 1)
        own, far = scatter_begin([*gn2_a, *gn2_b])
        packed = ffn_grads(n2_blocks, gf_blocks, (hid_a, hid_b), (gpre_a, gpre_b), dp_size)
        far, packed = after((far, packed))
        if not last:
            total_got, packed = after((total_got, packed))
            total = halve_end(total_kept, total_got)
            total_kept, total_got = sum_start(total, total_order, 2)
        if not last:
            previous = moving
        moving = Scatter([packed], steps_of("dp"))
        gn2 = (own + far.astype(F32)).astype(BF16).astype(F32)
        grad_norm, grad_gffn = rms_back(gn2, middle, gain_ffn[layer])
        grad_middle = grad_flow + grad_norm
        ga = grad_middle.astype(BF16)
        if last:
            orders = [steps_of("dp") + steps_of("tp")[1:]]
        else:
            (y_step, *dp_rest), x_steps = steps_of("dp"), steps_of("tp")[1:]
            orders = [x_steps + [y_step] + dp_rest, [y_step] + x_steps + dp_rest]
        place = jnp.stack([tp_index & 1] + [place_of(order) for order in orders] + [tp_index])
        parts, grads, zpre, zpost = attn_bwd(
            layer, tp_size, ga, w_out, q, k, v, p, u, tab, tabt, place, w_qkv, n1t, ot
        )
        core_step = steps_of("tp")[0]
        if last:
            parts, grads, moving.got = after((parts, grads, moving.got))
            y_middle = middle
            keep, send = grads
            total = halve_end(keep, swap(send, *core_step))
            own, far = scatter_begin(parts)
            moving.advance()
            far = after(far, total)
            (total_order,), total_place = orders, place
            total_kept, total_got = sum_start(total, total_order, 0)
        else:
            parts, grads, moving.got, total_got, previous.got = after(
                (parts, grads, moving.got, total_got, previous.got)
            )
            (summed,) = previous.finish()
            sharded[layer + 1] = (summed[:per], summed[per:].T)
        if not last:
            break
        gn1 = (own + far.astype(F32)).astype(BF16).astype(F32)
        grad_norm, grad_gattn = rms_back(gn1, stream, gain_attn[layer])
        grad_flow = grad_middle + grad_norm
        grad_mpre = jnp.sum(zpre.reshape(heads, heads, head_size), -1).T * (head_size**-0.5)
        grad_mpost = jnp.sum(zpost.reshape(heads, heads, head_size), -1)
        small[layer] = (grad_mpre, grad_mpost, grad_gattn, grad_gffn)

    total = halve_end(total_kept, total_got)
    grads, total = after((grads, total))
    got = [swap(send, *core_step) for send in grads[1::2]]
    pieces = [halve_end(keep, g) for keep, g in zip(grads[::2], got)]
    for stage in range(HALVINGS, len(total_order)):
        total_got = swap(total, *total_order[stage])
        pieces, total_got = after((pieces, total_got))
        total = halve_end(total, total_got)
    for stage in range(HALVINGS):
        kept, got = zip(*[sum_start(part, order, stage) for part, order in zip(pieces, orders)])
        if stage == 0:
            by_last, by_middle = [swap(total, *step) for step in total_order[HALVINGS - 1 : 0 : -1]]
            got, by_last, by_middle = after((got, by_last, by_middle))
            near_rows = spread(total, by_last)
        elif stage == 1:
            near_got = swap(near_rows, *total_order[0])
            by_both = swap(by_last, *total_order[1])
            got, by_both = after((got, by_both))
            far_rows = spread(by_middle, by_both)
        else:
            total_got = swap(far_rows, *total_order[0])
            got, near_got = after((got, near_got))
        if stage == HALVINGS - 1:
            got, far = after((got, far))
        pieces = [halve_end(a, b) for a, b in zip(kept, after(got))]
        if stage == HALVINGS - 1:
            gn1 = (own + far.astype(F32)).astype(BF16).astype(F32)
            grad_norm, grad_gattn = rms_back(gn1, stream, gain_attn[layer])
            grad_flow = grad_middle + grad_norm
            grad_mpre = jnp.sum(zpre.reshape(heads, heads, head_size), -1).T * (head_size**-0.5)
            grad_mpost = jnp.sum(zpost.reshape(heads, heads, head_size), -1)
            small[layer] = (grad_mpre, grad_mpost, grad_gattn, grad_gffn)
            mixes = jnp.concatenate([a.reshape(-1) for s in small for a in s[:2]])
            count = mixes.shape[0]
            mix_rows = -(-count // width)
            flat = jnp.concatenate(
                [jnp.pad(mixes, (0, mix_rows * width - count)).reshape(mix_rows, width)]
                + [g[None] for s in small for g in s[2:]]
            )
            flat = jnp.pad(flat, ((0, -flat.shape[0] % 8), (0, 0)))
            flat = Butterfly(flat)
        if stage == 1:
            moving.advance(*pieces)
            y_parts, parts, pieces = after(([*out_a, *out_b], parts, pieces))
            own, far = scatter_begin(parts)
            own_y, far_y = scatter_begin(y_parts)
    for stage in range(HALVINGS, len(orders[0])):
        got = [swap(part, *order[stage]) for part, order in zip(pieces, orders)]
        if stage == HALVINGS:
            flat.end(flat.start())
        flat_got = flat.start()
        if stage == HALVINGS:
            first_rows, second_rows = mirror(grad_flow)
            got, second_rows, total_got, moving.got, far_y = after((got, second_rows, total_got, moving.got, far_y))
            y_out = (y_middle + (own_y + far_y.astype(F32))).astype(BF16)
            y_first, y_second = mirror(y_out)
            grad_x = jnp.concatenate([first_rows, second_rows], 0)
            total = jnp.concatenate([near_rows, far_rows, near_got, total_got], 0)
            moving.advance()
        got, flat_got = after((got, flat_got))
        flat.end(flat_got)
        pieces = [halve_end(a, b) for a, b in zip(pieces, got)]
    total_other = swap(total, *core_step)
    replicated = ()
    for stage in range(HALVINGS - 1, -1, -1):
        got = [swap(part, *order[stage]) for part, order in zip(pieces, orders)]
        flat_got = flat.start()
        if stage == HALVINGS - 1:
            got, total_other = after((got, total_other))
        elif stage == HALVINGS - 2:
            replicated = expand(1, 0, total_place, [total])
            got, replicated, moving.got, y_second = after((got, replicated, moving.got, y_second))
            y_out = jnp.concatenate([y_first, y_second], 0)[:, None]
            (summed,) = moving.finish()
            sharded[0] = (summed[:per], summed[per:].T)
            sharded = [jnp.stack(members) for members in zip(*sharded)]
            grad_x = grad_x[:, None]
        elif stage == 0:
            replicated = expand(1, 1, total_place, [total_other], replicated)
            got, replicated, sharded, grad_x, y_out = after((got, replicated, sharded, grad_x, y_out))
        got, flat_got = after((got, flat_got))
        flat.end(flat_got)
        pieces = [spread(a, b) for a, b in zip(pieces, got)]
    got = [swap(part, *core_step) for part in pieces]
    while flat.steps:
        flat.end(flat.start())
    flat = flat.value
    replicated = expand(0, 0, place, pieces, replicated)
    got, replicated = after((got, replicated))
    replicated = expand(0, 1, place, got, replicated)
    mixes = flat[:mix_rows].reshape(-1)[:count].reshape(LAYERS, 2, heads, heads)
    gains = flat[mix_rows : mix_rows + 2 * LAYERS].reshape(LAYERS, 2, width)
    return (
        y_out,
        grad_x,
        *replicated,
        mixes[:, 0],
        mixes[:, 1],
        gains[:, 0],
        gains[:, 1],
        *sharded,
    )


def solution(mesh):
    in_specs = (
        P("tp", "dp", None),
        P(None, "dp"),
        P(),
        P(),
        P(),
        P(),
        P(),
        P(),
        P(None, None, "tp"),
        P(None, "tp", None),
        P("tp", "dp", None),
    )
    out_specs = (
        P("tp", "dp", None),
        P("tp", "dp", None),
        P(),
        P(),
        P(),
        P(),
        P(),
        P(),
        P(None, "dp", "tp"),
        P(None, "tp", "dp"),
    )
    return jax.shard_map(
        on_device, mesh=mesh, in_specs=in_specs, out_specs=out_specs, check_vma=False
    )
```

```python
import functools

import jax
import jax.numpy as jnp
from jax import lax
from jax.experimental import pallas as pl
from jax.experimental.pallas import tpu as pltpu
from jax.sharding import PartitionSpec as P

LAYERS = 2
EPSILON = 1e-06
NEGATIVE = -1e30
LOG2E = 1.4426950408889634
GROUPS = 4
PIECES = 8
GP = 4
GB = 4
VMEM = 60 * 1024 * 1024
SMALL = 18 * 1024 * 1024
F32 = jnp.float32
BF16 = jnp.bfloat16


def dot_nn(a, b):
    return lax.dot_general(a, b, (((1,), (0,)), ((), ())), preferred_element_type=F32)


def dot_nt(a, b):
    return lax.dot_general(a, b, (((1,), (1,)), ((), ())), preferred_element_type=F32)


def dot_tn(a, b):
    return lax.dot_general(a, b, (((0,), (0,)), ((), ())), preferred_element_type=F32)


def rms(values, gain):
    return values * lax.rsqrt(jnp.mean(values * values, -1, keepdims=True) + EPSILON) * gain


def rms_back(grad, values, gain):
    inv = lax.rsqrt(jnp.mean(values * values, -1, keepdims=True) + EPSILON)
    unit = values * inv
    scaled = grad * gain
    grad_values = (scaled - unit * jnp.mean(scaled * unit, -1, keepdims=True)) * inv
    return grad_values, jnp.sum(grad * unit, axis=0)


def whole(shape):
    return pl.BlockSpec(shape, lambda *_: (0,) * len(shape))


def layer_of(array, layer):
    shape = array.shape[1:]
    return pl.BlockSpec((1,) + shape, lambda *_: (layer,) + (0,) * len(shape))


def attn_fwd_body(blocks, heads, layer, plain, *refs):
    n_refs = refs[:blocks]
    x_hbm, wqkv_hbm, wout_hbm, tab_ref, gain_ref, qinfo_ref, kinfo_ref, at_ref = refs[blocks : blocks + 8]
    p_ref, u_ref, q_ref, k_hbm, v_hbm, ot_ref, n1t_hbm, xm_ref, n2_ref = refs[blocks + 8 : blocks + 17]
    bias_ref, acc_ref, k_ref, v_ref, n1t_ref, x_ref, wqkv_ref, wout_ref, sems = refs[blocks + 17 :]
    step = pl.program_id(0)
    rows, width = x_ref.shape
    q_cols, k_cols, v_cols = [slice(i * width, (i + 1) * width) for i in range(3)]
    weights = [
        pltpu.make_async_copy(wqkv_hbm.at[layer, :, cols], wqkv_ref.at[i], sems.at[i])
        for i, cols in enumerate((k_cols, v_cols, q_cols))
    ]
    last_used = [
        pltpu.make_async_copy(wout_hbm.at[layer], wout_ref, sems.at[3]),
        pltpu.make_async_copy(x_hbm, x_ref, sems.at[4]),
    ]
    early = [
        pltpu.make_async_copy(k_ref, k_hbm, sems.at[5]),
        pltpu.make_async_copy(v_ref, v_hbm, sems.at[6]),
    ]
    turned = pltpu.make_async_copy(n1t_ref, n1t_hbm, sems.at[7])
    half = rows // 2
    at = at_ref[0]

    def place(r, second):
        block = chunk_of(at ^ r, second, blocks, plain)
        return pl.ds(pl.multiple_of(block * half, half), half)

    @pl.when(step == 0)
    def _():
        for copy in weights + last_used:
            copy.start()
        for i, ref in enumerate((k_ref, v_ref)):
            weights[i].wait()
            for r in range(blocks):
                value = dot_nn(n_refs[r][...], wqkv_ref[i]).astype(BF16)
                ref[place(r, 0), :] = value[:half]
                ref[place(r, 1), :] = value[half:]
            early[i].start()
        weights[2].wait()
        n_second = n_refs[blocks - 1 if plain else 0]
        q_ref[:half] = dot_nn(n_refs[0][:half], wqkv_ref[2]).astype(BF16)
        q_ref[half:] = dot_nn(n_second[half:], wqkv_ref[2]).astype(BF16)
        ok = (qinfo_ref[:, 1:2] == kinfo_ref[1:2, :]) & (kinfo_ref[0:1, :] <= qinfo_ref[:, 0:1])
        bias_ref[...] = jnp.where(ok, 0.0, NEGATIVE)
        acc_ref[...] = jnp.zeros_like(acc_ref)

    def work(second, keys):
        here = pl.ds(pl.multiple_of(second * half, half), half)
        q = q_ref[here, :].astype(F32)
        gs = [step * GP + u for u in range(GP)]
        qm = jnp.concatenate([(q * (tab_ref[0, pl.ds(g, 1), :] * LOG2E)).astype(BF16) for g in gs], 0)
        m = dot_nt(qm, k_ref[:keys, :])
        bias = bias_ref[here, :keys]
        ps = []
        for u in range(GP):
            mu = m[u * half : (u + 1) * half] + bias
            e = jnp.exp2(mu - jnp.max(mu, -1, keepdims=True))
            p = (e * (1.0 / jnp.sum(e, -1, keepdims=True))).astype(BF16)
            p_ref[u, here, :keys] = p
            ps.append(p)
        ctx = dot_nn(jnp.concatenate(ps, 0), v_ref[:keys, :])
        total = acc_ref[here, :]
        for u in range(GP):
            cu = ctx[u * half : (u + 1) * half]
            u_ref[u, here, :] = cu.astype(BF16)
            total = total + cu * tab_ref[0, pl.ds(heads + gs[u], 1), :]
        acc_ref[here, :] = total

    for pairs in range(1, blocks + 1):
        late = at == blocks - pairs

        @pl.when(late | (at == pairs - 1))
        def _(pairs=pairs, late=late):
            work(late.astype(jnp.int32), 2 * pairs * half)

    @pl.when(step == 0)
    def _():
        for r in range(blocks):
            for second in range(2):
                n1t_ref[:, place(r, second)] = n_refs[r][second * half : (second + 1) * half, :].T
        turned.start()

    @pl.when(step == pl.num_programs(0) - 1)
    def _():
        o = acc_ref[...].astype(BF16)
        ot_ref[...] = o.T
        for copy in last_used + early + [turned]:
            copy.wait()
        xm = x_ref[...] + dot_nn(o, wout_ref[...])
        xm_ref[...] = xm
        n2_ref[...] = rms(xm, gain_ref[pl.ds(layer, 1), :]).astype(BF16)


def chunk_of(device, second, devices, plain):
    if not second:
        return 2 * device
    return 2 * device + 1 if plain else 2 * (devices - 1 - device) + 1


def attn_fwd(layer, plain, n_blocks, x, w_qkv, w_out, tab, gain, where):
    rows, width = x.shape
    blocks = len(n_blocks)
    heads = tab.shape[1] // 2
    keys = rows * blocks
    args = (*n_blocks, x, w_qkv, w_out, tab, gain, *where)
    in_specs = [whole(a.shape) for a in args]
    in_specs[blocks : blocks + 3] = [pl.BlockSpec(memory_space=pl.ANY)] * 3
    in_specs[blocks + 3] = layer_of(tab, layer)
    in_specs[-1] = pl.BlockSpec(memory_space=pltpu.SMEM)
    out = [
        ((heads, rows, keys), BF16),
        ((heads, rows, width), BF16),
        ((rows, width), BF16),
        ((keys, width), BF16),
        ((keys, width), BF16),
        ((width, rows), BF16),
        ((width, keys), BF16),
        ((rows, width), F32),
        ((rows, width), BF16),
    ]
    out_specs = [whole(s) for s, _ in out]
    out_specs[0] = pl.BlockSpec((GP, rows, keys), lambda i: (i, 0, 0))
    out_specs[1] = pl.BlockSpec((GP, rows, width), lambda i: (i, 0, 0))
    for i in (3, 4, 6):
        out_specs[i] = pl.BlockSpec(memory_space=pltpu.HBM)
    return pl.pallas_call(
        functools.partial(attn_fwd_body, blocks, heads, layer, plain),
        grid=(heads // GP,),
        in_specs=in_specs,
        out_specs=out_specs,
        out_shape=[jax.ShapeDtypeStruct(s, d) for s, d in out],
        scratch_shapes=[
            pltpu.VMEM((rows, keys), F32),
            pltpu.VMEM((rows, width), F32),
            pltpu.VMEM((keys, width), BF16),
            pltpu.VMEM((keys, width), BF16),
            pltpu.VMEM((width, keys), BF16),
            pltpu.VMEM((rows, width), F32),
            pltpu.VMEM((3, width, width), BF16),
            pltpu.VMEM((width, width), BF16),
            pltpu.SemaphoreType.DMA((8,)),
        ],
        compiler_params=pltpu.CompilerParams(vmem_limit_bytes=VMEM),
        cost_estimate=pl.CostEstimate(
            flops=2 * rows * keys * width * heads * 2, bytes_accessed=20_000_000, transcendentals=rows * keys * heads
        ),
        name="attn_fwd",
    )(*args)


def attn_bwd_body(heads, blocks, layer, parts, *refs):
    (ga_ref, wout_ref, q_ref, k_ref, v_ref, p_ref, u_ref, tab_ref, tabt_ref, place_ref) = refs[:10]
    wqkv_hbm, n1t_hbm, ot_hbm = refs[10:13]
    gn1_refs = refs[13 : 13 + blocks]
    grad_refs = refs[13 + blocks : 13 + blocks + 2 * parts]
    zpre_ref, zpost_ref = refs[13 + blocks + 2 * parts : 15 + blocks + 2 * parts]
    go_ref, got_ref, qt_ref, gq_acc, gk_acc, gv_acc, wqkv_ref, n1t_ref, ot_ref, sems = refs[15 + blocks + 2 * parts :]
    step = pl.program_id(0)
    rows, width = q_ref.shape

    late = [
        pltpu.make_async_copy(wqkv_hbm.at[layer], wqkv_ref, sems.at[0]),
        pltpu.make_async_copy(n1t_hbm, n1t_ref, sems.at[1]),
        pltpu.make_async_copy(ot_hbm, ot_ref, sems.at[2]),
    ]

    @pl.when(step == 0)
    def _():
        for copy in late:
            copy.start()
        go = dot_nt(ga_ref[...], wout_ref[0]).astype(BF16).astype(F32)
        go_ref[...] = go
        got_ref[...] = go.T
        qt_ref[...] = q_ref[...].astype(F32).T
        gq_acc[...] = jnp.zeros_like(gq_acc)
        gk_acc[...] = jnp.zeros_like(gk_acc)
        gv_acc[...] = jnp.zeros_like(gv_acc)
        zpre_ref[...] = jnp.zeros_like(zpre_ref)
        zpost_ref[...] = jnp.zeros_like(zpost_ref)

    half = rows // 2
    at = place_ref[1 + parts]
    lane = lax.broadcasted_iota(jnp.int32, tabt_ref.shape[1:], 1)
    gs = [step * GB + u for u in range(GB)]
    cols = []
    for g in gs:
        pre_col = jnp.sum(jnp.where(lane == g, tabt_ref[0], 0.0), 1, keepdims=True)
        post_col = jnp.sum(jnp.where(lane == heads + g, tabt_ref[0], 0.0), 1, keepdims=True)
        cols.append((pre_col, post_col))

    def work(second, keys):
        here = pl.ds(pl.multiple_of(second * half, half), half)
        go = go_ref[here, :]
        q = q_ref[here, :].astype(F32)
        mixed = [go * tab_ref[0, pl.ds(heads + g, 1), :] for g in gs]
        gp = dot_nt(jnp.concatenate([x.astype(BF16) for x in mixed], 0), v_ref[:keys, :])
        gms, ps, zposts = [], [], []
        for u in range(GB):
            ctx = u_ref[u, here, :].astype(F32)
            zposts.append(jnp.sum(ctx * go, axis=0, keepdims=True))
            delta = jnp.sum(ctx * mixed[u], axis=1, keepdims=True)
            p = p_ref[u, here, :keys]
            gms.append((p.astype(F32) * (gp[u * half : (u + 1) * half] - delta)).astype(BF16))
            ps.append(p)
        gm = jnp.concatenate(gms, 0)
        t = dot_nn(gm, k_ref[:keys, :])
        total = gq_acc[here, :]
        zpres = []
        for u in range(GB):
            tu = t[u * half : (u + 1) * half]
            zpres.append(jnp.sum(tu * q, axis=0, keepdims=True))
            total = total + tu * tab_ref[0, pl.ds(gs[u], 1), :]
        gq_acc[here, :] = total
        qm = jnp.concatenate([(qt_ref[:, here] * pre).astype(BF16) for pre, _ in cols], 1)
        gk_acc[:, :keys] += dot_nn(qm, gm)
        gm2 = jnp.concatenate([(got_ref[:, here] * post).astype(BF16) for _, post in cols], 1)
        gv_acc[:, :keys] += dot_nn(gm2, jnp.concatenate(ps, 0))
        return zpres, zposts

    for pairs in range(1, blocks + 1):
        is_late = at == blocks - pairs

        @pl.when(is_late | (at == pairs - 1))
        def _(pairs=pairs, is_late=is_late):
            zpres, zposts = work(is_late.astype(jnp.int32), 2 * pairs * half)
            for u, g in enumerate(gs):
                zpre_ref[pl.ds(g, 1), :] += zpres[u]
                zpost_ref[pl.ds(g, 1), :] += zposts[u]

    @pl.when(step == pl.num_programs(0) - 1)
    def _():
        for copy in late:
            copy.wait()
        gq = gq_acc[...].astype(BF16)
        gkt = gk_acc[...].astype(BF16)
        gvt = gv_acc[...].astype(BF16)
        ga = ga_ref[...]
        for r in range(blocks):
            there = [pl.ds(pl.multiple_of(chunk_of(at ^ r, x, blocks, False) * half, half), half) for x in range(2)]
            gk = jnp.concatenate([gk_acc[:, x].T.astype(BF16) for x in there], 0)
            gv = jnp.concatenate([gv_acc[:, x].T.astype(BF16) for x in there], 0)
            gn1 = dot_nt(gk, wqkv_ref[:, width : 2 * width]) + dot_nt(gv, wqkv_ref[:, 2 * width :])
            if r == 0:
                gn1 = gn1 + dot_nt(gq, wqkv_ref[:, :width])
            gn1_refs[r][...] = gn1.astype(BF16)
        hand = width // 2
        per = hand // PIECES
        own = [pl.ds(pl.multiple_of(chunk_of(at, x, blocks, False) * half, half), half) for x in range(2)]
        for side in range(2):
            core = place_ref[0] if side == 0 else 1 - place_ref[0]
            mine = pl.ds(pl.multiple_of(core * hand, hand), hand)
            n1t = n1t_ref[mine, :]
            n1t_own = jnp.concatenate([n1t_ref[mine, x] for x in own], 1)
            grads = (
                lambda: dot_nn(n1t_own, gq),
                lambda: dot_nt(n1t, gkt),
                lambda: dot_nt(n1t, gvt),
                lambda: dot_nn(ot_ref[mine, :], ga),
            )
            for index, grad in enumerate(grads):
                part = index * parts // len(grads)
                column = (index - part * (len(grads) // parts)) * width
                value = grad().astype(BF16)
                for piece in range(PIECES):
                    there = pl.multiple_of((piece ^ place_ref[1 + part]) * per, per)
                    grad_refs[2 * part + side][pl.ds(there, per), column : column + width] = value[
                        piece * per : (piece + 1) * per
                    ]


def attn_bwd(layer, blocks, ga, w_out, q, k, v, p, u, tab, tabt, place, w_qkv, n1t, ot):
    rows, width = q.shape
    keys = k.shape[0]
    heads = p.shape[0]
    parts = place.shape[0] - 2
    args = (ga, w_out, q, k, v, p, u, tab, tabt, place, w_qkv, n1t, ot)
    in_specs = [whole(a.shape) for a in args]
    in_specs[1] = layer_of(w_out, layer)
    in_specs[5] = pl.BlockSpec((GB, rows, keys), lambda i: (i, 0, 0))
    in_specs[6] = pl.BlockSpec((GB, rows, width), lambda i: (i, 0, 0))
    in_specs[7] = layer_of(tab, layer)
    in_specs[8] = layer_of(tabt, layer)
    in_specs[9] = pl.BlockSpec(memory_space=pltpu.SMEM)
    in_specs[10:13] = [pl.BlockSpec(memory_space=pl.ANY)] * 3
    out = (
        [((rows, width), BF16)] * blocks
        + [((width // 2, 4 // parts * width), BF16)] * (2 * parts)
        + [((heads, width), F32)] * 2
    )
    res = pl.pallas_call(
        functools.partial(attn_bwd_body, heads, blocks, layer, parts),
        grid=(heads // GB,),
        in_specs=in_specs,
        out_specs=[whole(s) for s, _ in out],
        out_shape=[jax.ShapeDtypeStruct(s, d) for s, d in out],
        scratch_shapes=[
            pltpu.VMEM((rows, width), F32),
            pltpu.VMEM((width, rows), F32),
            pltpu.VMEM((width, rows), F32),
            pltpu.VMEM((rows, width), F32),
            pltpu.VMEM((width, keys), F32),
            pltpu.VMEM((width, keys), F32),
            pltpu.VMEM(w_qkv.shape[1:], BF16),
            pltpu.VMEM(n1t.shape, BF16),
            pltpu.VMEM(ot.shape, BF16),
            pltpu.SemaphoreType.DMA((3,)),
        ],
        compiler_params=pltpu.CompilerParams(vmem_limit_bytes=VMEM),
        cost_estimate=pl.CostEstimate(
            flops=2 * rows * keys * width * heads * 4 * 2, bytes_accessed=20_000_000, transcendentals=0
        ),
        name="attn_bwd",
    )(*args)
    return res[:blocks], res[blocks:-2], res[-2], res[-1]


def expand_body(parts, place_ref, *refs):
    qkv_ref, out_ref = refs[-2:]
    width3 = qkv_ref.shape[2]
    inner = PIECES // GROUPS
    per = qkv_ref.shape[1] // inner
    column = 0
    for part, ref in enumerate(refs[:parts]):
        end = column + ref.shape[1]
        cut = min(end, width3)
        for piece in range(inner):
            here = slice(piece * per, (piece + 1) * per)
            there = piece ^ lax.rem(place_ref[1 + part], inner)
            value = ref[pl.ds(pl.multiple_of(there * per, per), per), :].astype(F32)
            qkv_ref[0, here, column:cut] = value[:, : cut - column]
            if end > width3:
                out_ref[0, here, :] = value[:, cut - column :]
        column = end


def expand(layer, side, place, halves, before=()):
    half = halves[0].shape[0]
    width = sum(h.shape[1] for h in halves) // 4
    per = half // GROUPS
    in_specs = []
    for part, array in enumerate(halves):

        def piece(i, place, part=part):
            return i ^ (place[1 + part] // (PIECES // GROUPS)), 0

        in_specs.append(pl.BlockSpec((per, array.shape[1]), piece))
    first = 1 + len(halves)
    in_specs += [pl.BlockSpec(memory_space=pl.ANY)] * len(before)

    def there(i, place):
        return layer, (place[0] ^ side) * GROUPS + i, 0

    return pl.pallas_call(
        functools.partial(expand_body, len(halves)),
        grid_spec=pltpu.PrefetchScalarGridSpec(
            num_scalar_prefetch=1,
            grid=(GROUPS,),
            in_specs=in_specs,
            out_specs=[pl.BlockSpec((1, per, 3 * width), there), pl.BlockSpec((1, per, width), there)],
        ),
        out_shape=[
            jax.ShapeDtypeStruct((LAYERS, 2 * half, 3 * width), F32),
            jax.ShapeDtypeStruct((LAYERS, 2 * half, width), F32),
        ],
        input_output_aliases={first + i: i for i in range(len(before))},
        compiler_params=pltpu.CompilerParams(vmem_limit_bytes=SMALL),
        cost_estimate=pl.CostEstimate(flops=0, bytes_accessed=7_000_000, transcendentals=0),
        name="expand",
    )(place, *halves, *before)


def ffn_fwd_body(blocks, *refs):
    n_refs = refs[:blocks]
    win_ref, wdown_ref = refs[blocks : blocks + 2]
    out_refs = refs[blocks + 2 : 2 * blocks + 2]
    hid_ref, dgelu_ref = refs[2 * blocks + 2 :]
    rows = n_refs[0].shape[0]
    for r in range(blocks):
        here = pl.ds(r * rows, rows)
        pre = dot_nn(n_refs[r][...], win_ref[0])
        cdf = 0.5 + 0.5 * lax.erf(pre * (0.5**0.5))
        hid = (pre * cdf).astype(BF16)
        hid_ref[here, :] = hid
        density = jnp.exp2(pre * pre * (-0.5 * LOG2E)) * 0.3989422804014327
        dgelu_ref[here, :] = (cdf + pre * density).astype(BF16)
        out_refs[r][...] = dot_nn(hid, wdown_ref[0]).astype(BF16)


def ffn_fwd(layer, n_blocks, w_in, w_down):
    blocks = len(n_blocks)
    rows, width = n_blocks[0].shape
    hidden = w_in.shape[2]
    args = (*n_blocks, w_in, w_down)
    in_specs = [whole(a.shape) for a in args]
    in_specs[blocks] = layer_of(w_in, layer)
    in_specs[blocks + 1] = layer_of(w_down, layer)
    out = [((rows, width), BF16)] * blocks + [((rows * blocks, hidden), BF16)] * 2
    res = pl.pallas_call(
        functools.partial(ffn_fwd_body, blocks),
        grid=(1,),
        in_specs=in_specs,
        out_specs=[whole(s) for s, _ in out],
        out_shape=[jax.ShapeDtypeStruct(s, d) for s, d in out],
        compiler_params=pltpu.CompilerParams(vmem_limit_bytes=SMALL),
        cost_estimate=pl.CostEstimate(
            flops=4 * rows * blocks * width * hidden, bytes_accessed=6_000_000, transcendentals=rows * blocks * hidden
        ),
        name="ffn_fwd",
    )(*args)
    return res[:blocks], res[blocks], res[blocks + 1]


def ffn_bwd_body(blocks, *refs):
    g_refs = refs[:blocks]
    dgelu_ref, win_ref, wdown_ref = refs[blocks : blocks + 3]
    out_refs = refs[blocks + 3 : 2 * blocks + 3]
    gpre_ref = refs[2 * blocks + 3]
    rows = g_refs[0].shape[0]
    for r in range(blocks):
        here = pl.ds(r * rows, rows)
        gh = dot_nt(g_refs[r][...], wdown_ref[0])
        gpre = (gh * dgelu_ref[here, :].astype(F32)).astype(BF16)
        gpre_ref[here, :] = gpre
        out_refs[r][...] = dot_nt(gpre, win_ref[0]).astype(BF16)


def ffn_bwd(layer, g_blocks, dgelu, w_in, w_down):
    blocks = len(g_blocks)
    rows, width = g_blocks[0].shape
    hidden = w_in.shape[2]
    args = (*g_blocks, dgelu, w_in, w_down)
    in_specs = [whole(a.shape) for a in args]
    in_specs[blocks + 1] = layer_of(w_in, layer)
    in_specs[blocks + 2] = layer_of(w_down, layer)
    out = [((rows, width), BF16)] * blocks + [((rows * blocks, hidden), BF16)]
    res = pl.pallas_call(
        functools.partial(ffn_bwd_body, blocks),
        grid=(1,),
        in_specs=in_specs,
        out_specs=[whole(s) for s, _ in out],
        out_shape=[jax.ShapeDtypeStruct(s, d) for s, d in out],
        compiler_params=pltpu.CompilerParams(vmem_limit_bytes=SMALL),
        cost_estimate=pl.CostEstimate(
            flops=4 * rows * blocks * width * hidden, bytes_accessed=6_000_000, transcendentals=0
        ),
        name="ffn_bwd",
    )(*args)
    return res[:blocks], res[blocks]


def ffn_grads_body(blocks, chunks, *refs):
    n_refs, g_refs = refs[:blocks], refs[blocks : 2 * blocks]
    hid_refs, gpre_refs = refs[2 * blocks : 2 * blocks + 2], refs[2 * blocks + 2 : 2 * blocks + 4]
    out_ref = refs[-1]
    rows, width = n_refs[0].shape
    per = width // chunks
    for part, (left_refs, right_refs) in enumerate(((n_refs, gpre_refs), (g_refs, hid_refs))):
        left = jnp.concatenate([ref[...].T for ref in left_refs], 1)
        right = jnp.concatenate([ref[...] for ref in right_refs], 0)
        grad = dot_nn(left, right).astype(BF16)
        for c in range(chunks):
            place = 2 * sum(((c >> i) & 1) * (chunks >> (i + 1)) for i in range(chunks.bit_length() - 1)) + part
            out_ref[place * per : (place + 1) * per, :] = grad[c * per : (c + 1) * per]


def ffn_grads(n_blocks, g_blocks, hids, gpres, chunks):
    blocks = len(n_blocks)
    rows, width = n_blocks[0].shape
    hidden = hids[0].shape[1]
    args = (*n_blocks, *g_blocks, *hids, *gpres)
    return pl.pallas_call(
        functools.partial(ffn_grads_body, blocks, chunks),
        grid=(1,),
        in_specs=[whole(a.shape) for a in args],
        out_specs=whole((2 * width, hidden)),
        out_shape=jax.ShapeDtypeStruct((2 * width, hidden), BF16),
        compiler_params=pltpu.CompilerParams(vmem_limit_bytes=VMEM),
        cost_estimate=pl.CostEstimate(
            flops=4 * rows * blocks * width * hidden, bytes_accessed=9_000_000, transcendentals=0
        ),
        name="ffn_grads",
    )(*args)


def swap(value, axis, bit):
    size = lax.axis_size(axis)
    return lax.ppermute(value, axis, [(i, i ^ bit) for i in range(size)])


def after(values, *done):
    return lax.optimization_barrier((values, done))[0]


def gather_near(value):
    half = lax.axis_size("tp") // 2
    far = swap(value, "tp", half)
    near = [value]
    bit = 1
    while bit < half:
        near += [swap(b, "tp", bit) for b in near]
        bit *= 2
    return near, far


def gather_far(far):
    half = lax.axis_size("tp") // 2
    blocks = [far]
    bit = 1
    while bit < half:
        blocks += [swap(b, "tp", bit) for b in blocks]
        bit *= 2
    return blocks


def gather_blocks(value):
    near, far = gather_near(value)
    return near + gather_far(far)


def scatter_begin(blocks):
    blocks = list(blocks)
    bit = 1
    while bit < lax.axis_size("tp") // 2:
        size = len(blocks)
        keep = [blocks[r] for r in range(size) if not r & 1]
        sent = [swap(blocks[r], "tp", bit) for r in range(size) if r & 1]
        blocks = [a.astype(F32) + b.astype(F32) for a, b in zip(keep, sent)]
        bit *= 2
        blocks = [blocks[0]] + [b.astype(BF16) for b in blocks[1:]]
    return blocks[0].astype(F32), swap(blocks[1], "tp", bit)


def halve_begin(part, axis, bit):
    mine = (lax.axis_index(axis) // bit) & 1
    pair = part.reshape(2, part.shape[0] // 2, part.shape[1])
    sent = lax.dynamic_index_in_dim(pair, 1 - mine, 0, keepdims=False)
    kept = lax.dynamic_index_in_dim(pair, mine, 0, keepdims=False)
    return kept, swap(sent, axis, bit)


def halve_end(kept, got):
    return (kept.astype(F32) + got.astype(F32)).astype(BF16)


class Scatter:
    def __init__(self, parts, steps):
        self.steps = list(steps)
        self.begin(parts)

    def begin(self, parts):
        step = self.steps.pop(0)
        self.kept, self.got = zip(*[halve_begin(part, *step) for part in parts])

    def advance(self, *done):
        if self.steps:
            got = after(self.got, *done)
            self.begin([halve_end(a, b) for a, b in zip(self.kept, got)])

    def finish(self, *done):
        while self.steps:
            self.advance(*done)
        return [a.astype(F32) + b.astype(F32) for a, b in zip(self.kept, after(self.got, *done))]


def steps_of(axis):
    return [(axis, 1 << i) for i in range(lax.axis_size(axis).bit_length() - 1)]


HALVINGS = PIECES.bit_length() - 1


def place_of(order):
    number = 0
    for axis, bit in order[:HALVINGS]:
        number = 2 * number + ((lax.axis_index(axis) // bit) & 1)
    return number


def sum_start(part, order, stage):
    if stage < HALVINGS:
        rows = part.shape[0] // 2
        return part[:rows], swap(part[rows:], *order[stage])
    return part, swap(part, *order[stage])


def spread(part, got):
    return jnp.concatenate([part, got], 0)


class Butterfly:
    def __init__(self, value):
        self.value = value
        self.steps = steps_of("tp") + steps_of("dp")
        self.got = None

    def start(self):
        if self.steps:
            self.got = swap(self.value, *self.steps.pop(0))
            return [self.got]
        return []

    def end(self, got):
        for g in got:
            self.value = self.value + g


def on_device(
    x_in, segments, w_qkv, w_out, mix_pre, mix_post, gain_attn, gain_ffn, w_in, w_down, cotangent
):
    rows, _, width = x_in.shape
    heads = mix_pre.shape[1]
    head_size = width // heads
    tp_size = lax.axis_size("tp")
    dp_size = lax.axis_size("dp")
    tp_index = lax.axis_index("tp")
    seg = segments[:, 0]
    side = rows // 2
    span = jnp.arange(side, dtype=jnp.int32)
    starts = [chunk_of(tp_index, x, tp_size, False) * side for x in range(2)]
    qpos = jnp.concatenate([start + span for start in starts])
    qseg = jnp.concatenate([lax.dynamic_slice_in_dim(seg, start, side, 0) for start in starts])
    qinfo = jnp.stack([qpos, qseg] + [qpos] * 6, 1)
    kinfo = jnp.pad(jnp.stack([jnp.arange(seg.shape[0], dtype=jnp.int32), seg]), ((0, 6), (0, 0)))
    where = (qinfo, kinfo, tp_index[None])

    of_head = (jnp.arange(width)[:, None] // head_size == jnp.arange(heads)[None]).astype(F32)

    def head_sums(rows_of_features):
        return jnp.dot(rows_of_features, of_head, precision=lax.Precision.HIGHEST)

    def mirror(value):
        moved = lax.ppermute(value[side:], "tp", [(i, tp_size - 1 - i) for i in range(tp_size)])
        return value[:side], moved

    tab = jnp.concatenate([jnp.swapaxes(mix_pre, 1, 2) * (head_size**-0.5), mix_post], 1)
    tabt = jnp.pad(jnp.repeat(jnp.swapaxes(tab, 1, 2), head_size, axis=1), ((0, 0), (0, 0), (0, 128 - 2 * heads)))
    tab = jnp.repeat(tab, head_size, axis=2)

    stream = x_in[:, 0].astype(F32)
    x_folded = jnp.concatenate(mirror(x_in[:, 0]), 0).astype(F32)
    kept = []
    half = tp_size // 2
    for layer in range(LAYERS):
        last = layer == LAYERS - 1
        n1_blocks = gather_blocks(rms(stream, gain_attn[layer]).astype(BF16))
        if last:
            low, n1_blocks[half] = after((cotangent[:, 0], n1_blocks[half]))
            grad_near, grad_far = gather_near(low)
        else:
            stream = x_folded
        p, u, q, k, v, ot, n1t, middle, n2 = attn_fwd(
            layer,
            layer == 0,
            n1_blocks,
            stream,
            w_qkv,
            w_out,
            tab,
            gain_ffn,
            where,
        )
        if last:
            n2, grad_near, grad_far = after((n2, grad_near, grad_far))
        near, far = gather_near(n2)
        out_a, hid_a, dgelu_a = ffn_fwd(layer, near, w_in, w_down)
        if last:
            given = grad_near + gather_far(grad_far)
            gf_blocks = [jnp.concatenate([given[r][:side], given[tp_size - 1 - r][side:]], 0) for r in range(tp_size)]
            gn2_a, gpre_a = ffn_bwd(layer, gf_blocks[:half], dgelu_a, w_in, w_down)
            far, gpre_a = after((far, gpre_a))
        far, hid_a = after((far, hid_a))
        n2_blocks = near + gather_far(far)
        out_b, hid_b, dgelu_b = ffn_fwd(layer, n2_blocks[half:], w_in, w_down)
        kept.append((stream, n1t, p, u, q, k, v, ot, middle, n2_blocks, hid_a, hid_b, dgelu_a, dgelu_b))
        if not last:
            own, far = scatter_begin([*out_a, *out_b])
            stream = middle + (own + far.astype(F32))

    grad_flow = gf_blocks[0].astype(F32)
    per = width // dp_size
    small = [None] * LAYERS
    sharded = [None] * LAYERS
    for layer in range(LAYERS - 1, -1, -1):
        last = layer == LAYERS - 1
        stream, n1t, p, u, q, k, v, ot, middle, n2_blocks, hid_a, hid_b, dgelu_a, dgelu_b = kept[layer]
        if not last:
            near, far = gather_near(grad_flow.astype(BF16))
            gn2_a, gpre_a = ffn_bwd(layer, near, dgelu_a, w_in, w_down)
            far, gpre_a = after((far, gpre_a))
            gf_blocks = near + gather_far(far)
        gn2_b, gpre_b = ffn_bwd(layer, gf_blocks[half:], dgelu_b, w_in, w_down)
        if not last:
            total_got, gpre_b = after((total_got, gpre_b))
            total = halve_end(total_kept, total_got)
            total_kept, total_got = sum_start(total, total_order, 1)
        own, far = scatter_begin([*gn2_a, *gn2_b])
        packed = ffn_grads(n2_blocks, gf_blocks, (hid_a, hid_b), (gpre_a, gpre_b), dp_size)
        far, packed = after((far, packed))
        if not last:
            total_got, packed = after((total_got, packed))
            total = halve_end(total_kept, total_got)
            total_kept, total_got = sum_start(total, total_order, 2)
        if not last:
            previous = moving
        moving = Scatter([packed], steps_of("dp"))
        gn2 = (own + far.astype(F32)).astype(BF16).astype(F32)
        grad_norm, grad_gffn = rms_back(gn2, middle, gain_ffn[layer])
        grad_middle = grad_flow + grad_norm
        ga = grad_middle.astype(BF16)
        if last:
            orders = [steps_of("dp") + steps_of("tp")[1:]]
        else:
            (y_step, *dp_rest), x_steps = steps_of("dp"), steps_of("tp")[1:]
            orders = [x_steps + [y_step] + dp_rest, [y_step] + x_steps + dp_rest]
        place = jnp.stack([tp_index & 1] + [place_of(order) for order in orders] + [tp_index])
        parts, grads, zpre, zpost = attn_bwd(
            layer, tp_size, ga, w_out, q, k, v, p, u, tab, tabt, place, w_qkv, n1t, ot
        )
        core_step = steps_of("tp")[0]
        if last:
            parts, grads, moving.got = after((parts, grads, moving.got))
            y_middle = middle
            keep, send = grads
            total = halve_end(keep, swap(send, *core_step))
            own, far = scatter_begin(parts)
            moving.advance()
            far, moving.got = after((far, moving.got), total)
            moving.advance()
            (total_order,), total_place = orders, place
            total_kept, total_got = sum_start(total, total_order, 0)
        else:
            parts, grads, moving.got, total_got, previous.got = after(
                (parts, grads, moving.got, total_got, previous.got)
            )
            (summed,) = previous.finish()
            sharded[layer + 1] = (summed[:per], summed[per:].T)
        if not last:
            break
        gn1 = (own + far.astype(F32)).astype(BF16).astype(F32)
        grad_norm, grad_gattn = rms_back(gn1, stream, gain_attn[layer])
        grad_flow = grad_middle + grad_norm
        grad_mpre = head_sums(zpre).T * (head_size**-0.5)
        grad_mpost = head_sums(zpost)
        small[layer] = (grad_mpre, grad_mpost, grad_gattn, grad_gffn)

    total = halve_end(total_kept, total_got)
    grads, total = after((grads, total))
    got = [swap(send, *core_step) for send in grads[1::2]]
    pieces = [halve_end(keep, g) for keep, g in zip(grads[::2], got)]
    for stage in range(HALVINGS, len(total_order)):
        total_got = swap(total, *total_order[stage])
        pieces, total_got = after((pieces, total_got))
        total = halve_end(total, total_got)
    for stage in range(HALVINGS):
        kept, got = zip(*[sum_start(part, order, stage) for part, order in zip(pieces, orders)])
        if stage == 0:
            by_last, by_middle = [swap(total, *step) for step in total_order[HALVINGS - 1 : 0 : -1]]
            got, by_last, by_middle = after((got, by_last, by_middle))
            near_rows = spread(total, by_last)
        elif stage == 1:
            near_got = swap(near_rows, *total_order[0])
            by_both = swap(by_last, *total_order[1])
            got, by_both = after((got, by_both))
            far_rows = spread(by_middle, by_both)
        else:
            total_got = swap(far_rows, *total_order[0])
            got, near_got = after((got, near_got))
        if stage == HALVINGS - 1:
            got, far = after((got, far))
        pieces = [halve_end(a, b) for a, b in zip(kept, after(got))]
        if stage == HALVINGS - 1:
            gn1 = (own + far.astype(F32)).astype(BF16).astype(F32)
            grad_norm, grad_gattn = rms_back(gn1, stream, gain_attn[layer])
            grad_flow = grad_middle + grad_norm
            grad_mpre = head_sums(zpre).T * (head_size**-0.5)
            grad_mpost = head_sums(zpost)
            small[layer] = (grad_mpre, grad_mpost, grad_gattn, grad_gffn)
            mixes = jnp.concatenate([a.reshape(-1) for s in small for a in s[:2]])
            count = mixes.shape[0]
            mix_rows = -(-count // width)
            flat = jnp.concatenate(
                [jnp.pad(mixes, (0, mix_rows * width - count)).reshape(mix_rows, width)]
                + [g[None] for s in small for g in s[2:]]
            )
            flat = jnp.pad(flat, ((0, -flat.shape[0] % 8), (0, 0)))
            flat = Butterfly(flat)
        if stage == 1:
            moving.advance(*pieces)
            y_parts, parts, pieces = after(([*out_a, *out_b], parts, pieces))
            own, far = scatter_begin(parts)
            own_y, far_y = scatter_begin(y_parts)
    for stage in range(HALVINGS, len(orders[0])):
        got = [swap(part, *order[stage]) for part, order in zip(pieces, orders)]
        if stage == HALVINGS:
            flat.end(flat.start())
        flat_got = flat.start()
        if stage == HALVINGS:
            first_rows, second_rows = mirror(grad_flow)
            got, second_rows, total_got, moving.got, far_y = after((got, second_rows, total_got, moving.got, far_y))
            y_out = (y_middle + (own_y + far_y.astype(F32))).astype(BF16)
            y_first, y_second = mirror(y_out)
            grad_x = jnp.concatenate([first_rows, second_rows], 0)
            total = jnp.concatenate([near_rows, far_rows, near_got, total_got], 0)
            moving.advance()
        got, flat_got = after((got, flat_got))
        flat.end(flat_got)
        pieces = [halve_end(a, b) for a, b in zip(pieces, got)]
    total_other = swap(total, *core_step)
    replicated = ()
    for stage in range(HALVINGS - 1, -1, -1):
        got = [swap(part, *order[stage]) for part, order in zip(pieces, orders)]
        flat_got = flat.start()
        if stage == HALVINGS - 1:
            got, total_other = after((got, total_other))
        elif stage == HALVINGS - 2:
            replicated = expand(1, 0, total_place, [total])
            got, replicated, moving.got, y_second = after((got, replicated, moving.got, y_second))
            y_out = jnp.concatenate([y_first, y_second], 0)[:, None]
            (summed,) = moving.finish()
            sharded[0] = (summed[:per], summed[per:].T)
            sharded = [jnp.stack(members) for members in zip(*sharded)]
            grad_x = grad_x[:, None]
        elif stage == 0:
            replicated = expand(1, 1, total_place, [total_other], replicated)
            got, replicated, sharded, grad_x, y_out = after((got, replicated, sharded, grad_x, y_out))
        got, flat_got = after((got, flat_got))
        flat.end(flat_got)
        pieces = [spread(a, b) for a, b in zip(pieces, got)]
    got = [swap(part, *core_step) for part in pieces]
    while flat.steps:
        flat.end(flat.start())
    flat = flat.value
    replicated = expand(0, 0, place, pieces, replicated)
    got, replicated = after((got, replicated))
    replicated = expand(0, 1, place, got, replicated)
    mixes = flat[:mix_rows].reshape(-1)[:count].reshape(LAYERS, 2, heads, heads)
    gains = flat[mix_rows : mix_rows + 2 * LAYERS].reshape(LAYERS, 2, width)
    return (
        y_out,
        grad_x,
        *replicated,
        mixes[:, 0],
        mixes[:, 1],
        gains[:, 0],
        gains[:, 1],
        *sharded,
    )


def solution(mesh):
    in_specs = (
        P("tp", "dp", None),
        P(None, "dp"),
        P(),
        P(),
        P(),
        P(),
        P(),
        P(),
        P(None, None, "tp"),
        P(None, "tp", None),
        P("tp", "dp", None),
    )
    out_specs = (
        P("tp", "dp", None),
        P("tp", "dp", None),
        P(),
        P(),
        P(),
        P(),
        P(),
        P(),
        P(None, "dp", "tp"),
        P(None, "tp", "dp"),
    )
    return jax.shard_map(
        on_device, mesh=mesh, in_specs=in_specs, out_specs=out_specs, check_vma=False
    )
```
